32 devices in a mesh: seq: 4 (over y, x), batch: 8 (over z, core).
Axes of the slice: x: 2, y: 2, z: 4, core: 2. Of those that a mesh axis runs over, the one named last changes fastest.
Arguments:
- inputs: bfloat16 [8, 512, 2048], P('batch', 'seq'), may hold values from -6 to 6
- cotangent: bfloat16 [8, 512, 2048], P('batch', 'seq'), may hold values from -6 to 6
- doc_lengths: int32 [8, 4], P('batch'), may hold values from 1 to 509, as said below
- head_width: int32 [8], P('batch'), may hold values from 16 to 64, as said below
- pre_gain: float32 [2048], replicated, may hold values from 0.5 to 1.5
- in_weight: bfloat16 [2048, 8448], P(('seq', 'batch')), may hold values from -0.125 to 0.125
- step_weight: bfloat16 [2048, 64], P(('seq', 'batch')), may hold values from -0.125 to 0.125
- conv_weight: float32 [4, 4352], replicated, may hold values from -0.8 to 0.8
- conv_bias: float32 [4352], replicated, may hold values from -0.5 to 0.5
- step_bias: float32 [64], replicated, may hold values from -7 to -5
- decay_log: float32 [64], replicated, may hold values from -2.3 to 3
- skip_gain: float32 [64], replicated, may hold values from 0.5 to 1.5
- norm_gain: float32 [4096], replicated, may hold values from 0.5 to 1.5
- out_weight: bfloat16 [4096, 2048], P(('seq', 'batch')), may hold values from -0.09375 to 0.09375
Outputs:
- output: bfloat16 [8, 512, 2048], P('batch', 'seq')
- grad_inputs: float32 [8, 512, 2048], P('batch', 'seq')
- grad_pre_gain: float32 [2048], replicated
- grad_in_weight: float32 [2048, 8448], P(('seq', 'batch'))
- grad_step_weight: float32 [2048, 64], P(('seq', 'batch'))
- grad_conv_weight: float32 [4, 4352], replicated
- grad_conv_bias: float32 [4352], replicated
- grad_step_bias: float32 [64], replicated
- grad_decay_log: float32 [64], replicated
- grad_skip_gain: float32 [64], replicated
- grad_norm_gain: float32 [4096], replicated
- grad_out_weight: float32 [4096, 2048], P(('seq', 'batch'))
The draws below stay inside these ranges and needn't reach their ends.
Inputs may be any that keep to these rules, and one draw needn't show every extreme that they name: `doc_lengths`: each row holds the lengths of the 4 documents of one packed sequence in order; they sum to 512. Some sequence has a document of the most length. `head_width`: heads used by each sequence's nested model, a multiple of a quarter of 64; some sequence uses all 64.
All inputs are finite; a program needn't handle non-finite values.
Results may differ from the reference program's by a relative error of at most 0.0095.
Values may be sent and summed in bfloat16 or wider, within the bound.
A program may use at most 448 MiB of HBM per device.

```python
from functools import partial
import jax
import jax.numpy as jnp
from jax import lax

D = 2048
H = 64
P_SIZE = 64
N = 128
CONV = 4
DOCS = 4
TOK_DEV = 128
E = 4096
CH = 4352
SEQS = 8
LENGTH = 512


def draw_doc_lengths(key, part):
    key = jax.random.fold_in(key, 11)
    first_key, second_key, third_key = jax.random.split(key, 3)
    short_docs = jax.random.randint(first_key, (SEQS, DOCS), 1, TOK_DEV // 4 + 1)
    long_slot = jax.random.randint(second_key, (SEQS, 1), 0, DOCS)
    tight_seq = jax.random.randint(third_key, (), 0, SEQS)
    short_docs = jnp.where((jnp.arange(SEQS) == tight_seq)[:, None], 1, short_docs)
    slot_ids = jnp.arange(DOCS)[None, :]
    others = jnp.sum(jnp.where(slot_ids == long_slot, 0, short_docs), axis=1, keepdims=True)
    return jnp.where(slot_ids == long_slot, LENGTH - others, short_docs).astype(jnp.int32)


def draw_head_width(key, part):
    key = jax.random.fold_in(key, 23)
    first_key, second_key = jax.random.split(key)
    quarters = jax.random.randint(first_key, (SEQS,), 1, 5)
    full_at = jax.random.randint(second_key, (), 0, SEQS)
    quarters = jnp.where(jnp.arange(SEQS) == full_at, 4, quarters)
    return (quarters * (H // 4)).astype(jnp.int32)


def level_of(rng, shape, shards, least, largest):
    def one(axis_at, shards_of):
        draws = jax.random.uniform(jax.random.fold_in(jax.random.fold_in(rng, 6), axis_at), (shards_of,), jnp.float32, least / len(shards), largest / len(shards))
        return jnp.repeat(jnp.exp(draws), shape[axis_at] // shards_of).reshape((-1,) + (1,) * (len(shape) - axis_at - 1))

    gain = one(*shards[0])
    for cut in shards[1:]:
        gain = gain * one(*cut)
    return gain


def bell_draw(key, dims, deviation, most, cuts=(), kind=jnp.bfloat16):
    values = jax.random.normal(key, dims, jnp.float32) * deviation
    if len(cuts) > 0:
        values = level_of(key, dims, cuts, -0.22, 0.18) * values
    return jnp.clip(values, min=-most, max=most).astype(kind)


def setup_inputs(seed: int = 0) -> dict:
    key_list = jax.random.split(jax.random.key(seed), 15)
    return {
        "inputs": bell_draw(key_list[0], (SEQS, LENGTH, D), 1.0, 6.0, ((0, 8), (1, 4))),
        "cotangent": bell_draw(key_list[1], (SEQS, LENGTH, D), 1.0, 6.0, ((0, 8), (1, 4))),
        "doc_lengths": draw_doc_lengths(jax.random.fold_in(key_list[14], 71), 0),
        "head_width": draw_head_width(jax.random.fold_in(key_list[14], 71), 0),
        "pre_gain": jnp.clip(1.0 + 0.1 * jax.random.normal(key_list[4], (D,), jnp.float32), 0.5, 1.5),
        "in_weight": bell_draw(key_list[5], (D, E + CH), D ** -0.5, 0.125, ((0, 32),)),
        "step_weight": bell_draw(key_list[6], (D, H), D ** -0.5, 0.125, ((0, 32),)),
        "conv_weight": jnp.clip(jax.random.uniform(key_list[7], (CONV, CH), jnp.float32, -0.8, 0.8), -0.8, 0.8),
        "conv_bias": jnp.clip(jax.random.uniform(key_list[8], (CH,), jnp.float32, -0.5, 0.5), -0.5, 0.5),
        "step_bias": jnp.clip(jax.random.uniform(key_list[9], (H,), jnp.float32, -7.0, -5.0), -7.0, -5.0),
        "decay_log": jnp.clip(jax.random.uniform(key_list[10], (H,), jnp.float32, -2.3, 3.0), -2.3, 3.0),
        "skip_gain": jnp.clip(jax.random.uniform(key_list[11], (H,), jnp.float32, 0.5, 1.5), 0.5, 1.5),
        "norm_gain": jnp.clip(1.0 + 0.1 * jax.random.normal(key_list[12], (E,), jnp.float32), 0.5, 1.5),
        "out_weight": bell_draw(key_list[13], (E, D), E ** -0.5, 0.09375, ((0, 32),)),
    }


epsilon = 1e-05
highest = lax.Precision.HIGHEST

@jax.custom_vjp
def low(v):
    return lax.optimization_barrier(v.astype(jnp.bfloat16)).astype(jnp.float32)

@jax.custom_vjp
def low_back(v):
    return v

def low_keep(v):
    return (low(v), None)

def low_pass(kept, grad):
    return (grad,)

def back_keep(v):
    return (v, None)

def back_low(kept, grad):
    return (low(grad),)
low.defvjp(low_keep, low_pass)
low_back.defvjp(back_keep, back_low)

def matmul(left, right):
    return jnp.dot(left, right, precision=highest, preferred_element_type=jnp.float32)

def doc_index(places, doc_ends):
    return lax.optimization_barrier(jnp.sum((places[:, None] >= doc_ends[None, :-1]).astype(jnp.int32), axis=1))

def within_group(scores, same_doc, grouped):
    values, step_sizes, cum_decay = grouped
    spread = cum_decay[:, :, None] - cum_decay[:, None, :]
    decay_rows = jnp.where(same_doc[None], jnp.exp(jnp.minimum(spread, 0.0)), 0.0)
    weights = decay_rows * scores[None] * step_sizes[:, None, :]
    return jnp.einsum('gts,gsp->gtp', weights, values, precision=highest)

def block_scan(state_in, pieces):
    values, write_keys, read_keys, step_sizes, log_decay, doc_ids, inflow = pieces
    length_block = values.shape[0]
    cum_decay = jnp.cumsum(log_decay, axis=0)
    row_ids = jnp.arange(length_block)
    same_doc = (doc_ids[:, None] == doc_ids[None, :]) & (row_ids[:, None] >= row_ids[None, :])
    scores = matmul(read_keys, write_keys.T)
    group_size = H // 4
    grouped = (values.transpose(1, 0, 2).reshape(4, group_size, length_block, P_SIZE), step_sizes.T.reshape(4, group_size, length_block), cum_decay.T.reshape(4, group_size, length_block))
    within = lax.map(jax.checkpoint(partial(within_group, scores, same_doc)), grouped)
    within = within.reshape(H, length_block, P_SIZE).transpose(1, 0, 2)
    carry_weight = inflow[:, None] * jnp.exp(cum_decay)
    carried = jnp.einsum('tn,hpn->thp', read_keys, state_in, precision=highest) * carry_weight[:, :, None]
    final_weight = jnp.where((doc_ids == doc_ids[-1])[:, None], jnp.exp(cum_decay[-1][None, :] - cum_decay), 0.0) * step_sizes
    block_add = jnp.einsum('thp,tn->hpn', values * final_weight[:, :, None], write_keys, precision=highest)
    block_gain = inflow[-1] * jnp.exp(cum_decay[-1])
    return (block_gain[:, None, None] * state_in + block_add, within + carried)

def sequence_forward(params, pieces):
    pre_gain, in_weight, step_weight, conv_weight, conv_bias, step_bias, decay_log, skip_gain, norm_gain, out_weight = params
    seq_rows, lengths, head_count = pieces
    places = jnp.arange(LENGTH, dtype=jnp.int32)
    doc_ends = jnp.cumsum(lengths)
    doc_ids = doc_index(places, doc_ends)
    block_start = places // TOK_DEV * TOK_DEV
    inflow = (doc_ids == doc_index(block_start - 1, doc_ends)).astype(jnp.float32)
    inv_rms = lax.rsqrt(lax.optimization_barrier(jnp.mean(seq_rows * seq_rows, axis=1, keepdims=True)) + epsilon)
    normed = low(seq_rows * inv_rms * pre_gain[None, :])
    projected = low_back(matmul(normed, in_weight))
    gate_rows = projected[:, :E]
    conv_in = low(projected[:, E:])
    step_raw = low_back(matmul(normed, step_weight))
    padded = jnp.concatenate([jnp.zeros((CONV - 1, CH), jnp.float32), conv_in], axis=0)
    conv_sum = conv_bias[None, :] + jnp.zeros((LENGTH, CH), jnp.float32)
    for tap_index in range(CONV):
        source = places - (CONV - 1 - tap_index)
        valid_rows = ((source >= 0) & (doc_index(source, doc_ends) == doc_ids)).astype(jnp.float32)
        conv_sum = conv_sum + conv_weight[tap_index][None, :] * padded[tap_index:tap_index + LENGTH] * valid_rows[:, None]
    activated = low(jax.nn.silu(conv_sum))
    values = activated[:, :E].reshape(LENGTH, H, P_SIZE)
    write_keys = activated[:, E:E + N]
    read_keys = activated[:, E + N:]
    step_sizes = jax.nn.softplus(step_raw + step_bias[None, :])
    log_decay = -step_sizes * jnp.exp(decay_log)[None, :]
    blocks = LENGTH // TOK_DEV
    stacked = (values.reshape(blocks, TOK_DEV, H, P_SIZE), write_keys.reshape(blocks, TOK_DEV, N), read_keys.reshape(blocks, TOK_DEV, N), step_sizes.reshape(blocks, TOK_DEV, H), log_decay.reshape(blocks, TOK_DEV, H), doc_ids.reshape(blocks, TOK_DEV), inflow.reshape(blocks, TOK_DEV))
    _, mixer_rows = lax.scan(jax.checkpoint(block_scan), jnp.zeros((H, P_SIZE, N), jnp.float32), stacked)
    mixer_rows = mixer_rows.reshape(LENGTH, H, P_SIZE) + skip_gain[None, :, None] * values
    head_mask = (jnp.arange(H) < head_count).astype(jnp.float32)
    masked = (mixer_rows * head_mask[None, :, None]).reshape(LENGTH, E)
    gated_rows = masked * jax.nn.silu(gate_rows)
    mean_square = lax.optimization_barrier(jnp.sum(gated_rows * gated_rows, axis=1, keepdims=True)) / (head_count * P_SIZE).astype(jnp.float32)
    mixed_rows = low(gated_rows * lax.rsqrt(mean_square + epsilon) * norm_gain[None, :])
    return seq_rows + matmul(mixed_rows, out_weight)

def reference(inputs, cotangent, doc_lengths, head_width, pre_gain, in_weight, step_weight, conv_weight, conv_bias, step_bias, decay_log, skip_gain, norm_gain, out_weight):
    params = (pre_gain, in_weight.astype(jnp.float32), step_weight.astype(jnp.float32), conv_weight, conv_bias, step_bias, decay_log, skip_gain, norm_gain, out_weight.astype(jnp.float32))

    def forward(all_rows, params):

        def one_sequence(running, pieces):
            return (running, jax.checkpoint(sequence_forward)(params, pieces))
        _, outputs = lax.scan(one_sequence, jnp.zeros((), jnp.float32), (all_rows, doc_lengths, head_width))
        return outputs
    result, pullback = jax.vjp(forward, inputs.astype(jnp.float32), params)
    grad_inputs, grad_params = pullback(cotangent.astype(jnp.float32))
    return (result.astype(jnp.bfloat16), grad_inputs, grad_params[0], grad_params[1], grad_params[2], grad_params[3], grad_params[4], grad_params[5], grad_params[6], grad_params[7], grad_params[8], grad_params[9])
```

```python
from functools import partial

import jax
import jax.numpy as jnp
from jax import lax
from jax.experimental import pallas as pl
from jax.experimental.pallas import tpu as pltpu
from jax.sharding import PartitionSpec as P

H = 64
P_SIZE = 64
N = 128
CONV = 4
E = 4096
KEYS = 2 * N
STEP_PAD = 128
CHUNK = 128
epsilon = 1e-05
f32 = jnp.float32
bf16 = jnp.bfloat16


def mm(a, b, dims):
    return lax.dot_general(a, b, (dims, ((), ())), preferred_element_type=f32)


NN = ((1,), (0,))
NT = ((1,), (1,))
TN = ((0,), (0,))


def pair_cols(low, col, first):
    return jnp.where(low, col[:, first : first + 1], col[:, first + 1 : first + 2])


def scan_forward_kernel(
    act_ref, cum_ref, cum_t_ref, dt_ref, dt_t_ref, doc_ref, doc_t_ref, flow_ref, skip_ref, y_ref, state_ref, state
):
    heads = cum_ref.shape[1]
    inner = heads * P_SIZE

    @pl.when(pl.program_id(0) == 0)
    def _():
        state[...] = jnp.zeros_like(state)

    state_ref[0] = state[...].astype(bf16)
    cum = cum_ref[...]
    last = cum[CHUNK - 1 :, :]
    doc = doc_ref[...]
    doc_t = doc_t_ref[...]
    flow = flow_ref[...]
    rows = lax.broadcasted_iota(jnp.int32, (CHUNK, CHUNK), 0)
    cols = lax.broadcasted_iota(jnp.int32, (CHUNK, CHUNK), 1)
    bias = jnp.where((doc == doc_t) & (rows >= cols), 0.0, -1e30)
    carry_w = flow * jnp.exp(cum)
    final_w = jnp.where(doc == doc[CHUNK - 1 :, :], jnp.exp(last - cum), 0.0) * dt_ref[...]
    gain = carry_w[CHUNK - 1 :, :]
    low = cols < P_SIZE
    low_row = low[:1]
    write = act_ref[:, inner : inner + N]
    read = act_ref[:, inner + N :]
    write_t = write.astype(f32).T.astype(bf16)
    scores = mm(read, write, NT)
    for pair in range(heads // 2):
        first = 2 * pair
        lanes = slice(pair * 128, pair * 128 + 128)
        x = act_ref[:, lanes]
        xf = x.astype(f32)
        weights = []
        for h in (first, first + 1):
            decay = jnp.exp(cum[:, h : h + 1] - cum_t_ref[h : h + 1, :] + bias)
            weights.append((decay * scores * dt_t_ref[h : h + 1, :]).astype(bf16))
        stacked = jnp.concatenate(
            [jnp.where(low, xf, 0.0).astype(bf16), jnp.where(low, 0.0, xf).astype(bf16)], axis=0
        )
        old = state[:, lanes]
        y = mm(jnp.concatenate(weights, axis=1), stacked, NN)
        y = y + pair_cols(low, carry_w, first) * mm(read, old.astype(bf16), NN)
        y_ref[:, lanes] = y + skip_ref[:, lanes] * xf
        state[:, lanes] = pair_cols(low_row, gain, first) * old + mm(
            write_t, (pair_cols(low, final_w, first) * xf).astype(bf16), NN
        )


def scan_backward_kernel(
    act_ref, cum_ref, cum_t_ref, dt_ref, doc_ref, doc_t_ref, flow_ref, skip_ref, state_ref, dy_ref,
    dact_ref, dcum_ref, dcum_t_ref, ddt_ref, dskip_ref, dstate,
):
    heads = cum_ref.shape[1]
    inner = heads * P_SIZE

    @pl.when(pl.program_id(0) == 0)
    def _():
        dstate[...] = jnp.zeros_like(dstate)
        dskip_ref[...] = jnp.zeros_like(dskip_ref)

    cum = cum_ref[...]
    dt = dt_ref[...]
    last = cum[CHUNK - 1 :, :]
    doc = doc_ref[...]
    doc_t = doc_t_ref[...]
    flow = flow_ref[...]
    rows = lax.broadcasted_iota(jnp.int32, (CHUNK, CHUNK), 0)
    cols = lax.broadcasted_iota(jnp.int32, (CHUNK, CHUNK), 1)
    bias = jnp.where((doc == doc_t) & (cols >= rows), 0.0, -1e30)
    carry_w = flow * jnp.exp(cum)
    final_d = jnp.where(doc == doc[CHUNK - 1 :, :], jnp.exp(last - cum), 0.0)
    final_w = final_d * dt
    gain = carry_w[CHUNK - 1 :, :]
    low = cols < P_SIZE
    low_row = low[:1]
    write = act_ref[:, inner : inner + N]
    read = act_ref[:, inner + N :]
    read_t = read.astype(f32).T.astype(bf16)
    scores_t = mm(write, read, NT)
    dscores_t = jnp.zeros((CHUNK, CHUNK), f32)
    dwrite = jnp.zeros((CHUNK, N), f32)
    dread = jnp.zeros((CHUNK, N), f32)
    end_row = lax.broadcasted_iota(jnp.int32, (CHUNK, 1), 0) == CHUNK - 1
    dcum_cols = []
    dcum_rows = []
    ddt_cols = []
    for pair in range(heads // 2):
        first = 2 * pair
        lanes = slice(pair * 128, pair * 128 + 128)
        x = act_ref[:, lanes]
        xf = x.astype(f32)
        dy = dy_ref[:, lanes]
        dyb = dy.astype(bf16)
        x_stack = jnp.concatenate(
            [jnp.where(low, xf, 0.0).astype(bf16), jnp.where(low, 0.0, xf).astype(bf16)], axis=0
        )
        dy_stack = jnp.concatenate(
            [jnp.where(low, dy, 0.0).astype(bf16), jnp.where(low, 0.0, dy).astype(bf16)], axis=0
        )
        dweights = mm(x_stack, dyb, NT)
        old = state_ref[0, :, lanes]
        grad = dstate[:, lanes]
        gradb = grad.astype(bf16)
        carried = mm(read, old, NN)
        pushed = mm(write, gradb, NN)
        carry_p = pair_cols(low, carry_w, first)
        final_p = pair_cols(low, final_w, first)
        carry_prod = dy * carried
        final_prod = xf * pushed
        gain_prod = jnp.sum(grad * old.astype(f32), axis=0, keepdims=True)
        weights = []
        for which, h in enumerate((first, first + 1)):
            col = dt[:, h : h + 1]
            decay = jnp.exp(cum_t_ref[h : h + 1, :] - cum[:, h : h + 1] + bias)
            weighted = decay * col
            weights.append((weighted * scores_t).astype(bf16))
            dw = dweights[which * CHUNK : (which + 1) * CHUNK]
            dscores_t = dscores_t + dw * weighted
            direct = dw * decay * scores_t
            ddt_in = jnp.sum(direct, axis=1, keepdims=True)
            dcum_rows.append(jnp.sum(direct * col, axis=0, keepdims=True))
            half = low if which == 0 else ~low
            half_row = low_row if which == 0 else ~low_row
            carry_sum = jnp.sum(jnp.where(half, carry_prod, 0.0), axis=1, keepdims=True)
            final_sum = jnp.sum(jnp.where(half, final_prod, 0.0), axis=1, keepdims=True)
            push = final_w[:, h : h + 1] * final_sum
            at_end = jnp.sum(push, axis=0, keepdims=True) + gain[:, h : h + 1] * jnp.sum(
                jnp.where(half_row, gain_prod, 0.0), axis=1, keepdims=True
            )
            ddt_cols.append(ddt_in + final_d[:, h : h + 1] * final_sum)
            dcum_cols.append(
                carry_w[:, h : h + 1] * carry_sum - push - col * ddt_in + jnp.where(end_row, at_end, 0.0)
            )
        dx = mm(jnp.concatenate(weights, axis=1), dy_stack, NN)
        dact_ref[:, lanes] = dx + final_p * pushed + skip_ref[:, lanes] * dy
        dskip_ref[:, lanes] += jnp.sum(dy * xf, axis=0, keepdims=True)
        dwrite = dwrite + mm((final_p * xf).astype(bf16), gradb, NT)
        carry_dy = (carry_p * dy).astype(bf16)
        dread = dread + mm(carry_dy, old, NT)
        dstate[:, lanes] = pair_cols(low_row, gain, first) * grad + mm(read_t, carry_dy, NN)
    dsb = dscores_t.astype(bf16)
    dact_ref[:, inner : inner + N] = dwrite + mm(dsb, read, NN)
    dact_ref[:, inner + N :] = dread + mm(dsb, write, TN)
    dcum_ref[...] = jnp.concatenate(dcum_cols, axis=1)
    dcum_t_ref[...] = jnp.concatenate(dcum_rows, axis=0)
    ddt_ref[...] = jnp.concatenate(ddt_cols, axis=1)


def scan_forward(act, cum, cum_t, dt, dt_t, doc, doc_t, flow, skip):
    length, channels = act.shape
    heads = cum.shape[1]
    inner = heads * P_SIZE
    steps = length // CHUNK
    row = lambda width: pl.BlockSpec((CHUNK, width), lambda i: (i, 0))
    lane = lambda height: pl.BlockSpec((height, CHUNK), lambda i: (0, i))
    return pl.pallas_call(
        scan_forward_kernel,
        grid=(steps,),
        in_specs=[
            row(channels), row(heads), lane(heads), row(heads), lane(heads), row(1), lane(1), row(1),
            pl.BlockSpec((1, inner), lambda i: (0, 0)),
        ],
        out_specs=[row(inner), pl.BlockSpec((1, N, inner), lambda i: (i, 0, 0))],
        out_shape=[
            jax.ShapeDtypeStruct((length, inner), f32),
            jax.ShapeDtypeStruct((steps, N, inner), bf16),
        ],
        scratch_shapes=[pltpu.VMEM((N, inner), f32)],
        compiler_params=pltpu.CompilerParams(vmem_limit_bytes=40 * 2**20),
        cost_estimate=pl.CostEstimate(
            flops=length * inner * 1024, bytes_accessed=length * inner * 10, transcendentals=length * heads * CHUNK
        ),
    )(act, cum, cum_t, dt, dt_t, doc, doc_t, flow, skip)


def scan_backward(act, cum, cum_t, dt, doc, doc_t, flow, skip, states, dy):
    length, channels = act.shape
    heads = cum.shape[1]
    inner = heads * P_SIZE
    steps = length // CHUNK
    row = lambda width: pl.BlockSpec((CHUNK, width), lambda i: (steps - 1 - i, 0))
    lane = lambda height: pl.BlockSpec((height, CHUNK), lambda i: (0, steps - 1 - i))
    whole = pl.BlockSpec((1, inner), lambda i: (0, 0))
    return pl.pallas_call(
        scan_backward_kernel,
        grid=(steps,),
        in_specs=[
            row(channels), row(heads), lane(heads), row(heads), row(1), lane(1), row(1), whole,
            pl.BlockSpec((1, N, inner), lambda i: (steps - 1 - i, 0, 0)), row(inner),
        ],
        out_specs=[row(channels), row(heads), lane(heads), row(heads), whole],
        out_shape=[
            jax.ShapeDtypeStruct((length, channels), f32),
            jax.ShapeDtypeStruct((length, heads), f32),
            jax.ShapeDtypeStruct((heads, length), f32),
            jax.ShapeDtypeStruct((length, heads), f32),
            jax.ShapeDtypeStruct((1, inner), f32),
        ],
        scratch_shapes=[pltpu.VMEM((N, inner), f32)],
        compiler_params=pltpu.CompilerParams(vmem_limit_bytes=40 * 2**20),
        cost_estimate=pl.CostEstimate(
            flops=length * inner * 3072, bytes_accessed=length * inner * 14, transcendentals=length * heads * CHUNK
        ),
    )(act, cum, cum_t, dt, doc, doc_t, flow, skip, states, dy)


def doc_index(places, doc_ends):
    return jnp.sum((places[:, None] >= doc_ends[None, :-1]).astype(jnp.int32), axis=1)


def convolve(conv_in, weight, bias, masks):
    length = conv_in.shape[0]
    padded = jnp.concatenate([jnp.zeros((CONV - 1, conv_in.shape[1]), conv_in.dtype), conv_in], axis=0)
    total = jnp.broadcast_to(bias[None, :], conv_in.shape)
    for k in range(CONV):
        total = total + weight[k][None, :] * padded[k : k + length].astype(f32) * masks[k][:, None]
    return total


def body(
    inputs, cotangent, doc_lengths, head_width, pre_gain, in_weight, step_weight, conv_weight, conv_bias,
    step_bias, decay_log, skip_gain, norm_gain, out_weight,
):
    peers = lax.axis_size("seq")
    groups = lax.axis_size("batch")
    mine = lax.axis_index("seq")
    tokens = inputs.shape[1]
    width = inputs.shape[2]
    length = tokens * peers
    heads = H // peers
    inner = heads * P_SIZE
    rows = in_weight.shape[0]
    channels = inner + KEYS
    seq_rows = inputs[0].astype(f32)
    cot_rows = cotangent[0]

    def per_peer(part):
        return part.reshape(rows, peers, -1).transpose(1, 0, 2)

    keys_part = jnp.broadcast_to(in_weight[None, :, 2 * E :], (peers, rows, KEYS))
    step_part = jnp.pad(per_peer(step_weight), ((0, 0), (0, 0), (0, STEP_PAD - heads)))
    value_send = jnp.concatenate([per_peer(in_weight[:, E : 2 * E]), keys_part, step_part], axis=2)
    gate_send = per_peer(in_weight[:, :E])
    value_w = lax.all_to_all(value_send, "seq", 0, 0)
    gate_w = lax.all_to_all(gate_send, "seq", 0, 0)
    value_w = lax.all_gather(value_w.reshape(peers * rows, -1), "batch", axis=0, tiled=True)
    gate_w = lax.all_gather(gate_w.reshape(peers * rows, -1), "batch", axis=0, tiled=True)
    out_w = lax.all_gather(out_weight, "batch", axis=0, tiled=True)

    inv_rms = lax.rsqrt(jnp.mean(seq_rows * seq_rows, axis=1, keepdims=True) + epsilon)
    normed = (seq_rows * inv_rms * pre_gain[None, :]).astype(bf16)
    normed = normed.reshape(tokens, peers, groups, rows).transpose(0, 2, 1, 3).reshape(tokens, width)
    normed = lax.all_gather(normed, "seq", axis=0, tiled=True)
    cot_all = lax.all_gather(cot_rows, "seq", axis=0, tiled=True)

    places = jnp.arange(length, dtype=jnp.int32)
    doc_ends = jnp.cumsum(doc_lengths[0])
    doc_ids = doc_index(places, doc_ends)
    flow = (doc_ids == doc_index(places // CHUNK * CHUNK - 1, doc_ends)).astype(f32)[:, None]
    doc = doc_ids[:, None]
    doc_t = doc_ids[None, :]
    head_count = head_width[0]
    head_total = (head_count * P_SIZE).astype(f32)
    my_heads = mine * heads + jnp.arange(heads)
    head_mask = jnp.repeat((my_heads < head_count).astype(f32), P_SIZE)[None, :]
    masks = []
    for k in range(CONV):
        source = places - (CONV - 1 - k)
        masks.append(((source >= 0) & (doc_index(source, doc_ends) == doc_ids)).astype(f32))

    def own(vector, size):
        return lax.dynamic_slice_in_dim(vector, mine * size, size, axis=-1)

    conv_w = jnp.concatenate([own(conv_weight[:, :E], inner), conv_weight[:, E:]], axis=1)
    conv_b = jnp.concatenate([own(conv_bias[:E], inner), conv_bias[E:]])
    step_b = own(step_bias, heads)
    rate = jnp.exp(own(decay_log, heads))
    skip = jnp.repeat(own(skip_gain, heads), P_SIZE)[None, :]
    gain = own(norm_gain, inner)[None, :]

    value_out = mm(normed, value_w, NN)
    conv_in = value_out[:, :channels].astype(bf16)
    step_raw = value_out[:, channels : channels + heads] + step_b[None, :]
    gate = mm(normed, gate_w, NN)
    conv_sum = convolve(conv_in, conv_w, conv_b, masks)
    act = jax.nn.silu(conv_sum).astype(bf16)
    dt = jax.nn.softplus(step_raw)
    log_decay = -dt * rate[None, :]
    cum = jnp.cumsum(log_decay.reshape(-1, CHUNK, heads), axis=1).reshape(length, heads)
    y, states = scan_forward(act, cum, cum.T, dt, dt.T, doc, doc_t, flow, skip)
    grad_mixed = mm(cot_all, out_w, NT)
    sig_gate = jax.nn.sigmoid(gate)
    silu_gate = gate * sig_gate
    masked = y * head_mask
    gated = masked * silu_gate
    scaled = grad_mixed * gain
    partial_sums = jnp.stack([jnp.sum(gated * gated, axis=1), jnp.sum(scaled * gated, axis=1)])
    sums = jnp.sum(lax.all_gather(partial_sums, "seq", axis=0), axis=0)
    inv = lax.rsqrt(sums[0] / head_total + epsilon)[:, None]
    pull = inv * inv * inv * sums[1][:, None] / head_total
    mixed = (gated * inv * gain).astype(bf16)
    branch = mm(mixed, out_w, NN).astype(bf16)
    branch = lax.all_to_all(branch.reshape(peers, tokens, width), "seq", 0, 0)
    output = (seq_rows + jnp.sum(branch.astype(f32), axis=0)).astype(bf16)[None]

    out_term = mm(mixed, cot_all, TN).astype(bf16)
    grad_out_weight = lax.psum_scatter(out_term, "batch", scatter_dimension=0, tiled=True).astype(f32)
    grad_norm_gain = jnp.sum(grad_mixed * gated * inv, axis=0)
    grad_gated = inv * scaled - pull * gated
    dy = grad_gated * silu_gate * head_mask
    grad_gate = (grad_gated * masked * (sig_gate * (1.0 + gate * (1.0 - sig_gate)))).astype(bf16)
    gate_term = mm(normed, grad_gate, TN).astype(bf16)
    gate_term = lax.psum_scatter(gate_term, "batch", scatter_dimension=0, tiled=True)
    dact, dcum, dcum_t, ddt, dskip = scan_backward(
        act, cum, cum.T, dt, doc, doc_t, flow, skip, states, dy
    )
    dcum = (dcum + dcum_t.T).reshape(-1, CHUNK, heads)
    dlog = lax.cumsum(dcum, axis=1, reverse=True).reshape(length, heads)
    grad_dt = ddt - rate[None, :] * dlog
    grad_decay_log = -jnp.sum(dt * rate[None, :] * dlog, axis=0)
    grad_step_f32 = grad_dt * jax.nn.sigmoid(step_raw)
    grad_step_bias = jnp.sum(grad_step_f32, axis=0)
    grad_skip = jnp.sum(dskip.reshape(heads, P_SIZE), axis=1)
    sig = jax.nn.sigmoid(conv_sum)
    dconv = dact * (sig * (1.0 + conv_sum * (1.0 - sig)))
    padded = jnp.concatenate([jnp.zeros((CONV - 1, channels), bf16), conv_in], axis=0)
    grad_conv_bias = jnp.sum(dconv, axis=0)
    conv_rows = []
    grad_conv_in = jnp.zeros_like(dconv)
    for k in range(CONV):
        taken = dconv * masks[k][:, None]
        conv_rows.append(jnp.sum(taken * padded[k : k + length].astype(f32), axis=0))
        lead = CONV - 1 - k
        moved = jnp.concatenate([taken[lead:], jnp.zeros((lead, channels), f32)], axis=0)
        grad_conv_in = grad_conv_in + conv_w[k][None, :] * moved
    grad_conv_weight = jnp.stack(conv_rows)
    grad_step_raw = jnp.pad(grad_step_f32.astype(bf16), ((0, 0), (0, STEP_PAD - heads)))
    grad_value = jnp.concatenate([grad_conv_in.astype(bf16), grad_step_raw], axis=1)
    value_term = mm(normed, grad_value, TN).astype(bf16)
    value_term = lax.psum_scatter(value_term, "batch", scatter_dimension=0, tiled=True)
    grad_normed = mm(grad_gate, gate_w, NT) + mm(grad_value, value_w, NT)
    grad_normed = grad_normed.astype(bf16).reshape(peers, tokens, width)
    grad_normed = jnp.sum(lax.all_to_all(grad_normed, "seq", 0, 0).astype(f32), axis=0)
    grad_normed = grad_normed.reshape(tokens, groups, peers, rows).transpose(0, 2, 1, 3).reshape(tokens, width)

    scaled_in = grad_normed * pre_gain[None, :]
    dot = jnp.mean(scaled_in * seq_rows, axis=1, keepdims=True)
    grad_seq = inv_rms * scaled_in - seq_rows * (inv_rms * inv_rms * inv_rms * dot)
    grad_pre_gain = jnp.sum(grad_normed * seq_rows * inv_rms, axis=0)
    grad_inputs = (grad_seq + cot_rows.astype(f32))[None]

    gate_back = lax.all_to_all(gate_term.reshape(peers, rows, inner), "seq", 0, 0)
    value_back = lax.all_to_all(value_term.reshape(peers, rows, -1), "seq", 0, 0)

    def join(part):
        return part.astype(f32).transpose(1, 0, 2).reshape(rows, -1)

    grad_in_weight = jnp.concatenate(
        [
            join(gate_back),
            join(value_back[:, :, :inner]),
            jnp.sum(value_back[:, :, inner:channels].astype(f32), axis=0),
        ],
        axis=1,
    )
    grad_step_weight = join(value_back[:, :, channels : channels + heads])

    def spread(part, total):
        full = jnp.zeros(part.shape[:-1] + (total,), f32)
        return lax.dynamic_update_slice_in_dim(full, part, mine * part.shape[-1], axis=-1)

    conv_all = jnp.concatenate([grad_conv_weight, grad_conv_bias[None]], axis=0)
    small = lax.psum(
        (
            grad_pre_gain,
            jnp.concatenate([spread(conv_all[:, :inner], E), conv_all[:, inner:]], axis=1),
            spread(grad_step_bias, H),
            spread(grad_decay_log, H),
            spread(grad_skip, H),
            spread(grad_norm_gain, E),
        ),
        ("seq", "batch"),
    )
    return (
        output, grad_inputs, small[0], grad_in_weight, grad_step_weight, small[1][:CONV], small[1][CONV],
        small[2], small[3], small[4], small[5], grad_out_weight,
    )


def solution(mesh):
    both = P(("seq", "batch"), None)
    tok = P("batch", "seq", None)
    in_specs = (
        tok, tok, P("batch", None), P("batch"), P(), both, both, P(), P(), P(), P(), P(), P(), both,
    )
    out_specs = (tok, tok, P(), both, both, P(), P(), P(), P(), P(), P(), both)
    return jax.shard_map(body, mesh=mesh, in_specs=in_specs, out_specs=out_specs, check_vma=False)
```

```python
from functools import partial

import jax
import jax.numpy as jnp
from jax import lax
from jax.experimental import pallas as pl
from jax.experimental.pallas import tpu as pltpu
from jax.sharding import PartitionSpec as P

H = 64
P_SIZE = 64
N = 128
CONV = 4
DOCS = 4
E = 4096
KEYS = 2 * N
STEP_PAD = 128
CHUNK = 128
epsilon = 1e-05
f32 = jnp.float32
bf16 = jnp.bfloat16


def mm(a, b, dims):
    return lax.dot_general(a, b, (dims, ((), ())), preferred_element_type=f32)


NN = ((1,), (0,))
NT = ((1,), (1,))
TN = ((0,), (0,))


def pair_cols(low, col, first):
    return jnp.where(low, col[:, first : first + 1], col[:, first + 1 : first + 2])


def scan_forward_kernel(
    val_ref, key_ref, cum_ref, cum_t_ref, dt_ref, dt_t_ref, doc_ref, doc_t_ref, flow_ref, skip_ref, y_ref, state_ref, state
):
    heads = cum_ref.shape[1]

    @pl.when(pl.program_id(0) == 0)
    def _():
        state[...] = jnp.zeros_like(state)

    state_ref[0] = state[...].astype(bf16)
    cum = cum_ref[...]
    last = cum[CHUNK - 1 :, :]
    doc = doc_ref[...]
    doc_t = doc_t_ref[...]
    flow = flow_ref[...]
    rows = lax.broadcasted_iota(jnp.int32, (CHUNK, CHUNK), 0)
    cols = lax.broadcasted_iota(jnp.int32, (CHUNK, CHUNK), 1)
    bias = jnp.where((doc == doc_t) & (rows >= cols), 0.0, -1e30)
    carry_w = flow * jnp.exp(cum)
    final_w = jnp.where(doc == doc[CHUNK - 1 :, :], jnp.exp(last - cum), 0.0) * dt_ref[...]
    gain = carry_w[CHUNK - 1 :, :]
    low = cols < P_SIZE
    low_row = low[:1]
    write = key_ref[:, :N]
    read = key_ref[:, N:]
    write_t = write.astype(f32).T.astype(bf16)
    scores = mm(read, write, NT)
    for pair in range(heads // 2):
        first = 2 * pair
        lanes = slice(pair * 128, pair * 128 + 128)
        x = val_ref[:, lanes]
        xf = x.astype(f32)
        weights = []
        for h in (first, first + 1):
            decay = jnp.exp(cum[:, h : h + 1] - cum_t_ref[h : h + 1, :] + bias)
            weights.append((decay * scores * dt_t_ref[h : h + 1, :]).astype(bf16))
        stacked = jnp.concatenate(
            [jnp.where(low, xf, 0.0).astype(bf16), jnp.where(low, 0.0, xf).astype(bf16)], axis=0
        )
        old = state[:, lanes]
        y = mm(jnp.concatenate(weights, axis=1), stacked, NN)
        y = y + pair_cols(low, carry_w, first) * mm(read, old.astype(bf16), NN)
        y_ref[:, lanes] = y + skip_ref[:, lanes] * xf
        state[:, lanes] = pair_cols(low_row, gain, first) * old + mm(
            write_t, (pair_cols(low, final_w, first) * xf).astype(bf16), NN
        )


def scan_backward_kernel(
    val_ref, key_ref, cum_ref, cum_t_ref, dt_ref, doc_ref, doc_t_ref, flow_ref, skip_ref, state_ref, dy_ref,
    dval_ref, dkey_ref, dcum_ref, dcum_t_ref, ddt_ref, dskip_ref, dstate,
):
    heads = cum_ref.shape[1]

    @pl.when(pl.program_id(0) == 0)
    def _():
        dstate[...] = jnp.zeros_like(dstate)
        dskip_ref[...] = jnp.zeros_like(dskip_ref)

    cum = cum_ref[...]
    dt = dt_ref[...]
    last = cum[CHUNK - 1 :, :]
    doc = doc_ref[...]
    doc_t = doc_t_ref[...]
    flow = flow_ref[...]
    rows = lax.broadcasted_iota(jnp.int32, (CHUNK, CHUNK), 0)
    cols = lax.broadcasted_iota(jnp.int32, (CHUNK, CHUNK), 1)
    bias = jnp.where((doc == doc_t) & (cols >= rows), 0.0, -1e30)
    carry_w = flow * jnp.exp(cum)
    final_d = jnp.where(doc == doc[CHUNK - 1 :, :], jnp.exp(last - cum), 0.0)
    final_w = final_d * dt
    gain = carry_w[CHUNK - 1 :, :]
    low = cols < P_SIZE
    low_row = low[:1]
    write = key_ref[:, :N]
    read = key_ref[:, N:]
    read_t = read.astype(f32).T.astype(bf16)
    scores_t = mm(write, read, NT)
    dscores_t = jnp.zeros((CHUNK, CHUNK), f32)
    dwrite = jnp.zeros((CHUNK, N), f32)
    dread = jnp.zeros((CHUNK, N), f32)
    end_row = lax.broadcasted_iota(jnp.int32, (CHUNK, 1), 0) == CHUNK - 1
    dcum_cols = []
    dcum_rows = []
    ddt_cols = []
    for pair in range(heads // 2):
        first = 2 * pair
        lanes = slice(pair * 128, pair * 128 + 128)
        x = val_ref[:, lanes]
        xf = x.astype(f32)
        dy = dy_ref[:, lanes]
        dyb = dy.astype(bf16)
        x_stack = jnp.concatenate(
            [jnp.where(low, xf, 0.0).astype(bf16), jnp.where(low, 0.0, xf).astype(bf16)], axis=0
        )
        dy_stack = jnp.concatenate(
            [jnp.where(low, dy, 0.0).astype(bf16), jnp.where(low, 0.0, dy).astype(bf16)], axis=0
        )
        dweights = mm(x_stack, dyb, NT)
        old = state_ref[0, :, lanes]
        grad = dstate[:, lanes]
        gradb = grad.astype(bf16)
        carried = mm(read, old, NN)
        pushed = mm(write, gradb, NN)
        carry_p = pair_cols(low, carry_w, first)
        final_p = pair_cols(low, final_w, first)
        carry_prod = dy * carried
        final_prod = xf * pushed
        gain_prod = jnp.sum(grad * old.astype(f32), axis=0, keepdims=True)
        weights = []
        for which, h in enumerate((first, first + 1)):
            col = dt[:, h : h + 1]
            decay = jnp.exp(cum_t_ref[h : h + 1, :] - cum[:, h : h + 1] + bias)
            weighted = decay * col
            weights.append((weighted * scores_t).astype(bf16))
            dw = dweights[which * CHUNK : (which + 1) * CHUNK]
            dscores_t = dscores_t + dw * weighted
            direct = dw * decay * scores_t
            ddt_in = jnp.sum(direct, axis=1, keepdims=True)
            dcum_rows.append(jnp.sum(direct * col, axis=0, keepdims=True))
            half = low if which == 0 else ~low
            half_row = low_row if which == 0 else ~low_row
            carry_sum = jnp.sum(jnp.where(half, carry_prod, 0.0), axis=1, keepdims=True)
            final_sum = jnp.sum(jnp.where(half, final_prod, 0.0), axis=1, keepdims=True)
            push = final_w[:, h : h + 1] * final_sum
            at_end = jnp.sum(push, axis=0, keepdims=True) + gain[:, h : h + 1] * jnp.sum(
                jnp.where(half_row, gain_prod, 0.0), axis=1, keepdims=True
            )
            ddt_cols.append(ddt_in + final_d[:, h : h + 1] * final_sum)
            dcum_cols.append(
                carry_w[:, h : h + 1] * carry_sum - push - col * ddt_in + jnp.where(end_row, at_end, 0.0)
            )
        dx = mm(jnp.concatenate(weights, axis=1), dy_stack, NN)
        dval_ref[:, lanes] = dx + final_p * pushed + skip_ref[:, lanes] * dy
        dskip_ref[:, lanes] += jnp.sum(dy * xf, axis=0, keepdims=True)
        dwrite = dwrite + mm((final_p * xf).astype(bf16), gradb, NT)
        carry_dy = (carry_p * dy).astype(bf16)
        dread = dread + mm(carry_dy, old, NT)
        dstate[:, lanes] = pair_cols(low_row, gain, first) * grad + mm(read_t, carry_dy, NN)
    dsb = dscores_t.astype(bf16)
    dkey_ref[:, :N] = dwrite + mm(dsb, read, NN)
    dkey_ref[:, N:] = dread + mm(dsb, write, TN)
    dcum_ref[...] = jnp.concatenate(dcum_cols, axis=1)
    dcum_t_ref[...] = jnp.concatenate(dcum_rows, axis=0)
    ddt_ref[...] = jnp.concatenate(ddt_cols, axis=1)


def scan_forward(val, keys, cum, cum_t, dt, dt_t, doc, doc_t, flow, skip):
    length = val.shape[0]
    heads = cum.shape[1]
    inner = heads * P_SIZE
    steps = length // CHUNK
    row = lambda width: pl.BlockSpec((CHUNK, width), lambda i: (i, 0))
    lane = lambda height: pl.BlockSpec((height, CHUNK), lambda i: (0, i))
    return pl.pallas_call(
        scan_forward_kernel,
        grid=(steps,),
        in_specs=[
            row(inner), row(KEYS), row(heads), lane(heads), row(heads), lane(heads), row(1), lane(1), row(1),
            pl.BlockSpec((1, inner), lambda i: (0, 0)),
        ],
        out_specs=[row(inner), pl.BlockSpec((1, N, inner), lambda i: (i, 0, 0))],
        out_shape=[
            jax.ShapeDtypeStruct((length, inner), f32),
            jax.ShapeDtypeStruct((steps, N, inner), bf16),
        ],
        scratch_shapes=[pltpu.VMEM((N, inner), f32)],
        compiler_params=pltpu.CompilerParams(vmem_limit_bytes=40 * 2**20),
        cost_estimate=pl.CostEstimate(
            flops=length * inner * 1024, bytes_accessed=length * inner * 10, transcendentals=length * heads * CHUNK
        ),
    )(val, keys, cum, cum_t, dt, dt_t, doc, doc_t, flow, skip)


def scan_backward(val, keys, cum, cum_t, dt, doc, doc_t, flow, skip, states, dy):
    length = val.shape[0]
    heads = cum.shape[1]
    inner = heads * P_SIZE
    steps = length // CHUNK
    row = lambda width: pl.BlockSpec((CHUNK, width), lambda i: (steps - 1 - i, 0))
    lane = lambda height: pl.BlockSpec((height, CHUNK), lambda i: (0, steps - 1 - i))
    whole = pl.BlockSpec((1, inner), lambda i: (0, 0))
    return pl.pallas_call(
        scan_backward_kernel,
        grid=(steps,),
        in_specs=[
            row(inner), row(KEYS), row(heads), lane(heads), row(heads), row(1), lane(1), row(1), whole,
            pl.BlockSpec((1, N, inner), lambda i: (steps - 1 - i, 0, 0)), row(inner),
        ],
        out_specs=[row(inner), row(KEYS), row(heads), lane(heads), row(heads), whole],
        out_shape=[
            jax.ShapeDtypeStruct((length, inner), f32),
            jax.ShapeDtypeStruct((length, KEYS), f32),
            jax.ShapeDtypeStruct((length, heads), f32),
            jax.ShapeDtypeStruct((heads, length), f32),
            jax.ShapeDtypeStruct((length, heads), f32),
            jax.ShapeDtypeStruct((1, inner), f32),
        ],
        scratch_shapes=[pltpu.VMEM((N, inner), f32)],
        compiler_params=pltpu.CompilerParams(vmem_limit_bytes=40 * 2**20),
        cost_estimate=pl.CostEstimate(
            flops=length * inner * 3072, bytes_accessed=length * inner * 14, transcendentals=length * heads * CHUNK
        ),
    )(val, keys, cum, cum_t, dt, doc, doc_t, flow, skip, states, dy)


MESH = pl.DeviceIdType.MESH
HBM = pl.BlockSpec(memory_space=pl.ANY)
VMEM = pl.BlockSpec(memory_space=pltpu.VMEM)


def z_pair(peers, groups):
    planes = groups // 2
    return 2 if planes % 2 == 0 and (E // (peers * planes)) % (2 * P_SIZE) == 0 else 1


def flip(value, bits):
    bit = 1
    while bit <= bits:
        if bits & bit:
            value = value + bit - 2 * bit * (value // bit % 2)
        bit *= 2
    return value


class Place:
    def __init__(self):
        self.peers = lax.axis_size("seq")
        groups = lax.axis_size("batch")
        self.near = z_pair(self.peers, groups)
        self.far = groups // 2 // self.near
        self.s = lax.axis_index("seq")
        b = lax.axis_index("batch")
        self.c = b % 2
        self.zl = b // 2 % self.near
        self.zh = b // 2 // self.near

    def at(self, s=0, zl=0, zh=0, c=0):
        return (flip(self.s, s), (flip(self.zh, zh) * self.near + flip(self.zl, zl)) * 2 + flip(self.c, c))

    def partners(self):
        cube = [self.at(s=o // self.near, zl=o % self.near) for o in range(1, self.peers * self.near)]
        return cube, [self.at(zh=o) for o in range(1, self.far)], [self.at(c=1)]


def greet(devices):
    barrier = pltpu.get_barrier_semaphore()
    for device in devices:
        pl.semaphore_signal(barrier, inc=1, device_id=device, device_id_type=MESH)
    pl.semaphore_wait(barrier, len(devices))


class Mover:
    def __init__(self, send, recv, local):
        self.send, self.recv, self.local = send, recv, local
        self.sent, self.kept = 0, 0
        self.open = []

    def put(self, src, dst, device):
        copy = pltpu.make_async_remote_copy(
            src_ref=src, dst_ref=dst, send_sem=self.send.at[self.sent], recv_sem=self.recv.at[self.sent],
            device_id=device, device_id_type=MESH,
        )
        copy.start()
        self.sent += 1
        self.open.append(copy)
        return copy

    def keep(self, src, dst):
        copy = pltpu.make_async_copy(src, dst, self.local.at[self.kept])
        copy.start()
        self.kept += 1
        return copy

    def close(self):
        for copy in self.open:
            copy.wait_send()


def run_paths(paths):
    paths = list(paths)
    while paths:
        alive = []
        for path in paths:
            try:
                next(path)
                alive.append(path)
            except StopIteration:
                pass
        paths = alive


def bits_of(peers):
    return [1 << i for i in range(peers.bit_length() - 1)]


def combos(bits):
    out = [0]
    for bit in reversed(bits):
        out = [bit | o for o in out] + out
    return out


def gather_kernel(
    send_ref, key_ref, out_ref, rows_ref, cot_ref, meta_ref,
    w_ref, k_ref, o_ref, x_ref, ct_ref, m_ref, send, recv, local,
):
    me = Place()
    s, zl, zh, c = me.s, me.zl, me.zh, me.c
    cube, far, sibling = me.partners()
    greet(cube + far + sibling)
    mover = Mover(send, recv, local)
    bits = bits_of(me.peers)

    def rows_path(src, dst, order):
        own = mover.keep(src, dst.at[zl, s])
        near = [mover.put(src, dst.at[zl, s], me.at(zl=o)) for o in range(1, me.near)]
        yield
        own.wait()
        for copy in near:
            copy.wait_recv()
        held = [0]
        for bit in order:
            copies = [mover.put(dst.at[:, flip(s, h)], dst.at[:, flip(s, h)], me.at(s=bit)) for h in held]
            held = held + [h ^ bit for h in held]
            yield
            for copy in copies:
                copy.wait_recv()

    def meta_path():
        own = mover.keep(meta_ref, m_ref.at[zl])
        near = [mover.put(meta_ref, m_ref.at[zl], me.at(zl=o)) for o in range(1, me.near)]
        yield
        own.wait()
        for copy in near:
            copy.wait_recv()

    def key_path():
        own = mover.keep(key_ref, k_ref.at[zh, c, s, zl])
        copies = [mover.put(key_ref, k_ref.at[zh, c, s, zl], me.at(zh=o)) for o in range(1, me.far)]
        yield
        own.wait()
        for copy in copies:
            copy.wait_recv()
        block = k_ref.at[:, c, s, zl]
        copies = [mover.put(block, block, me.at(zl=o)) for o in range(1, me.near)]
        yield
        for copy in copies:
            copy.wait_recv()
        held = [0]
        for bit in bits:
            copies = [mover.put(k_ref.at[:, c, flip(s, h)], k_ref.at[:, c, flip(s, h)], me.at(s=bit)) for h in held]
            held = held + [h ^ bit for h in held]
            yield
            for copy in copies:
                copy.wait_recv()
        copy = mover.put(k_ref.at[:, c], k_ref.at[:, c], me.at(c=1))
        yield
        copy.wait_recv()

    def spread_path(copies, view):
        last = []
        for o, copy in copies:
            yield
            copy.wait_recv()
            last.append(mover.put(view(flip(zh, o)), view(flip(zh, o)), me.at(c=1)))
        return last

    def out_path():
        own = mover.keep(out_ref, o_ref.at[zh, c])
        copies = [(o, mover.put(out_ref, o_ref.at[zh, c], me.at(zh=o))) for o in range(1, me.far)]
        first = mover.put(out_ref, o_ref.at[zh, c], me.at(c=1))
        last = yield from spread_path(copies, lambda h: o_ref.at[h, c])
        yield
        own.wait()
        for copy in last + [first]:
            copy.wait_recv()

    weights = {}

    def weight_path():
        for step in range(me.peers):
            for o in range(me.near):
                if step or o:
                    weights[step, o] = mover.put(
                        send_ref.at[flip(s, step), flip(zl, o)], w_ref.at[zh, c, s, zl], me.at(s=step, zl=o)
                    )
                else:
                    weights[step, o] = mover.keep(send_ref.at[s, zl], w_ref.at[zh, c, s, zl])
        pieces = []
        for step in range(me.peers):
            yield
            for o in range(me.near):
                if step or o:
                    weights[step, o].wait_recv()
                else:
                    weights[step, o].wait()
            block = w_ref.at[zh, c, flip(s, step)]
            copies = [(o, mover.put(block, block, me.at(zh=o))) for o in range(1, me.far)]
            pieces.append((step, copies, mover.put(block, block, me.at(c=1))))
        last = []
        for step, copies, first in pieces:
            last.append(first)
            last += yield from spread_path(copies, lambda h, step=step: w_ref.at[h, c, flip(s, step)])
        yield
        for copy in last:
            copy.wait_recv()

    run_paths(
        [
            rows_path(rows_ref, x_ref, bits), rows_path(cot_ref, ct_ref, bits[::-1]), meta_path(), key_path(),
            weight_path(), out_path(),
        ]
    )
    mover.close()


def remote_params(identity):
    return pltpu.CompilerParams(collective_id=identity, has_side_effects=True, vmem_limit_bytes=58 * 2**20)


def sems(copies, kept):
    return [pltpu.SemaphoreType.DMA((copies,)), pltpu.SemaphoreType.DMA((copies,)), pltpu.SemaphoreType.DMA((kept,))]


def gather(send, keys, out_w, rows, cot, meta):
    me = Place()
    peers, near, far = me.peers, me.near, me.far
    shape = lambda lead, part: jax.ShapeDtypeStruct(lead + part, bf16)
    copies = (peers * near - 1) + (peers + 1) * (2 * far - 1) + 3 * (near + peers - 2) + near - 1 + far
    return pl.pallas_call(
        gather_kernel,
        out_shape=[
            shape((far, 2, peers, near), send.shape[2:]),
            shape((far, 2, peers, near), keys.shape),
            shape((far, 2), out_w.shape),
            shape((near, peers), rows.shape),
            shape((near, peers), cot.shape),
            jax.ShapeDtypeStruct((near,) + meta.shape, meta.dtype),
        ],
        in_specs=[HBM] * 6,
        out_specs=[HBM] * 6,
        scratch_shapes=sems(copies, 8),
        compiler_params=remote_params(0),
        name="gather_all",
    )(send, keys, out_w, rows, cot, meta)


def total_kernel(part_ref, sum_ref, box, send, recv, local):
    me = Place()
    cube = me.partners()[0]
    greet(cube)
    mover = Mover(send, recv, local)
    copies = [mover.put(part_ref, box.at[i], device) for i, device in enumerate(cube)]
    total = part_ref[...]
    for i, copy in enumerate(copies):
        copy.wait_recv()
        total = total + box[i]
    sum_ref[...] = total
    mover.close()


def cube_total(part):
    me = Place()
    count = me.peers * me.near - 1
    return pl.pallas_call(
        total_kernel,
        out_shape=jax.ShapeDtypeStruct(part.shape, f32),
        in_specs=[VMEM],
        out_specs=VMEM,
        scratch_shapes=[pltpu.VMEM((count,) + part.shape, f32)] + sems(count, 1),
        compiler_params=remote_params(1),
        name="cube_total",
    )(part)


def add_rows(out, parts):
    shape = out.shape
    tile = min(16, shape[-2])
    lead = [()]
    for size in shape[:-2]:
        lead = [l + (i,) for l in lead for i in range(size)]
    for l in lead:

        def step(i, carry, l=l):
            at = l + (pl.ds(pl.multiple_of(i * tile, tile), tile), slice(None))
            total = parts[0][at].astype(f32)
            for part in parts[1:]:
                total = total + part[at].astype(f32)
            out[at] = total.astype(out.dtype)
            return carry

        lax.fori_loop(0, shape[-2] // tile, step, 0)


def scatter_kernel(
    bp_ref, gn_ref, gw_ref, go_ref, gk_ref, v_ref,
    ob_ref, og_ref, ow_ref, oo_ref, ok_ref, ov_ref,
    b_own, b_box, b_near, n_own, n_box, n_near, w_own, w_box, w_far, o_own, o_box, o_far,
    k_own, k_box, k_near, k_far, k_bits, v_box, send, recv, local,
):
    me = Place()
    s, zl, zh, c = me.s, me.zl, me.zh, me.c
    cube, far, sibling = me.partners()
    greet(cube + far + sibling)
    mover = Mover(send, recv, local)
    bits = bits_of(me.peers)

    def halve(own, box, order, first_src):
        base = 0
        todo = combos(order[1:])
        copies = [mover.put(first_src(flip(s, order[0] ^ o)), box.at[base + j], me.at(s=order[0])) for j, o in enumerate(todo)]
        for i, bit in enumerate(order):
            rest = order[i + 1 :]
            count = 1 << len(rest)
            offset = (1 << (len(order) - 1)) - count
            coming = []
            for j in range(count):
                yield
                copies[j].wait_recv()
                add_rows(own.at[offset + j], [own.at[offset + j], box.at[base + j]])
                if rest and j < count // 2:
                    coming.append(mover.put(own.at[offset + j], box.at[base + count + j], me.at(s=rest[0])))
            base += count
            copies = coming

    def rows_path(src, own, box, near_box, out, order):
        loads = [mover.keep(src.at[:, flip(s, o)], own.at[j]) for j, o in enumerate(combos(order[1:]))]

        def first_src(at):
            return src.at[:, at]

        path = halve(own, box, order, first_src)
        next(path)
        for load in loads:
            load.wait()
        yield
        yield from path
        last = own.shape[0] - 1
        copies = [mover.put(own.at[last, flip(zl, o)], near_box.at[o - 1], me.at(zl=o)) for o in range(1, me.near)]
        yield
        for copy in copies:
            copy.wait_recv()
        add_rows(out, [own.at[last, zl]] + [near_box.at[o - 1] for o in range(1, me.near)])

    def weight_path():
        order = [(o, k) for o in range(1, me.far) for k in range(me.peers)] + [(0, k) for k in range(me.peers)]
        loads, copies = {}, {}
        for o, k in order:
            copies[o, k] = mover.put(gw_ref.at[flip(zh, o), 1 - c, flip(s, k)], w_box.at[o, k], me.at(c=1))
            loads[o, k] = mover.keep(gw_ref.at[flip(zh, o), c, flip(s, k)], w_own.at[o, k])
        far_copies = {}
        for o, k in order:
            yield
            loads[o, k].wait()
            copies[o, k].wait_recv()
            if o:
                add_rows(w_own.at[o, k], [w_own.at[o, k], w_box.at[o, k]])
                far_copies[o, k] = mover.put(w_own.at[o, k], w_far.at[o - 1, k], me.at(zh=o))
        ends = []
        for k in range(me.peers):
            yield
            for o in range(1, me.far):
                far_copies[o, k].wait_recv()
            parts = [w_own.at[0, k], w_box.at[0, k]] + [w_far.at[o - 1, k] for o in range(1, me.far)]
            add_rows(w_own.at[0, k], parts)
            for o in range(me.near):
                if k or o:
                    ends.append(mover.put(w_own.at[0, k, flip(zl, o)], ow_ref.at[s, zl], me.at(s=k, zl=o)))
                else:
                    own = mover.keep(w_own.at[0, 0, zl], ow_ref.at[s, zl])
        yield
        own.wait()
        for copy in ends:
            copy.wait_recv()

    def out_path():
        order = list(range(1, me.far)) + [0]
        copies, loads = {}, {}
        for o in order:
            copies[o] = mover.put(go_ref.at[flip(zh, o), 1 - c], o_box.at[o], me.at(c=1))
            loads[o] = mover.keep(go_ref.at[flip(zh, o), c], o_own.at[o])
        for _ in range(me.far * me.peers):
            yield
        far_copies = {}
        for o in order:
            loads[o].wait()
            copies[o].wait_recv()
            if o:
                add_rows(o_own.at[o], [o_own.at[o], o_box.at[o]])
                far_copies[o] = mover.put(o_own.at[o], o_far.at[o - 1], me.at(zh=o))
        for _ in range(me.peers):
            yield
        for o in range(1, me.far):
            far_copies[o].wait_recv()
        add_rows(oo_ref, [o_own.at[0], o_box.at[0]] + [o_far.at[o - 1] for o in range(1, me.far)])

    def key_path():
        blocks = combos(bits)
        copies, loads = [], []
        for j, o in enumerate(blocks):
            copies.append(mover.put(gk_ref.at[:, 1 - c, flip(s, o)], k_box.at[j], me.at(c=1)))
            loads.append(mover.keep(gk_ref.at[:, c, flip(s, o)], k_own.at[j]))
        half = me.peers // 2
        sent = []
        for j in range(me.peers):
            yield
            loads[j].wait()
            copies[j].wait_recv()
            add_rows(k_own.at[j], [k_own.at[j], k_box.at[j]])
            if j < half:
                sent.append(mover.put(k_own.at[j], k_bits.at[j], me.at(s=bits[0])))
        base = 0
        for i, bit in enumerate(bits):
            count = me.peers >> (i + 1)
            offset = me.peers - count
            coming = []
            for j in range(count):
                yield
                sent[j].wait_recv()
                add_rows(k_own.at[offset + j], [k_own.at[offset + j], k_bits.at[base + j]])
                if i + 1 < len(bits) and j < count // 2:
                    coming.append(mover.put(k_own.at[offset + j], k_bits.at[base + count + j], me.at(s=bits[i + 1])))
            base += count
            sent = coming
        end = k_own.at[me.peers - 1]
        copies = [mover.put(end.at[:, flip(zl, o)], k_near.at[o - 1], me.at(zl=o)) for o in range(1, me.near)]
        yield
        for copy in copies:
            copy.wait_recv()
        add_rows(end.at[:, zl], [end.at[:, zl]] + [k_near.at[o - 1] for o in range(1, me.near)])
        copies = [mover.put(end.at[flip(zh, o), zl], k_far.at[o - 1], me.at(zh=o)) for o in range(1, me.far)]
        yield
        for copy in copies:
            copy.wait_recv()
        add_rows(ok_ref, [end.at[zh, zl]] + [k_far.at[o - 1] for o in range(1, me.far)])

    def small_path():
        turns = [me.at(c=1)] + [me.at(zl=o) for o in bits_of(me.near)]
        turns += [me.at(s=o) for o in bits] + [me.at(zh=o) for o in bits_of(me.far)]
        rows = v_ref.shape[0]
        v_box[0] = v_ref[...]
        for i, device in enumerate(turns):
            copy = mover.put(v_box.at[2 * i], v_box.at[2 * i + 1], device)
            yield
            copy.wait_recv()
            v_box[2 * i + 2] = v_box[2 * i] + v_box[2 * i + 1]
        ov_ref[...] = v_box[2 * len(turns)]

    run_paths(
        [
            weight_path(),
            rows_path(gn_ref, n_own, n_box, n_near, og_ref, bits[::-1]),
            rows_path(bp_ref, b_own, b_box, b_near, ob_ref, bits),
            key_path(),
            small_path(),
            out_path(),
        ]
    )
    mover.close()


def scatter(branch, grads, gw, go, gk, small):
    me = Place()
    peers, near, far = me.peers, me.near, me.far
    tokens, width = branch.shape[2:]
    stages = len(bits_of(peers)) + len(bits_of(near)) + len(bits_of(far)) + 1
    vm = lambda *shape: pltpu.VMEM(shape, bf16)
    rows_scratch = [vm(peers // 2, near, tokens, width), vm(peers - 1, near, tokens, width), vm(max(near - 1, 1), tokens, width)]
    block = gw.shape[3:]
    kblock = gk.shape[3:]
    oblock = go.shape[2:]
    copies = 2 * (peers + near - 2) + 2 * far * peers + peers * (near - 1) + peers - 1 + 3 * far + 2 * peers + near - 4 + stages
    kept = peers + far * peers + 1 + far + peers + 4
    return pl.pallas_call(
        scatter_kernel,
        out_shape=[
            jax.ShapeDtypeStruct((tokens, width), f32),
            jax.ShapeDtypeStruct((tokens, width), f32),
            jax.ShapeDtypeStruct((peers,) + block, bf16),
            jax.ShapeDtypeStruct(oblock, f32),
            jax.ShapeDtypeStruct(kblock[1:], f32),
            jax.ShapeDtypeStruct(small.shape, f32),
        ],
        in_specs=[HBM] * 5 + [VMEM],
        out_specs=[VMEM, VMEM, HBM, VMEM, VMEM, VMEM],
        scratch_shapes=rows_scratch
        + rows_scratch
        + [vm(far, peers, *block), vm(far, peers, *block), vm(max(far - 1, 1), peers, *block)]
        + [vm(far, *oblock), vm(far, *oblock), vm(max(far - 1, 1), *oblock)]
        + [
            vm(peers, far, *kblock), vm(peers, far, *kblock), vm(max(near - 1, 1), far, *kblock[1:]),
            vm(max(far - 1, 1), *kblock[1:]), vm(peers - 1, far, *kblock),
            pltpu.VMEM((2 * stages + 1,) + small.shape, f32),
        ]
        + sems(copies, kept),
        compiler_params=remote_params(2),
        name="scatter_all",
    )(branch, grads, gw, go, gk, small)


def doc_index(places, doc_ends):
    return jnp.sum((places[:, None] >= doc_ends[None, :-1]).astype(jnp.int32), axis=1)


def moved_down(rows, by):
    return jnp.concatenate([jnp.zeros((by,) + rows.shape[1:], rows.dtype), rows[: rows.shape[0] - by]], axis=0)


def moved_up(rows, by):
    return jnp.concatenate([rows[by:], jnp.zeros((by,) + rows.shape[1:], rows.dtype)], axis=0)


def convolve(conv_in, weight, bias, masks):
    total = jnp.broadcast_to(bias[None, :], conv_in.shape)
    for k in range(CONV):
        total = total + weight[k][None, :] * moved_down(conv_in, CONV - 1 - k).astype(f32) * masks[k][:, None]
    return total


def convolve_back(dact, conv_in, conv_sum, weight, masks):
    sig = jax.nn.sigmoid(conv_sum)
    dconv = dact * (sig * (1.0 + conv_sum * (1.0 - sig)))
    sums = []
    grad_in = jnp.zeros_like(dconv)
    for k in range(CONV):
        taken = dconv * masks[k][:, None]
        sums.append(jnp.sum(taken * moved_down(conv_in, CONV - 1 - k).astype(f32), axis=0))
        grad_in = grad_in + weight[k][None, :] * moved_up(taken, CONV - 1 - k)
    sums.append(jnp.sum(dconv, axis=0))
    return grad_in.astype(bf16), jnp.stack(sums)


def body(
    inputs, cotangent, doc_lengths, head_width, pre_gain, in_weight, step_weight, conv_weight, conv_bias,
    step_bias, decay_log, skip_gain, norm_gain, out_weight,
):
    me = Place()
    peers, near, far = me.peers, me.near, me.far
    outer = far if near > 1 else 1
    tokens = inputs.shape[1]
    width = inputs.shape[2]
    span = tokens * peers
    length = span * near
    heads = H // (peers * near)
    inner = heads * P_SIZE
    rows = in_weight.shape[0]
    seq_rows = inputs[0].astype(f32)
    cot_rows = cotangent[0]

    def per_group(part):
        lead = part.shape[0]
        return part.reshape(lead, peers, outer, near, -1).transpose(1, 3, 0, 2, 4).reshape(peers, near, lead, -1)

    def whole_again(part):
        lead = part.shape[2]
        return part.reshape(peers, near, lead, outer, -1).transpose(2, 0, 3, 1, 4).reshape(lead, -1)

    def own(vector):
        part = vector.reshape(-1, peers, outer, near, vector.shape[-1] // (peers * outer * near))
        part = lax.dynamic_index_in_dim(part, me.s, 1, False)
        part = lax.dynamic_index_in_dim(part, me.zl, 2, False)
        return part.reshape(vector.shape[:-1] + (-1,))

    def spread(part):
        lead = part.shape[:-1]
        part = part.reshape(-1, 1, outer, 1, part.shape[-1] // outer)
        full = jnp.zeros((part.shape[0], peers, outer, near, part.shape[-1]), part.dtype)
        return lax.dynamic_update_slice(full, part, (0, me.s, 0, me.zl, 0)).reshape(lead + (-1,))

    def to_gathered(part):
        part = part.reshape(part.shape[0], peers, far, near, 2, rows)
        return part.transpose(0, 2, 4, 1, 3, 5).reshape(part.shape[0], width)

    def from_gathered(part):
        part = part.reshape(part.shape[0], far, 2, peers, near, rows)
        return part.transpose(0, 3, 1, 4, 2, 5).reshape(part.shape[0], width)

    send = jnp.concatenate([per_group(in_weight[:, :E]), per_group(in_weight[:, E : 2 * E])], axis=-1)
    key_send = jnp.concatenate(
        [in_weight[:, 2 * E :], step_weight, jnp.zeros((rows, STEP_PAD - H), bf16)], axis=1
    )
    inv_rms = lax.rsqrt(jnp.mean(seq_rows * seq_rows, axis=1, keepdims=True) + epsilon)
    normed = to_gathered((seq_rows * inv_rms * pre_gain[None, :]).astype(bf16))
    meta = jnp.zeros((8, 128), jnp.int32)
    meta = meta.at[0, :DOCS].set(doc_lengths[0]).at[1, 0].set(head_width[0])
    in_w, key_w, out_w, normed, cot_all, meta = gather(send, key_send, out_weight, normed, cot_rows, meta)
    in_w = in_w.reshape(width, 2 * inner)
    key_w = key_w.reshape(width, -1)
    out_w = out_w.reshape(inner, width)
    normed = normed.reshape(length, width)
    cot_all = cot_all.reshape(length, width)

    places = jnp.arange(span, dtype=jnp.int32)
    doc_ids = jnp.concatenate(
        [doc_index(places, jnp.cumsum(meta[i, 0, :DOCS])) + i * DOCS for i in range(near)]
    )
    before = jnp.concatenate([jnp.full((1,), -1, jnp.int32), doc_ids[CHUNK - 1 : -1 : CHUNK]])
    flow = (doc_ids == jnp.repeat(before, CHUNK)).astype(f32)[:, None]
    doc = doc_ids[:, None]
    doc_t = doc_ids[None, :]
    counts = meta[:, 1, 0]
    head_total = jnp.repeat((counts * P_SIZE).astype(f32), span)[:, None]
    my_heads = own(jnp.arange(H, dtype=jnp.int32))
    head_mask = jnp.repeat((my_heads[None, :] < counts[:, None]).astype(f32), P_SIZE, axis=1)
    head_mask = jnp.repeat(head_mask, span, axis=0)
    masks = []
    for k in range(CONV):
        lag = CONV - 1 - k
        masks.append((jnp.concatenate([jnp.full((lag,), -1, jnp.int32), doc_ids[: length - lag]]) == doc_ids).astype(f32))

    conv_all = jnp.concatenate([conv_weight, conv_bias[None]], axis=0)
    conv_v = own(conv_all[:, :E])
    conv_k = conv_all[:, E:]
    step_b = own(step_bias)
    rate = jnp.exp(own(decay_log))
    skip = jnp.repeat(own(skip_gain), P_SIZE)[None, :]
    gain = own(norm_gain)[None, :]

    projected = mm(normed, in_w, NN)
    gate = projected[:, :inner]
    value_in = projected[:, inner:].astype(bf16)
    key_out = mm(normed, key_w, NN)
    key_in = key_out[:, :KEYS].astype(bf16)
    step_raw = own(key_out[:, KEYS : KEYS + H]) + step_b[None, :]
    value_sum = convolve(value_in, conv_v[:CONV], conv_v[CONV], masks)
    values = jax.nn.silu(value_sum).astype(bf16)
    key_sum = convolve(key_in, conv_k[:CONV], conv_k[CONV], masks)
    keys = jax.nn.silu(key_sum).astype(bf16)
    dt = jax.nn.softplus(step_raw)
    log_decay = -dt * rate[None, :]
    cum = jnp.cumsum(log_decay.reshape(-1, CHUNK, heads), axis=1).reshape(length, heads)
    y, states = scan_forward(values, keys, cum, cum.T, dt, dt.T, doc, doc_t, flow, skip)
    grad_mixed = mm(cot_all, out_w, NT)
    sig_gate = jax.nn.sigmoid(gate)
    silu_gate = gate * sig_gate
    masked = y * head_mask
    gated = masked * silu_gate
    scaled = grad_mixed * gain
    part = jnp.stack([jnp.sum(gated * gated, axis=1), jnp.sum(scaled * gated, axis=1)])
    sums = cube_total(part.reshape(-1, 128)).reshape(2, length, 1)
    inv = lax.rsqrt(sums[0] / head_total + epsilon)
    pull = inv * inv * inv * sums[1] / head_total
    mixed = (gated * inv * gain).astype(bf16)
    branch = mm(mixed, out_w, NN).astype(bf16)

    grad_out = mm(mixed, cot_all, TN).astype(bf16)
    grad_norm_gain = jnp.sum(grad_mixed * gated * inv, axis=0)
    grad_gated = inv * scaled - pull * gated
    dy = grad_gated * silu_gate * head_mask
    grad_gate = (grad_gated * masked * (sig_gate * (1.0 + gate * (1.0 - sig_gate)))).astype(bf16)
    dvalues, dkeys, dcum, dcum_t, ddt, dskip = scan_backward(
        values, keys, cum, cum.T, dt, doc, doc_t, flow, skip, states, dy
    )
    dcum = (dcum + dcum_t.T).reshape(-1, CHUNK, heads)
    dlog = lax.cumsum(dcum, axis=1, reverse=True).reshape(length, heads)
    grad_dt = ddt - rate[None, :] * dlog
    grad_decay_log = -jnp.sum(dt * rate[None, :] * dlog, axis=0)
    grad_step = grad_dt * jax.nn.sigmoid(step_raw)
    grad_step_bias = jnp.sum(grad_step, axis=0)
    grad_skip = jnp.sum(dskip.reshape(heads, P_SIZE), axis=1)
    grad_value_in, sums_v = convolve_back(dvalues, value_in, value_sum, conv_v[:CONV], masks)
    grad_key_in, sums_k = convolve_back(dkeys, key_in, key_sum, conv_k[:CONV], masks)
    grad_cols = jnp.concatenate([grad_gate, grad_value_in], axis=1)
    step_cols = jnp.pad(spread(grad_step.astype(bf16)), ((0, 0), (0, STEP_PAD - H)))
    key_cols = jnp.concatenate([grad_key_in, step_cols], axis=1)
    grad_in = mm(normed, grad_cols, TN).astype(bf16)
    grad_keys = mm(normed, key_cols, TN).astype(bf16)
    grad_normed = mm(grad_cols, in_w, NT) + mm(key_cols, key_w, NT)
    grad_pre_gain = from_gathered(jnp.sum(grad_normed * normed.astype(f32), axis=0)[None])[0] / pre_gain

    small = jnp.concatenate(
        [
            grad_pre_gain,
            jnp.concatenate([spread(sums_v), sums_k], axis=1).reshape(-1),
            spread(grad_step_bias),
            spread(grad_decay_log),
            spread(grad_skip),
            spread(grad_norm_gain),
        ]
    )
    count = small.shape[0]
    padded = -count % 1024
    small = jnp.pad(small, (0, padded)).reshape(-1, 128)
    rows_of = lambda part: part.reshape(near, peers, tokens, width)
    blocks = (far, 2, peers, near, rows)
    branch, grad_normed, grad_in, grad_out_weight, grad_keys, small = scatter(
        rows_of(branch),
        rows_of(grad_normed.astype(bf16)),
        grad_in.reshape(blocks + (2 * inner,)),
        grad_out.reshape(far, 2, -1, width),
        grad_keys.reshape(blocks + (KEYS + STEP_PAD,)),
        small,
    )
    output = (seq_rows + branch).astype(bf16)[None]
    grad_normed = from_gathered(grad_normed)
    scaled_in = grad_normed * pre_gain[None, :]
    dot = jnp.mean(scaled_in * seq_rows, axis=1, keepdims=True)
    grad_seq = inv_rms * scaled_in - seq_rows * (inv_rms * inv_rms * inv_rms * dot)
    grad_inputs = (grad_seq + cot_rows.astype(f32))[None]
    grad_in = grad_in.astype(f32)
    grad_in_weight = jnp.concatenate(
        [whole_again(grad_in[..., :inner]), whole_again(grad_in[..., inner:]), grad_keys[:, :KEYS]], axis=1
    )
    grad_step_weight = grad_keys[:, KEYS : KEYS + H]
    small = small.reshape(-1)
    sizes = [width, (CONV + 1) * conv_weight.shape[1], H, H, H, E]
    parts = []
    for size in sizes:
        parts.append(small[:size])
        small = small[size:]
    conv_sums = parts[1].reshape(CONV + 1, -1)
    return (
        output, grad_inputs, parts[0], grad_in_weight, grad_step_weight, conv_sums[:CONV], conv_sums[CONV],
        parts[2], parts[3], parts[4], parts[5], grad_out_weight,
    )


def solution(mesh):
    both = P(("seq", "batch"), None)
    tok = P("batch", "seq", None)
    in_specs = (
        tok, tok, P("batch", None), P("batch"), P(), both, both, P(), P(), P(), P(), P(), P(), both,
    )
    out_specs = (tok, tok, P(), both, both, P(), P(), P(), P(), P(), P(), both)
    return jax.shard_map(body, mesh=mesh, in_specs=in_specs, out_specs=out_specs, check_vma=False)
```

```python
from functools import partial

import jax
import jax.numpy as jnp
from jax import lax
from jax.experimental import pallas as pl
from jax.experimental.pallas import tpu as pltpu
from jax.sharding import PartitionSpec as P

H = 64
P_SIZE = 64
N = 128
CONV = 4
DOCS = 4
E = 4096
KEYS = 2 * N
STEP_PAD = 128
CHUNK = 128
epsilon = 1e-05
f32 = jnp.float32
bf16 = jnp.bfloat16


def mm(a, b, dims):
    return lax.dot_general(a, b, (dims, ((), ())), preferred_element_type=f32)


NN = ((1,), (0,))
NT = ((1,), (1,))
TN = ((0,), (0,))


def pair_cols(low, col, first):
    return jnp.where(low, col[:, first : first + 1], col[:, first + 1 : first + 2])


def scan_forward_kernel(
    val_ref, key_ref, cum_ref, cum_t_ref, dt_ref, dt_t_ref, doc_ref, doc_t_ref, flow_ref, skip_ref, y_ref, state_ref, state
):
    heads = cum_ref.shape[1]

    @pl.when(pl.program_id(0) == 0)
    def _():
        state[...] = jnp.zeros_like(state)

    state_ref[0] = state[...].astype(bf16)
    cum = cum_ref[...]
    last = cum[CHUNK - 1 :, :]
    doc = doc_ref[...]
    doc_t = doc_t_ref[...]
    flow = flow_ref[...]
    rows = lax.broadcasted_iota(jnp.int32, (CHUNK, CHUNK), 0)
    cols = lax.broadcasted_iota(jnp.int32, (CHUNK, CHUNK), 1)
    bias = jnp.where((doc == doc_t) & (rows >= cols), 0.0, -1e30)
    carry_w = flow * jnp.exp(cum)
    final_w = jnp.where(doc == doc[CHUNK - 1 :, :], jnp.exp(last - cum), 0.0) * dt_ref[...]
    gain = carry_w[CHUNK - 1 :, :]
    low = cols < P_SIZE
    low_row = low[:1]
    write = key_ref[:, :N]
    read = key_ref[:, N:]
    write_t = write.astype(f32).T.astype(bf16)
    scores = mm(read, write, NT)
    for pair in range(heads // 2):
        first = 2 * pair
        lanes = slice(pair * 128, pair * 128 + 128)
        x = val_ref[:, lanes]
        xf = x.astype(f32)
        weights = []
        for h in (first, first + 1):
            decay = jnp.exp(cum[:, h : h + 1] - cum_t_ref[h : h + 1, :] + bias)
            weights.append((decay * scores * dt_t_ref[h : h + 1, :]).astype(bf16))
        stacked = jnp.concatenate(
            [jnp.where(low, xf, 0.0).astype(bf16), jnp.where(low, 0.0, xf).astype(bf16)], axis=0
        )
        old = state[:, lanes]
        y = mm(jnp.concatenate(weights, axis=1), stacked, NN)
        y = y + pair_cols(low, carry_w, first) * mm(read, old.astype(bf16), NN)
        y_ref[:, lanes] = y + skip_ref[:, lanes] * xf
        state[:, lanes] = pair_cols(low_row, gain, first) * old + mm(
            write_t, (pair_cols(low, final_w, first) * xf).astype(bf16), NN
        )


def scan_backward_kernel(
    val_ref, key_ref, cum_ref, cum_t_ref, dt_ref, doc_ref, doc_t_ref, flow_ref, skip_ref, state_ref, dy_ref,
    dval_ref, dkey_ref, dcum_ref, dcum_t_ref, ddt_ref, dskip_ref, dstate,
):
    heads = cum_ref.shape[1]

    @pl.when(pl.program_id(0) == 0)
    def _():
        dstate[...] = jnp.zeros_like(dstate)
        dskip_ref[...] = jnp.zeros_like(dskip_ref)

    cum = cum_ref[...]
    dt = dt_ref[...]
    last = cum[CHUNK - 1 :, :]
    doc = doc_ref[...]
    doc_t = doc_t_ref[...]
    flow = flow_ref[...]
    rows = lax.broadcasted_iota(jnp.int32, (CHUNK, CHUNK), 0)
    cols = lax.broadcasted_iota(jnp.int32, (CHUNK, CHUNK), 1)
    bias = jnp.where((doc == doc_t) & (cols >= rows), 0.0, -1e30)
    carry_w = flow * jnp.exp(cum)
    final_d = jnp.where(doc == doc[CHUNK - 1 :, :], jnp.exp(last - cum), 0.0)
    final_w = final_d * dt
    gain = carry_w[CHUNK - 1 :, :]
    low = cols < P_SIZE
    low_row = low[:1]
    write = key_ref[:, :N]
    read = key_ref[:, N:]
    read_t = read.astype(f32).T.astype(bf16)
    scores_t = mm(write, read, NT)
    dscores_t = jnp.zeros((CHUNK, CHUNK), f32)
    dwrite = jnp.zeros((CHUNK, N), f32)
    dread = jnp.zeros((CHUNK, N), f32)
    end_row = lax.broadcasted_iota(jnp.int32, (CHUNK, 1), 0) == CHUNK - 1
    dcum_cols = []
    dcum_rows = []
    ddt_cols = []
    for pair in range(heads // 2):
        first = 2 * pair
        lanes = slice(pair * 128, pair * 128 + 128)
        x = val_ref[:, lanes]
        xf = x.astype(f32)
        dy = dy_ref[:, lanes]
        dyb = dy.astype(bf16)
        x_stack = jnp.concatenate(
            [jnp.where(low, xf, 0.0).astype(bf16), jnp.where(low, 0.0, xf).astype(bf16)], axis=0
        )
        dy_stack = jnp.concatenate(
            [jnp.where(low, dy, 0.0).astype(bf16), jnp.where(low, 0.0, dy).astype(bf16)], axis=0
        )
        dweights = mm(x_stack, dyb, NT)
        old = state_ref[0, :, lanes]
        grad = dstate[:, lanes]
        gradb = grad.astype(bf16)
        carried = mm(read, old, NN)
        pushed = mm(write, gradb, NN)
        carry_p = pair_cols(low, carry_w, first)
        final_p = pair_cols(low, final_w, first)
        carry_prod = dy * carried
        final_prod = xf * pushed
        gain_prod = jnp.sum(grad * old.astype(f32), axis=0, keepdims=True)
        weights = []
        for which, h in enumerate((first, first + 1)):
            col = dt[:, h : h + 1]
            decay = jnp.exp(cum_t_ref[h : h + 1, :] - cum[:, h : h + 1] + bias)
            weighted = decay * col
            weights.append((weighted * scores_t).astype(bf16))
            dw = dweights[which * CHUNK : (which + 1) * CHUNK]
            dscores_t = dscores_t + dw * weighted
            direct = dw * decay * scores_t
            ddt_in = jnp.sum(direct, axis=1, keepdims=True)
            dcum_rows.append(jnp.sum(direct * col, axis=0, keepdims=True))
            half = low if which == 0 else ~low
            half_row = low_row if which == 0 else ~low_row
            carry_sum = jnp.sum(jnp.where(half, carry_prod, 0.0), axis=1, keepdims=True)
            final_sum = jnp.sum(jnp.where(half, final_prod, 0.0), axis=1, keepdims=True)
            push = final_w[:, h : h + 1] * final_sum
            at_end = jnp.sum(push, axis=0, keepdims=True) + gain[:, h : h + 1] * jnp.sum(
                jnp.where(half_row, gain_prod, 0.0), axis=1, keepdims=True
            )
            ddt_cols.append(ddt_in + final_d[:, h : h + 1] * final_sum)
            dcum_cols.append(
                carry_w[:, h : h + 1] * carry_sum - push - col * ddt_in + jnp.where(end_row, at_end, 0.0)
            )
        dx = mm(jnp.concatenate(weights, axis=1), dy_stack, NN)
        dval_ref[:, lanes] = dx + final_p * pushed + skip_ref[:, lanes] * dy
        dskip_ref[:, lanes] += jnp.sum(dy * xf, axis=0, keepdims=True)
        dwrite = dwrite + mm((final_p * xf).astype(bf16), gradb, NT)
        carry_dy = (carry_p * dy).astype(bf16)
        dread = dread + mm(carry_dy, old, NT)
        dstate[:, lanes] = pair_cols(low_row, gain, first) * grad + mm(read_t, carry_dy, NN)
    dsb = dscores_t.astype(bf16)
    dkey_ref[:, :N] = dwrite + mm(dsb, read, NN)
    dkey_ref[:, N:] = dread + mm(dsb, write, TN)
    dcum_ref[...] = jnp.concatenate(dcum_cols, axis=1)
    dcum_t_ref[...] = jnp.concatenate(dcum_rows, axis=0)
    ddt_ref[...] = jnp.concatenate(ddt_cols, axis=1)


def scan_forward(val, keys, cum, cum_t, dt, dt_t, doc, doc_t, flow, skip):
    length = val.shape[0]
    heads = cum.shape[1]
    inner = heads * P_SIZE
    steps = length // CHUNK
    row = lambda width: pl.BlockSpec((CHUNK, width), lambda i: (i, 0))
    lane = lambda height: pl.BlockSpec((height, CHUNK), lambda i: (0, i))
    return pl.pallas_call(
        scan_forward_kernel,
        grid=(steps,),
        in_specs=[
            row(inner), row(KEYS), row(heads), lane(heads), row(heads), lane(heads), row(1), lane(1), row(1),
            pl.BlockSpec((1, inner), lambda i: (0, 0)),
        ],
        out_specs=[row(inner), pl.BlockSpec((1, N, inner), lambda i: (i, 0, 0))],
        out_shape=[
            jax.ShapeDtypeStruct((length, inner), f32),
            jax.ShapeDtypeStruct((steps, N, inner), bf16),
        ],
        scratch_shapes=[pltpu.VMEM((N, inner), f32)],
        compiler_params=pltpu.CompilerParams(vmem_limit_bytes=40 * 2**20),
        cost_estimate=pl.CostEstimate(
            flops=length * inner * 1024, bytes_accessed=length * inner * 10, transcendentals=length * heads * CHUNK
        ),
    )(val, keys, cum, cum_t, dt, dt_t, doc, doc_t, flow, skip)


def scan_backward(val, keys, cum, cum_t, dt, doc, doc_t, flow, skip, states, dy):
    length = val.shape[0]
    heads = cum.shape[1]
    inner = heads * P_SIZE
    steps = length // CHUNK
    row = lambda width: pl.BlockSpec((CHUNK, width), lambda i: (steps - 1 - i, 0))
    lane = lambda height: pl.BlockSpec((height, CHUNK), lambda i: (0, steps - 1 - i))
    whole = pl.BlockSpec((1, inner), lambda i: (0, 0))
    return pl.pallas_call(
        scan_backward_kernel,
        grid=(steps,),
        in_specs=[
            row(inner), row(KEYS), row(heads), lane(heads), row(heads), row(1), lane(1), row(1), whole,
            pl.BlockSpec((1, N, inner), lambda i: (steps - 1 - i, 0, 0)), row(inner),
        ],
        out_specs=[row(inner), row(KEYS), row(heads), lane(heads), row(heads), whole],
        out_shape=[
            jax.ShapeDtypeStruct((length, inner), f32),
            jax.ShapeDtypeStruct((length, KEYS), f32),
            jax.ShapeDtypeStruct((length, heads), f32),
            jax.ShapeDtypeStruct((heads, length), f32),
            jax.ShapeDtypeStruct((length, heads), f32),
            jax.ShapeDtypeStruct((1, inner), f32),
        ],
        scratch_shapes=[pltpu.VMEM((N, inner), f32)],
        compiler_params=pltpu.CompilerParams(vmem_limit_bytes=40 * 2**20),
        cost_estimate=pl.CostEstimate(
            flops=length * inner * 3072, bytes_accessed=length * inner * 14, transcendentals=length * heads * CHUNK
        ),
    )(val, keys, cum, cum_t, dt, doc, doc_t, flow, skip, states, dy)


MESH = pl.DeviceIdType.MESH
HBM = pl.BlockSpec(memory_space=pl.ANY)
VMEM = pl.BlockSpec(memory_space=pltpu.VMEM)


def z_pair(peers, groups):
    planes = groups // 2
    return 2 if planes % 2 == 0 and (E // (peers * planes)) % (2 * P_SIZE) == 0 else 1


def flip(value, bits):
    bit = 1
    while bit <= bits:
        if bits & bit:
            value = value + bit - 2 * bit * (value // bit % 2)
        bit *= 2
    return value


class Place:
    def __init__(self):
        self.peers = lax.axis_size("seq")
        groups = lax.axis_size("batch")
        self.near = z_pair(self.peers, groups)
        self.far = groups // 2 // self.near
        self.s = lax.axis_index("seq")
        b = lax.axis_index("batch")
        self.c = b % 2
        self.zl = b // 2 % self.near
        self.zh = b // 2 // self.near

    def at(self, s=0, zl=0, zh=0, c=0):
        return (flip(self.s, s), (flip(self.zh, zh) * self.near + flip(self.zl, zl)) * 2 + flip(self.c, c))

    def column_runs(self, s, zl, width):
        outer = self.far if self.near > 1 else 1
        run = width // (2 * outer)
        runs = []
        for part in range(2):
            for i in range(outer):
                first = part * E + ((s * outer + i) * self.near + zl) * run
                runs.append((pl.ds(pl.multiple_of(first, 128), run), pl.ds((part * outer + i) * run, run)))
        return runs

    def partners(self):
        cube = [self.at(s=o // self.near, zl=o % self.near) for o in range(1, self.peers * self.near)]
        return cube, [self.at(zh=o) for o in range(1, self.far)], [self.at(c=1)]


def greet(devices):
    barrier = pltpu.get_barrier_semaphore()
    for device in devices:
        pl.semaphore_signal(barrier, inc=1, device_id=device, device_id_type=MESH)
    pl.semaphore_wait(barrier, len(devices))


class Mover:
    def __init__(self, send, recv, local):
        self.send, self.recv, self.local = send, recv, local
        self.sent, self.kept = 0, 0
        self.open = []

    def put(self, src, dst, device):
        copy = pltpu.make_async_remote_copy(
            src_ref=src, dst_ref=dst, send_sem=self.send.at[self.sent], recv_sem=self.recv.at[self.sent],
            device_id=device, device_id_type=MESH,
        )
        copy.start()
        self.sent += 1
        self.open.append(copy)
        return copy

    def keep(self, src, dst):
        copy = pltpu.make_async_copy(src, dst, self.local.at[self.kept])
        copy.start()
        self.kept += 1
        return copy

    def close(self):
        for copy in self.open:
            copy.wait_send()


def run_paths(paths):
    paths = list(paths)
    while paths:
        alive = []
        for path in paths:
            try:
                next(path)
                alive.append(path)
            except StopIteration:
                pass
        paths = alive


def turn(paths):
    for path in paths:
        next(path, None)


def bits_of(peers):
    return [1 << i for i in range(peers.bit_length() - 1)]


def combos(bits):
    out = [0]
    for bit in reversed(bits):
        out = [bit | o for o in out] + out
    return out


def gather_kernel(
    in_ref, key_ref, out_ref, rows_ref, cot_ref, meta_ref,
    w_ref, k_ref, o_ref, x_ref, ct_ref, m_ref, send, recv, local,
):
    me = Place()
    s, zl, zh, c = me.s, me.zl, me.zh, me.c
    cube, far, sibling = me.partners()
    greet(cube + far + sibling)
    mover = Mover(send, recv, local)
    bits = bits_of(me.peers)

    def plane_path(src, dst, order, near):
        view = dst.at[flip(zl, near)]
        if near:
            copy = mover.put(src, dst.at[zl, s], me.at(zl=near))
            yield
            copy.wait_recv()
        else:
            own = mover.keep(src, view.at[s])
        held = [0]
        for bit in order:
            copies = []
            for h in held:
                at = view.at[flip(s, h)]
                copies.append(mover.put(at if near or h else src, at if near else dst.at[zl, flip(s, h)], me.at(s=bit)))
            held = held + [h ^ bit for h in held]
            yield
            for copy in copies:
                copy.wait_recv()
        if not near:
            own.wait()

    def meta_path():
        own = mover.keep(meta_ref, m_ref.at[zl])
        near = [mover.put(meta_ref, m_ref.at[zl], me.at(zl=o)) for o in range(1, me.near)]
        yield
        own.wait()
        for copy in near:
            copy.wait_recv()

    def key_path():
        block = k_ref.at[s, zh, zl, c]
        own = mover.keep(key_ref, block)
        copies = [mover.put(key_ref, block, me.at(zh=o)) for o in range(1, me.far)]
        yield
        own.wait()
        for copy in copies:
            copy.wait_recv()
        block = k_ref.at[s, :, zl, c]
        copies = [mover.put(block, block, me.at(zl=o)) for o in range(1, me.near)]
        yield
        for copy in copies:
            copy.wait_recv()
        held = [0]
        for bit in bits:
            copies = []
            for h in held:
                block = k_ref.at[flip(s, h), :, :, c]
                copies.append(mover.put(block, block, me.at(s=bit)))
            held = held + [h ^ bit for h in held]
            yield
            for copy in copies:
                copy.wait_recv()
        block = k_ref.at[:, :, :, c]
        copy = mover.put(block, block, me.at(c=1))
        yield
        copy.wait_recv()

    def spread_path(copies, view):
        last = []
        for o, copy in copies:
            yield
            copy.wait_recv()
            last.append(mover.put(view(flip(zh, o)), view(flip(zh, o)), me.at(c=1)))
        return last

    def out_path():
        own = mover.keep(out_ref, o_ref.at[zh, c])
        copies = [(o, mover.put(out_ref, o_ref.at[zh, c], me.at(zh=o))) for o in range(1, me.far)]
        first = mover.put(out_ref, o_ref.at[zh, c], me.at(c=1))
        last = yield from spread_path(copies, lambda h: o_ref.at[h, c])
        yield
        own.wait()
        for copy in last + [first]:
            copy.wait_recv()

    def weight_path():
        moves = {}
        for step in range(me.peers):
            for o in range(me.near):
                to_s, to_zl = flip(s, step), flip(zl, o)
                for src, dst in me.column_runs(to_s, to_zl, w_ref.shape[-1]):
                    src = in_ref.at[:, src]
                    dst = w_ref.at[s, zh, zl, c, :, dst]
                    if step or o:
                        copy = mover.put(src, dst, me.at(s=step, zl=o))
                    else:
                        copy = mover.keep(src, dst)
                    moves.setdefault(step, []).append(copy)
        pieces = []
        for step in range(me.peers):
            yield
            for i, copy in enumerate(moves[step]):
                if step == 0 and i < len(moves[0]) // me.near:
                    copy.wait()
                else:
                    copy.wait_recv()
            block = w_ref.at[flip(s, step), zh, :, c]
            copies = [(o, mover.put(block, block, me.at(zh=o))) for o in range(1, me.far)]
            pieces.append((step, copies, mover.put(block, block, me.at(c=1))))
        last = []
        for step, copies, first in pieces:
            last.append(first)
            last += yield from spread_path(copies, lambda h, step=step: w_ref.at[flip(s, step), h, :, c])
        yield
        for copy in last:
            copy.wait_recv()

    own_x = plane_path(rows_ref, x_ref, bits, 0)
    own_c = plane_path(cot_ref, ct_ref, bits[::-1], 0)
    near_x = [plane_path(rows_ref, x_ref, bits, o) for o in range(1, me.near)]
    near_c = [plane_path(cot_ref, ct_ref, bits[::-1], o) for o in range(1, me.near)]
    near = near_x + near_c
    keys, weights, outs = key_path(), weight_path(), out_path()
    turn([own_x, own_c, weights] + near + [keys, outs])
    extra = meta_path()
    turn([extra, own_x, own_c] + [weights] * me.peers + [keys] + near + [keys])
    turn([own_x, own_c] + near + [keys, outs, weights, keys, weights])
    run_paths([weights, extra, keys, outs, own_x, own_c] + near)
    mover.close()


def remote_params(identity):
    return pltpu.CompilerParams(collective_id=identity, has_side_effects=True, vmem_limit_bytes=58 * 2**20)


def sems(copies, kept):
    return [pltpu.SemaphoreType.DMA((copies,)), pltpu.SemaphoreType.DMA((copies,)), pltpu.SemaphoreType.DMA((kept,))]


def gather(in_w, keys, out_w, rows, cot, meta):
    me = Place()
    peers, near, far = me.peers, me.near, me.far
    shape = lambda lead, part: jax.ShapeDtypeStruct(lead + part, bf16)
    columns = 2 * E // (peers * near)
    runs = 2 * (far if near > 1 else 1)
    copies = runs * (peers * near - 1) + (peers + 1) * (2 * far - 1) + 2 * (near * peers - 1)
    copies += 2 * near + peers + far - 3
    return pl.pallas_call(
        gather_kernel,
        out_shape=[
            shape((peers, far, near, 2), (in_w.shape[0], columns)),
            shape((peers, far, near, 2), keys.shape),
            shape((far, 2), out_w.shape),
            shape((near, peers), rows.shape),
            shape((near, peers), cot.shape),
            jax.ShapeDtypeStruct((near,) + meta.shape, meta.dtype),
        ],
        in_specs=[HBM] * 6,
        out_specs=[HBM] * 6,
        scratch_shapes=sems(copies, runs + 5),
        compiler_params=remote_params(0),
        name="gather_all",
    )(in_w, keys, out_w, rows, cot, meta)


def total_kernel(part_ref, sum_ref, box, send, recv, local):
    me = Place()
    cube = me.partners()[0]
    greet(cube)
    mover = Mover(send, recv, local)
    copies = [mover.put(part_ref, box.at[i], device) for i, device in enumerate(cube)]
    total = part_ref[...]
    for i, copy in enumerate(copies):
        copy.wait_recv()
        total = total + box[i]
    sum_ref[...] = total
    mover.close()


def cube_total(part):
    me = Place()
    count = me.peers * me.near - 1
    return pl.pallas_call(
        total_kernel,
        out_shape=jax.ShapeDtypeStruct(part.shape, f32),
        in_specs=[VMEM],
        out_specs=VMEM,
        scratch_shapes=[pltpu.VMEM((count,) + part.shape, f32)] + sems(count, 1),
        compiler_params=remote_params(1),
        name="cube_total",
    )(part)


def add_rows(out, parts):
    shape = out.shape
    tile = min(16, shape[-2])
    lead = [()]
    for size in shape[:-2]:
        lead = [l + (i,) for l in lead for i in range(size)]
    for l in lead:

        def step(i, carry, l=l):
            at = l + (pl.ds(pl.multiple_of(i * tile, tile), tile), slice(None))
            total = parts[0][at].astype(f32)
            for part in parts[1:]:
                total = total + part[at].astype(f32)
            out[at] = total.astype(out.dtype)
            return carry

        lax.fori_loop(0, shape[-2] // tile, step, 0)


def scatter_kernel(
    bp_ref, gn_ref, gw_ref, go_ref, gk_ref, v_ref, u_ref,
    ob_ref, og_ref, ow_ref, oo_ref, ok_ref, ov_ref, ou_ref,
    b_own, b_box, b_near, n_own, n_box, n_near, w_own, w_box, w_far, o_own, o_box, o_far,
    k_own, k_box, k_near, k_far, k_bits, v_box, u_box, send, recv, local,
):
    me = Place()
    s, zl, zh, c = me.s, me.zl, me.zh, me.c
    cube, far, sibling = me.partners()
    greet(cube + far + sibling)
    mover = Mover(send, recv, local)
    bits = bits_of(me.peers)

    def rows_path(src, own, box, near_box, out, order, near, arrivals):
        own, box = own.at[near], box.at[near]
        at_zl = src.at[flip(zl, near)]
        todo = combos(order[1:])
        copies, loads = [], []
        for j, o in enumerate(todo):
            copies.append(mover.put(at_zl.at[flip(s, order[0] ^ o)], box.at[j], me.at(s=order[0])))
            loads.append(mover.keep(at_zl.at[flip(s, o)], own.at[j]))
        base = 0
        for i, bit in enumerate(order):
            rest = order[i + 1 :]
            count = 1 << len(rest)
            offset = (1 << (len(order) - 1)) - count
            coming = []
            for j in range(count):
                yield
                copies[j].wait_recv()
                if i == 0:
                    loads[j].wait()
                if rest or near:
                    add_rows(own.at[offset + j], [own.at[offset + j], box.at[base + j]])
                if rest and j < count // 2:
                    coming.append(mover.put(own.at[offset + j], box.at[base + count + j], me.at(s=rest[0])))
            copies = coming
            last = base
            base += count
        end = (1 << (len(order) - 1)) - 1
        if near:
            arrivals.append(mover.put(own.at[end], near_box.at[near - 1], me.at(zl=near)))
            yield
        else:
            yield
            for _ in range(me.near - 1):
                arrivals.pop(0).wait_recv()
            add_rows(out, [own.at[end], box.at[last]] + [near_box.at[o - 1] for o in range(1, me.near)])

    def weight_path():
        order = [(o, k) for o in range(1, me.far) for k in range(me.peers)] + [(0, k) for k in range(me.peers)]
        loads, copies = {}, {}
        for o, k in order:
            copies[o, k] = mover.put(gw_ref.at[flip(s, k), flip(zh, o), :, 1 - c], w_box.at[o, k], me.at(c=1))
            loads[o, k] = mover.keep(gw_ref.at[flip(s, k), flip(zh, o), :, c], w_own.at[o, k])
        far_copies = {}
        for o, k in order:
            yield
            loads[o, k].wait()
            copies[o, k].wait_recv()
            if o:
                add_rows(w_own.at[o, k], [w_own.at[o, k], w_box.at[o, k]])
                far_copies[o, k] = mover.put(w_own.at[o, k], w_far.at[o - 1, k], me.at(zh=o))
        ends, kept = [], []
        for k in range(me.peers):
            yield
            for o in range(1, me.far):
                far_copies[o, k].wait_recv()
            parts = [w_own.at[0, k], w_box.at[0, k]] + [w_far.at[o - 1, k] for o in range(1, me.far)]
            add_rows(w_own.at[0, k], parts)
            for o in range(me.near):
                for whole, mine in me.column_runs(s, zl, w_own.shape[-1]):
                    src = w_own.at[0, k, flip(zl, o), :, mine]
                    if k or o:
                        ends.append(mover.put(src, ow_ref.at[:, whole], me.at(s=k, zl=o)))
                    else:
                        kept.append(mover.keep(src, ow_ref.at[:, whole]))
        yield
        for copy in kept:
            copy.wait()
        for copy in ends:
            copy.wait_recv()

    def out_path():
        order = list(range(1, me.far)) + [0]
        copies, loads = {}, {}
        for o in order:
            copies[o] = mover.put(go_ref.at[flip(zh, o), 1 - c], o_box.at[o], me.at(c=1))
            loads[o] = mover.keep(go_ref.at[flip(zh, o), c], o_own.at[o])
        yield
        far_copies = {}
        for o in order:
            loads[o].wait()
            copies[o].wait_recv()
            if o:
                add_rows(o_own.at[o], [o_own.at[o], o_box.at[o]])
                far_copies[o] = mover.put(o_own.at[o], o_far.at[o - 1], me.at(zh=o))
        for _ in range(2 * me.peers + 4):
            yield
        for o in range(1, me.far):
            far_copies[o].wait_recv()
        add_rows(oo_ref, [o_own.at[0], o_box.at[0]] + [o_far.at[o - 1] for o in range(1, me.far)])

    def key_path():
        blocks = combos(bits)
        copies, loads = [], []
        for j, o in enumerate(blocks):
            copies.append(mover.put(gk_ref.at[flip(s, o), :, :, 1 - c], k_box.at[j], me.at(c=1)))
            loads.append(mover.keep(gk_ref.at[flip(s, o), :, :, c], k_own.at[j]))
        half = me.peers // 2
        sent = []
        for j in range(me.peers):
            yield
            loads[j].wait()
            copies[j].wait_recv()
            add_rows(k_own.at[j], [k_own.at[j], k_box.at[j]])
            if j < half:
                sent.append(mover.put(k_own.at[j], k_bits.at[j], me.at(s=bits[0])))
        base = 0
        for i, bit in enumerate(bits):
            count = me.peers >> (i + 1)
            offset = me.peers - count
            coming = []
            for j in range(count):
                yield
                sent[j].wait_recv()
                add_rows(k_own.at[offset + j], [k_own.at[offset + j], k_bits.at[base + j]])
                if i + 1 < len(bits) and j < count // 2:
                    coming.append(mover.put(k_own.at[offset + j], k_bits.at[base + count + j], me.at(s=bits[i + 1])))
            base += count
            sent = coming
        end = k_own.at[me.peers - 1]
        copies = [mover.put(end.at[:, flip(zl, o)], k_near.at[o - 1], me.at(zl=o)) for o in range(1, me.near)]
        yield
        for copy in copies:
            copy.wait_recv()
        add_rows(end.at[:, zl], [end.at[:, zl]] + [k_near.at[o - 1] for o in range(1, me.near)])
        copies = [mover.put(end.at[flip(zh, o), zl], k_far.at[o - 1], me.at(zh=o)) for o in range(1, me.far)]
        yield
        for copy in copies:
            copy.wait_recv()
        add_rows(ok_ref, [end.at[zh, zl]] + [k_far.at[o - 1] for o in range(1, me.far)])

    def small_path():
        turns = [me.at(c=1)] + [me.at(zl=o) for o in bits_of(me.near)]
        turns += [me.at(s=o) for o in bits] + [me.at(zh=o) for o in bits_of(me.far)]
        pairs = [(v_ref, v_box, ov_ref), (u_ref, u_box, ou_ref)]
        for src, box, _ in pairs:
            box[0] = src[...]
        for i, device in enumerate(turns):
            copies = [mover.put(box.at[2 * i], box.at[2 * i + 1], device) for _, box, _ in pairs]
            yield
            for copy, (_, box, _) in zip(copies, pairs):
                copy.wait_recv()
                box[2 * i + 2] = box[2 * i] + box[2 * i + 1]
        for _, box, out in pairs:
            out[...] = box[2 * len(turns)]

    arrivals_n, arrivals_b = [], []
    orders = (bits[::-1], bits)
    grads = (gn_ref, n_own, n_box, n_near, og_ref, orders[0])
    branch = (bp_ref, b_own, b_box, b_near, ob_ref, orders[1])
    near_n = [rows_path(*grads, o, arrivals_n) for o in range(1, me.near)]
    near_b = [rows_path(*branch, o, arrivals_b) for o in range(1, me.near)]
    own_n, own_b = rows_path(*grads, 0, arrivals_n), rows_path(*branch, 0, arrivals_b)
    near, own = near_n + near_b, [own_n, own_b]
    weights, keys, small, outs = weight_path(), key_path(), small_path(), out_path()
    turn([weights] + near + own + [keys, small, outs])
    turn([weights] * (me.far * me.peers) + [outs, keys] * me.peers)
    run_paths(near + [keys, small] + own + [weights, outs])
    mover.close()


def scatter(branch, grads, gw, go, gk, small, conv):
    me = Place()
    peers, near, far = me.peers, me.near, me.far
    tokens, width = branch.shape[2:]
    stages = len(bits_of(peers)) + len(bits_of(near)) + len(bits_of(far)) + 1
    vm = lambda *shape: pltpu.VMEM(shape, bf16)
    boxes = lambda part: pltpu.VMEM((2 * stages + 1,) + part.shape, f32)
    rows_scratch = [
        vm(near, peers // 2, tokens, width), vm(near, peers - 1, tokens, width), vm(max(near - 1, 1), tokens, width)
    ]
    block = gw.shape[2:3] + gw.shape[4:]
    kblock = gk.shape[2:3] + gk.shape[4:]
    oblock = go.shape[2:]
    runs = 2 * (far if near > 1 else 1)
    copies = 2 * (peers * near - 1) + (2 * far - 1) * peers + runs * (peers * near - 1) + 2 * far - 1
    copies += 2 * peers - 1 + near - 1 + far - 1 + 2 * stages
    kept = peers * near + far * peers + runs + far + peers
    same = lambda part: jax.ShapeDtypeStruct(part.shape, part.dtype)
    return pl.pallas_call(
        scatter_kernel,
        out_shape=[
            jax.ShapeDtypeStruct((tokens, width), f32),
            jax.ShapeDtypeStruct((tokens, width), f32),
            jax.ShapeDtypeStruct((block[1], 2 * E), bf16),
            jax.ShapeDtypeStruct(oblock, f32),
            jax.ShapeDtypeStruct(kblock[1:], f32),
            same(small),
            same(conv),
        ],
        in_specs=[HBM] * 5 + [VMEM] * 2,
        out_specs=[VMEM, VMEM, HBM, VMEM, VMEM, VMEM, VMEM],
        scratch_shapes=rows_scratch
        + rows_scratch
        + [vm(far, peers, *block), vm(far, peers, *block), vm(max(far - 1, 1), peers, *block)]
        + [vm(far, *oblock), vm(far, *oblock), vm(max(far - 1, 1), *oblock)]
        + [
            vm(peers, far, *kblock), vm(peers, far, *kblock), vm(max(near - 1, 1), far, *kblock[1:]),
            vm(max(far - 1, 1), *kblock[1:]), vm(peers - 1, far, *kblock), boxes(small), boxes(conv),
        ]
        + sems(copies, kept),
        compiler_params=remote_params(2),
        name="scatter_all",
    )(branch, grads, gw, go, gk, small, conv)


def doc_index(places, doc_ends):
    return jnp.sum((places[:, None] >= doc_ends[None, :-1]).astype(jnp.int32), axis=1)


def moved_down(rows, by):
    return jnp.concatenate([jnp.zeros((by,) + rows.shape[1:], rows.dtype), rows[: rows.shape[0] - by]], axis=0)


def moved_up(rows, by):
    return jnp.concatenate([rows[by:], jnp.zeros((by,) + rows.shape[1:], rows.dtype)], axis=0)


def convolve(conv_in, weight, bias, masks):
    total = jnp.broadcast_to(bias[None, :], conv_in.shape)
    for k in range(CONV):
        total = total + weight[k][None, :] * moved_down(conv_in, CONV - 1 - k).astype(f32) * masks[k][:, None]
    return total


def convolve_back(dact, conv_in, conv_sum, weight, masks):
    sig = jax.nn.sigmoid(conv_sum)
    dconv = dact * (sig * (1.0 + conv_sum * (1.0 - sig)))
    sums = []
    grad_in = jnp.zeros_like(dconv)
    for k in range(CONV):
        taken = dconv * masks[k][:, None]
        sums.append(jnp.sum(taken * moved_down(conv_in, CONV - 1 - k).astype(f32), axis=0))
        grad_in = grad_in + weight[k][None, :] * moved_up(taken, CONV - 1 - k)
    sums.append(jnp.sum(dconv, axis=0))
    return grad_in.astype(bf16), jnp.stack(sums)


def body(
    inputs, cotangent, doc_lengths, head_width, pre_gain, in_weight, step_weight, conv_weight, conv_bias,
    step_bias, decay_log, skip_gain, norm_gain, out_weight,
):
    me = Place()
    peers, near, far = me.peers, me.near, me.far
    outer = far if near > 1 else 1
    tokens = inputs.shape[1]
    width = inputs.shape[2]
    span = tokens * peers
    length = span * near
    heads = H // (peers * near)
    inner = heads * P_SIZE
    rows = in_weight.shape[0]
    seq_rows = inputs[0].astype(f32)
    cot_rows = cotangent[0]

    def own(vector):
        part = vector.reshape(-1, peers, outer, near, vector.shape[-1] // (peers * outer * near))
        part = lax.dynamic_index_in_dim(part, me.s, 1, False)
        part = lax.dynamic_index_in_dim(part, me.zl, 2, False)
        return part.reshape(vector.shape[:-1] + (-1,))

    def spread(part):
        lead = part.shape[:-1]
        part = part.reshape(-1, 1, outer, 1, part.shape[-1] // outer)
        full = jnp.zeros((part.shape[0], peers, outer, near, part.shape[-1]), part.dtype)
        return lax.dynamic_update_slice(full, part, (0, me.s, 0, me.zl, 0)).reshape(lead + (-1,))

    key_send = jnp.concatenate(
        [in_weight[:, 2 * E :], step_weight, jnp.zeros((rows, STEP_PAD - H), bf16)], axis=1
    )
    inv_rms = lax.rsqrt(jnp.mean(seq_rows * seq_rows, axis=1, keepdims=True) + epsilon)
    normed = (seq_rows * inv_rms * pre_gain[None, :]).astype(bf16)
    meta = jnp.zeros((8, 128), jnp.int32)
    meta = meta.at[0, :DOCS].set(doc_lengths[0]).at[1, 0].set(head_width[0])
    in_w, key_w, out_w, normed, cot_all, meta = gather(in_weight, key_send, out_weight, normed, cot_rows, meta)
    in_w = in_w.reshape(width, 2 * inner)
    key_w = key_w.reshape(width, -1)
    out_w = out_w.reshape(inner, width)
    normed = normed.reshape(length, width)
    cot_all = cot_all.reshape(length, width)

    places = jnp.arange(span, dtype=jnp.int32)
    doc_ids = jnp.concatenate(
        [doc_index(places, jnp.cumsum(meta[i, 0, :DOCS])) + i * DOCS for i in range(near)]
    )
    before = jnp.concatenate([jnp.full((1,), -1, jnp.int32), doc_ids[CHUNK - 1 : -1 : CHUNK]])
    flow = (doc_ids == jnp.repeat(before, CHUNK)).astype(f32)[:, None]
    doc = doc_ids[:, None]
    doc_t = doc_ids[None, :]
    counts = meta[:, 1, 0]
    head_total = jnp.repeat((counts * P_SIZE).astype(f32), span)[:, None]
    my_heads = own(jnp.arange(H, dtype=jnp.int32))
    head_mask = jnp.repeat((my_heads[None, :] < counts[:, None]).astype(f32), P_SIZE, axis=1)
    head_mask = jnp.repeat(head_mask, span, axis=0)
    masks = []
    for k in range(CONV):
        lag = CONV - 1 - k
        masks.append((jnp.concatenate([jnp.full((lag,), -1, jnp.int32), doc_ids[: length - lag]]) == doc_ids).astype(f32))

    conv_all = jnp.concatenate([conv_weight, conv_bias[None]], axis=0)
    conv_v = own(conv_all[:, :E])
    conv_k = conv_all[:, E:]
    step_b = own(step_bias)
    rate = jnp.exp(own(decay_log))
    skip = jnp.repeat(own(skip_gain), P_SIZE)[None, :]
    gain = own(norm_gain)[None, :]

    projected = mm(normed, in_w, NN)
    gate = projected[:, :inner]
    value_in = projected[:, inner:].astype(bf16)
    key_out = mm(normed, key_w, NN)
    key_in = key_out[:, :KEYS].astype(bf16)
    step_raw = own(key_out[:, KEYS : KEYS + H]) + step_b[None, :]
    value_sum = convolve(value_in, conv_v[:CONV], conv_v[CONV], masks)
    values = jax.nn.silu(value_sum).astype(bf16)
    key_sum = convolve(key_in, conv_k[:CONV], conv_k[CONV], masks)
    keys = jax.nn.silu(key_sum).astype(bf16)
    dt = jax.nn.softplus(step_raw)
    log_decay = -dt * rate[None, :]
    cum = jnp.cumsum(log_decay.reshape(-1, CHUNK, heads), axis=1).reshape(length, heads)
    y, states = scan_forward(values, keys, cum, cum.T, dt, dt.T, doc, doc_t, flow, skip)
    grad_mixed = mm(cot_all, out_w, NT)
    sig_gate = jax.nn.sigmoid(gate)
    silu_gate = gate * sig_gate
    masked = y * head_mask
    gated = masked * silu_gate
    scaled = grad_mixed * gain
    part = jnp.stack([jnp.sum(gated * gated, axis=1), jnp.sum(scaled * gated, axis=1)])
    sums = cube_total(part.reshape(-1, 128)).reshape(2, length, 1)
    inv = lax.rsqrt(sums[0] / head_total + epsilon)
    pull = inv * inv * inv * sums[1] / head_total
    mixed = (gated * inv * gain).astype(bf16)
    branch = mm(mixed, out_w, NN).astype(bf16)

    grad_out = mm(mixed, cot_all, TN).astype(bf16)
    grad_norm_gain = jnp.sum(grad_mixed * gated * inv, axis=0)
    grad_gated = inv * scaled - pull * gated
    dy = grad_gated * silu_gate * head_mask
    grad_gate = (grad_gated * masked * (sig_gate * (1.0 + gate * (1.0 - sig_gate)))).astype(bf16)
    dvalues, dkeys, dcum, dcum_t, ddt, dskip = scan_backward(
        values, keys, cum, cum.T, dt, doc, doc_t, flow, skip, states, dy
    )
    dcum = (dcum + dcum_t.T).reshape(-1, CHUNK, heads)
    dlog = lax.cumsum(dcum, axis=1, reverse=True).reshape(length, heads)
    grad_dt = ddt - rate[None, :] * dlog
    grad_decay_log = -jnp.sum(dt * rate[None, :] * dlog, axis=0)
    grad_step = grad_dt * jax.nn.sigmoid(step_raw)
    grad_step_bias = jnp.sum(grad_step, axis=0)
    grad_skip = jnp.sum(dskip.reshape(heads, P_SIZE), axis=1)
    grad_value_in, sums_v = convolve_back(dvalues, value_in, value_sum, conv_v[:CONV], masks)
    grad_key_in, sums_k = convolve_back(dkeys, key_in, key_sum, conv_k[:CONV], masks)
    grad_cols = jnp.concatenate([grad_gate, grad_value_in], axis=1)
    step_cols = jnp.pad(spread(grad_step.astype(bf16)), ((0, 0), (0, STEP_PAD - H)))
    key_cols = jnp.concatenate([grad_key_in, step_cols], axis=1)
    grad_in = mm(normed, grad_cols, TN).astype(bf16)
    grad_keys = mm(normed, key_cols, TN).astype(bf16)
    grad_normed = mm(grad_cols, in_w, NT) + mm(key_cols, key_w, NT)
    grad_pre_gain = jnp.sum(grad_normed * normed.astype(f32), axis=0) / pre_gain

    small = jnp.concatenate(
        [grad_pre_gain, spread(grad_norm_gain), spread(grad_step_bias), spread(grad_decay_log), spread(grad_skip)]
    )
    small = jnp.pad(small, (0, -small.shape[0] % 1024)).reshape(-1, 128)
    conv_sums = jnp.concatenate([spread(sums_v), sums_k], axis=1)
    conv_sums = jnp.pad(conv_sums, ((0, 8 - conv_sums.shape[0]), (0, 0)))
    rows_of = lambda part: part.reshape(near, peers, tokens, width)
    blocks = (peers, far, near, 2, rows)
    branch, grad_normed, grad_in, grad_out_weight, grad_keys, small, conv_sums = scatter(
        rows_of(branch),
        rows_of(grad_normed.astype(bf16)),
        grad_in.reshape(blocks + (2 * inner,)),
        grad_out.reshape(far, 2, -1, width),
        grad_keys.reshape(blocks + (KEYS + STEP_PAD,)),
        small,
        conv_sums,
    )
    output = (seq_rows + branch).astype(bf16)[None]
    scaled_in = grad_normed * pre_gain[None, :]
    dot = jnp.mean(scaled_in * seq_rows, axis=1, keepdims=True)
    grad_seq = inv_rms * scaled_in - seq_rows * (inv_rms * inv_rms * inv_rms * dot)
    grad_inputs = (grad_seq + cot_rows.astype(f32))[None]
    grad_in_weight = jnp.concatenate([grad_in.astype(f32), grad_keys[:, :KEYS]], axis=1)
    grad_step_weight = grad_keys[:, KEYS : KEYS + H]
    small = small.reshape(-1)
    parts = []
    for size in (width, E, H, H, H):
        parts.append(small[:size])
        small = small[size:]
    return (
        output, grad_inputs, parts[0], grad_in_weight, grad_step_weight, conv_sums[:CONV], conv_sums[CONV],
        parts[2], parts[3], parts[4], parts[1], grad_out_weight,
    )


def solution(mesh):
    both = P(("seq", "batch"), None)
    tok = P("batch", "seq", None)
    in_specs = (
        tok, tok, P("batch", None), P("batch"), P(), both, both, P(), P(), P(), P(), P(), P(), both,
    )
    out_specs = (tok, tok, P(), both, both, P(), P(), P(), P(), P(), P(), both)
    return jax.shard_map(body, mesh=mesh, in_specs=in_specs, out_specs=out_specs, check_vma=False)
```

```python
from functools import partial

import jax
import jax.numpy as jnp
from jax import lax
from jax.experimental import pallas as pl
from jax.experimental.pallas import tpu as pltpu
from jax.sharding import PartitionSpec as P

H = 64
P_SIZE = 64
N = 128
CONV = 4
DOCS = 4
E = 4096
KEYS = 2 * N
STEP_PAD = 128
CHUNK = 128
LANES = 128
epsilon = 1e-05
f32 = jnp.float32
bf16 = jnp.bfloat16


def mm(a, b, dims, precision=None):
    return lax.dot_general(a, b, (dims, ((), ())), precision=precision, preferred_element_type=f32)


NN = ((1,), (0,))
NT = ((1,), (1,))
TN = ((0,), (0,))
exact = lax.Precision.HIGHEST


def pair_cols(low, col, first):
    return jnp.where(low, col[:, first : first + 1], col[:, first + 1 : first + 2])


def iota(shape, axis):
    return lax.broadcasted_iota(jnp.int32, shape, axis)


class Docs:
    def __init__(self, meta_ref, chunk, span):
        per = span // CHUNK
        seq = chunk // per
        self.start = (chunk - seq * per) * CHUNK
        self.ends = []
        total = 0
        for i in range(DOCS - 1):
            total = total + meta_ref[seq, i]
            self.ends.append(total)
        self.count = meta_ref[seq, DOCS]
        self.pos = self.start + iota((CHUNK, 1), 0)
        self.doc = self.index(self.pos)

    def index(self, places):
        found = (places >= self.ends[0]).astype(jnp.int32)
        for end in self.ends[1:]:
            found = found + (places >= end).astype(jnp.int32)
        return found

    def lag(self, by):
        source = self.pos - by
        return ((source >= 0) & (self.index(source) == self.doc)).astype(f32)

    def flow(self):
        return ((self.start > 0) & (self.index(self.start - 1) == self.doc)).astype(f32)

    def row(self):
        return self.index(self.start + iota((1, CHUNK), 1))

    def tail(self):
        return (self.doc == self.index(self.start + CHUNK - 1)).astype(f32)


def shift_down(rows, before, by):
    if by == 0:
        return rows
    moved = pltpu.roll(rows, by, 0)
    top = jnp.where(iota((8, 1), 0) < by, pltpu.roll(before, by, 0), moved[:8])
    return jnp.concatenate([top, moved[8:]], axis=0)


def shift_up(rows, after, by):
    if by == 0:
        return rows
    size = rows.shape[0]
    moved = pltpu.roll(rows, size - by, 0)
    end = jnp.where(iota((8, 1), 0) >= 8 - by, pltpu.roll(after, 8 - by, 0), moved[size - 8 :])
    return jnp.concatenate([moved[: size - 8], end], axis=0)


def silu_slope(v, sig):
    return sig * (1.0 + v * (1.0 - sig))


def forward_kernel(
    meta_ref, proj_ref, key_ref, grad_ref, chan_ref, conv_k_ref, head_ref,
    val_out, key_out, vsum_ref, ksum_ref, raw_ref, cum_ref, y_ref, state_ref, sums_ref,
    state, last_v, last_k,
    *, span, heads,
):
    i = pl.program_id(0)
    chunks = pl.num_programs(0)
    inner = heads * P_SIZE

    @pl.when(i == 0)
    def _():
        state[...] = jnp.zeros_like(state)
        last_v[...] = jnp.zeros_like(last_v)
        last_k[...] = jnp.zeros_like(last_k)

    docs = Docs(meta_ref, i, span)
    lags = [docs.lag(by) for by in range(1, CONV)]

    def convolve(rows, before, weight, bias):
        total = bias + weight[CONV - 1 :] * rows
        for by in range(1, CONV):
            at = CONV - 1 - by
            total = total + weight[at : at + 1] * (shift_down(rows, before, by) * lags[by - 1])
        return total

    rows_v = proj_ref[:, inner:].astype(bf16).astype(f32)
    vsum = convolve(rows_v, last_v[...], chan_ref[:CONV, :], chan_ref[CONV : CONV + 1, :])
    last_v[...] = rows_v[CHUNK - 8 :]
    vsum_ref[...] = vsum
    val_out[...] = (vsum * jax.nn.sigmoid(vsum)).astype(bf16)
    rows_k = key_ref[:, :KEYS].astype(bf16).astype(f32)
    ksum = convolve(rows_k, last_k[...], conv_k_ref[:CONV, :], conv_k_ref[CONV : CONV + 1, :])
    last_k[...] = rows_k[CHUNK - 8 :]
    ksum_ref[...] = ksum
    keys = (ksum * jax.nn.sigmoid(ksum)).astype(bf16)
    key_out[...] = keys

    rows = iota((CHUNK, CHUNK), 0)
    cols = iota((CHUNK, CHUNK), 1)
    chosen = (rows == head_ref[2:3, :].astype(jnp.int32)).astype(f32)
    raw = mm(key_ref[:, KEYS:], chosen, NN, exact) + head_ref[:1, :]
    raw_ref[...] = raw
    dt = jax.nn.softplus(raw)
    cum = mm((rows >= cols).astype(f32), -dt * head_ref[1:2, :], NN, exact)
    cum_ref[...] = cum
    cum_t = cum.T
    dt_t = dt.T

    state_ref[0] = state[...].astype(bf16)
    bias = jnp.where((docs.doc == docs.row()) & (rows >= cols), 0.0, -1e30)
    carry_w = docs.flow() * jnp.exp(cum)
    final_w = docs.tail() * jnp.exp(cum[CHUNK - 1 :, :] - cum) * dt
    gain = carry_w[CHUNK - 1 :, :]
    low = cols < P_SIZE
    low_row = low[:1]
    write = keys[:, :N]
    read = keys[:, N:]
    write_t = write.astype(f32).T.astype(bf16)
    scores = mm(read, write, NT)
    square = jnp.zeros((CHUNK, LANES), f32)
    cross = jnp.zeros((CHUNK, LANES), f32)
    count = docs.count.astype(f32)
    for pair in range(heads // 2):
        first = 2 * pair
        lanes = slice(pair * 128, pair * 128 + 128)
        xf = val_out[:, lanes].astype(f32)
        weights = []
        for h in (first, first + 1):
            decay = jnp.exp(cum[:, h : h + 1] - cum_t[h : h + 1, :] + bias)
            weights.append((decay * scores * dt_t[h : h + 1, :]).astype(bf16))
        stacked = jnp.concatenate(
            [jnp.where(low, xf, 0.0).astype(bf16), jnp.where(low, 0.0, xf).astype(bf16)], axis=0
        )
        old = state[:, lanes]
        y = mm(jnp.concatenate(weights, axis=1), stacked, NN)
        y = y + pair_cols(low, carry_w, first) * mm(read, old.astype(bf16), NN)
        y = y + chan_ref[6:7, lanes] * xf
        y = jnp.where(chan_ref[7:8, lanes] < count, y, 0.0)
        y_ref[:, lanes] = y
        state[:, lanes] = pair_cols(low_row, gain, first) * old + mm(
            write_t, (pair_cols(low, final_w, first) * xf).astype(bf16), NN
        )
        gate = proj_ref[:, lanes]
        gated = y * (gate * jax.nn.sigmoid(gate))
        square = square + gated * gated
        cross = cross + gated * (grad_ref[:, lanes] * chan_ref[5:6, lanes])
    sums_ref[pl.ds(i, 1), :] = jnp.sum(square.T, axis=0, keepdims=True)
    sums_ref[pl.ds(chunks + i, 1), :] = jnp.sum(cross.T, axis=0, keepdims=True)


def backward_kernel(
    meta_ref, proj_ref, key_in_ref, grad_ref, chan_ref, conv_k_ref, head_ref,
    val_ref, key_ref, vsum_ref, ksum_ref, raw_ref, cum_ref, y_ref, state_ref, sums_ref,
    mixed_ref, cols_ref, key_cols_ref, chan_sums, key_sums, head_sums,
    dstate, dv, next_v, next_k, next_lags,
    *, span, heads,
):
    chunks = pl.num_programs(0)
    i = chunks - 1 - pl.program_id(0)
    inner = heads * P_SIZE

    @pl.when(pl.program_id(0) == 0)
    def _():
        for ref in (dstate, next_v, next_k, next_lags, chan_sums, key_sums, head_sums):
            ref[...] = jnp.zeros_like(ref)

    docs = Docs(meta_ref, i, span)
    rows = iota((CHUNK, CHUNK), 0)
    cols = iota((CHUNK, CHUNK), 1)
    raw = raw_ref[...]
    dt = jax.nn.softplus(raw)
    cum = cum_ref[...]
    cum_t = cum.T
    count = docs.count.astype(f32)
    head_total = count * P_SIZE

    def column(row):
        return jnp.broadcast_to(row, (CHUNK, CHUNK)).T

    inv = lax.rsqrt(column(sums_ref[pl.ds(i, 1), :]) / head_total + epsilon)
    pull = inv * inv * inv * column(sums_ref[pl.ds(chunks + i, 1), :]) / head_total

    bias = jnp.where((docs.doc == docs.row()) & (cols >= rows), 0.0, -1e30)
    carry_w = docs.flow() * jnp.exp(cum)
    final_d = docs.tail() * jnp.exp(cum[CHUNK - 1 :, :] - cum)
    final_w = final_d * dt
    gain = carry_w[CHUNK - 1 :, :]
    low = cols < P_SIZE
    low_row = low[:1]
    write = key_ref[:, :N]
    read = key_ref[:, N:]
    read_t = read.astype(f32).T.astype(bf16)
    scores_t = mm(write, read, NT)
    dscores_t = jnp.zeros((CHUNK, CHUNK), f32)
    dwrite = jnp.zeros((CHUNK, N), f32)
    dread = jnp.zeros((CHUNK, N), f32)
    end_row = iota((CHUNK, 1), 0) == CHUNK - 1
    dcum = jnp.zeros((CHUNK, LANES), f32)
    ddt = jnp.zeros((CHUNK, LANES), f32)
    dcum_rows = []
    for pair in range(heads // 2):
        first = 2 * pair
        lanes = slice(pair * 128, pair * 128 + 128)
        gate = proj_ref[:, lanes]
        sig = jax.nn.sigmoid(gate)
        silu = gate * sig
        masked = y_ref[:, lanes]
        gated = masked * silu
        norm_gain = chan_ref[5:6, lanes]
        gm = grad_ref[:, lanes]
        unit = gated * inv
        mixed_ref[:, lanes] = (unit * norm_gain).astype(bf16)
        chan_sums[5:6, lanes] += jnp.sum(gm * unit, axis=0, keepdims=True)
        grad_gated = inv * (gm * norm_gain) - pull * gated
        cols_ref[:, lanes] = (grad_gated * masked * silu_slope(gate, sig)).astype(bf16)
        dy = jnp.where(chan_ref[7:8, lanes] < count, grad_gated * silu, 0.0)
        xf = val_ref[:, lanes].astype(f32)
        dyb = dy.astype(bf16)
        x_stack = jnp.concatenate(
            [jnp.where(low, xf, 0.0).astype(bf16), jnp.where(low, 0.0, xf).astype(bf16)], axis=0
        )
        dy_stack = jnp.concatenate(
            [jnp.where(low, dy, 0.0).astype(bf16), jnp.where(low, 0.0, dy).astype(bf16)], axis=0
        )
        dweights = mm(x_stack, dyb, NT)
        old = state_ref[0, :, lanes]
        grad = dstate[:, lanes]
        gradb = grad.astype(bf16)
        carried = mm(read, old, NN)
        pushed = mm(write, gradb, NN)
        carry_p = pair_cols(low, carry_w, first)
        final_p = pair_cols(low, final_w, first)
        carry_prod = dy * carried
        final_prod = xf * pushed
        gain_prod = jnp.sum(grad * old.astype(f32), axis=0, keepdims=True)
        weights = []
        for which, h in enumerate((first, first + 1)):
            col = dt[:, h : h + 1]
            decay = jnp.exp(cum_t[h : h + 1, :] - cum[:, h : h + 1] + bias)
            weighted = decay * col
            weights.append((weighted * scores_t).astype(bf16))
            dw = dweights[which * CHUNK : (which + 1) * CHUNK]
            dscores_t = dscores_t + dw * weighted
            direct = dw * decay * scores_t
            ddt_in = jnp.sum(direct, axis=1, keepdims=True)
            dcum_rows.append(jnp.sum(direct * col, axis=0, keepdims=True))
            half = low if which == 0 else ~low
            half_row = low_row if which == 0 else ~low_row
            carry_sum = jnp.sum(jnp.where(half, carry_prod, 0.0), axis=1, keepdims=True)
            final_sum = jnp.sum(jnp.where(half, final_prod, 0.0), axis=1, keepdims=True)
            push = final_w[:, h : h + 1] * final_sum
            at_end = jnp.sum(push, axis=0, keepdims=True) + gain[:, h : h + 1] * jnp.sum(
                jnp.where(half_row, gain_prod, 0.0), axis=1, keepdims=True
            )
            here = cols == h
            ddt = jnp.where(here, ddt_in + final_d[:, h : h + 1] * final_sum, ddt)
            dcum = jnp.where(
                here,
                carry_w[:, h : h + 1] * carry_sum - push - col * ddt_in + jnp.where(end_row, at_end, 0.0),
                dcum,
            )
        dx = mm(jnp.concatenate(weights, axis=1), dy_stack, NN)
        dv[:, lanes] = dx + final_p * pushed + chan_ref[6:7, lanes] * dy
        chan_sums[6:7, lanes] += jnp.sum(dy * xf, axis=0, keepdims=True)
        dwrite = dwrite + mm((final_p * xf).astype(bf16), gradb, NT)
        carry_dy = (carry_p * dy).astype(bf16)
        dread = dread + mm(carry_dy, old, NT)
        dstate[:, lanes] = pair_cols(low_row, gain, first) * grad + mm(read_t, carry_dy, NN)
    dsb = dscores_t.astype(bf16)
    dkeys = jnp.concatenate([dwrite + mm(dsb, read, NN), dread + mm(dsb, write, TN)], axis=1)

    extra = jnp.concatenate(dcum_rows + [jnp.zeros((LANES - heads, CHUNK), f32)], axis=0)
    dlog = mm((cols >= rows).astype(f32), dcum + extra.T, NN, exact)
    rate = head_ref[1:2, :]
    grad_step = (ddt - rate * dlog) * jax.nn.sigmoid(raw)
    head_sums[:1, :] += jnp.sum(grad_step, axis=0, keepdims=True)
    head_sums[1:2, :] -= jnp.sum(dt * rate * dlog, axis=0, keepdims=True)
    chosen = (rows == head_ref[2:3, :].astype(jnp.int32)).astype(bf16)
    key_cols_ref[:, KEYS:] = mm(grad_step.astype(bf16), chosen, NT).astype(bf16)

    lags = [docs.lag(by) for by in range(1, CONV)]

    def convolve_back(dact, total, rows_in, after, weight, sums):
        dconv = dact * silu_slope(total, jax.nn.sigmoid(total))
        grad_in = weight[CONV - 1 :] * dconv
        sums[CONV : CONV + 1, :] += jnp.sum(dconv, axis=0, keepdims=True)
        sums[CONV - 1 : CONV, :] += jnp.sum(dconv * rows_in, axis=0, keepdims=True)
        for by in range(1, CONV):
            at = CONV - 1 - by
            moved = shift_up(dconv * lags[by - 1], after[...] * next_lags[:, by - 1 : by], by)
            grad_in = grad_in + weight[at : at + 1] * moved
            sums[at : at + 1, :] += jnp.sum(moved * rows_in, axis=0, keepdims=True)
        after[...] = dconv[:8]
        return grad_in.astype(bf16)

    rows_v = proj_ref[:, inner:].astype(bf16).astype(f32)
    cols_ref[:, inner:] = convolve_back(dv[...], vsum_ref[...], rows_v, next_v, chan_ref[:CONV, :], chan_sums)
    rows_k = key_in_ref[:, :KEYS].astype(bf16).astype(f32)
    key_cols_ref[:, :KEYS] = convolve_back(
        dkeys, ksum_ref[...], rows_k, next_k, conv_k_ref[:CONV, :], key_sums
    )
    for by in range(1, CONV):
        next_lags[:, by - 1 : by] = lags[by - 1][:8]


def mixer_forward(meta, projected, key_out, grad_mixed, chan, conv_k, head_vec, span, heads):
    length = projected.shape[0]
    inner = heads * P_SIZE
    chunks = length // CHUNK
    row = lambda width: pl.BlockSpec((CHUNK, width), lambda i: (i, 0))
    all_of = lambda *shape: pl.BlockSpec(shape, lambda i: (0,) * len(shape))
    out = lambda width, dtype: jax.ShapeDtypeStruct((length, width), dtype)
    return pl.pallas_call(
        partial(forward_kernel, span=span, heads=heads),
        grid=(chunks,),
        in_specs=[
            pl.BlockSpec(memory_space=pltpu.SMEM), row(2 * inner), row(KEYS + STEP_PAD), row(inner),
            all_of(8, inner), all_of(8, KEYS), all_of(8, LANES),
        ],
        out_specs=[
            row(inner), row(KEYS), row(inner), row(KEYS), row(LANES), row(LANES), row(inner),
            pl.BlockSpec((1, N, inner), lambda i: (i, 0, 0)), all_of(2 * chunks, LANES),
        ],
        out_shape=[
            out(inner, bf16), out(KEYS, bf16), out(inner, f32), out(KEYS, f32), out(LANES, f32), out(LANES, f32),
            out(inner, f32), jax.ShapeDtypeStruct((chunks, N, inner), bf16),
            jax.ShapeDtypeStruct((2 * chunks, LANES), f32),
        ],
        scratch_shapes=[pltpu.VMEM((N, inner), f32), pltpu.VMEM((8, inner), f32), pltpu.VMEM((8, KEYS), f32)],
        compiler_params=pltpu.CompilerParams(vmem_limit_bytes=32 * 2**20),
        cost_estimate=pl.CostEstimate(
            flops=length * inner * 1024, bytes_accessed=length * inner * 24, transcendentals=length * heads * CHUNK
        ),
        name="mixer_forward",
    )(meta, projected, key_out, grad_mixed, chan, conv_k, head_vec)


def mixer_backward(meta, projected, key_out, grad_mixed, chan, conv_k, head_vec, kept, sums, span, heads):
    length = projected.shape[0]
    inner = heads * P_SIZE
    chunks = length // CHUNK
    row = lambda width: pl.BlockSpec((CHUNK, width), lambda i: (chunks - 1 - i, 0))
    all_of = lambda *shape: pl.BlockSpec(shape, lambda i: (0,) * len(shape))
    out = lambda width: jax.ShapeDtypeStruct((length, width), bf16)
    return pl.pallas_call(
        partial(backward_kernel, span=span, heads=heads),
        grid=(chunks,),
        in_specs=[
            pl.BlockSpec(memory_space=pltpu.SMEM), row(2 * inner), row(KEYS + STEP_PAD), row(inner),
            all_of(8, inner), all_of(8, KEYS), all_of(8, LANES),
            row(inner), row(KEYS), row(inner), row(KEYS), row(LANES), row(LANES), row(inner),
            pl.BlockSpec((1, N, inner), lambda i: (chunks - 1 - i, 0, 0)), all_of(2 * chunks, LANES),
        ],
        out_specs=[
            row(inner), row(2 * inner), row(KEYS + STEP_PAD), all_of(8, inner), all_of(8, KEYS), all_of(8, LANES),
        ],
        out_shape=[
            out(inner), out(2 * inner), out(KEYS + STEP_PAD), jax.ShapeDtypeStruct((8, inner), f32),
            jax.ShapeDtypeStruct((8, KEYS), f32), jax.ShapeDtypeStruct((8, LANES), f32),
        ],
        scratch_shapes=[
            pltpu.VMEM((N, inner), f32), pltpu.VMEM((CHUNK, inner), f32), pltpu.VMEM((8, inner), f32),
            pltpu.VMEM((8, KEYS), f32), pltpu.VMEM((8, LANES), f32),
        ],
        compiler_params=pltpu.CompilerParams(vmem_limit_bytes=32 * 2**20),
        cost_estimate=pl.CostEstimate(
            flops=length * inner * 3072, bytes_accessed=length * inner * 30, transcendentals=length * heads * CHUNK
        ),
        name="mixer_backward",
    )(meta, projected, key_out, grad_mixed, chan, conv_k, head_vec, *kept, sums)


MESH = pl.DeviceIdType.MESH
HBM = pl.BlockSpec(memory_space=pl.ANY)
VMEM = pl.BlockSpec(memory_space=pltpu.VMEM)


def z_pair(peers, groups):
    planes = groups // 2
    return 2 if planes % 2 == 0 and (E // (peers * planes)) % (2 * P_SIZE) == 0 else 1


def flip(value, bits):
    bit = 1
    while bit <= bits:
        if bits & bit:
            value = value + bit - 2 * bit * (value // bit % 2)
        bit *= 2
    return value


class Place:
    def __init__(self):
        self.peers = lax.axis_size("seq")
        groups = lax.axis_size("batch")
        self.near = z_pair(self.peers, groups)
        self.far = groups // 2 // self.near
        self.s = lax.axis_index("seq")
        b = lax.axis_index("batch")
        self.c = b % 2
        self.zl = b // 2 % self.near
        self.zh = b // 2 // self.near

    def at(self, s=0, zl=0, zh=0, c=0):
        return (flip(self.s, s), (flip(self.zh, zh) * self.near + flip(self.zl, zl)) * 2 + flip(self.c, c))

    def column_runs(self, s, zl, width):
        outer = self.far if self.near > 1 else 1
        run = width // (2 * outer)
        runs = []
        for part in range(2):
            for i in range(outer):
                first = part * E + ((s * outer + i) * self.near + zl) * run
                runs.append((pl.ds(pl.multiple_of(first, 128), run), pl.ds((part * outer + i) * run, run)))
        return runs

    def partners(self):
        cube = [self.at(s=o // self.near, zl=o % self.near) for o in range(1, self.peers * self.near)]
        return cube, [self.at(zh=o) for o in range(1, self.far)], [self.at(c=1)]


def greet(devices):
    barrier = pltpu.get_barrier_semaphore()
    for device in devices:
        pl.semaphore_signal(barrier, inc=1, device_id=device, device_id_type=MESH)
    pl.semaphore_wait(barrier, len(devices))


class Mover:
    def __init__(self, send, recv, local):
        self.send, self.recv, self.local = send, recv, local
        self.sent, self.kept = 0, 0
        self.open = []

    def put(self, src, dst, device):
        copy = pltpu.make_async_remote_copy(
            src_ref=src, dst_ref=dst, send_sem=self.send.at[self.sent], recv_sem=self.recv.at[self.sent],
            device_id=device, device_id_type=MESH,
        )
        copy.start()
        self.sent += 1
        self.open.append(copy)
        return copy

    def keep(self, src, dst):
        copy = pltpu.make_async_copy(src, dst, self.local.at[self.kept])
        copy.start()
        self.kept += 1
        return copy

    def close(self):
        for copy in self.open:
            copy.wait_send()


def run_paths(paths):
    paths = list(paths)
    while paths:
        alive = []
        for path in paths:
            try:
                next(path)
                alive.append(path)
            except StopIteration:
                pass
        paths = alive


def turn(paths):
    for path in paths:
        next(path, None)


def bits_of(peers):
    return [1 << i for i in range(peers.bit_length() - 1)]


def combos(bits):
    out = [0]
    for bit in reversed(bits):
        out = [bit | o for o in out] + out
    return out


def gather_kernel(
    in_ref, key_ref, out_ref, rows_ref, cot_ref, meta_ref,
    w_ref, k_ref, o_ref, x_ref, ct_ref, m_ref, send, recv, local,
):
    me = Place()
    s, zl, zh, c = me.s, me.zl, me.zh, me.c
    cube, far, sibling = me.partners()
    greet(cube + far + sibling)
    mover = Mover(send, recv, local)
    bits = bits_of(me.peers)

    def plane_path(src, dst, order, near):
        view = dst.at[flip(zl, near)]
        if near:
            copy = mover.put(src, dst.at[zl, s], me.at(zl=near))
            yield
            copy.wait_recv()
        else:
            own = mover.keep(src, view.at[s])
        held = [0]
        for bit in order:
            copies = []
            for h in held:
                at = view.at[flip(s, h)]
                copies.append(mover.put(at if near or h else src, at if near else dst.at[zl, flip(s, h)], me.at(s=bit)))
            held = held + [h ^ bit for h in held]
            yield
            for copy in copies:
                copy.wait_recv()
        if not near:
            own.wait()

    def meta_path():
        own = mover.keep(meta_ref, m_ref.at[zl])
        near = [mover.put(meta_ref, m_ref.at[zl], me.at(zl=o)) for o in range(1, me.near)]
        yield
        own.wait()
        for copy in near:
            copy.wait_recv()

    def key_path():
        block = k_ref.at[s, zh, zl, c]
        own = mover.keep(key_ref, block)
        copies = [mover.put(key_ref, block, me.at(zh=o)) for o in range(1, me.far)]
        yield
        own.wait()
        for copy in copies:
            copy.wait_recv()
        block = k_ref.at[s, :, zl, c]
        copies = [mover.put(block, block, me.at(zl=o)) for o in range(1, me.near)]
        yield
        for copy in copies:
            copy.wait_recv()
        held = [0]
        for bit in bits:
            copies = []
            for h in held:
                block = k_ref.at[flip(s, h), :, :, c]
                copies.append(mover.put(block, block, me.at(s=bit)))
            held = held + [h ^ bit for h in held]
            yield
            for copy in copies:
                copy.wait_recv()
        block = k_ref.at[:, :, :, c]
        copy = mover.put(block, block, me.at(c=1))
        yield
        copy.wait_recv()

    def spread_path(copies, view):
        last = []
        for o, copy in copies:
            yield
            copy.wait_recv()
            last.append(mover.put(view(flip(zh, o)), view(flip(zh, o)), me.at(c=1)))
        return last

    def out_path():
        own = mover.keep(out_ref, o_ref.at[zh, c])
        copies = [(o, mover.put(out_ref, o_ref.at[zh, c], me.at(zh=o))) for o in range(1, me.far)]
        first = mover.put(out_ref, o_ref.at[zh, c], me.at(c=1))
        last = yield from spread_path(copies, lambda h: o_ref.at[h, c])
        yield
        own.wait()
        for copy in last + [first]:
            copy.wait_recv()

    def weight_path():
        moves = {}
        for step in range(me.peers):
            for o in range(me.near):
                to_s, to_zl = flip(s, step), flip(zl, o)
                for src, dst in me.column_runs(to_s, to_zl, w_ref.shape[-1]):
                    src = in_ref.at[:, src]
                    dst = w_ref.at[s, zh, zl, c, :, dst]
                    if step or o:
                        copy = mover.put(src, dst, me.at(s=step, zl=o))
                    else:
                        copy = mover.keep(src, dst)
                    moves.setdefault(step, []).append(copy)
        pieces = []
        for step in range(me.peers):
            yield
            for i, copy in enumerate(moves[step]):
                if step == 0 and i < len(moves[0]) // me.near:
                    copy.wait()
                else:
                    copy.wait_recv()
            block = w_ref.at[flip(s, step), zh, :, c]
            copies = [(o, mover.put(block, block, me.at(zh=o))) for o in range(1, me.far)]
            pieces.append((step, copies, mover.put(block, block, me.at(c=1))))
        last = []
        for step, copies, first in pieces:
            last.append(first)
            last += yield from spread_path(copies, lambda h, step=step: w_ref.at[flip(s, step), h, :, c])
        yield
        for copy in last:
            copy.wait_recv()

    own_x = plane_path(rows_ref, x_ref, bits, 0)
    own_c = plane_path(cot_ref, ct_ref, bits[::-1], 0)
    near_x = [plane_path(rows_ref, x_ref, bits, o) for o in range(1, me.near)]
    near_c = [plane_path(cot_ref, ct_ref, bits[::-1], o) for o in range(1, me.near)]
    near = near_x + near_c
    keys, weights, outs = key_path(), weight_path(), out_path()
    turn([own_x, own_c, weights] + near + [keys, outs])
    extra = meta_path()
    turn([extra, own_x, own_c] + [weights] * me.peers + [keys] + near + [keys])
    turn([own_x, own_c] + near + [keys, outs, weights, keys, weights])
    run_paths([weights, extra, keys, outs, own_x, own_c] + near)
    mover.close()


def remote_params(identity, mib):
    return pltpu.CompilerParams(collective_id=identity, has_side_effects=True, vmem_limit_bytes=mib * 2**20)


def sems(copies, kept):
    return [pltpu.SemaphoreType.DMA((copies,)), pltpu.SemaphoreType.DMA((copies,)), pltpu.SemaphoreType.DMA((kept,))]


def gather(in_w, keys, out_w, rows, cot, meta):
    me = Place()
    peers, near, far = me.peers, me.near, me.far
    shape = lambda lead, part: jax.ShapeDtypeStruct(lead + part, bf16)
    columns = 2 * E // (peers * near)
    runs = 2 * (far if near > 1 else 1)
    copies = runs * (peers * near - 1) + (peers + 1) * (2 * far - 1) + 2 * (near * peers - 1)
    copies += 2 * near + peers + far - 3
    return pl.pallas_call(
        gather_kernel,
        out_shape=[
            shape((peers, far, near, 2), (in_w.shape[0], columns)),
            shape((peers, far, near, 2), keys.shape),
            shape((far, 2), out_w.shape),
            shape((near, peers), rows.shape),
            shape((near, peers), cot.shape),
            jax.ShapeDtypeStruct((near,) + meta.shape, meta.dtype),
        ],
        in_specs=[HBM] * 6,
        out_specs=[HBM] * 6,
        scratch_shapes=sems(copies, runs + 5),
        compiler_params=remote_params(0, 4),
        name="gather_all",
    )(in_w, keys, out_w, rows, cot, meta)


def total_kernel(part_ref, sum_ref, box, send, recv, local):
    me = Place()
    cube = me.partners()[0]
    greet(cube)
    mover = Mover(send, recv, local)
    copies = [mover.put(part_ref, box.at[i], device) for i, device in enumerate(cube)]
    total = part_ref[...]
    for i, copy in enumerate(copies):
        copy.wait_recv()
        total = total + box[i]
    sum_ref[...] = total
    mover.close()


def cube_total(part):
    me = Place()
    count = me.peers * me.near - 1
    return pl.pallas_call(
        total_kernel,
        out_shape=jax.ShapeDtypeStruct(part.shape, f32),
        in_specs=[VMEM],
        out_specs=VMEM,
        scratch_shapes=[pltpu.VMEM((count,) + part.shape, f32)] + sems(count, 1),
        compiler_params=remote_params(1, 4),
        name="cube_total",
    )(part)


def add_rows(out, parts):
    shape = out.shape
    tile = min(16, shape[-2])
    lead = [()]
    for size in shape[:-2]:
        lead = [l + (i,) for l in lead for i in range(size)]
    for l in lead:

        def step(i, carry, l=l):
            at = l + (pl.ds(pl.multiple_of(i * tile, tile), tile), slice(None))
            total = parts[0][at].astype(f32)
            for part in parts[1:]:
                total = total + part[at].astype(f32)
            out[at] = total.astype(out.dtype)
            return carry

        lax.fori_loop(0, shape[-2] // tile, step, 0)


def scatter_kernel(
    bp_ref, gn_ref, gw_ref, go_ref, gk_ref, v_ref, u_ref,
    ob_ref, og_ref, ow_ref, oo_ref, ok_ref, ov_ref, ou_ref,
    b_own, b_box, b_near, n_own, n_box, n_near, w_own, w_box, w_far, o_own, o_box, o_far,
    k_own, k_box, k_near, k_far, k_bits, v_box, u_box, send, recv, local,
):
    me = Place()
    s, zl, zh, c = me.s, me.zl, me.zh, me.c
    cube, far, sibling = me.partners()
    greet(cube + far + sibling)
    mover = Mover(send, recv, local)
    bits = bits_of(me.peers)

    def rows_path(src, own, box, near_box, out, order, near, arrivals):
        own, box = own.at[near], box.at[near]
        at_zl = src.at[flip(zl, near)]
        todo = combos(order[1:])
        copies, loads = [], []
        for j, o in enumerate(todo):
            copies.append(mover.put(at_zl.at[flip(s, order[0] ^ o)], box.at[j], me.at(s=order[0])))
            loads.append(mover.keep(at_zl.at[flip(s, o)], own.at[j]))
        base = 0
        for i, bit in enumerate(order):
            rest = order[i + 1 :]
            count = 1 << len(rest)
            offset = (1 << (len(order) - 1)) - count
            coming = []
            for j in range(count):
                yield
                copies[j].wait_recv()
                if i == 0:
                    loads[j].wait()
                if rest or near:
                    add_rows(own.at[offset + j], [own.at[offset + j], box.at[base + j]])
                if rest and j < count // 2:
                    coming.append(mover.put(own.at[offset + j], box.at[base + count + j], me.at(s=rest[0])))
            copies = coming
            last = base
            base += count
        end = (1 << (len(order) - 1)) - 1
        if near:
            arrivals.append(mover.put(own.at[end], near_box.at[near - 1], me.at(zl=near)))
            yield
        else:
            yield
            for _ in range(me.near - 1):
                arrivals.pop(0).wait_recv()
            add_rows(out, [own.at[end], box.at[last]] + [near_box.at[o - 1] for o in range(1, me.near)])

    def weight_path():
        order = [(o, k) for o in range(1, me.far) for k in range(me.peers)] + [(0, k) for k in range(me.peers)]
        loads, copies = {}, {}
        for o, k in order:
            copies[o, k] = mover.put(gw_ref.at[flip(s, k), flip(zh, o), :, 1 - c], w_box.at[o, k], me.at(c=1))
            loads[o, k] = mover.keep(gw_ref.at[flip(s, k), flip(zh, o), :, c], w_own.at[o, k])
        far_copies = {}
        for o, k in order:
            yield
            loads[o, k].wait()
            copies[o, k].wait_recv()
            if o:
                add_rows(w_own.at[o, k], [w_own.at[o, k], w_box.at[o, k]])
                far_copies[o, k] = mover.put(w_own.at[o, k], w_far.at[o - 1, k], me.at(zh=o))
        ends, kept = [], []
        for k in range(me.peers):
            yield
            for o in range(1, me.far):
                far_copies[o, k].wait_recv()
            parts = [w_own.at[0, k], w_box.at[0, k]] + [w_far.at[o - 1, k] for o in range(1, me.far)]
            add_rows(w_own.at[0, k], parts)
            for o in range(me.near):
                for whole, mine in me.column_runs(s, zl, w_own.shape[-1]):
                    src = w_own.at[0, k, flip(zl, o), :, mine]
                    if k or o:
                        ends.append(mover.put(src, ow_ref.at[:, whole], me.at(s=k, zl=o)))
                    else:
                        kept.append(mover.keep(src, ow_ref.at[:, whole]))
        yield
        for copy in kept:
            copy.wait()
        for copy in ends:
            copy.wait_recv()

    def out_path():
        order = list(range(1, me.far)) + [0]
        copies, loads = {}, {}
        for o in order:
            copies[o] = mover.put(go_ref.at[flip(zh, o), 1 - c], o_box.at[o], me.at(c=1))
            loads[o] = mover.keep(go_ref.at[flip(zh, o), c], o_own.at[o])
        yield
        far_copies = {}
        for o in order:
            loads[o].wait()
            copies[o].wait_recv()
            if o:
                add_rows(o_own.at[o], [o_own.at[o], o_box.at[o]])
                far_copies[o] = mover.put(o_own.at[o], o_far.at[o - 1], me.at(zh=o))
        for _ in range(2 * me.peers + 4):
            yield
        for o in range(1, me.far):
            far_copies[o].wait_recv()
        add_rows(oo_ref, [o_own.at[0], o_box.at[0]] + [o_far.at[o - 1] for o in range(1, me.far)])

    def key_path():
        blocks = combos(bits)
        copies, loads = [], []
        for j, o in enumerate(blocks):
            copies.append(mover.put(gk_ref.at[flip(s, o), :, :, 1 - c], k_box.at[j], me.at(c=1)))
            loads.append(mover.keep(gk_ref.at[flip(s, o), :, :, c], k_own.at[j]))
        half = me.peers // 2
        sent = []
        for j in range(me.peers):
            yield
            loads[j].wait()
            copies[j].wait_recv()
            add_rows(k_own.at[j], [k_own.at[j], k_box.at[j]])
            if j < half:
                sent.append(mover.put(k_own.at[j], k_bits.at[j], me.at(s=bits[0])))
        base = 0
        for i, bit in enumerate(bits):
            count = me.peers >> (i + 1)
            offset = me.peers - count
            coming = []
            for j in range(count):
                yield
                sent[j].wait_recv()
                add_rows(k_own.at[offset + j], [k_own.at[offset + j], k_bits.at[base + j]])
                if i + 1 < len(bits) and j < count // 2:
                    coming.append(mover.put(k_own.at[offset + j], k_bits.at[base + count + j], me.at(s=bits[i + 1])))
            base += count
            sent = coming
        end = k_own.at[me.peers - 1]
        copies = [mover.put(end.at[:, flip(zl, o)], k_near.at[o - 1], me.at(zl=o)) for o in range(1, me.near)]
        yield
        for copy in copies:
            copy.wait_recv()
        add_rows(end.at[:, zl], [end.at[:, zl]] + [k_near.at[o - 1] for o in range(1, me.near)])
        copies = [mover.put(end.at[flip(zh, o), zl], k_far.at[o - 1], me.at(zh=o)) for o in range(1, me.far)]
        yield
        for copy in copies:
            copy.wait_recv()
        add_rows(ok_ref, [end.at[zh, zl]] + [k_far.at[o - 1] for o in range(1, me.far)])

    def small_path():
        turns = [me.at(c=1)] + [me.at(zl=o) for o in bits_of(me.near)]
        turns += [me.at(s=o) for o in bits] + [me.at(zh=o) for o in bits_of(me.far)]
        pairs = [(v_ref, v_box, ov_ref), (u_ref, u_box, ou_ref)]
        for src, box, _ in pairs:
            box[0] = src[...]
        for i, device in enumerate(turns):
            copies = [mover.put(box.at[2 * i], box.at[2 * i + 1], device) for _, box, _ in pairs]
            yield
            for copy, (_, box, _) in zip(copies, pairs):
                copy.wait_recv()
                box[2 * i + 2] = box[2 * i] + box[2 * i + 1]
        for _, box, out in pairs:
            out[...] = box[2 * len(turns)]

    arrivals_n, arrivals_b = [], []
    orders = (bits[::-1], bits)
    grads = (gn_ref, n_own, n_box, n_near, og_ref, orders[0])
    branch = (bp_ref, b_own, b_box, b_near, ob_ref, orders[1])
    near_n = [rows_path(*grads, o, arrivals_n) for o in range(1, me.near)]
    near_b = [rows_path(*branch, o, arrivals_b) for o in range(1, me.near)]
    own_n, own_b = rows_path(*grads, 0, arrivals_n), rows_path(*branch, 0, arrivals_b)
    near, own = near_n + near_b, [own_n, own_b]
    weights, keys, small, outs = weight_path(), key_path(), small_path(), out_path()
    turn([weights] + near + own + [keys, small, outs])
    turn([weights] * (me.far * me.peers) + [outs, keys] * me.peers)
    run_paths(near + [keys, small] + own + [weights, outs])
    mover.close()


def scatter(branch, grads, gw, go, gk, small, conv):
    me = Place()
    peers, near, far = me.peers, me.near, me.far
    tokens, width = branch.shape[2:]
    stages = len(bits_of(peers)) + len(bits_of(near)) + len(bits_of(far)) + 1
    vm = lambda *shape: pltpu.VMEM(shape, bf16)
    boxes = lambda part: pltpu.VMEM((2 * stages + 1,) + part.shape, f32)
    rows_scratch = [
        vm(near, peers // 2, tokens, width), vm(near, peers - 1, tokens, width), vm(max(near - 1, 1), tokens, width)
    ]
    block = gw.shape[2:3] + gw.shape[4:]
    kblock = gk.shape[2:3] + gk.shape[4:]
    oblock = go.shape[2:]
    runs = 2 * (far if near > 1 else 1)
    copies = 2 * (peers * near - 1) + (2 * far - 1) * peers + runs * (peers * near - 1) + 2 * far - 1
    copies += 2 * peers - 1 + near - 1 + far - 1 + 2 * stages
    kept = peers * near + far * peers + runs + far + peers
    same = lambda part: jax.ShapeDtypeStruct(part.shape, part.dtype)
    return pl.pallas_call(
        scatter_kernel,
        out_shape=[
            jax.ShapeDtypeStruct((tokens, width), f32),
            jax.ShapeDtypeStruct((tokens, width), f32),
            jax.ShapeDtypeStruct((block[1], 2 * E), bf16),
            jax.ShapeDtypeStruct(oblock, f32),
            jax.ShapeDtypeStruct(kblock[1:], f32),
            same(small),
            same(conv),
        ],
        in_specs=[HBM] * 5 + [VMEM] * 2,
        out_specs=[VMEM, VMEM, HBM, VMEM, VMEM, VMEM, VMEM],
        scratch_shapes=rows_scratch
        + rows_scratch
        + [vm(far, peers, *block), vm(far, peers, *block), vm(max(far - 1, 1), peers, *block)]
        + [vm(far, *oblock), vm(far, *oblock), vm(max(far - 1, 1), *oblock)]
        + [
            vm(peers, far, *kblock), vm(peers, far, *kblock), vm(max(near - 1, 1), far, *kblock[1:]),
            vm(max(far - 1, 1), *kblock[1:]), vm(peers - 1, far, *kblock), boxes(small), boxes(conv),
        ]
        + sems(copies, kept),
        compiler_params=remote_params(2, 58),
        name="scatter_all",
    )(branch, grads, gw, go, gk, small, conv)


def body(
    inputs, cotangent, doc_lengths, head_width, pre_gain, in_weight, step_weight, conv_weight, conv_bias,
    step_bias, decay_log, skip_gain, norm_gain, out_weight,
):
    me = Place()
    peers, near, far = me.peers, me.near, me.far
    outer = far if near > 1 else 1
    tokens = inputs.shape[1]
    width = inputs.shape[2]
    span = tokens * peers
    length = span * near
    heads = H // (peers * near)
    inner = heads * P_SIZE
    rows = in_weight.shape[0]
    seq_rows = inputs[0].astype(f32)
    cot_rows = cotangent[0]

    def own(vector):
        part = vector.reshape(-1, peers, outer, near, vector.shape[-1] // (peers * outer * near))
        part = lax.dynamic_slice(part, (0, me.s, 0, me.zl, 0), (part.shape[0], 1, outer, 1, part.shape[4]))
        return part.reshape(vector.shape[:-1] + (-1,))

    def spread(part):
        lead = part.shape[:-1]
        part = part.reshape(-1, 1, outer, 1, part.shape[-1] // outer)
        full = jnp.zeros((part.shape[0], peers, outer, near, part.shape[-1]), part.dtype)
        return lax.dynamic_update_slice(full, part, (0, me.s, 0, me.zl, 0)).reshape(lead + (-1,))

    key_send = jnp.concatenate(
        [in_weight[:, 2 * E :], step_weight, jnp.zeros((rows, STEP_PAD - H), bf16)], axis=1
    )
    inv_rms = lax.rsqrt(jnp.mean(seq_rows * seq_rows, axis=1, keepdims=True) + epsilon)
    normed = (seq_rows * inv_rms * pre_gain[None, :]).astype(bf16)
    meta = jnp.pad(jnp.concatenate([doc_lengths[0], head_width])[None], ((0, 7), (0, 123)))
    in_w, key_w, out_w, normed, cot_all, meta = gather(in_weight, key_send, out_weight, normed, cot_rows, meta)
    in_w = in_w.reshape(width, 2 * inner)
    key_w = key_w.reshape(width, -1)
    out_w = out_w.reshape(inner, width)
    normed = normed.reshape(length, width)
    cot_all = cot_all.reshape(length, width)
    meta = meta[:, 0, :8]

    head_ids = jnp.arange(H, dtype=f32)
    chan = own(
        jnp.concatenate(
            [
                conv_weight[:, :E],
                conv_bias[None, :E],
                norm_gain[None],
                jnp.repeat(skip_gain, P_SIZE)[None],
                jnp.repeat(head_ids, P_SIZE)[None],
            ],
            axis=0,
        )
    )
    conv_k = jnp.concatenate([conv_weight[:, E:], conv_bias[None, E:], jnp.zeros((3, KEYS), f32)], axis=0)
    head_vec = own(jnp.stack([step_bias, jnp.exp(decay_log), head_ids + 1.0]))
    head_vec = jnp.pad(head_vec, ((0, 5), (0, LANES - heads))) - jnp.where(jnp.arange(8) == 2, 1.0, 0.0)[:, None]

    projected = mm(normed, in_w, NN)
    key_out = mm(normed, key_w, NN)
    grad_mixed = mm(cot_all, out_w, NT)
    mixer_args = (meta, projected, key_out, grad_mixed, chan, conv_k, head_vec)
    *kept, part = mixer_forward(*mixer_args, span, heads)
    sums = cube_total(part)
    mixed, grad_cols, key_cols, chan_sums, key_sums, head_sums = mixer_backward(
        *mixer_args, kept, sums, span, heads
    )
    branch = mm(mixed, out_w, NN).astype(bf16)
    grad_out = mm(mixed, cot_all, TN).astype(bf16)
    grad_in = mm(normed, grad_cols, TN).astype(bf16)
    grad_keys = mm(normed, key_cols, TN).astype(bf16)
    grad_normed = mm(grad_cols, in_w, NT) + mm(key_cols, key_w, NT)
    grad_pre_gain = jnp.sum(grad_normed * normed.astype(f32), axis=0) / pre_gain

    grad_skip = jnp.sum(chan_sums[6].reshape(heads, P_SIZE), axis=1)
    head_sums = spread(jnp.concatenate([head_sums[:2, :heads], grad_skip[None]], axis=0))
    chan_sums = spread(chan_sums[:6])
    small = jnp.concatenate([grad_pre_gain, chan_sums[5], head_sums.reshape(-1)])
    small = jnp.pad(small, (0, -small.shape[0] % 1024)).reshape(-1, 128)
    conv_sums = jnp.pad(jnp.concatenate([chan_sums[:5], key_sums[:5]], axis=1), ((0, 3), (0, 0)))
    rows_of = lambda part: part.reshape(near, peers, tokens, width)
    blocks = (peers, far, near, 2, rows)
    branch, grad_normed, grad_in, grad_out_weight, grad_keys, small, conv_sums = scatter(
        rows_of(branch),
        rows_of(grad_normed.astype(bf16)),
        grad_in.reshape(blocks + (2 * inner,)),
        grad_out.reshape(far, 2, -1, width),
        grad_keys.reshape(blocks + (KEYS + STEP_PAD,)),
        small,
        conv_sums,
    )
    output = (seq_rows + branch).astype(bf16)[None]
    scaled_in = grad_normed * pre_gain[None, :]
    dot = jnp.mean(scaled_in * seq_rows, axis=1, keepdims=True)
    grad_seq = inv_rms * scaled_in - seq_rows * (inv_rms * inv_rms * inv_rms * dot)
    grad_inputs = (grad_seq + cot_rows.astype(f32))[None]
    grad_in_weight = jnp.concatenate([grad_in.astype(f32), grad_keys[:, :KEYS]], axis=1)
    grad_step_weight = grad_keys[:, KEYS : KEYS + H]
    small = small.reshape(-1)
    parts = []
    for size in (width, E, H, H, H):
        parts.append(small[:size])
        small = small[size:]
    return (
        output, grad_inputs, parts[0], grad_in_weight, grad_step_weight, conv_sums[:CONV], conv_sums[CONV],
        parts[2], parts[3], parts[4], parts[1], grad_out_weight,
    )


def solution(mesh):
    both = P(("seq", "batch"), None)
    tok = P("batch", "seq", None)
    in_specs = (
        tok, tok, P("batch", None), P("batch"), P(), both, both, P(), P(), P(), P(), P(), P(), both,
    )
    out_specs = (tok, tok, P(), both, both, P(), P(), P(), P(), P(), P(), both)
    return jax.shard_map(body, mesh=mesh, in_specs=in_specs, out_specs=out_specs, check_vma=False)
```

```python
from functools import partial

import jax
import jax.numpy as jnp
from jax import lax
from jax.experimental import pallas as pl
from jax.experimental.pallas import tpu as pltpu
from jax.sharding import PartitionSpec as P

H = 64
P_SIZE = 64
N = 128
CONV = 4
DOCS = 4
E = 4096
KEYS = 2 * N
STEP_PAD = 128
CHUNK = 128
LANES = 128
epsilon = 1e-05
f32 = jnp.float32
bf16 = jnp.bfloat16


def mm(a, b, dims, precision=None):
    return lax.dot_general(a, b, (dims, ((), ())), precision=precision, preferred_element_type=f32)


NN = ((1,), (0,))
NT = ((1,), (1,))
TN = ((0,), (0,))
exact = lax.Precision.HIGHEST


def pair_cols(low, col, first):
    return jnp.where(low, col[:, first : first + 1], col[:, first + 1 : first + 2])


def iota(shape, axis):
    return lax.broadcasted_iota(jnp.int32, shape, axis)


class Docs:
    def __init__(self, meta_ref, chunk, span):
        per = span // CHUNK
        seq = chunk // per
        self.start = (chunk - seq * per) * CHUNK
        self.ends = []
        total = 0
        for i in range(DOCS - 1):
            total = total + meta_ref[seq, i]
            self.ends.append(total)
        self.count = meta_ref[seq, DOCS]
        self.pos = self.start + iota((CHUNK, 1), 0)
        self.doc = self.index(self.pos)

    def index(self, places):
        found = (places >= self.ends[0]).astype(jnp.int32)
        for end in self.ends[1:]:
            found = found + (places >= end).astype(jnp.int32)
        return found

    def lag(self, by):
        source = self.pos - by
        return ((source >= 0) & (self.index(source) == self.doc)).astype(f32)

    def flow(self):
        return ((self.start > 0) & (self.index(self.start - 1) == self.doc)).astype(f32)

    def row(self):
        return self.index(self.start + iota((1, CHUNK), 1))

    def tail(self):
        return (self.doc == self.index(self.start + CHUNK - 1)).astype(f32)


def shift_down(rows, before, by):
    if by == 0:
        return rows
    moved = pltpu.roll(rows, by, 0)
    top = jnp.where(iota((8, 1), 0) < by, pltpu.roll(before, by, 0), moved[:8])
    return jnp.concatenate([top, moved[8:]], axis=0)


def shift_up(rows, after, by):
    if by == 0:
        return rows
    size = rows.shape[0]
    moved = pltpu.roll(rows, size - by, 0)
    end = jnp.where(iota((8, 1), 0) >= 8 - by, pltpu.roll(after, 8 - by, 0), moved[size - 8 :])
    return jnp.concatenate([moved[: size - 8], end], axis=0)


def silu_slope(v, sig):
    return sig * (1.0 + v * (1.0 - sig))


def forward_kernel(
    meta_ref, proj_ref, grad_ref, chan_ref, conv_k_ref, head_ref,
    val_out, key_out, vsum_ref, ksum_ref, raw_ref, cum_ref, y_ref, gated_ref, state_ref, sums_ref,
    state, last_v, last_k,
    *, span, heads,
):
    i = pl.program_id(0)
    chunks = pl.num_programs(0)
    inner = heads * P_SIZE

    @pl.when(i == 0)
    def _():
        state[...] = jnp.zeros_like(state)
        last_v[...] = jnp.zeros_like(last_v)
        last_k[...] = jnp.zeros_like(last_k)

    docs = Docs(meta_ref, i, span)
    lags = [docs.lag(by) for by in range(1, CONV)]

    def convolve(rows, before, weight, bias):
        total = bias + weight[CONV - 1 :] * rows
        for by in range(1, CONV):
            at = CONV - 1 - by
            total = total + weight[at : at + 1] * (shift_down(rows, before, by) * lags[by - 1])
        return total

    rows_v = proj_ref[:, inner : 2 * inner].astype(bf16).astype(f32)
    vsum = convolve(rows_v, last_v[...], chan_ref[:CONV, :], chan_ref[CONV : CONV + 1, :])
    last_v[...] = rows_v[CHUNK - 8 :]
    vsum_ref[...] = vsum
    val_out[...] = (vsum * jax.nn.sigmoid(vsum)).astype(bf16)
    rows_k = proj_ref[:, 2 * inner : 2 * inner + KEYS].astype(bf16).astype(f32)
    ksum = convolve(rows_k, last_k[...], conv_k_ref[:CONV, :], conv_k_ref[CONV : CONV + 1, :])
    last_k[...] = rows_k[CHUNK - 8 :]
    ksum_ref[...] = ksum
    keys = (ksum * jax.nn.sigmoid(ksum)).astype(bf16)
    key_out[...] = keys

    rows = iota((CHUNK, CHUNK), 0)
    cols = iota((CHUNK, CHUNK), 1)
    chosen = (rows == head_ref[2:3, :].astype(jnp.int32)).astype(f32)
    raw = mm(proj_ref[:, 2 * inner + KEYS :], chosen, NN, exact) + head_ref[:1, :]
    raw_ref[...] = raw
    dt = jax.nn.softplus(raw)
    cum = mm((rows >= cols).astype(f32), -dt * head_ref[1:2, :], NN, exact)
    cum_ref[...] = cum
    cum_t = cum.T
    dt_t = dt.T

    state_ref[0] = state[...].astype(bf16)
    bias = jnp.where((docs.doc == docs.row()) & (rows >= cols), 0.0, -1e30)
    carry_w = docs.flow() * jnp.exp(cum)
    final_w = docs.tail() * jnp.exp(cum[CHUNK - 1 :, :] - cum) * dt
    gain = carry_w[CHUNK - 1 :, :]
    low = cols < P_SIZE
    low_row = low[:1]
    write = keys[:, :N]
    read = keys[:, N:]
    write_t = write.astype(f32).T.astype(bf16)
    scores = mm(read, write, NT)
    square = jnp.zeros((CHUNK, LANES), f32)
    cross = jnp.zeros((CHUNK, LANES), f32)
    count = docs.count.astype(f32)
    for pair in range(heads // 2):
        first = 2 * pair
        lanes = slice(pair * 128, pair * 128 + 128)
        xf = val_out[:, lanes].astype(f32)
        weights = []
        for h in (first, first + 1):
            decay = jnp.exp(cum[:, h : h + 1] - cum_t[h : h + 1, :] + bias)
            weights.append((decay * scores * dt_t[h : h + 1, :]).astype(bf16))
        stacked = jnp.concatenate(
            [jnp.where(low, xf, 0.0).astype(bf16), jnp.where(low, 0.0, xf).astype(bf16)], axis=0
        )
        old = state[:, lanes]
        y = mm(jnp.concatenate(weights, axis=1), stacked, NN)
        y = y + pair_cols(low, carry_w, first) * mm(read, old.astype(bf16), NN)
        y = y + chan_ref[6:7, lanes] * xf
        y = jnp.where(chan_ref[7:8, lanes] < count, y, 0.0)
        y_ref[:, lanes] = y
        state[:, lanes] = pair_cols(low_row, gain, first) * old + mm(
            write_t, (pair_cols(low, final_w, first) * xf).astype(bf16), NN
        )
        gate = proj_ref[:, lanes]
        gated = y * (gate * jax.nn.sigmoid(gate))
        gated_ref[:, lanes] = gated
        square = square + gated * gated
        cross = cross + gated * (grad_ref[:, lanes] * chan_ref[5:6, lanes])
    share = 1.0 / (count * P_SIZE)
    sums_ref[pl.ds(i, 1), :] = jnp.sum(square.T, axis=0, keepdims=True) * share
    sums_ref[pl.ds(chunks + i, 1), :] = jnp.sum(cross.T, axis=0, keepdims=True) * share


def backward_kernel(
    meta_ref, proj_ref, grad_ref, chan_ref, conv_k_ref, head_ref,
    val_ref, key_ref, vsum_ref, ksum_ref, raw_ref, cum_ref, y_ref, state_ref, sums_ref, branch_ref, go_ref,
    cols_ref, chan_sums, key_sums, head_sums, b_out, o_out,
    dstate, dv, next_v, next_k, next_lags, *early_refs,
    span, heads,
):
    chunks = pl.num_programs(0)
    i = chunks - 1 - pl.program_id(0)
    inner = heads * P_SIZE
    early = Early(branch_ref, go_ref, (b_out, o_out) + early_refs)

    @pl.when(pl.program_id(0) == 0)
    def _():
        early.start()
        for ref in (dstate, next_v, next_k, next_lags, chan_sums, key_sums, head_sums):
            ref[...] = jnp.zeros_like(ref)

    docs = Docs(meta_ref, i, span)
    rows = iota((CHUNK, CHUNK), 0)
    cols = iota((CHUNK, CHUNK), 1)
    raw = raw_ref[...]
    dt = jax.nn.softplus(raw)
    cum = cum_ref[...]
    cum_t = cum.T
    count = docs.count.astype(f32)

    def column(row):
        return jnp.broadcast_to(row, (CHUNK, CHUNK)).T

    inv = lax.rsqrt(column(sums_ref[pl.ds(i, 1), :]) + epsilon)
    pull = inv * inv * inv * column(sums_ref[pl.ds(chunks + i, 1), :])

    bias = jnp.where((docs.doc == docs.row()) & (cols >= rows), 0.0, -1e30)
    carry_w = docs.flow() * jnp.exp(cum)
    final_d = docs.tail() * jnp.exp(cum[CHUNK - 1 :, :] - cum)
    final_w = final_d * dt
    gain = carry_w[CHUNK - 1 :, :]
    low = cols < P_SIZE
    low_row = low[:1]
    write = key_ref[:, :N]
    read = key_ref[:, N:]
    read_t = read.astype(f32).T.astype(bf16)
    scores_t = mm(write, read, NT)
    dscores_t = jnp.zeros((CHUNK, CHUNK), f32)
    dwrite = jnp.zeros((CHUNK, N), f32)
    dread = jnp.zeros((CHUNK, N), f32)
    end_row = iota((CHUNK, 1), 0) == CHUNK - 1
    dcum = jnp.zeros((CHUNK, LANES), f32)
    ddt = jnp.zeros((CHUNK, LANES), f32)
    dcum_rows = []
    for pair in range(heads // 2):
        first = 2 * pair
        lanes = slice(pair * 128, pair * 128 + 128)
        gate = proj_ref[:, lanes]
        sig = jax.nn.sigmoid(gate)
        silu = gate * sig
        masked = y_ref[:, lanes]
        gated = masked * silu
        norm_gain = chan_ref[5:6, lanes]
        gm = grad_ref[:, lanes]
        unit = gated * inv
        chan_sums[5:6, lanes] += jnp.sum(gm * unit, axis=0, keepdims=True)
        grad_gated = inv * (gm * norm_gain) - pull * gated
        cols_ref[:, lanes] = (grad_gated * masked * silu_slope(gate, sig)).astype(bf16)
        dy = jnp.where(chan_ref[7:8, lanes] < count, grad_gated * silu, 0.0)
        xf = val_ref[:, lanes].astype(f32)
        dyb = dy.astype(bf16)
        x_stack = jnp.concatenate(
            [jnp.where(low, xf, 0.0).astype(bf16), jnp.where(low, 0.0, xf).astype(bf16)], axis=0
        )
        dy_stack = jnp.concatenate(
            [jnp.where(low, dy, 0.0).astype(bf16), jnp.where(low, 0.0, dy).astype(bf16)], axis=0
        )
        dweights = mm(x_stack, dyb, NT)
        old = state_ref[0, :, lanes]
        grad = dstate[:, lanes]
        gradb = grad.astype(bf16)
        carried = mm(read, old, NN)
        pushed = mm(write, gradb, NN)
        carry_p = pair_cols(low, carry_w, first)
        final_p = pair_cols(low, final_w, first)
        carry_prod = dy * carried
        final_prod = xf * pushed
        gain_prod = jnp.sum(grad * old.astype(f32), axis=0, keepdims=True)
        weights = []
        for which, h in enumerate((first, first + 1)):
            col = dt[:, h : h + 1]
            decay = jnp.exp(cum_t[h : h + 1, :] - cum[:, h : h + 1] + bias)
            weighted = decay * col
            weights.append((weighted * scores_t).astype(bf16))
            dw = dweights[which * CHUNK : (which + 1) * CHUNK]
            dscores_t = dscores_t + dw * weighted
            direct = dw * decay * scores_t
            ddt_in = jnp.sum(direct, axis=1, keepdims=True)
            dcum_rows.append(jnp.sum(direct * col, axis=0, keepdims=True))
            half = low if which == 0 else ~low
            half_row = low_row if which == 0 else ~low_row
            carry_sum = jnp.sum(jnp.where(half, carry_prod, 0.0), axis=1, keepdims=True)
            final_sum = jnp.sum(jnp.where(half, final_prod, 0.0), axis=1, keepdims=True)
            push = final_w[:, h : h + 1] * final_sum
            at_end = jnp.sum(push, axis=0, keepdims=True) + gain[:, h : h + 1] * jnp.sum(
                jnp.where(half_row, gain_prod, 0.0), axis=1, keepdims=True
            )
            here = cols == h
            ddt = jnp.where(here, ddt_in + final_d[:, h : h + 1] * final_sum, ddt)
            dcum = jnp.where(
                here,
                carry_w[:, h : h + 1] * carry_sum - push - col * ddt_in + jnp.where(end_row, at_end, 0.0),
                dcum,
            )
        dx = mm(jnp.concatenate(weights, axis=1), dy_stack, NN)
        dv[:, lanes] = dx + final_p * pushed + chan_ref[6:7, lanes] * dy
        chan_sums[6:7, lanes] += jnp.sum(dy * xf, axis=0, keepdims=True)
        dwrite = dwrite + mm((final_p * xf).astype(bf16), gradb, NT)
        carry_dy = (carry_p * dy).astype(bf16)
        dread = dread + mm(carry_dy, old, NT)
        dstate[:, lanes] = pair_cols(low_row, gain, first) * grad + mm(read_t, carry_dy, NN)
    dsb = dscores_t.astype(bf16)
    dkeys = jnp.concatenate([dwrite + mm(dsb, read, NN), dread + mm(dsb, write, TN)], axis=1)

    extra = jnp.concatenate(dcum_rows + [jnp.zeros((LANES - heads, CHUNK), f32)], axis=0)
    dlog = mm((cols >= rows).astype(f32), dcum + extra.T, NN, exact)
    rate = head_ref[1:2, :]
    grad_step = (ddt - rate * dlog) * jax.nn.sigmoid(raw)
    head_sums[:1, :] += jnp.sum(grad_step, axis=0, keepdims=True)
    head_sums[1:2, :] -= jnp.sum(dt * rate * dlog, axis=0, keepdims=True)
    chosen = (rows == head_ref[2:3, :].astype(jnp.int32)).astype(bf16)
    cols_ref[:, 2 * inner + KEYS :] = mm(grad_step.astype(bf16), chosen, NT).astype(bf16)

    lags = [docs.lag(by) for by in range(1, CONV)]

    def convolve_back(dact, total, rows_in, after, weight, sums):
        dconv = dact * silu_slope(total, jax.nn.sigmoid(total))
        grad_in = weight[CONV - 1 :] * dconv
        sums[CONV : CONV + 1, :] += jnp.sum(dconv, axis=0, keepdims=True)
        sums[CONV - 1 : CONV, :] += jnp.sum(dconv * rows_in, axis=0, keepdims=True)
        for by in range(1, CONV):
            at = CONV - 1 - by
            moved = shift_up(dconv * lags[by - 1], after[...] * next_lags[:, by - 1 : by], by)
            grad_in = grad_in + weight[at : at + 1] * moved
            sums[at : at + 1, :] += jnp.sum(moved * rows_in, axis=0, keepdims=True)
        after[...] = dconv[:8]
        return grad_in.astype(bf16)

    rows_v = proj_ref[:, inner : 2 * inner].astype(bf16).astype(f32)
    cols_ref[:, inner : 2 * inner] = convolve_back(dv[...], vsum_ref[...], rows_v, next_v, chan_ref[:CONV, :], chan_sums)
    rows_k = proj_ref[:, 2 * inner : 2 * inner + KEYS].astype(bf16).astype(f32)
    cols_ref[:, 2 * inner : 2 * inner + KEYS] = convolve_back(
        dkeys, ksum_ref[...], rows_k, next_k, conv_k_ref[:CONV, :], key_sums
    )
    for by in range(1, CONV):
        next_lags[:, by - 1 : by] = lags[by - 1][:8]

    @pl.when(pl.program_id(0) == 1)
    def _():
        early.middle()

    @pl.when(pl.program_id(0) == chunks - 1)
    def _():
        early.end()


def mixer_forward(meta, projected, grad_mixed, chan, conv_k, head_vec, span, heads):
    length = projected.shape[0]
    inner = heads * P_SIZE
    chunks = length // CHUNK
    row = lambda width: pl.BlockSpec((CHUNK, width), lambda i: (i, 0))
    all_of = lambda *shape: pl.BlockSpec(shape, lambda i: (0,) * len(shape))
    out = lambda width, dtype: jax.ShapeDtypeStruct((length, width), dtype)
    return pl.pallas_call(
        partial(forward_kernel, span=span, heads=heads),
        grid=(chunks,),
        in_specs=[
            pl.BlockSpec(memory_space=pltpu.SMEM), row(2 * inner + KEYS + STEP_PAD), row(inner),
            all_of(8, inner), all_of(8, KEYS), all_of(8, LANES),
        ],
        out_specs=[
            row(inner), row(KEYS), row(inner), row(KEYS), row(LANES), row(LANES), row(inner), row(inner),
            pl.BlockSpec((1, N, inner), lambda i: (i, 0, 0)), all_of(2 * chunks, LANES),
        ],
        out_shape=[
            out(inner, bf16), out(KEYS, bf16), out(inner, f32), out(KEYS, f32), out(LANES, f32), out(LANES, f32),
            out(inner, f32), out(inner, f32), jax.ShapeDtypeStruct((chunks, N, inner), bf16),
            jax.ShapeDtypeStruct((2 * chunks, LANES), f32),
        ],
        scratch_shapes=[pltpu.VMEM((N, inner), f32), pltpu.VMEM((8, inner), f32), pltpu.VMEM((8, KEYS), f32)],
        compiler_params=pltpu.CompilerParams(vmem_limit_bytes=16 * 2**20),
        cost_estimate=pl.CostEstimate(
            flops=length * inner * 1024, bytes_accessed=length * inner * 24, transcendentals=length * heads * CHUNK
        ),
        name="mixer_forward",
    )(meta, projected, grad_mixed, chan, conv_k, head_vec)


def mixer_backward(meta, projected, grad_mixed, chan, conv_k, head_vec, kept, sums, branch, grad_out, span, heads):
    length = projected.shape[0]
    inner = heads * P_SIZE
    chunks = length // CHUNK
    me = Place()
    near, peers, tokens, width = branch.shape
    far = me.far
    part = grad_out.shape[2:]
    copies = near * peers // 2 + 2 * far - 1
    vm = lambda *shape: pltpu.VMEM(shape, bf16)
    row = lambda width: pl.BlockSpec((CHUNK, width), lambda i: (chunks - 1 - i, 0))
    all_of = lambda *shape: pl.BlockSpec(shape, lambda i: (0,) * len(shape))
    out = lambda width: jax.ShapeDtypeStruct((length, width), bf16)
    return pl.pallas_call(
        partial(backward_kernel, span=span, heads=heads),
        grid=(chunks,),
        in_specs=[
            pl.BlockSpec(memory_space=pltpu.SMEM), row(2 * inner + KEYS + STEP_PAD), row(inner),
            all_of(8, inner), all_of(8, KEYS), all_of(8, LANES),
            row(inner), row(KEYS), row(inner), row(KEYS), row(LANES), row(LANES), row(inner),
            pl.BlockSpec((1, N, inner), lambda i: (chunks - 1 - i, 0, 0)), all_of(2 * chunks, LANES), HBM, HBM,
        ],
        out_specs=[
            row(2 * inner + KEYS + STEP_PAD), all_of(8, inner), all_of(8, KEYS), all_of(8, LANES),
            VMEM, VMEM,
        ],
        out_shape=[
            out(2 * inner + KEYS + STEP_PAD), jax.ShapeDtypeStruct((8, inner), f32),
            jax.ShapeDtypeStruct((8, KEYS), f32), jax.ShapeDtypeStruct((8, LANES), f32),
            jax.ShapeDtypeStruct((near, peers // 2, tokens, width), bf16), jax.ShapeDtypeStruct(part, f32),
        ],
        scratch_shapes=[
            pltpu.VMEM((N, inner), f32), pltpu.VMEM((CHUNK, inner), f32), pltpu.VMEM((8, inner), f32),
            pltpu.VMEM((8, KEYS), f32), pltpu.VMEM((8, LANES), f32),
            vm(near, peers // 2, tokens, width), vm(near, peers // 2, tokens, width),
            vm(far, *part), vm(far, *part), vm(max(far - 1, 1), *part),
        ]
        + sems(copies, near * peers // 2 + far),
        compiler_params=remote_params(3, 32),
        cost_estimate=pl.CostEstimate(
            flops=length * inner * 3072, bytes_accessed=length * inner * 30, transcendentals=length * heads * CHUNK
        ),
        name="mixer_backward",
    )(meta, projected, grad_mixed, chan, conv_k, head_vec, *kept, sums, branch, grad_out)


MESH = pl.DeviceIdType.MESH
HBM = pl.BlockSpec(memory_space=pl.ANY)
VMEM = pl.BlockSpec(memory_space=pltpu.VMEM)


def z_pair(peers, groups):
    planes = groups // 2
    return 2 if planes % 2 == 0 and (E // (peers * planes)) % (2 * P_SIZE) == 0 else 1


def flip(value, bits):
    bit = 1
    while bit <= bits:
        if bits & bit:
            value = value + bit - 2 * bit * (value // bit % 2)
        bit *= 2
    return value


class Place:
    def __init__(self):
        self.peers = lax.axis_size("seq")
        groups = lax.axis_size("batch")
        self.near = z_pair(self.peers, groups)
        self.far = groups // 2 // self.near
        self.s = lax.axis_index("seq")
        b = lax.axis_index("batch")
        self.c = b % 2
        self.zl = b // 2 % self.near
        self.zh = b // 2 // self.near

    def at(self, s=0, zl=0, zh=0, c=0):
        return (flip(self.s, s), (flip(self.zh, zh) * self.near + flip(self.zl, zl)) * 2 + flip(self.c, c))

    def column_runs(self, s, zl, width):
        outer = self.far if self.near > 1 else 1
        run = width // (2 * outer)
        runs = []
        for part in range(2):
            for i in range(outer):
                first = part * E + ((s * outer + i) * self.near + zl) * run
                runs.append((pl.ds(pl.multiple_of(first, 128), run), pl.ds((part * outer + i) * run, run)))
        return runs

    def partners(self):
        cube = [self.at(s=o // self.near, zl=o % self.near) for o in range(1, self.peers * self.near)]
        return cube, [self.at(zh=o) for o in range(1, self.far)], [self.at(c=1)]


def greet(devices):
    barrier = pltpu.get_barrier_semaphore()
    for device in devices:
        pl.semaphore_signal(barrier, inc=1, device_id=device, device_id_type=MESH)
    pl.semaphore_wait(barrier, len(devices))


class Mover:
    def __init__(self, send, recv, local):
        self.send, self.recv, self.local = send, recv, local
        self.sent, self.kept = 0, 0
        self.open = []

    def plan(self, src, dst, device):
        copy = pltpu.make_async_remote_copy(
            src_ref=src, dst_ref=dst, send_sem=self.send.at[self.sent], recv_sem=self.recv.at[self.sent],
            device_id=device, device_id_type=MESH,
        )
        self.sent += 1
        self.open.append(copy)
        return copy

    def put(self, src, dst, device):
        copy = self.plan(src, dst, device)
        copy.start()
        return copy

    def plan_keep(self, src, dst):
        self.kept += 1
        return pltpu.make_async_copy(src, dst, self.local.at[self.kept - 1])

    def keep(self, src, dst):
        copy = self.plan_keep(src, dst)
        copy.start()
        return copy

    def close(self):
        for copy in self.open:
            copy.wait_send()


def run_paths(paths):
    paths = list(paths)
    while paths:
        alive = []
        for path in paths:
            try:
                next(path)
                alive.append(path)
            except StopIteration:
                pass
        paths = alive


def turn(paths):
    for path in paths:
        next(path, None)


def bits_of(peers):
    return [1 << i for i in range(peers.bit_length() - 1)]


def combos(bits):
    out = [0]
    for bit in reversed(bits):
        out = [bit | o for o in out] + out
    return out


def gather_kernel(
    in_ref, key_ref, out_ref, rows_ref, cot_ref, meta_ref,
    w_ref, o_ref, x_ref, ct_ref, m_ref, send, recv, local,
):
    me = Place()
    s, zl, zh, c = me.s, me.zl, me.zh, me.c
    columns = w_ref.shape[-1] - key_ref.shape[-1]
    mine, shared = pl.ds(0, columns), pl.ds(columns, key_ref.shape[-1])
    cube, far, sibling = me.partners()
    greet(cube + far + sibling)
    mover = Mover(send, recv, local)
    bits = bits_of(me.peers)

    def plane_path(src, dst, order, near):
        view = dst.at[flip(zl, near)]
        if near:
            copy = mover.put(src, dst.at[zl, s], me.at(zl=near))
            yield
            copy.wait_recv()
        else:
            own = mover.keep(src, view.at[s])
        held = [0]
        for bit in order:
            copies = []
            for h in held:
                at = view.at[flip(s, h)]
                copies.append(mover.put(at if near or h else src, at if near else dst.at[zl, flip(s, h)], me.at(s=bit)))
            held = held + [h ^ bit for h in held]
            yield
            for copy in copies:
                copy.wait_recv()
        if not near:
            own.wait()

    def meta_path():
        own = mover.keep(meta_ref, m_ref.at[zl])
        near = [mover.put(meta_ref, m_ref.at[zl], me.at(zl=o)) for o in range(1, me.near)]
        yield
        own.wait()
        for copy in near:
            copy.wait_recv()

    def key_path():
        block = w_ref.at[s, zh, zl, c, :, shared]
        own = mover.keep(key_ref, block)
        copies = [mover.put(key_ref, block, me.at(zh=o)) for o in range(1, me.far)]
        yield
        own.wait()
        for copy in copies:
            copy.wait_recv()
        block = w_ref.at[s, :, zl, c, :, shared]
        copies = [mover.put(block, block, me.at(zl=o)) for o in range(1, me.near)]
        yield
        for copy in copies:
            copy.wait_recv()
        held = [0]
        for bit in bits:
            copies = []
            for h in held:
                block = w_ref.at[flip(s, h), :, :, c, :, shared]
                copies.append(mover.put(block, block, me.at(s=bit)))
            held = held + [h ^ bit for h in held]
            yield
            for copy in copies:
                copy.wait_recv()
        block = w_ref.at[:, :, :, c, :, shared]
        copy = mover.put(block, block, me.at(c=1))
        yield
        copy.wait_recv()

    def spread_path(copies, view):
        last = []
        for o, copy in copies:
            yield
            copy.wait_recv()
            last.append(mover.put(view(flip(zh, o)), view(flip(zh, o)), me.at(c=1)))
        return last

    def out_path():
        own = mover.keep(out_ref, o_ref.at[zh, c])
        copies = [(o, mover.put(out_ref, o_ref.at[zh, c], me.at(zh=o))) for o in range(1, me.far)]
        first = mover.put(out_ref, o_ref.at[zh, c], me.at(c=1))
        last = yield from spread_path(copies, lambda h: o_ref.at[h, c])
        yield
        own.wait()
        for copy in last + [first]:
            copy.wait_recv()

    def weight_path():
        moves = {}
        for step in range(me.peers):
            for o in range(me.near):
                to_s, to_zl = flip(s, step), flip(zl, o)
                for src, dst in me.column_runs(to_s, to_zl, columns):
                    src = in_ref.at[:, src]
                    dst = w_ref.at[s, zh, zl, c, :, dst]
                    if step or o:
                        copy = mover.put(src, dst, me.at(s=step, zl=o))
                    else:
                        copy = mover.keep(src, dst)
                    moves.setdefault(step, []).append(copy)
        pieces = []
        for step in range(me.peers):
            yield
            for i, copy in enumerate(moves[step]):
                if step == 0 and i < len(moves[0]) // me.near:
                    copy.wait()
                else:
                    copy.wait_recv()
            block = w_ref.at[flip(s, step), zh, :, c, :, mine]
            copies = [(o, mover.put(block, block, me.at(zh=o))) for o in range(1, me.far)]
            pieces.append((step, copies, mover.put(block, block, me.at(c=1))))
        last = []
        for step, copies, first in pieces:
            last.append(first)
            last += yield from spread_path(copies, lambda h, step=step: w_ref.at[flip(s, step), h, :, c, :, mine])
        yield
        for copy in last:
            copy.wait_recv()

    own_x = plane_path(rows_ref, x_ref, bits, 0)
    own_c = plane_path(cot_ref, ct_ref, bits[::-1], 0)
    near_x = [plane_path(rows_ref, x_ref, bits, o) for o in range(1, me.near)]
    near_c = [plane_path(cot_ref, ct_ref, bits[::-1], o) for o in range(1, me.near)]
    near = near_x + near_c
    keys, weights, outs = key_path(), weight_path(), out_path()
    turn([own_x, own_c, weights] + near + [keys, outs])
    extra = meta_path()
    turn([extra, own_x, own_c] + [weights] * me.peers + [keys] + near + [keys])
    turn([own_x, own_c] + near + [keys, outs, weights, keys, weights])
    run_paths([weights, extra, keys, outs, own_x, own_c] + near)
    mover.close()


def remote_params(identity, mib):
    return pltpu.CompilerParams(collective_id=identity, has_side_effects=True, vmem_limit_bytes=mib * 2**20)


def sems(copies, kept):
    return [pltpu.SemaphoreType.DMA((copies,)), pltpu.SemaphoreType.DMA((copies,)), pltpu.SemaphoreType.DMA((kept,))]


def gather(in_w, keys, out_w, rows, cot, meta):
    me = Place()
    peers, near, far = me.peers, me.near, me.far
    shape = lambda lead, part: jax.ShapeDtypeStruct(lead + part, bf16)
    columns = 2 * E // (peers * near)
    runs = 2 * (far if near > 1 else 1)
    copies = runs * (peers * near - 1) + (peers + 1) * (2 * far - 1) + 2 * (near * peers - 1)
    copies += 2 * near + peers + far - 3
    return pl.pallas_call(
        gather_kernel,
        out_shape=[
            shape((peers, far, near, 2), (in_w.shape[0], columns + keys.shape[1])),
            shape((far, 2), out_w.shape),
            shape((near, peers), rows.shape),
            shape((near, peers), cot.shape),
            jax.ShapeDtypeStruct((near,) + meta.shape, meta.dtype),
        ],
        in_specs=[HBM] * 6,
        out_specs=[HBM] * 5,
        scratch_shapes=sems(copies, runs + 5),
        compiler_params=remote_params(0, 4),
        name="gather_all",
    )(in_w, keys, out_w, rows, cot, meta)


def total_kernel(part_ref, gated_ref, chan_ref, sum_ref, mixed_ref, box, send, recv, local):
    me = Place()
    cube = me.partners()[0]
    greet(cube)
    mover = Mover(send, recv, local)
    copies = [mover.put(part_ref, box.at[i], device) for i, device in enumerate(cube)]
    total = part_ref[...]
    for i, copy in enumerate(copies):
        copy.wait_recv()
        total = total + box[i]
    sum_ref[...] = total
    chunks = part_ref.shape[0] // 2

    def step(i, carry):
        at = pl.ds(pl.multiple_of(i * CHUNK, CHUNK), CHUNK)
        inv = lax.rsqrt(jnp.broadcast_to(sum_ref[pl.ds(i, 1), :], (CHUNK, CHUNK)).T + epsilon)
        for lane in range(0, gated_ref.shape[1], LANES):
            lanes = slice(lane, lane + LANES)
            mixed_ref[at, lanes] = (gated_ref[at, lanes] * inv * chan_ref[5:6, lanes]).astype(bf16)
        return carry

    lax.fori_loop(0, chunks, step, 0)
    mover.close()


def cube_total(part, gated, chan):
    me = Place()
    count = me.peers * me.near - 1
    return pl.pallas_call(
        total_kernel,
        out_shape=[jax.ShapeDtypeStruct(part.shape, f32), jax.ShapeDtypeStruct(gated.shape, bf16)],
        in_specs=[VMEM] * 3,
        out_specs=[VMEM] * 2,
        scratch_shapes=[pltpu.VMEM((count,) + part.shape, f32)] + sems(count, 1),
        compiler_params=remote_params(1, 12),
        name="cube_total",
    )(part, gated, chan)


def add_rows(out, parts):
    shape = out.shape
    tile = min(16, shape[-2])
    lead = [()]
    for size in shape[:-2]:
        lead = [l + (i,) for l in lead for i in range(size)]
    for l in lead:

        def step(i, carry, l=l):
            at = l + (pl.ds(pl.multiple_of(i * tile, tile), tile), slice(None))
            total = parts[0][at].astype(f32)
            for part in parts[1:]:
                total = total + part[at].astype(f32)
            out[at] = total.astype(out.dtype)
            return carry

        lax.fori_loop(0, shape[-2] // tile, step, 0)


def scatter_kernel(
    gn_ref, gw_ref, b_ref, v_ref, u_ref, og_ref, ow_ref, ob_ref, ok_ref, ov_ref, ou_ref,
    n_own, n_box, n_near, b_own, b_box, b_near, w_own, w_box, w_far,
    k_own, k_box, k_near, k_far, k_bits, v_box, u_box, send, recv, local,
):
    me = Place()
    s, zl, zh, c = me.s, me.zl, me.zh, me.c
    cube, far, sibling = me.partners()
    greet(cube + far + sibling)
    mover = Mover(send, recv, local)
    bits = bits_of(me.peers)
    columns = w_own.shape[-1]
    mine, shared = pl.ds(0, columns), pl.ds(columns, k_own.shape[-1])

    def rows_path(src, own, box, near_box, out, order, near, arrivals, done=0):
        own, box = own.at[near], box.at[near]
        copies, loads = [], []
        if done:
            half = me.peers // 4
            for j in range(half):
                copies.append(mover.put(src.at[near, j], box.at[j], me.at(s=order[1])))
                loads.append(mover.keep(src.at[near, half + j], own.at[half + j]))
        else:
            at_zl = src.at[flip(zl, near)]
            for j, o in enumerate(combos(order[1:])):
                copies.append(mover.put(at_zl.at[flip(s, order[0] ^ o)], box.at[j], me.at(s=order[0])))
                loads.append(mover.keep(at_zl.at[flip(s, o)], own.at[j]))
        base = 0
        for i in range(done, len(order)):
            rest = order[i + 1 :]
            count = 1 << len(rest)
            offset = (1 << (len(order) - 1)) - count
            coming = []
            for j in range(count):
                yield
                copies[j].wait_recv()
                if i == done:
                    loads[j].wait()
                if rest or near:
                    add_rows(own.at[offset + j], [own.at[offset + j], box.at[base + j]])
                if rest and j < count // 2:
                    coming.append(mover.put(own.at[offset + j], box.at[base + count + j], me.at(s=rest[0])))
            copies = coming
            last = base
            base += count
        end = (1 << (len(order) - 1)) - 1
        if near:
            arrivals.append(mover.put(own.at[end], near_box.at[near - 1], me.at(zl=near)))
            yield
        else:
            yield
            for _ in range(me.near - 1):
                arrivals.pop(0).wait_recv()
            add_rows(out, [own.at[end], box.at[last]] + [near_box.at[o - 1] for o in range(1, me.near)])

    def weight_path():
        order = [(o, k) for o in range(1, me.far) for k in range(me.peers)] + [(0, k) for k in range(me.peers)]
        loads, copies = {}, {}
        for o, k in order:
            copies[o, k] = mover.put(gw_ref.at[flip(s, k), flip(zh, o), :, 1 - c, :, mine], w_box.at[o, k], me.at(c=1))
            loads[o, k] = mover.keep(gw_ref.at[flip(s, k), flip(zh, o), :, c, :, mine], w_own.at[o, k])
        far_copies = {}
        for o, k in order:
            yield
            loads[o, k].wait()
            copies[o, k].wait_recv()
            if o:
                add_rows(w_own.at[o, k], [w_own.at[o, k], w_box.at[o, k]])
                far_copies[o, k] = mover.put(w_own.at[o, k], w_far.at[o - 1, k], me.at(zh=o))
        ends, kept = [], []
        for k in range(me.peers):
            yield
            for o in range(1, me.far):
                far_copies[o, k].wait_recv()
            parts = [w_own.at[0, k], w_box.at[0, k]] + [w_far.at[o - 1, k] for o in range(1, me.far)]
            add_rows(w_own.at[0, k], parts)
            for o in range(me.near):
                for whole, part in me.column_runs(s, zl, columns):
                    src = w_own.at[0, k, flip(zl, o), :, part]
                    if k or o:
                        ends.append(mover.put(src, ow_ref.at[:, whole], me.at(s=k, zl=o)))
                    else:
                        kept.append(mover.keep(src, ow_ref.at[:, whole]))
        yield
        for copy in kept:
            copy.wait()
        for copy in ends:
            copy.wait_recv()

    def key_path():
        blocks = combos(bits)
        copies, loads = [], []
        for j, o in enumerate(blocks):
            copies.append(mover.put(gw_ref.at[flip(s, o), :, :, 1 - c, :, shared], k_box.at[j], me.at(c=1)))
            loads.append(mover.keep(gw_ref.at[flip(s, o), :, :, c, :, shared], k_own.at[j]))
        half = me.peers // 2
        sent = []
        for j in range(me.peers):
            yield
            loads[j].wait()
            copies[j].wait_recv()
            add_rows(k_own.at[j], [k_own.at[j], k_box.at[j]])
            if j < half:
                sent.append(mover.put(k_own.at[j], k_bits.at[j], me.at(s=bits[0])))
        base = 0
        for i, bit in enumerate(bits):
            count = me.peers >> (i + 1)
            offset = me.peers - count
            coming = []
            for j in range(count):
                yield
                sent[j].wait_recv()
                add_rows(k_own.at[offset + j], [k_own.at[offset + j], k_bits.at[base + j]])
                if i + 1 < len(bits) and j < count // 2:
                    coming.append(mover.put(k_own.at[offset + j], k_bits.at[base + count + j], me.at(s=bits[i + 1])))
            base += count
            sent = coming
        end = k_own.at[me.peers - 1]
        copies = [mover.put(end.at[:, flip(zl, o)], k_near.at[o - 1], me.at(zl=o)) for o in range(1, me.near)]
        yield
        for copy in copies:
            copy.wait_recv()
        add_rows(end.at[:, zl], [end.at[:, zl]] + [k_near.at[o - 1] for o in range(1, me.near)])
        copies = [mover.put(end.at[flip(zh, o), zl], k_far.at[o - 1], me.at(zh=o)) for o in range(1, me.far)]
        yield
        for copy in copies:
            copy.wait_recv()
        add_rows(ok_ref, [end.at[zh, zl]] + [k_far.at[o - 1] for o in range(1, me.far)])

    def small_path():
        turns = [me.at(c=1)] + [me.at(zl=o) for o in bits_of(me.near)]
        turns += [me.at(s=o) for o in bits] + [me.at(zh=o) for o in bits_of(me.far)]
        pairs = [(v_ref, v_box, ov_ref), (u_ref, u_box, ou_ref)]
        for src, box, _ in pairs:
            box[0] = src[...]
        for i, device in enumerate(turns):
            copies = [mover.put(box.at[2 * i], box.at[2 * i + 1], device) for _, box, _ in pairs]
            yield
            for copy, (_, box, _) in zip(copies, pairs):
                copy.wait_recv()
                box[2 * i + 2] = box[2 * i] + box[2 * i + 1]
        for _, box, out in pairs:
            out[...] = box[2 * len(turns)]

    coming_n, coming_b = [], []
    grads = (gn_ref, n_own, n_box, n_near, og_ref)
    branch = (b_ref, b_own, b_box, b_near, ob_ref)
    orders = lambda o: bits if o else bits[::-1]
    near_n = [rows_path(*grads, orders(o), o, coming_n) for o in range(1, me.near)]
    near_b = [rows_path(*branch, orders(o), o, coming_b, 1) for o in range(1, me.near)]
    own_n = rows_path(*grads, orders(0), 0, coming_n)
    own_b = rows_path(*branch, orders(0), 0, coming_b, 1)
    weights, keys, small = weight_path(), key_path(), small_path()
    turn([weights] + near_b + near_n + [own_n, keys, own_b, small])
    turn([weights] * (me.far * me.peers) + [keys] * me.peers)
    run_paths(near_b + near_n + [keys, small, own_b, own_n, weights])
    mover.close()


def scatter(grads, gw, branch, small, conv):
    me = Place()
    peers, near, far = me.peers, me.near, me.far
    tokens, width = grads.shape[2:]
    stages = len(bits_of(peers)) + len(bits_of(near)) + len(bits_of(far)) + 1
    vm = lambda *shape: pltpu.VMEM(shape, bf16)
    boxes = lambda part: pltpu.VMEM((2 * stages + 1,) + part.shape, f32)
    keys = KEYS + STEP_PAD
    rows = gw.shape[4]
    block = (near, rows, gw.shape[5] - keys)
    kblock = (near, rows, keys)
    runs = 2 * (far if near > 1 else 1)
    copies = peers * near - 1 + (2 * far - 1) * peers + runs * (peers * near - 1)
    copies += 2 * peers - 1 + near - 1 + far - 1 + 2 * stages + peers // 2 * near - 1
    kept = peers * near + far * peers + runs + peers + near * peers // 4
    same = lambda part: jax.ShapeDtypeStruct(part.shape, part.dtype)
    return pl.pallas_call(
        scatter_kernel,
        out_shape=[
            jax.ShapeDtypeStruct((tokens, width), f32),
            jax.ShapeDtypeStruct((rows, 2 * E), bf16),
            jax.ShapeDtypeStruct((tokens, width), f32),
            jax.ShapeDtypeStruct((rows, keys), f32),
            same(small),
            same(conv),
        ],
        in_specs=[HBM] * 3 + [VMEM] * 2,
        out_specs=[VMEM, HBM, VMEM, VMEM, VMEM, VMEM],
        scratch_shapes=[
            vm(near, peers // 2, tokens, width), vm(near, peers - 1, tokens, width), vm(max(near - 1, 1), tokens, width),
            vm(near, peers // 2, tokens, width), vm(near, peers // 2 - 1, tokens, width), vm(max(near - 1, 1), tokens, width),
            vm(far, peers, *block), vm(far, peers, *block), vm(max(far - 1, 1), peers, *block),
            vm(peers, far, *kblock), vm(peers, far, *kblock), vm(max(near - 1, 1), far, *kblock[1:]),
            vm(max(far - 1, 1), *kblock[1:]), vm(peers - 1, far, *kblock), boxes(small), boxes(conv),
        ]
        + sems(copies, kept),
        compiler_params=remote_params(2, 40),
        cost_estimate=pl.CostEstimate(flops=0, bytes_accessed=250 * 10**6, transcendentals=0),
        name="scatter_all",
    )(grads, gw, branch, small, conv)


class Early:
    def __init__(self, b_ref, go_ref, refs):
        self.b_out, self.o_out, self.b_own, self.b_box, self.o_own, self.o_box, self.o_far, send, recv, local = refs
        me = self.me = Place()
        mover = self.mover = Mover(send, recv, local)
        bits = bits_of(me.peers)
        self.rows, self.outs, self.far = [], [], []
        for o in range(me.near):
            order = bits if o else bits[::-1]
            at_zl = b_ref.at[flip(me.zl, o)]
            for j, left in enumerate(combos(order[1:])):
                put = mover.plan(at_zl.at[flip(me.s, order[0] ^ left)], self.b_box.at[o, j], me.at(s=order[0]))
                self.rows.append((put, mover.plan_keep(at_zl.at[flip(me.s, left)], self.b_own.at[o, j]), (o, j)))
        for o in range(me.far):
            put = mover.plan(go_ref.at[flip(me.zh, o), 1 - me.c], self.o_box.at[o], me.at(c=1))
            self.outs.append((put, mover.plan_keep(go_ref.at[flip(me.zh, o), me.c], self.o_own.at[o])))
        for o in range(1, me.far):
            self.far.append(mover.plan(self.o_own.at[o], self.o_far.at[o - 1], me.at(zh=o)))

    def start(self):
        _, far, sibling = self.me.partners()
        bits = bits_of(self.me.peers)
        greet([self.me.at(s=bit) for bit in sorted({bits[0], bits[-1]})] + far + sibling)
        for put, load in self.outs:
            put.start()
            load.start()
        for put, load, _ in self.rows:
            put.start()
            load.start()

    def middle(self):
        for o, (put, load) in enumerate(self.outs):
            load.wait()
            put.wait_recv()
            if o:
                add_rows(self.o_own.at[o], [self.o_own.at[o], self.o_box.at[o]])
                self.far[o - 1].start()

    def end(self):
        for put, load, at in self.rows:
            load.wait()
            put.wait_recv()
            add_rows(self.b_out.at[at], [self.b_own.at[at], self.b_box.at[at]])
        for put in self.far:
            put.wait_recv()
        add_rows(self.o_out, [self.o_own.at[0], self.o_box.at[0]] + [self.o_far.at[o] for o in range(self.me.far - 1)])
        self.mover.close()


def body(
    inputs, cotangent, doc_lengths, head_width, pre_gain, in_weight, step_weight, conv_weight, conv_bias,
    step_bias, decay_log, skip_gain, norm_gain, out_weight,
):
    me = Place()
    peers, near, far = me.peers, me.near, me.far
    outer = far if near > 1 else 1
    tokens = inputs.shape[1]
    width = inputs.shape[2]
    span = tokens * peers
    length = span * near
    heads = H // (peers * near)
    inner = heads * P_SIZE
    rows = in_weight.shape[0]
    seq_rows = inputs[0].astype(f32)
    cot_rows = cotangent[0]

    def own(vector):
        part = vector.reshape(-1, peers, outer, near, vector.shape[-1] // (peers * outer * near))
        part = lax.dynamic_slice(part, (0, me.s, 0, me.zl, 0), (part.shape[0], 1, outer, 1, part.shape[4]))
        return part.reshape(vector.shape[:-1] + (-1,))

    def spread(part):
        lead = part.shape[:-1]
        part = part.reshape(-1, 1, outer, 1, part.shape[-1] // outer)
        full = jnp.zeros((part.shape[0], peers, outer, near, part.shape[-1]), part.dtype)
        return lax.dynamic_update_slice(full, part, (0, me.s, 0, me.zl, 0)).reshape(lead + (-1,))

    key_send = jnp.concatenate(
        [in_weight[:, 2 * E :], step_weight, jnp.zeros((rows, STEP_PAD - H), bf16)], axis=1
    )
    inv_rms = lax.rsqrt(jnp.mean(seq_rows * seq_rows, axis=1, keepdims=True) + epsilon)
    normed = (seq_rows * inv_rms * pre_gain[None, :]).astype(bf16)
    meta = jnp.pad(jnp.concatenate([doc_lengths[0], head_width])[None], ((0, 7), (0, 123)))
    in_w, out_w, normed, cot_all, meta = gather(in_weight, key_send, out_weight, normed, cot_rows, meta)
    in_w = in_w.reshape(width, -1)
    out_w = out_w.reshape(inner, width)
    normed = normed.reshape(length, width)
    cot_all = cot_all.reshape(length, width)
    meta = meta[:, 0, :8]

    head_ids = jnp.arange(H, dtype=f32)
    chan = own(
        jnp.concatenate(
            [
                conv_weight[:, :E],
                conv_bias[None, :E],
                norm_gain[None],
                jnp.repeat(skip_gain, P_SIZE)[None],
                jnp.repeat(head_ids, P_SIZE)[None],
            ],
            axis=0,
        )
    )
    conv_k = jnp.concatenate([conv_weight[:, E:], conv_bias[None, E:], jnp.zeros((3, KEYS), f32)], axis=0)
    head_vec = own(jnp.stack([step_bias, jnp.exp(decay_log), head_ids + 1.0]))
    head_vec = jnp.pad(head_vec, ((0, 5), (0, LANES - heads))) - jnp.where(jnp.arange(8) == 2, 1.0, 0.0)[:, None]

    projected = mm(normed, in_w, NN)
    grad_mixed = mm(cot_all, out_w, NT)
    mixer_args = (meta, projected, grad_mixed, chan, conv_k, head_vec)
    *kept, gated, states, part = mixer_forward(*mixer_args, span, heads)
    sums, mixed = cube_total(part, gated, chan)
    branch = mm(mixed, out_w, NN).astype(bf16)
    grad_out = mm(mixed, cot_all, TN).astype(bf16)
    grad_cols, chan_sums, key_sums, head_sums, branch, grad_out_weight = mixer_backward(
        *mixer_args, (*kept, states), sums, branch.reshape(near, peers, tokens, width),
        grad_out.reshape(far, 2, -1, width), span, heads,
    )
    grad_in = mm(normed, grad_cols, TN).astype(bf16)
    grad_normed = mm(grad_cols, in_w, NT)
    grad_pre_gain = jnp.sum(grad_normed * normed.astype(f32), axis=0) / pre_gain

    grad_skip = jnp.sum(chan_sums[6].reshape(heads, P_SIZE), axis=1)
    head_sums = spread(jnp.concatenate([head_sums[:2, :heads], grad_skip[None]], axis=0))
    chan_sums = spread(chan_sums[:6])
    small = jnp.concatenate([grad_pre_gain, chan_sums[5], head_sums.reshape(-1)])
    small = jnp.pad(small, (0, -small.shape[0] % 1024)).reshape(-1, 128)
    conv_sums = jnp.pad(jnp.concatenate([chan_sums[:5], key_sums[:5]], axis=1), ((0, 3), (0, 0)))
    grad_normed, grad_in, branch, grad_keys, small, conv_sums = scatter(
        grad_normed.astype(bf16).reshape(near, peers, tokens, width),
        grad_in.reshape(peers, far, near, 2, rows, -1),
        branch,
        small,
        conv_sums,
    )
    output = (seq_rows + branch).astype(bf16)[None]
    scaled_in = grad_normed * pre_gain[None, :]
    dot = jnp.mean(scaled_in * seq_rows, axis=1, keepdims=True)
    grad_seq = inv_rms * scaled_in - seq_rows * (inv_rms * inv_rms * inv_rms * dot)
    grad_inputs = (grad_seq + cot_rows.astype(f32))[None]
    grad_in_weight = jnp.concatenate([grad_in.astype(f32), grad_keys[:, :KEYS]], axis=1)
    grad_step_weight = grad_keys[:, KEYS : KEYS + H]
    small = small.reshape(-1)
    parts = []
    for size in (width, E, H, H, H):
        parts.append(small[:size])
        small = small[size:]
    return (
        output, grad_inputs, parts[0], grad_in_weight, grad_step_weight, conv_sums[:CONV], conv_sums[CONV],
        parts[2], parts[3], parts[4], parts[1], grad_out_weight,
    )


def solution(mesh):
    both = P(("seq", "batch"), None)
    tok = P("batch", "seq", None)
    in_specs = (
        tok, tok, P("batch", None), P("batch"), P(), both, both, P(), P(), P(), P(), P(), P(), both,
    )
    out_specs = (tok, tok, P(), both, both, P(), P(), P(), P(), P(), P(), both)
    return jax.shard_map(body, mesh=mesh, in_specs=in_specs, out_specs=out_specs, check_vma=False)
```

```python
from functools import partial

import jax
import jax.numpy as jnp
from jax import lax
from jax.experimental import pallas as pl
from jax.experimental.pallas import tpu as pltpu
from jax.sharding import PartitionSpec as P

H = 64
P_SIZE = 64
N = 128
CONV = 4
DOCS = 4
E = 4096
KEYS = 2 * N
STEP_PAD = 128
CHUNK = 128
LANES = 128
epsilon = 1e-05
f32 = jnp.float32
bf16 = jnp.bfloat16


def mm(a, b, dims, precision=None):
    return lax.dot_general(a, b, (dims, ((), ())), precision=precision, preferred_element_type=f32)


NN = ((1,), (0,))
NT = ((1,), (1,))
TN = ((0,), (0,))
exact = lax.Precision.HIGHEST


def pair_cols(low, col, first):
    return jnp.where(low, col[:, first : first + 1], col[:, first + 1 : first + 2])


def iota(shape, axis):
    return lax.broadcasted_iota(jnp.int32, shape, axis)


class Docs:
    def __init__(self, meta_ref, chunk, span):
        per = span // CHUNK
        seq = chunk // per
        self.start = (chunk - seq * per) * CHUNK
        self.ends = []
        total = 0
        for i in range(DOCS - 1):
            total = total + meta_ref[seq, i]
            self.ends.append(total)
        self.count = meta_ref[seq, DOCS]
        self.pos = self.start + iota((CHUNK, 1), 0)
        self.doc = self.index(self.pos)

    def index(self, places):
        found = (places >= self.ends[0]).astype(jnp.int32)
        for end in self.ends[1:]:
            found = found + (places >= end).astype(jnp.int32)
        return found

    def lag(self, by):
        source = self.pos - by
        return ((source >= 0) & (self.index(source) == self.doc)).astype(f32)

    def flow(self):
        return ((self.start > 0) & (self.index(self.start - 1) == self.doc)).astype(f32)

    def row(self):
        return self.index(self.start + iota((1, CHUNK), 1))

    def tail(self):
        return (self.doc == self.index(self.start + CHUNK - 1)).astype(f32)


def shift_down(rows, before, by):
    if by == 0:
        return rows
    moved = pltpu.roll(rows, by, 0)
    top = jnp.where(iota((8, 1), 0) < by, pltpu.roll(before, by, 0), moved[:8])
    return jnp.concatenate([top, moved[8:]], axis=0)


def shift_up(rows, after, by):
    if by == 0:
        return rows
    size = rows.shape[0]
    moved = pltpu.roll(rows, size - by, 0)
    end = jnp.where(iota((8, 1), 0) >= 8 - by, pltpu.roll(after, 8 - by, 0), moved[size - 8 :])
    return jnp.concatenate([moved[: size - 8], end], axis=0)


def silu_slope(v, sig):
    return sig * (1.0 + v * (1.0 - sig))


def own_parameters(chan_ref, head_ref, conv_ref, bias_ref, norm_ref, step_b_ref, decay_ref, skip_ref, heads):
    me = Place()
    inner = heads * P_SIZE
    for whole, part in me.channel_runs(inner):
        chan_ref[:CONV, part] = conv_ref[:, whole]
        chan_ref[CONV : CONV + 1, part] = bias_ref[:, whole]
        chan_ref[5:6, part] = norm_ref[:, whole]
    ids = me.heads_at(iota((1, inner), 1), P_SIZE, inner)
    chosen = (iota((H, inner), 0) == ids).astype(f32)
    chan_ref[6:7, :] = mm(jnp.broadcast_to(skip_ref[...], (8, H)), chosen, NN, exact)[:1]
    chan_ref[7:8, :] = ids.astype(f32)
    lanes = iota((1, LANES), 1)
    ids = jnp.where(lanes < heads, me.heads_at(lanes, 1, heads), -1)
    chosen = (iota((H, LANES), 0) == ids).astype(f32)
    head_ref[...] = jnp.zeros_like(head_ref)
    head_ref[:1, :] = mm(jnp.broadcast_to(step_b_ref[...], (8, H)), chosen, NN, exact)[:1]
    head_ref[1:2, :] = mm(jnp.broadcast_to(jnp.exp(decay_ref[...]), (8, H)), chosen, NN, exact)[:1]
    head_ref[2:3, :] = ids.astype(f32)


def whole_sums(out_ref, chan_sums, key_sums, head_sums, head_ref, chan_ref, heads):
    me = Place()
    inner = heads * P_SIZE
    out_ref[...] = jnp.zeros_like(out_ref)
    for whole, part in me.channel_runs(inner):
        out_ref[:6, whole] = chan_sums[:6, part]
    out_ref[:5, E:] = key_sums[:5, :]
    chosen = (iota((H, LANES), 0) == head_ref[2:3, :].astype(jnp.int32)).astype(f32)
    steps = mm(head_sums[...], chosen, NT, exact)
    chosen = (iota((H, inner), 0) == chan_ref[7:8, :].astype(jnp.int32)).astype(f32)
    skips = mm(chan_sums[...], chosen, NT, exact)
    out_ref[7:8, :H] = steps[:1]
    out_ref[7:8, LANES : LANES + H] = steps[1:2]
    out_ref[7:8, 2 * LANES : 2 * LANES + H] = skips[6:7]


def forward_kernel(
    meta_ref, proj_ref, grad_ref, conv_ref, bias_ref, norm_ref, step_b_ref, decay_ref, skip_ref,
    val_out, key_out, vsum_ref, ksum_ref, raw_ref, cum_ref, y_ref, gated_ref, state_ref, sums_ref, chan_ref, head_ref,
    state, last_v, last_k,
    *, span, heads,
):
    i = pl.program_id(0)
    chunks = pl.num_programs(0)
    inner = heads * P_SIZE

    @pl.when(i == 0)
    def _():
        own_parameters(chan_ref, head_ref, conv_ref, bias_ref, norm_ref, step_b_ref, decay_ref, skip_ref, heads)
        state[...] = jnp.zeros_like(state)
        last_v[...] = jnp.zeros_like(last_v)
        last_k[...] = jnp.zeros_like(last_k)

    docs = Docs(meta_ref, i, span)
    lags = [docs.lag(by) for by in range(1, CONV)]

    def convolve(rows, before, weight, bias):
        total = bias + weight[CONV - 1 :] * rows
        for by in range(1, CONV):
            at = CONV - 1 - by
            total = total + weight[at : at + 1] * (shift_down(rows, before, by) * lags[by - 1])
        return total

    rows_v = proj_ref[:, inner : 2 * inner].astype(bf16).astype(f32)
    vsum = convolve(rows_v, last_v[...], chan_ref[:CONV, :], chan_ref[CONV : CONV + 1, :])
    last_v[...] = rows_v[CHUNK - 8 :]
    vsum_ref[...] = vsum
    val_out[...] = (vsum * jax.nn.sigmoid(vsum)).astype(bf16)
    rows_k = proj_ref[:, 2 * inner : 2 * inner + KEYS].astype(bf16).astype(f32)
    ksum = convolve(rows_k, last_k[...], conv_ref[:, E:], bias_ref[:, E:])
    last_k[...] = rows_k[CHUNK - 8 :]
    ksum_ref[...] = ksum
    keys = (ksum * jax.nn.sigmoid(ksum)).astype(bf16)
    key_out[...] = keys

    rows = iota((CHUNK, CHUNK), 0)
    cols = iota((CHUNK, CHUNK), 1)
    chosen = (rows == head_ref[2:3, :].astype(jnp.int32)).astype(f32)
    raw = mm(proj_ref[:, 2 * inner + KEYS :], chosen, NN, exact) + head_ref[:1, :]
    raw_ref[...] = raw
    dt = jax.nn.softplus(raw)
    cum = mm((rows >= cols).astype(f32), -dt * head_ref[1:2, :], NN, exact)
    cum_ref[...] = cum
    cum_t = cum.T
    dt_t = dt.T

    state_ref[0] = state[...].astype(bf16)
    bias = jnp.where((docs.doc == docs.row()) & (rows >= cols), 0.0, -1e30)
    carry_w = docs.flow() * jnp.exp(cum)
    final_w = docs.tail() * jnp.exp(cum[CHUNK - 1 :, :] - cum) * dt
    gain = carry_w[CHUNK - 1 :, :]
    low = cols < P_SIZE
    low_row = low[:1]
    write = keys[:, :N]
    read = keys[:, N:]
    write_t = write.astype(f32).T.astype(bf16)
    scores = mm(read, write, NT)
    square = jnp.zeros((CHUNK, LANES), f32)
    cross = jnp.zeros((CHUNK, LANES), f32)
    count = docs.count.astype(f32)
    for pair in range(heads // 2):
        first = 2 * pair
        lanes = slice(pair * 128, pair * 128 + 128)
        xf = val_out[:, lanes].astype(f32)
        weights = []
        for h in (first, first + 1):
            decay = jnp.exp(cum[:, h : h + 1] - cum_t[h : h + 1, :] + bias)
            weights.append((decay * scores * dt_t[h : h + 1, :]).astype(bf16))
        stacked = jnp.concatenate(
            [jnp.where(low, xf, 0.0).astype(bf16), jnp.where(low, 0.0, xf).astype(bf16)], axis=0
        )
        old = state[:, lanes]
        y = mm(jnp.concatenate(weights, axis=1), stacked, NN)
        y = y + pair_cols(low, carry_w, first) * mm(read, old.astype(bf16), NN)
        y = y + chan_ref[6:7, lanes] * xf
        y = jnp.where(chan_ref[7:8, lanes] < count, y, 0.0)
        y_ref[:, lanes] = y
        state[:, lanes] = pair_cols(low_row, gain, first) * old + mm(
            write_t, (pair_cols(low, final_w, first) * xf).astype(bf16), NN
        )
        gate = proj_ref[:, lanes]
        gated = y * (gate * jax.nn.sigmoid(gate))
        gated_ref[:, lanes] = gated
        square = square + gated * gated
        cross = cross + gated * (grad_ref[:, lanes] * chan_ref[5:6, lanes])
    share = 1.0 / (count * P_SIZE)
    sums_ref[pl.ds(i, 1), :] = jnp.sum(square.T, axis=0, keepdims=True) * share
    sums_ref[pl.ds(chunks + i, 1), :] = jnp.sum(cross.T, axis=0, keepdims=True) * share


def backward_kernel(
    meta_ref, proj_ref, grad_ref, chan_ref, conv_ref, head_ref,
    val_ref, key_ref, vsum_ref, ksum_ref, raw_ref, cum_ref, y_ref, state_ref, sums_ref, branch_ref, go_ref,
    cols_ref, all_sums, b_out, o_out,
    chan_sums, key_sums, head_sums, dstate, dv, next_v, next_k, next_lags, *early_refs,
    span, heads,
):
    chunks = pl.num_programs(0)
    i = chunks - 1 - pl.program_id(0)
    inner = heads * P_SIZE
    early = Early(branch_ref, go_ref, (b_out, o_out) + early_refs)

    @pl.when(pl.program_id(0) == 0)
    def _():
        early.start()
        for ref in (dstate, next_v, next_k, next_lags, chan_sums, key_sums, head_sums):
            ref[...] = jnp.zeros_like(ref)

    docs = Docs(meta_ref, i, span)
    rows = iota((CHUNK, CHUNK), 0)
    cols = iota((CHUNK, CHUNK), 1)
    raw = raw_ref[...]
    dt = jax.nn.softplus(raw)
    cum = cum_ref[...]
    cum_t = cum.T
    count = docs.count.astype(f32)

    def column(row):
        return jnp.broadcast_to(row, (CHUNK, CHUNK)).T

    inv = lax.rsqrt(column(sums_ref[pl.ds(i, 1), :]) + epsilon)
    pull = inv * inv * inv * column(sums_ref[pl.ds(chunks + i, 1), :])

    bias = jnp.where((docs.doc == docs.row()) & (cols >= rows), 0.0, -1e30)
    carry_w = docs.flow() * jnp.exp(cum)
    final_d = docs.tail() * jnp.exp(cum[CHUNK - 1 :, :] - cum)
    final_w = final_d * dt
    gain = carry_w[CHUNK - 1 :, :]
    low = cols < P_SIZE
    low_row = low[:1]
    write = key_ref[:, :N]
    read = key_ref[:, N:]
    read_t = read.astype(f32).T.astype(bf16)
    scores_t = mm(write, read, NT)
    dscores_t = jnp.zeros((CHUNK, CHUNK), f32)
    dwrite = jnp.zeros((CHUNK, N), f32)
    dread = jnp.zeros((CHUNK, N), f32)
    end_row = iota((CHUNK, 1), 0) == CHUNK - 1
    dcum = jnp.zeros((CHUNK, LANES), f32)
    ddt = jnp.zeros((CHUNK, LANES), f32)
    dcum_rows = []
    for pair in range(heads // 2):
        first = 2 * pair
        lanes = slice(pair * 128, pair * 128 + 128)
        gate = proj_ref[:, lanes]
        sig = jax.nn.sigmoid(gate)
        silu = gate * sig
        masked = y_ref[:, lanes]
        gated = masked * silu
        norm_gain = chan_ref[5:6, lanes]
        gm = grad_ref[:, lanes]
        unit = gated * inv
        chan_sums[5:6, lanes] += jnp.sum(gm * unit, axis=0, keepdims=True)
        grad_gated = inv * (gm * norm_gain) - pull * gated
        cols_ref[:, lanes] = (grad_gated * masked * silu_slope(gate, sig)).astype(bf16)
        dy = jnp.where(chan_ref[7:8, lanes] < count, grad_gated * silu, 0.0)
        xf = val_ref[:, lanes].astype(f32)
        dyb = dy.astype(bf16)
        x_stack = jnp.concatenate(
            [jnp.where(low, xf, 0.0).astype(bf16), jnp.where(low, 0.0, xf).astype(bf16)], axis=0
        )
        dy_stack = jnp.concatenate(
            [jnp.where(low, dy, 0.0).astype(bf16), jnp.where(low, 0.0, dy).astype(bf16)], axis=0
        )
        dweights = mm(x_stack, dyb, NT)
        old = state_ref[0, :, lanes]
        grad = dstate[:, lanes]
        gradb = grad.astype(bf16)
        carried = mm(read, old, NN)
        pushed = mm(write, gradb, NN)
        carry_p = pair_cols(low, carry_w, first)
        final_p = pair_cols(low, final_w, first)
        carry_prod = dy * carried
        final_prod = xf * pushed
        gain_prod = jnp.sum(grad * old.astype(f32), axis=0, keepdims=True)
        weights = []
        for which, h in enumerate((first, first + 1)):
            col = dt[:, h : h + 1]
            decay = jnp.exp(cum_t[h : h + 1, :] - cum[:, h : h + 1] + bias)
            weighted = decay * col
            weights.append((weighted * scores_t).astype(bf16))
            dw = dweights[which * CHUNK : (which + 1) * CHUNK]
            dscores_t = dscores_t + dw * weighted
            direct = dw * decay * scores_t
            ddt_in = jnp.sum(direct, axis=1, keepdims=True)
            dcum_rows.append(jnp.sum(direct * col, axis=0, keepdims=True))
            half = low if which == 0 else ~low
            half_row = low_row if which == 0 else ~low_row
            carry_sum = jnp.sum(jnp.where(half, carry_prod, 0.0), axis=1, keepdims=True)
            final_sum = jnp.sum(jnp.where(half, final_prod, 0.0), axis=1, keepdims=True)
            push = final_w[:, h : h + 1] * final_sum
            at_end = jnp.sum(push, axis=0, keepdims=True) + gain[:, h : h + 1] * jnp.sum(
                jnp.where(half_row, gain_prod, 0.0), axis=1, keepdims=True
            )
            here = cols == h
            ddt = jnp.where(here, ddt_in + final_d[:, h : h + 1] * final_sum, ddt)
            dcum = jnp.where(
                here,
                carry_w[:, h : h + 1] * carry_sum - push - col * ddt_in + jnp.where(end_row, at_end, 0.0),
                dcum,
            )
        dx = mm(jnp.concatenate(weights, axis=1), dy_stack, NN)
        dv[:, lanes] = dx + final_p * pushed + chan_ref[6:7, lanes] * dy
        chan_sums[6:7, lanes] += jnp.sum(dy * xf, axis=0, keepdims=True)
        dwrite = dwrite + mm((final_p * xf).astype(bf16), gradb, NT)
        carry_dy = (carry_p * dy).astype(bf16)
        dread = dread + mm(carry_dy, old, NT)
        dstate[:, lanes] = pair_cols(low_row, gain, first) * grad + mm(read_t, carry_dy, NN)
    dsb = dscores_t.astype(bf16)
    dkeys = jnp.concatenate([dwrite + mm(dsb, read, NN), dread + mm(dsb, write, TN)], axis=1)

    extra = jnp.concatenate(dcum_rows + [jnp.zeros((LANES - heads, CHUNK), f32)], axis=0)
    dlog = mm((cols >= rows).astype(f32), dcum + extra.T, NN, exact)
    rate = head_ref[1:2, :]
    grad_step = (ddt - rate * dlog) * jax.nn.sigmoid(raw)
    head_sums[:1, :] += jnp.sum(grad_step, axis=0, keepdims=True)
    head_sums[1:2, :] -= jnp.sum(dt * rate * dlog, axis=0, keepdims=True)
    chosen = (rows == head_ref[2:3, :].astype(jnp.int32)).astype(bf16)
    cols_ref[:, 2 * inner + KEYS :] = mm(grad_step.astype(bf16), chosen, NT).astype(bf16)

    lags = [docs.lag(by) for by in range(1, CONV)]

    def convolve_back(dact, total, rows_in, after, weight, sums):
        dconv = dact * silu_slope(total, jax.nn.sigmoid(total))
        grad_in = weight[CONV - 1 :] * dconv
        sums[CONV : CONV + 1, :] += jnp.sum(dconv, axis=0, keepdims=True)
        sums[CONV - 1 : CONV, :] += jnp.sum(dconv * rows_in, axis=0, keepdims=True)
        for by in range(1, CONV):
            at = CONV - 1 - by
            moved = shift_up(dconv * lags[by - 1], after[...] * next_lags[:, by - 1 : by], by)
            grad_in = grad_in + weight[at : at + 1] * moved
            sums[at : at + 1, :] += jnp.sum(moved * rows_in, axis=0, keepdims=True)
        after[...] = dconv[:8]
        return grad_in.astype(bf16)

    rows_v = proj_ref[:, inner : 2 * inner].astype(bf16).astype(f32)
    cols_ref[:, inner : 2 * inner] = convolve_back(dv[...], vsum_ref[...], rows_v, next_v, chan_ref[:CONV, :], chan_sums)
    rows_k = proj_ref[:, 2 * inner : 2 * inner + KEYS].astype(bf16).astype(f32)
    cols_ref[:, 2 * inner : 2 * inner + KEYS] = convolve_back(
        dkeys, ksum_ref[...], rows_k, next_k, conv_ref[:, E:], key_sums
    )
    for by in range(1, CONV):
        next_lags[:, by - 1 : by] = lags[by - 1][:8]

    @pl.when(pl.program_id(0) == 0)
    def _():
        early.middle()

    @pl.when(pl.program_id(0) == chunks - 1)
    def _():
        whole_sums(all_sums, chan_sums, key_sums, head_sums, head_ref, chan_ref, heads)
        early.end()


def mixer_forward(meta, projected, grad_mixed, params, span, heads):
    length = projected.shape[0]
    inner = heads * P_SIZE
    chunks = length // CHUNK
    row = lambda width: pl.BlockSpec((CHUNK, width), lambda i: (i, 0))
    all_of = lambda *shape: pl.BlockSpec(shape, lambda i: (0,) * len(shape))
    out = lambda width, dtype: jax.ShapeDtypeStruct((length, width), dtype)
    return pl.pallas_call(
        partial(forward_kernel, span=span, heads=heads),
        grid=(chunks,),
        in_specs=[
            pl.BlockSpec(memory_space=pltpu.SMEM), row(2 * inner + KEYS + STEP_PAD), row(inner),
        ]
        + [all_of(*part.shape) for part in params],
        out_specs=[
            row(inner), row(KEYS), row(inner), row(KEYS), row(LANES), row(LANES), row(inner), row(inner),
            pl.BlockSpec((1, N, inner), lambda i: (i, 0, 0)), all_of(2 * chunks, LANES),
            all_of(8, inner), all_of(8, LANES),
        ],
        out_shape=[
            out(inner, bf16), out(KEYS, bf16), out(inner, f32), out(KEYS, f32), out(LANES, f32), out(LANES, f32),
            out(inner, f32), out(inner, f32), jax.ShapeDtypeStruct((chunks, N, inner), bf16),
            jax.ShapeDtypeStruct((2 * chunks, LANES), f32), jax.ShapeDtypeStruct((8, inner), f32),
            jax.ShapeDtypeStruct((8, LANES), f32),
        ],
        scratch_shapes=[pltpu.VMEM((N, inner), f32), pltpu.VMEM((8, inner), f32), pltpu.VMEM((8, KEYS), f32)],
        compiler_params=pltpu.CompilerParams(vmem_limit_bytes=16 * 2**20),
        cost_estimate=pl.CostEstimate(
            flops=length * inner * 1024, bytes_accessed=length * inner * 24, transcendentals=length * heads * CHUNK
        ),
        name="mixer_forward",
    )(meta, projected, grad_mixed, *params)


def mixer_backward(meta, projected, grad_mixed, chan, conv, head_vec, kept, sums, branch, grad_out, span, heads):
    length = projected.shape[0]
    inner = heads * P_SIZE
    chunks = length // CHUNK
    me = Place()
    near, peers, tokens, width = branch.shape
    far = me.far
    part = grad_out.shape[2:]
    copies = near * peers // 2 + 2 * far - 1
    vm = lambda *shape: pltpu.VMEM(shape, bf16)
    row = lambda width: pl.BlockSpec((CHUNK, width), lambda i: (chunks - 1 - i, 0))
    all_of = lambda *shape: pl.BlockSpec(shape, lambda i: (0,) * len(shape))
    out = lambda width: jax.ShapeDtypeStruct((length, width), bf16)
    return pl.pallas_call(
        partial(backward_kernel, span=span, heads=heads),
        grid=(chunks,),
        in_specs=[
            pl.BlockSpec(memory_space=pltpu.SMEM), row(2 * inner + KEYS + STEP_PAD), row(inner),
            all_of(8, inner), all_of(*conv.shape), all_of(8, LANES),
            row(inner), row(KEYS), row(inner), row(KEYS), row(LANES), row(LANES), row(inner),
            pl.BlockSpec((1, N, inner), lambda i: (chunks - 1 - i, 0, 0)), all_of(2 * chunks, LANES), HBM, HBM,
        ],
        out_specs=[
            row(2 * inner + KEYS + STEP_PAD), all_of(8, conv.shape[1]), VMEM, VMEM,
        ],
        out_shape=[
            out(2 * inner + KEYS + STEP_PAD), jax.ShapeDtypeStruct((8, conv.shape[1]), f32),
            jax.ShapeDtypeStruct((near, peers // 2, tokens, width), bf16), jax.ShapeDtypeStruct(part, f32),
        ],
        scratch_shapes=[
            pltpu.VMEM((8, inner), f32), pltpu.VMEM((8, KEYS), f32), pltpu.VMEM((8, LANES), f32),
            pltpu.VMEM((N, inner), f32), pltpu.VMEM((CHUNK, inner), f32), pltpu.VMEM((8, inner), f32),
            pltpu.VMEM((8, KEYS), f32), pltpu.VMEM((8, LANES), f32),
            vm(near, peers // 2, tokens, width), vm(near, peers // 2, tokens, width),
            vm(far, *part), vm(far, *part), vm(max(far - 1, 1), *part),
        ]
        + sems(copies, near * peers // 2 + far),
        compiler_params=remote_params(3, 32),
        cost_estimate=pl.CostEstimate(
            flops=length * inner * 3072, bytes_accessed=length * inner * 30, transcendentals=length * heads * CHUNK
        ),
        name="mixer_backward",
    )(meta, projected, grad_mixed, chan, conv, head_vec, *kept, sums, branch, grad_out)


MESH = pl.DeviceIdType.MESH
HBM = pl.BlockSpec(memory_space=pl.ANY)
VMEM = pl.BlockSpec(memory_space=pltpu.VMEM)


def z_pair(peers, groups):
    planes = groups // 2
    return 2 if planes % 2 == 0 and (E // (peers * planes)) % (2 * P_SIZE) == 0 else 1


def flip(value, bits):
    bit = 1
    while bit <= bits:
        if bits & bit:
            value = value + bit - 2 * bit * (value // bit % 2)
        bit *= 2
    return value


class Place:
    def __init__(self):
        self.peers = lax.axis_size("seq")
        groups = lax.axis_size("batch")
        self.near = z_pair(self.peers, groups)
        self.far = groups // 2 // self.near
        self.s = lax.axis_index("seq")
        b = lax.axis_index("batch")
        self.c = b % 2
        self.zl = b // 2 % self.near
        self.zh = b // 2 // self.near

    def at(self, s=0, zl=0, zh=0, c=0):
        return (flip(self.s, s), (flip(self.zh, zh) * self.near + flip(self.zl, zl)) * 2 + flip(self.c, c))

    def heads_at(self, index, per, width):
        outer = self.far if self.near > 1 else 1
        run = width // outer
        return (((self.s * outer + index // run) * self.near + self.zl) * run + index % run) // per

    def channel_runs(self, width):
        outer = self.far if self.near > 1 else 1
        run = width // outer
        runs = []
        for i in range(outer):
            first = ((self.s * outer + i) * self.near + self.zl) * run
            runs.append((pl.ds(pl.multiple_of(first, 128), run), slice(i * run, (i + 1) * run)))
        return runs

    def column_runs(self, s, zl, width):
        outer = self.far if self.near > 1 else 1
        run = width // (2 * outer)
        runs = []
        for part in range(2):
            for i in range(outer):
                first = part * E + ((s * outer + i) * self.near + zl) * run
                runs.append((pl.ds(pl.multiple_of(first, 128), run), pl.ds((part * outer + i) * run, run)))
        return runs

    def partners(self):
        cube = [self.at(s=o // self.near, zl=o % self.near) for o in range(1, self.peers * self.near)]
        return cube, [self.at(zh=o) for o in range(1, self.far)], [self.at(c=1)]


def greet(devices):
    barrier = pltpu.get_barrier_semaphore()
    for device in devices:
        pl.semaphore_signal(barrier, inc=1, device_id=device, device_id_type=MESH)
    pl.semaphore_wait(barrier, len(devices))


class Mover:
    def __init__(self, send, recv, local):
        self.send, self.recv, self.local = send, recv, local
        self.sent, self.kept = 0, 0
        self.open = []

    def plan(self, src, dst, device):
        copy = pltpu.make_async_remote_copy(
            src_ref=src, dst_ref=dst, send_sem=self.send.at[self.sent], recv_sem=self.recv.at[self.sent],
            device_id=device, device_id_type=MESH,
        )
        self.sent += 1
        self.open.append(copy)
        return copy

    def put(self, src, dst, device):
        copy = self.plan(src, dst, device)
        copy.start()
        return copy

    def plan_keep(self, src, dst):
        self.kept += 1
        return pltpu.make_async_copy(src, dst, self.local.at[self.kept - 1])

    def keep(self, src, dst):
        copy = self.plan_keep(src, dst)
        copy.start()
        return copy

    def close(self):
        for copy in self.open:
            copy.wait_send()


def run_paths(paths):
    paths = list(paths)
    while paths:
        alive = []
        for path in paths:
            try:
                next(path)
                alive.append(path)
            except StopIteration:
                pass
        paths = alive


def turn(paths):
    for path in paths:
        next(path, None)


def bits_of(peers):
    return [1 << i for i in range(peers.bit_length() - 1)]


def combos(bits):
    out = [0]
    for bit in reversed(bits):
        out = [bit | o for o in out] + out
    return out


def gather_kernel(
    in_ref, steps_ref, out_ref, rows_ref, cot_ref, meta_ref,
    w_ref, o_ref, x_ref, ct_ref, m_ref, send, recv, local,
):
    me = Place()
    s, zl, zh, c = me.s, me.zl, me.zh, me.c
    columns = w_ref.shape[-1] - KEYS - STEP_PAD
    mine, shared = pl.ds(0, columns), pl.ds(columns, KEYS + STEP_PAD)
    cube, far, sibling = me.partners()
    greet(cube + far + sibling)
    mover = Mover(send, recv, local)
    bits = bits_of(me.peers)

    def plane_path(src, dst, order, near):
        view = dst.at[flip(zl, near)]
        if near:
            copy = mover.put(src, dst.at[zl, s], me.at(zl=near))
            yield
            copy.wait_recv()
        else:
            own = mover.keep(src, view.at[s])
        held = [0]
        for bit in order:
            copies = []
            for h in held:
                at = view.at[flip(s, h)]
                copies.append(mover.put(at if near or h else src, at if near else dst.at[zl, flip(s, h)], me.at(s=bit)))
            held = held + [h ^ bit for h in held]
            yield
            for copy in copies:
                copy.wait_recv()
        if not near:
            own.wait()

    def meta_path():
        own = mover.keep(meta_ref, m_ref.at[zl])
        near = [mover.put(meta_ref, m_ref.at[zl], me.at(zl=o)) for o in range(1, me.near)]
        yield
        own.wait()
        for copy in near:
            copy.wait_recv()

    def key_path():
        block = w_ref.at[s, zh, zl, c]
        parts = [
            (in_ref.at[:, pl.ds(2 * E, KEYS)], block.at[:, pl.ds(columns, KEYS)]),
            (steps_ref, block.at[:, pl.ds(columns + KEYS, STEP_PAD)]),
        ]
        own = [mover.keep(*part) for part in parts]
        copies = [mover.put(*part, me.at(zh=o)) for o in range(1, me.far) for part in parts]
        yield
        for copy in own:
            copy.wait()
        for copy in copies:
            copy.wait_recv()
        block = w_ref.at[s, :, zl, c, :, shared]
        copies = [mover.put(block, block, me.at(zl=o)) for o in range(1, me.near)]
        yield
        for copy in copies:
            copy.wait_recv()
        held = [0]
        for bit in bits:
            copies = []
            for h in held:
                block = w_ref.at[flip(s, h), :, :, c, :, shared]
                copies.append(mover.put(block, block, me.at(s=bit)))
            held = held + [h ^ bit for h in held]
            yield
            for copy in copies:
                copy.wait_recv()
        block = w_ref.at[:, :, :, c, :, shared]
        copy = mover.put(block, block, me.at(c=1))
        yield
        copy.wait_recv()

    def spread_path(copies, view):
        last = []
        for o, copy in copies:
            yield
            copy.wait_recv()
            last.append(mover.put(view(flip(zh, o)), view(flip(zh, o)), me.at(c=1)))
        return last

    def out_path():
        own = mover.keep(out_ref, o_ref.at[zh, c])
        copies = [(o, mover.put(out_ref, o_ref.at[zh, c], me.at(zh=o))) for o in range(1, me.far)]
        first = mover.put(out_ref, o_ref.at[zh, c], me.at(c=1))
        last = yield from spread_path(copies, lambda h: o_ref.at[h, c])
        yield
        own.wait()
        for copy in last + [first]:
            copy.wait_recv()

    def weight_path():
        moves = {}
        for step in range(me.peers):
            for o in range(me.near):
                to_s, to_zl = flip(s, step), flip(zl, o)
                for src, dst in me.column_runs(to_s, to_zl, columns):
                    src = in_ref.at[:, src]
                    dst = w_ref.at[s, zh, zl, c, :, dst]
                    if step or o:
                        copy = mover.put(src, dst, me.at(s=step, zl=o))
                    else:
                        copy = mover.keep(src, dst)
                    moves.setdefault(step, []).append(copy)
        pieces = []
        for step in range(me.peers):
            yield
            for i, copy in enumerate(moves[step]):
                if step == 0 and i < len(moves[0]) // me.near:
                    copy.wait()
                else:
                    copy.wait_recv()
            block = w_ref.at[flip(s, step), zh, :, c, :, mine]
            copies = [(o, mover.put(block, block, me.at(zh=o))) for o in range(1, me.far)]
            pieces.append((step, copies, mover.put(block, block, me.at(c=1))))
        last = []
        for step, copies, first in pieces:
            last.append(first)
            last += yield from spread_path(copies, lambda h, step=step: w_ref.at[flip(s, step), h, :, c, :, mine])
        yield
        for copy in last:
            copy.wait_recv()

    own_x = plane_path(rows_ref, x_ref, bits, 0)
    own_c = plane_path(cot_ref, ct_ref, bits[::-1], 0)
    near_x = [plane_path(rows_ref, x_ref, bits, o) for o in range(1, me.near)]
    near_c = [plane_path(cot_ref, ct_ref, bits[::-1], o) for o in range(1, me.near)]
    near = near_x + near_c
    keys, weights, outs = key_path(), weight_path(), out_path()
    turn([own_x, own_c, weights] + near + [keys, outs])
    extra = meta_path()
    turn([extra, own_x, own_c] + [weights] * me.peers + [keys] + near + [keys])
    turn([own_x, own_c] + near + [keys, outs, weights, keys, weights])
    run_paths([weights, extra, keys, outs, own_x, own_c] + near)
    mover.close()


def remote_params(identity, mib):
    return pltpu.CompilerParams(collective_id=identity, has_side_effects=True, vmem_limit_bytes=mib * 2**20)


def sems(copies, kept):
    return [pltpu.SemaphoreType.DMA((copies,)), pltpu.SemaphoreType.DMA((copies,)), pltpu.SemaphoreType.DMA((kept,))]


def gather(in_w, steps, out_w, rows, cot, meta):
    me = Place()
    peers, near, far = me.peers, me.near, me.far
    shape = lambda lead, part: jax.ShapeDtypeStruct(lead + part, bf16)
    columns = 2 * E // (peers * near)
    runs = 2 * (far if near > 1 else 1)
    copies = runs * (peers * near - 1) + (peers + 1) * (2 * far - 1) + 2 * (near * peers - 1)
    copies += 2 * near + peers + 2 * far - 4
    return pl.pallas_call(
        gather_kernel,
        out_shape=[
            shape((peers, far, near, 2), (in_w.shape[0], columns + KEYS + STEP_PAD)),
            shape((far, 2), out_w.shape),
            shape((near, peers), rows.shape),
            shape((near, peers), cot.shape),
            jax.ShapeDtypeStruct((near,) + meta.shape, meta.dtype),
        ],
        in_specs=[HBM] * 6,
        out_specs=[HBM] * 5,
        scratch_shapes=sems(copies, runs + 6),
        compiler_params=remote_params(0, 58),
        name="gather_all",
    )(in_w, steps, out_w, rows, cot, meta)


def total_kernel(part_ref, gated_ref, chan_ref, sum_ref, mixed_ref, box, send, recv, local):
    me = Place()
    cube = me.partners()[0]
    greet(cube)
    mover = Mover(send, recv, local)
    copies = [mover.put(part_ref, box.at[i], device) for i, device in enumerate(cube)]
    total = part_ref[...]
    for i, copy in enumerate(copies):
        copy.wait_recv()
        total = total + box[i]
    sum_ref[...] = total
    chunks = part_ref.shape[0] // 2

    def step(i, carry):
        at = pl.ds(pl.multiple_of(i * CHUNK, CHUNK), CHUNK)
        inv = lax.rsqrt(jnp.broadcast_to(sum_ref[pl.ds(i, 1), :], (CHUNK, CHUNK)).T + epsilon)
        for lane in range(0, gated_ref.shape[1], LANES):
            lanes = slice(lane, lane + LANES)
            mixed_ref[at, lanes] = (gated_ref[at, lanes] * inv * chan_ref[5:6, lanes]).astype(bf16)
        return carry

    lax.fori_loop(0, chunks, step, 0)
    mover.close()


def cube_total(part, gated, chan):
    me = Place()
    count = me.peers * me.near - 1
    return pl.pallas_call(
        total_kernel,
        out_shape=[jax.ShapeDtypeStruct(part.shape, f32), jax.ShapeDtypeStruct(gated.shape, bf16)],
        in_specs=[VMEM] * 3,
        out_specs=[VMEM] * 2,
        scratch_shapes=[pltpu.VMEM((count,) + part.shape, f32)] + sems(count, 1),
        compiler_params=remote_params(1, 12),
        name="cube_total",
    )(part, gated, chan)


def add_rows(out, parts):
    shape = out.shape
    tile = min(16, shape[-2])
    lead = [()]
    for size in shape[:-2]:
        lead = [l + (i,) for l in lead for i in range(size)]
    for l in lead:

        def step(i, carry, l=l):
            at = l + (pl.ds(pl.multiple_of(i * tile, tile), tile), slice(None))
            total = parts[0][at].astype(f32)
            for part in parts[1:]:
                total = total + part[at].astype(f32)
            out[at] = total.astype(out.dtype)
            return carry

        lax.fori_loop(0, shape[-2] // tile, step, 0)


def scatter_kernel(
    gn_ref, gw_ref, b_ref, u_ref, p_ref, gain_ref, og_ref, ow_ref, ob_ref, ok_ref, ou_ref,
    n_own, n_box, n_near, b_own, b_box, b_near, w_own, w_box, w_far,
    k_own, k_box, k_near, k_far, k_bits, u_box, send, recv, local,
):
    me = Place()
    s, zl, zh, c = me.s, me.zl, me.zh, me.c
    cube, far, sibling = me.partners()
    greet(cube + far + sibling)
    mover = Mover(send, recv, local)
    bits = bits_of(me.peers)
    columns = w_own.shape[-1]
    mine, shared = pl.ds(0, columns), pl.ds(columns, k_own.shape[-1])

    def rows_path(src, own, box, near_box, out, order, near, arrivals, done=0):
        own, box = own.at[near], box.at[near]
        copies, loads = [], []
        if done:
            half = me.peers // 4
            for j in range(half):
                copies.append(mover.put(src.at[near, j], box.at[j], me.at(s=order[1])))
                loads.append(mover.keep(src.at[near, half + j], own.at[half + j]))
        else:
            at_zl = src.at[flip(zl, near)]
            for j, o in enumerate(combos(order[1:])):
                copies.append(mover.put(at_zl.at[flip(s, order[0] ^ o)], box.at[j], me.at(s=order[0])))
                loads.append(mover.keep(at_zl.at[flip(s, o)], own.at[j]))
        base = 0
        for i in range(done, len(order)):
            rest = order[i + 1 :]
            count = 1 << len(rest)
            offset = (1 << (len(order) - 1)) - count
            coming = []
            for j in range(count):
                yield
                copies[j].wait_recv()
                if i == done:
                    loads[j].wait()
                if rest or near:
                    add_rows(own.at[offset + j], [own.at[offset + j], box.at[base + j]])
                if rest and j < count // 2:
                    coming.append(mover.put(own.at[offset + j], box.at[base + count + j], me.at(s=rest[0])))
            copies = coming
            last = base
            base += count
        end = (1 << (len(order) - 1)) - 1
        if near:
            arrivals.append(mover.put(own.at[end], near_box.at[near - 1], me.at(zl=near)))
            yield
        else:
            yield
            for _ in range(me.near - 1):
                arrivals.pop(0).wait_recv()
            add_rows(out, [own.at[end], box.at[last]] + [near_box.at[o - 1] for o in range(1, me.near)])

    def weight_path():
        order = [(o, k) for o in range(1, me.far) for k in range(me.peers)] + [(0, k) for k in range(me.peers)]
        loads, copies = {}, {}
        for o, k in order:
            copies[o, k] = mover.put(gw_ref.at[flip(s, k), flip(zh, o), :, 1 - c, :, mine], w_box.at[o, k], me.at(c=1))
            loads[o, k] = mover.keep(gw_ref.at[flip(s, k), flip(zh, o), :, c, :, mine], w_own.at[o, k])
        far_copies = {}
        for o, k in order:
            yield
            loads[o, k].wait()
            copies[o, k].wait_recv()
            if o:
                add_rows(w_own.at[o, k], [w_own.at[o, k], w_box.at[o, k]])
                far_copies[o, k] = mover.put(w_own.at[o, k], w_far.at[o - 1, k], me.at(zh=o))
        ends, kept = [], []
        for k in range(me.peers):
            yield
            for o in range(1, me.far):
                far_copies[o, k].wait_recv()
            parts = [w_own.at[0, k], w_box.at[0, k]] + [w_far.at[o - 1, k] for o in range(1, me.far)]
            add_rows(w_own.at[0, k], parts)
            for o in range(me.near):
                for whole, part in me.column_runs(s, zl, columns):
                    src = w_own.at[0, k, flip(zl, o), :, part]
                    if k or o:
                        ends.append(mover.put(src, ow_ref.at[:, whole], me.at(s=k, zl=o)))
                    else:
                        kept.append(mover.keep(src, ow_ref.at[:, whole]))
        yield
        for copy in kept:
            copy.wait()
        for copy in ends:
            copy.wait_recv()

    def key_path():
        blocks = combos(bits)
        copies, loads = [], []
        for j, o in enumerate(blocks):
            copies.append(mover.put(gw_ref.at[flip(s, o), :, :, 1 - c, :, shared], k_box.at[j], me.at(c=1)))
            loads.append(mover.keep(gw_ref.at[flip(s, o), :, :, c, :, shared], k_own.at[j]))
        half = me.peers // 2
        sent = []
        for j in range(me.peers):
            yield
            loads[j].wait()
            copies[j].wait_recv()
            add_rows(k_own.at[j], [k_own.at[j], k_box.at[j]])
            if j < half:
                sent.append(mover.put(k_own.at[j], k_bits.at[j], me.at(s=bits[0])))
        base = 0
        for i, bit in enumerate(bits):
            count = me.peers >> (i + 1)
            offset = me.peers - count
            coming = []
            for j in range(count):
                yield
                sent[j].wait_recv()
                add_rows(k_own.at[offset + j], [k_own.at[offset + j], k_bits.at[base + j]])
                if i + 1 < len(bits) and j < count // 2:
                    coming.append(mover.put(k_own.at[offset + j], k_bits.at[base + count + j], me.at(s=bits[i + 1])))
            base += count
            sent = coming
        end = k_own.at[me.peers - 1]
        copies = [mover.put(end.at[:, flip(zl, o)], k_near.at[o - 1], me.at(zl=o)) for o in range(1, me.near)]
        yield
        for copy in copies:
            copy.wait_recv()
        add_rows(end.at[:, zl], [end.at[:, zl]] + [k_near.at[o - 1] for o in range(1, me.near)])
        copies = [mover.put(end.at[flip(zh, o), zl], k_far.at[o - 1], me.at(zh=o)) for o in range(1, me.far)]
        yield
        for copy in copies:
            copy.wait_recv()
        add_rows(ok_ref, [end.at[zh, zl]] + [k_far.at[o - 1] for o in range(1, me.far)])

    def small_path():
        turns = [me.at(c=1)] + [me.at(zl=o) for o in bits_of(me.near)]
        turns += [me.at(s=o) for o in bits] + [me.at(zh=o) for o in bits_of(me.far)]
        u_box[0] = u_ref[...]
        u_box[0, 6:7, : p_ref.shape[1]] = p_ref[...] / gain_ref[...]
        for i, device in enumerate(turns):
            copy = mover.put(u_box.at[2 * i], u_box.at[2 * i + 1], device)
            yield
            copy.wait_recv()
            u_box[2 * i + 2] = u_box[2 * i] + u_box[2 * i + 1]
        ou_ref[...] = u_box[2 * len(turns)]

    coming_n, coming_b = [], []
    grads = (gn_ref, n_own, n_box, n_near, og_ref)
    branch = (b_ref, b_own, b_box, b_near, ob_ref)
    orders = lambda o: bits if o else bits[::-1]
    near_n = [rows_path(*grads, orders(o), o, coming_n) for o in range(1, me.near)]
    near_b = [rows_path(*branch, orders(o), o, coming_b, 1) for o in range(1, me.near)]
    own_n = rows_path(*grads, orders(0), 0, coming_n)
    own_b = rows_path(*branch, orders(0), 0, coming_b, 1)
    weights, keys, small = weight_path(), key_path(), small_path()
    turn(near_b + near_n + [weights, own_n, keys, own_b, small])
    turn([weights] * (me.far * me.peers) + [keys] * me.peers + [small])
    turn(near_b + near_n + [keys, own_b, small] + near_b + near_n + [keys, small, keys, own_b, own_n])
    run_paths(near_b + near_n + [keys, small, weights, own_b, own_n])
    mover.close()


def scatter(grads, gw, branch, small, products, gain):
    me = Place()
    peers, near, far = me.peers, me.near, me.far
    tokens, width = grads.shape[2:]
    stages = len(bits_of(peers)) + len(bits_of(near)) + len(bits_of(far)) + 1
    vm = lambda *shape: pltpu.VMEM(shape, bf16)
    boxes = lambda part: pltpu.VMEM((2 * stages + 1,) + part.shape, f32)
    keys = KEYS + STEP_PAD
    rows = gw.shape[4]
    block = (near, rows, gw.shape[5] - keys)
    kblock = (near, rows, keys)
    runs = 2 * (far if near > 1 else 1)
    copies = peers * near - 1 + (2 * far - 1) * peers + runs * (peers * near - 1)
    copies += 2 * peers - 1 + near - 1 + far - 1 + stages + peers // 2 * near - 1
    kept = peers * near + far * peers + runs + peers + near * peers // 4
    same = lambda part: jax.ShapeDtypeStruct(part.shape, part.dtype)
    return pl.pallas_call(
        scatter_kernel,
        out_shape=[
            jax.ShapeDtypeStruct((tokens, width), f32),
            jax.ShapeDtypeStruct((rows, 2 * E), bf16),
            jax.ShapeDtypeStruct((tokens, width), f32),
            jax.ShapeDtypeStruct((rows, keys), f32),
            same(small),
        ],
        in_specs=[HBM] * 3 + [VMEM] * 3,
        out_specs=[VMEM, HBM, VMEM, VMEM, VMEM],
        scratch_shapes=[
            vm(near, peers // 2, tokens, width), vm(near, peers - 1, tokens, width), vm(max(near - 1, 1), tokens, width),
            vm(near, peers // 2, tokens, width), vm(near, peers // 2 - 1, tokens, width), vm(max(near - 1, 1), tokens, width),
            vm(far, peers, *block), vm(far, peers, *block), vm(max(far - 1, 1), peers, *block),
            vm(peers, far, *kblock), vm(peers, far, *kblock), vm(max(near - 1, 1), far, *kblock[1:]),
            vm(max(far - 1, 1), *kblock[1:]), vm(peers - 1, far, *kblock), boxes(small),
        ]
        + sems(copies, kept),
        compiler_params=remote_params(2, 40),
        cost_estimate=pl.CostEstimate(flops=0, bytes_accessed=250 * 10**6, transcendentals=0),
        name="scatter_all",
    )(grads, gw, branch, small, products, gain)


class Early:
    def __init__(self, b_ref, go_ref, refs):
        self.b_out, self.o_out, self.b_own, self.b_box, self.o_own, self.o_box, self.o_far, send, recv, local = refs
        me = self.me = Place()
        mover = self.mover = Mover(send, recv, local)
        bits = bits_of(me.peers)
        self.rows, self.outs, self.far = [], [], []
        for o in range(me.near):
            order = bits if o else bits[::-1]
            at_zl = b_ref.at[flip(me.zl, o)]
            for j, left in enumerate(combos(order[1:])):
                put = mover.plan(at_zl.at[flip(me.s, order[0] ^ left)], self.b_box.at[o, j], me.at(s=order[0]))
                self.rows.append((put, mover.plan_keep(at_zl.at[flip(me.s, left)], self.b_own.at[o, j]), (o, j)))
        for o in range(me.far):
            put = mover.plan(go_ref.at[flip(me.zh, o), 1 - me.c], self.o_box.at[o], me.at(c=1))
            self.outs.append((put, mover.plan_keep(go_ref.at[flip(me.zh, o), me.c], self.o_own.at[o])))
        for o in range(1, me.far):
            self.far.append(mover.plan(self.o_own.at[o], self.o_far.at[o - 1], me.at(zh=o)))

    def start(self):
        _, far, sibling = self.me.partners()
        bits = bits_of(self.me.peers)
        greet([self.me.at(s=bit) for bit in sorted({bits[0], bits[-1]})] + far + sibling)
        for put, load in self.outs:
            put.start()
            load.start()
        for put, load, _ in self.rows:
            put.start()
            load.start()

    def middle(self):
        for o, (put, load) in enumerate(self.outs):
            load.wait()
            put.wait_recv()
            if o:
                add_rows(self.o_own.at[o], [self.o_own.at[o], self.o_box.at[o]])
                self.far[o - 1].start()

    def end(self):
        for put, load, at in self.rows:
            load.wait()
            put.wait_recv()
            add_rows(self.b_out.at[at], [self.b_own.at[at], self.b_box.at[at]])
        for put in self.far:
            put.wait_recv()
        add_rows(self.o_out, [self.o_own.at[0], self.o_box.at[0]] + [self.o_far.at[o] for o in range(self.me.far - 1)])
        self.mover.close()


def prepare_kernel(x_ref, gain_ref, step_ref, lengths_ref, width_ref, normed_ref, inv_ref, steps_ref, meta_ref):
    x = x_ref[0].astype(f32)
    inv = lax.rsqrt(jnp.mean(x * x, axis=1, keepdims=True) + epsilon)
    normed_ref[...] = (x * inv * gain_ref[...]).astype(bf16)
    inv_ref[...] = jnp.broadcast_to(inv, inv_ref.shape)
    steps_ref[...] = jnp.zeros_like(steps_ref)
    steps_ref[:, :H] = step_ref[...]
    lanes = iota(meta_ref.shape, 1)
    meta = jnp.where(lanes == DOCS, width_ref[0], 0)
    for i in range(DOCS):
        meta = jnp.where(lanes == i, lengths_ref[0, i], meta)
    meta_ref[...] = meta


def prepare(inputs, gain, step_weight, doc_lengths, head_width):
    tokens, width = inputs.shape[1:]
    smem = pl.BlockSpec(memory_space=pltpu.SMEM)
    return pl.pallas_call(
        prepare_kernel,
        out_shape=[
            jax.ShapeDtypeStruct((tokens, width), bf16),
            jax.ShapeDtypeStruct((tokens, LANES), f32),
            jax.ShapeDtypeStruct((step_weight.shape[0], STEP_PAD), bf16),
            jax.ShapeDtypeStruct((8, LANES), jnp.int32),
        ],
        in_specs=[VMEM] * 3 + [smem] * 2,
        out_specs=[VMEM] * 4,
        compiler_params=pltpu.CompilerParams(vmem_limit_bytes=16 * 2**20),
        name="prepare",
    )(inputs, gain, step_weight, doc_lengths, head_width)


def finish_kernel(
    x_ref, cot_ref, gain_ref, inv_ref, og_ref, ob_ref, ow_ref, ok_ref, u_ref,
    out_ref, gx_ref, gw_ref, gs_ref, gc_ref, gb_ref, gp_ref, gn_ref, g0_ref, g1_ref, g2_ref,
):
    x = x_ref[0].astype(f32)
    out_ref[0] = (x + ob_ref[...]).astype(bf16)
    inv = inv_ref[:, :1]
    scaled = og_ref[...] * gain_ref[...]
    dot = jnp.mean(scaled * x, axis=1, keepdims=True)
    gx_ref[0] = inv * scaled - x * (inv * inv * inv * dot) + cot_ref[0].astype(f32)
    gw_ref[:, : 2 * E] = ow_ref[...].astype(f32)
    gw_ref[:, 2 * E :] = ok_ref[:, :KEYS]
    gs_ref[...] = ok_ref[:, KEYS : KEYS + H]
    gc_ref[...] = u_ref[:CONV, :]
    gb_ref[...] = u_ref[CONV : CONV + 1, :]
    gn_ref[...] = u_ref[5:6, :E]
    gp_ref[...] = u_ref[6:7, : gp_ref.shape[1]]
    for i, ref in enumerate((g0_ref, g1_ref, g2_ref)):
        ref[...] = u_ref[7:8, i * LANES : i * LANES + H]


def finish(inputs, cotangent, gain, inv, sums):
    tokens, width = inputs.shape[1:]
    og, ow, ob, ok, u = sums
    shape = lambda *dims: jax.ShapeDtypeStruct(dims, f32)
    rows = ow.shape[0]
    return pl.pallas_call(
        finish_kernel,
        out_shape=[
            jax.ShapeDtypeStruct(inputs.shape, bf16), shape(*inputs.shape), shape(rows, 2 * E + KEYS), shape(rows, H),
            shape(CONV, E + KEYS), shape(1, E + KEYS), shape(1, width), shape(1, E), shape(1, H), shape(1, H), shape(1, H),
        ],
        in_specs=[VMEM] * 9,
        out_specs=[VMEM] * 11,
        compiler_params=pltpu.CompilerParams(vmem_limit_bytes=32 * 2**20),
        name="finish",
    )(inputs, cotangent, gain, inv, og, ob, ow, ok, u)


def body(
    inputs, cotangent, doc_lengths, head_width, pre_gain, in_weight, step_weight, conv_weight, conv_bias,
    step_bias, decay_log, skip_gain, norm_gain, out_weight,
):
    me = Place()
    peers, near, far = me.peers, me.near, me.far
    tokens, width = inputs.shape[1:]
    span = tokens * peers
    length = span * near
    heads = H // (peers * near)
    inner = heads * P_SIZE
    rows = in_weight.shape[0]
    row = lambda vector: vector[None, :]

    normed, inv, steps, meta = prepare(inputs, row(pre_gain), step_weight, doc_lengths, head_width)
    in_w, out_w, normed, cot_all, meta = gather(in_weight, steps, out_weight, normed, cotangent[0], meta)
    in_w = in_w.reshape(width, -1)
    out_w = out_w.reshape(inner, width)
    normed = normed.reshape(length, width)
    cot_all = cot_all.reshape(length, width)
    meta = meta[:, 0, :8]

    params = (conv_weight, row(conv_bias), row(norm_gain), row(step_bias), row(decay_log), row(skip_gain))
    projected = mm(normed, in_w, NN)
    grad_mixed = mm(cot_all, out_w, NT)
    *kept, gated, states, part, chan, head_vec = mixer_forward(meta, projected, grad_mixed, params, span, heads)
    sums, mixed = cube_total(part, gated, chan)
    branch = mm(mixed, out_w, NN).astype(bf16)
    grad_out = mm(mixed, cot_all, TN).astype(bf16)
    grad_cols, small, branch, grad_out_weight = mixer_backward(
        meta, projected, grad_mixed, chan, conv_weight, head_vec, (*kept, states), sums,
        branch.reshape(near, peers, tokens, width), grad_out.reshape(far, 2, -1, width), span, heads,
    )
    grad_in = mm(normed, grad_cols, TN).astype(bf16)
    grad_normed = mm(grad_cols, in_w, NT)
    products = jnp.sum(grad_normed * normed.astype(f32), axis=0)
    summed = scatter(
        grad_normed.astype(bf16).reshape(near, peers, tokens, width),
        grad_in.reshape(peers, far, near, 2, rows, -1),
        branch,
        small,
        row(products),
        row(pre_gain),
    )
    outs = finish(inputs, cotangent, row(pre_gain), inv, summed)
    output, grad_inputs, grad_in_weight, grad_step_weight, grad_conv_weight = outs[:5]
    grad_conv_bias, grad_pre_gain, grad_norm_gain, grad_step_bias, grad_decay_log, grad_skip = [o[0] for o in outs[5:]]
    return (
        output, grad_inputs, grad_pre_gain, grad_in_weight, grad_step_weight, grad_conv_weight, grad_conv_bias,
        grad_step_bias, grad_decay_log, grad_skip, grad_norm_gain, grad_out_weight,
    )


def solution(mesh):
    both = P(("seq", "batch"), None)
    tok = P("batch", "seq", None)
    in_specs = (
        tok, tok, P("batch", None), P("batch"), P(), both, both, P(), P(), P(), P(), P(), P(), both,
    )
    out_specs = (tok, tok, P(), both, both, P(), P(), P(), P(), P(), P(), both)
    return jax.shard_map(body, mesh=mesh, in_specs=in_specs, out_specs=out_specs, check_vma=False)
```

```python
from functools import partial

import jax
import jax.numpy as jnp
from jax import lax
from jax.experimental import pallas as pl
from jax.experimental.pallas import tpu as pltpu
from jax.sharding import PartitionSpec as P

H = 64
P_SIZE = 64
N = 128
CONV = 4
DOCS = 4
E = 4096
KEYS = 2 * N
STEP_PAD = 128
CHUNK = 128
LANES = 128
epsilon = 1e-05
f32 = jnp.float32
bf16 = jnp.bfloat16


def mm(a, b, dims, precision=None):
    return lax.dot_general(a, b, (dims, ((), ())), precision=precision, preferred_element_type=f32)


NN = ((1,), (0,))
NT = ((1,), (1,))
TN = ((0,), (0,))
exact = lax.Precision.HIGHEST


def pair_cols(low, col, first):
    return jnp.where(low, col[:, first : first + 1], col[:, first + 1 : first + 2])


def iota(shape, axis):
    return lax.broadcasted_iota(jnp.int32, shape, axis)


class Docs:
    def __init__(self, meta_ref, chunk, span):
        per = span // CHUNK
        seq = chunk // per
        self.start = (chunk - seq * per) * CHUNK
        self.ends = []
        total = 0
        for i in range(DOCS - 1):
            total = total + meta_ref[seq, i]
            self.ends.append(total)
        self.count = meta_ref[seq, DOCS]
        self.pos = self.start + iota((CHUNK, 1), 0)
        self.doc = self.index(self.pos)

    def index(self, places):
        found = (places >= self.ends[0]).astype(jnp.int32)
        for end in self.ends[1:]:
            found = found + (places >= end).astype(jnp.int32)
        return found

    def lag(self, by):
        source = self.pos - by
        return ((source >= 0) & (self.index(source) == self.doc)).astype(f32)

    def flow(self):
        return ((self.start > 0) & (self.index(self.start - 1) == self.doc)).astype(f32)

    def row(self):
        return self.index(self.start + iota((1, CHUNK), 1))

    def tail(self):
        return (self.doc == self.index(self.start + CHUNK - 1)).astype(f32)


def shift_down(rows, before, by):
    if by == 0:
        return rows
    moved = pltpu.roll(rows, by, 0)
    top = jnp.where(iota((8, 1), 0) < by, pltpu.roll(before, by, 0), moved[:8])
    return jnp.concatenate([top, moved[8:]], axis=0)


def shift_up(rows, after, by):
    if by == 0:
        return rows
    size = rows.shape[0]
    moved = pltpu.roll(rows, size - by, 0)
    end = jnp.where(iota((8, 1), 0) >= 8 - by, pltpu.roll(after, 8 - by, 0), moved[size - 8 :])
    return jnp.concatenate([moved[: size - 8], end], axis=0)


def silu_slope(v, sig):
    return sig * (1.0 + v * (1.0 - sig))


def own_parameters(chan_ref, head_ref, conv_ref, bias_ref, norm_ref, step_b_ref, decay_ref, skip_ref, heads):
    me = Place()
    inner = heads * P_SIZE
    for whole, part in me.channel_runs(inner):
        chan_ref[:CONV, part] = conv_ref[:, whole]
        chan_ref[CONV : CONV + 1, part] = bias_ref[:, whole]
        chan_ref[5:6, part] = norm_ref[:, whole]
    ids = me.heads_at(iota((1, inner), 1), P_SIZE, inner)
    chosen = (iota((H, inner), 0) == ids).astype(f32)
    chan_ref[6:7, :] = mm(jnp.broadcast_to(skip_ref[...], (8, H)), chosen, NN, exact)[:1]
    chan_ref[7:8, :] = ids.astype(f32)
    lanes = iota((1, LANES), 1)
    ids = jnp.where(lanes < heads, me.heads_at(lanes, 1, heads), -1)
    chosen = (iota((H, LANES), 0) == ids).astype(f32)
    head_ref[...] = jnp.zeros_like(head_ref)
    head_ref[:1, :] = mm(jnp.broadcast_to(step_b_ref[...], (8, H)), chosen, NN, exact)[:1]
    head_ref[1:2, :] = mm(jnp.broadcast_to(jnp.exp(decay_ref[...]), (8, H)), chosen, NN, exact)[:1]
    head_ref[2:3, :] = ids.astype(f32)


def whole_sums(out_ref, chan_sums, key_sums, head_sums, head_ref, chan_ref, heads):
    me = Place()
    inner = heads * P_SIZE
    out_ref[...] = jnp.zeros_like(out_ref)
    for whole, part in me.channel_runs(inner):
        out_ref[:6, whole] = chan_sums[:6, part]
    out_ref[:5, E:] = key_sums[:5, :]
    chosen = (iota((H, LANES), 0) == head_ref[2:3, :].astype(jnp.int32)).astype(f32)
    steps = mm(head_sums[...], chosen, NT, exact)
    chosen = (iota((H, inner), 0) == chan_ref[7:8, :].astype(jnp.int32)).astype(f32)
    skips = mm(chan_sums[...], chosen, NT, exact)
    out_ref[7:8, :H] = steps[:1]
    out_ref[7:8, LANES : LANES + H] = steps[1:2]
    out_ref[7:8, 2 * LANES : 2 * LANES + H] = skips[6:7]


def forward_kernel(
    meta_ref, proj_ref, conv_ref, bias_ref, norm_ref, step_b_ref, decay_ref, skip_ref, cot_in, out_in,
    val_out, key_out, vsum_ref, ksum_ref, raw_ref, cum_ref, y_ref, gated_ref, state_ref, sums_ref, chan_ref, head_ref,
    cot_out, out_out, state, last_v, last_k, send, recv,
    *, span, heads,
):
    i = pl.program_id(0)
    chunks = pl.num_programs(0)
    inner = heads * P_SIZE
    late = Late(cot_in, cot_out, out_in, out_out, send, recv)

    @pl.when(i == 0)
    def _():
        late.start()
        own_parameters(chan_ref, head_ref, conv_ref, bias_ref, norm_ref, step_b_ref, decay_ref, skip_ref, heads)
        state[...] = jnp.zeros_like(state)
        last_v[...] = jnp.zeros_like(last_v)
        last_k[...] = jnp.zeros_like(last_k)

    @pl.when(i == chunks - 1)
    def _():
        late.middle()

    docs = Docs(meta_ref, i, span)
    lags = [docs.lag(by) for by in range(1, CONV)]

    def convolve(rows, before, weight, bias):
        total = bias + weight[CONV - 1 :] * rows
        for by in range(1, CONV):
            at = CONV - 1 - by
            total = total + weight[at : at + 1] * (shift_down(rows, before, by) * lags[by - 1])
        return total

    rows_v = proj_ref[:, inner : 2 * inner].astype(bf16).astype(f32)
    vsum = convolve(rows_v, last_v[...], chan_ref[:CONV, :], chan_ref[CONV : CONV + 1, :])
    last_v[...] = rows_v[CHUNK - 8 :]
    vsum_ref[...] = vsum
    val_out[...] = (vsum * jax.nn.sigmoid(vsum)).astype(bf16)
    rows_k = proj_ref[:, 2 * inner : 2 * inner + KEYS].astype(bf16).astype(f32)
    ksum = convolve(rows_k, last_k[...], conv_ref[:, E:], bias_ref[:, E:])
    last_k[...] = rows_k[CHUNK - 8 :]
    ksum_ref[...] = ksum
    keys = (ksum * jax.nn.sigmoid(ksum)).astype(bf16)
    key_out[...] = keys

    rows = iota((CHUNK, CHUNK), 0)
    cols = iota((CHUNK, CHUNK), 1)
    chosen = (rows == head_ref[2:3, :].astype(jnp.int32)).astype(f32)
    raw = mm(proj_ref[:, 2 * inner + KEYS :], chosen, NN, exact) + head_ref[:1, :]
    raw_ref[...] = raw
    dt = jax.nn.softplus(raw)
    cum = mm((rows >= cols).astype(f32), -dt * head_ref[1:2, :], NN, exact)
    cum_ref[...] = cum
    cum_t = cum.T
    dt_t = dt.T

    state_ref[0] = state[...].astype(bf16)
    bias = jnp.where((docs.doc == docs.row()) & (rows >= cols), 0.0, -1e30)
    carry_w = docs.flow() * jnp.exp(cum)
    final_w = docs.tail() * jnp.exp(cum[CHUNK - 1 :, :] - cum) * dt
    gain = carry_w[CHUNK - 1 :, :]
    low = cols < P_SIZE
    low_row = low[:1]
    write = keys[:, :N]
    read = keys[:, N:]
    write_t = write.astype(f32).T.astype(bf16)
    scores = mm(read, write, NT)
    square = jnp.zeros((CHUNK, LANES), f32)
    count = docs.count.astype(f32)
    for pair in range(heads // 2):
        first = 2 * pair
        lanes = slice(pair * 128, pair * 128 + 128)
        xf = val_out[:, lanes].astype(f32)
        weights = []
        for h in (first, first + 1):
            decay = jnp.exp(cum[:, h : h + 1] - cum_t[h : h + 1, :] + bias)
            weights.append((decay * scores * dt_t[h : h + 1, :]).astype(bf16))
        stacked = jnp.concatenate(
            [jnp.where(low, xf, 0.0).astype(bf16), jnp.where(low, 0.0, xf).astype(bf16)], axis=0
        )
        old = state[:, lanes]
        y = mm(jnp.concatenate(weights, axis=1), stacked, NN)
        y = y + pair_cols(low, carry_w, first) * mm(read, old.astype(bf16), NN)
        y = y + chan_ref[6:7, lanes] * xf
        y = jnp.where(chan_ref[7:8, lanes] < count, y, 0.0)
        y_ref[:, lanes] = y
        state[:, lanes] = pair_cols(low_row, gain, first) * old + mm(
            write_t, (pair_cols(low, final_w, first) * xf).astype(bf16), NN
        )
        gate = proj_ref[:, lanes]
        gated = y * (gate * jax.nn.sigmoid(gate))
        gated_ref[:, lanes] = gated
        square = square + gated * gated
    share = 1.0 / (count * P_SIZE)
    sums_ref[pl.ds(i, 1), :] = jnp.sum(square.T, axis=0, keepdims=True) * share
    sums_ref[pl.ds(chunks + i, 1), :] = jnp.full((1, LANES), share, f32)

    @pl.when(i == chunks - 1)
    def _():
        late.end()


def backward_kernel(
    meta_ref, proj_ref, grad_ref, chan_ref, conv_ref, head_ref,
    val_ref, key_ref, vsum_ref, ksum_ref, raw_ref, cum_ref, y_ref, state_ref, sums_ref, branch_ref, go_ref,
    cols_ref, all_sums, b_out, o_out,
    chan_sums, key_sums, head_sums, dstate, dv, next_v, next_k, next_lags, *early_refs,
    span, heads,
):
    chunks = pl.num_programs(0)
    i = chunks - 1 - pl.program_id(0)
    inner = heads * P_SIZE
    early = Early(branch_ref, go_ref, (b_out, o_out) + early_refs)

    @pl.when(pl.program_id(0) == 0)
    def _():
        early.start()
        for ref in (dstate, next_v, next_k, next_lags, chan_sums, key_sums, head_sums):
            ref[...] = jnp.zeros_like(ref)

    docs = Docs(meta_ref, i, span)
    rows = iota((CHUNK, CHUNK), 0)
    cols = iota((CHUNK, CHUNK), 1)
    raw = raw_ref[...]
    dt = jax.nn.softplus(raw)
    cum = cum_ref[...]
    cum_t = cum.T
    count = docs.count.astype(f32)

    def column(row):
        return jnp.broadcast_to(row, (CHUNK, CHUNK)).T

    inv = lax.rsqrt(column(sums_ref[pl.ds(i, 1), :]) + epsilon)
    pull = inv * inv * inv * column(sums_ref[pl.ds(chunks + i, 1), :])

    bias = jnp.where((docs.doc == docs.row()) & (cols >= rows), 0.0, -1e30)
    carry_w = docs.flow() * jnp.exp(cum)
    final_d = docs.tail() * jnp.exp(cum[CHUNK - 1 :, :] - cum)
    final_w = final_d * dt
    gain = carry_w[CHUNK - 1 :, :]
    low = cols < P_SIZE
    low_row = low[:1]
    write = key_ref[:, :N]
    read = key_ref[:, N:]
    read_t = read.astype(f32).T.astype(bf16)
    scores_t = mm(write, read, NT)
    dscores_t = jnp.zeros((CHUNK, CHUNK), f32)
    dwrite = jnp.zeros((CHUNK, N), f32)
    dread = jnp.zeros((CHUNK, N), f32)
    end_row = iota((CHUNK, 1), 0) == CHUNK - 1
    dcum = jnp.zeros((CHUNK, LANES), f32)
    ddt = jnp.zeros((CHUNK, LANES), f32)
    dcum_rows = []
    for pair in range(heads // 2):
        first = 2 * pair
        lanes = slice(pair * 128, pair * 128 + 128)
        gate = proj_ref[:, lanes]
        sig = jax.nn.sigmoid(gate)
        silu = gate * sig
        masked = y_ref[:, lanes]
        gated = masked * silu
        norm_gain = chan_ref[5:6, lanes]
        gm = grad_ref[:, lanes]
        unit = gated * inv
        chan_sums[5:6, lanes] += jnp.sum(gm * unit, axis=0, keepdims=True)
        grad_gated = inv * (gm * norm_gain) - pull * gated
        cols_ref[:, lanes] = (grad_gated * masked * silu_slope(gate, sig)).astype(bf16)
        dy = jnp.where(chan_ref[7:8, lanes] < count, grad_gated * silu, 0.0)
        xf = val_ref[:, lanes].astype(f32)
        dyb = dy.astype(bf16)
        x_stack = jnp.concatenate(
            [jnp.where(low, xf, 0.0).astype(bf16), jnp.where(low, 0.0, xf).astype(bf16)], axis=0
        )
        dy_stack = jnp.concatenate(
            [jnp.where(low, dy, 0.0).astype(bf16), jnp.where(low, 0.0, dy).astype(bf16)], axis=0
        )
        dweights = mm(x_stack, dyb, NT)
        old = state_ref[0, :, lanes]
        grad = dstate[:, lanes]
        gradb = grad.astype(bf16)
        carried = mm(read, old, NN)
        pushed = mm(write, gradb, NN)
        carry_p = pair_cols(low, carry_w, first)
        final_p = pair_cols(low, final_w, first)
        carry_prod = dy * carried
        final_prod = xf * pushed
        gain_prod = jnp.sum(grad * old.astype(f32), axis=0, keepdims=True)
        weights = []
        for which, h in enumerate((first, first + 1)):
            col = dt[:, h : h + 1]
            decay = jnp.exp(cum_t[h : h + 1, :] - cum[:, h : h + 1] + bias)
            weighted = decay * col
            weights.append((weighted * scores_t).astype(bf16))
            dw = dweights[which * CHUNK : (which + 1) * CHUNK]
            dscores_t = dscores_t + dw * weighted
            direct = dw * decay * scores_t
            ddt_in = jnp.sum(direct, axis=1, keepdims=True)
            dcum_rows.append(jnp.sum(direct * col, axis=0, keepdims=True))
            half = low if which == 0 else ~low
            half_row = low_row if which == 0 else ~low_row
            carry_sum = jnp.sum(jnp.where(half, carry_prod, 0.0), axis=1, keepdims=True)
            final_sum = jnp.sum(jnp.where(half, final_prod, 0.0), axis=1, keepdims=True)
            push = final_w[:, h : h + 1] * final_sum
            at_end = jnp.sum(push, axis=0, keepdims=True) + gain[:, h : h + 1] * jnp.sum(
                jnp.where(half_row, gain_prod, 0.0), axis=1, keepdims=True
            )
            here = cols == h
            ddt = jnp.where(here, ddt_in + final_d[:, h : h + 1] * final_sum, ddt)
            dcum = jnp.where(
                here,
                carry_w[:, h : h + 1] * carry_sum - push - col * ddt_in + jnp.where(end_row, at_end, 0.0),
                dcum,
            )
        dx = mm(jnp.concatenate(weights, axis=1), dy_stack, NN)
        dv[:, lanes] = dx + final_p * pushed + chan_ref[6:7, lanes] * dy
        chan_sums[6:7, lanes] += jnp.sum(dy * xf, axis=0, keepdims=True)
        dwrite = dwrite + mm((final_p * xf).astype(bf16), gradb, NT)
        carry_dy = (carry_p * dy).astype(bf16)
        dread = dread + mm(carry_dy, old, NT)
        dstate[:, lanes] = pair_cols(low_row, gain, first) * grad + mm(read_t, carry_dy, NN)
    dsb = dscores_t.astype(bf16)
    dkeys = jnp.concatenate([dwrite + mm(dsb, read, NN), dread + mm(dsb, write, TN)], axis=1)

    extra = jnp.concatenate(dcum_rows + [jnp.zeros((LANES - heads, CHUNK), f32)], axis=0)
    dlog = mm((cols >= rows).astype(f32), dcum + extra.T, NN, exact)
    rate = head_ref[1:2, :]
    grad_step = (ddt - rate * dlog) * jax.nn.sigmoid(raw)
    head_sums[:1, :] += jnp.sum(grad_step, axis=0, keepdims=True)
    head_sums[1:2, :] -= jnp.sum(dt * rate * dlog, axis=0, keepdims=True)
    chosen = (rows == head_ref[2:3, :].astype(jnp.int32)).astype(bf16)
    cols_ref[:, 2 * inner + KEYS :] = mm(grad_step.astype(bf16), chosen, NT).astype(bf16)

    lags = [docs.lag(by) for by in range(1, CONV)]

    def convolve_back(dact, total, rows_in, after, weight, sums):
        dconv = dact * silu_slope(total, jax.nn.sigmoid(total))
        grad_in = weight[CONV - 1 :] * dconv
        sums[CONV : CONV + 1, :] += jnp.sum(dconv, axis=0, keepdims=True)
        sums[CONV - 1 : CONV, :] += jnp.sum(dconv * rows_in, axis=0, keepdims=True)
        for by in range(1, CONV):
            at = CONV - 1 - by
            moved = shift_up(dconv * lags[by - 1], after[...] * next_lags[:, by - 1 : by], by)
            grad_in = grad_in + weight[at : at + 1] * moved
            sums[at : at + 1, :] += jnp.sum(moved * rows_in, axis=0, keepdims=True)
        after[...] = dconv[:8]
        return grad_in.astype(bf16)

    rows_v = proj_ref[:, inner : 2 * inner].astype(bf16).astype(f32)
    cols_ref[:, inner : 2 * inner] = convolve_back(dv[...], vsum_ref[...], rows_v, next_v, chan_ref[:CONV, :], chan_sums)
    rows_k = proj_ref[:, 2 * inner : 2 * inner + KEYS].astype(bf16).astype(f32)
    cols_ref[:, 2 * inner : 2 * inner + KEYS] = convolve_back(
        dkeys, ksum_ref[...], rows_k, next_k, conv_ref[:, E:], key_sums
    )
    for by in range(1, CONV):
        next_lags[:, by - 1 : by] = lags[by - 1][:8]

    @pl.when(pl.program_id(0) == 0)
    def _():
        early.middle()

    @pl.when(pl.program_id(0) == chunks - 1)
    def _():
        whole_sums(all_sums, chan_sums, key_sums, head_sums, head_ref, chan_ref, heads)
        early.end()


def mixer_forward(meta, projected, params, cot, out_w, span, heads):
    length = projected.shape[0]
    inner = heads * P_SIZE
    chunks = length // CHUNK
    copies = sum(len(left_over(cot_order(o))) for o in range(cot.shape[0])) + 2 * (out_w.shape[0] - 1)
    row = lambda width: pl.BlockSpec((CHUNK, width), lambda i: (i, 0))
    all_of = lambda *shape: pl.BlockSpec(shape, lambda i: (0,) * len(shape))
    out = lambda width, dtype: jax.ShapeDtypeStruct((length, width), dtype)
    return pl.pallas_call(
        partial(forward_kernel, span=span, heads=heads),
        grid=(chunks,),
        in_specs=[
            pl.BlockSpec(memory_space=pltpu.SMEM), row(2 * inner + KEYS + STEP_PAD),
        ]
        + [all_of(*part.shape) for part in params]
        + [HBM] * 2,
        out_specs=[
            row(inner), row(KEYS), row(inner), row(KEYS), row(LANES), row(LANES), row(inner), row(inner),
            pl.BlockSpec((1, N, inner), lambda i: (i, 0, 0)), all_of(2 * chunks, LANES),
            all_of(8, inner), all_of(8, LANES), HBM, HBM,
        ],
        out_shape=[
            out(inner, bf16), out(KEYS, bf16), out(inner, f32), out(KEYS, f32), out(LANES, f32), out(LANES, f32),
            out(inner, f32), out(inner, f32), jax.ShapeDtypeStruct((chunks, N, inner), bf16),
            jax.ShapeDtypeStruct((2 * chunks, LANES), f32), jax.ShapeDtypeStruct((8, inner), f32),
            jax.ShapeDtypeStruct((8, LANES), f32), jax.ShapeDtypeStruct(cot.shape, bf16),
            jax.ShapeDtypeStruct(out_w.shape, bf16),
        ],
        input_output_aliases={2 + len(params): 12, 3 + len(params): 13},
        scratch_shapes=[pltpu.VMEM((N, inner), f32), pltpu.VMEM((8, inner), f32), pltpu.VMEM((8, KEYS), f32)]
        + sems(copies, 1)[:2],
        compiler_params=remote_params(4, 16),
        cost_estimate=pl.CostEstimate(
            flops=length * inner * 1024, bytes_accessed=length * inner * 24, transcendentals=length * heads * CHUNK
        ),
        name="mixer_forward",
    )(meta, projected, *params, cot, out_w)


def mixer_backward(meta, projected, grad_mixed, chan, conv, head_vec, kept, sums, branch, grad_out, span, heads):
    length = projected.shape[0]
    inner = heads * P_SIZE
    chunks = length // CHUNK
    me = Place()
    near, peers, tokens, width = branch.shape
    far = me.far
    part = grad_out.shape[2:]
    copies = near * peers // 2 + 2 * far - 1
    vm = lambda *shape: pltpu.VMEM(shape, bf16)
    row = lambda width: pl.BlockSpec((CHUNK, width), lambda i: (chunks - 1 - i, 0))
    all_of = lambda *shape: pl.BlockSpec(shape, lambda i: (0,) * len(shape))
    out = lambda width: jax.ShapeDtypeStruct((length, width), bf16)
    return pl.pallas_call(
        partial(backward_kernel, span=span, heads=heads),
        grid=(chunks,),
        in_specs=[
            pl.BlockSpec(memory_space=pltpu.SMEM), row(2 * inner + KEYS + STEP_PAD), row(inner),
            all_of(8, inner), all_of(*conv.shape), all_of(8, LANES),
            row(inner), row(KEYS), row(inner), row(KEYS), row(LANES), row(LANES), row(inner),
            pl.BlockSpec((1, N, inner), lambda i: (chunks - 1 - i, 0, 0)), all_of(2 * chunks, LANES), HBM, HBM,
        ],
        out_specs=[
            row(2 * inner + KEYS + STEP_PAD), all_of(8, conv.shape[1]), VMEM, VMEM,
        ],
        out_shape=[
            out(2 * inner + KEYS + STEP_PAD), jax.ShapeDtypeStruct((8, conv.shape[1]), f32),
            jax.ShapeDtypeStruct((near, peers // 2, tokens, width), bf16), jax.ShapeDtypeStruct(part, f32),
        ],
        scratch_shapes=[
            pltpu.VMEM((8, inner), f32), pltpu.VMEM((8, KEYS), f32), pltpu.VMEM((8, LANES), f32),
            pltpu.VMEM((N, inner), f32), pltpu.VMEM((CHUNK, inner), f32), pltpu.VMEM((8, inner), f32),
            pltpu.VMEM((8, KEYS), f32), pltpu.VMEM((8, LANES), f32),
            vm(near, peers // 2, tokens, width), vm(near, peers // 2, tokens, width),
            vm(far, *part), vm(far, *part), vm(max(far - 1, 1), *part),
        ]
        + sems(copies, near * peers // 2 + far),
        compiler_params=remote_params(3, 32),
        cost_estimate=pl.CostEstimate(
            flops=length * inner * 3072, bytes_accessed=length * inner * 30, transcendentals=length * heads * CHUNK
        ),
        name="mixer_backward",
    )(meta, projected, grad_mixed, chan, conv, head_vec, *kept, sums, branch, grad_out)


MESH = pl.DeviceIdType.MESH
HBM = pl.BlockSpec(memory_space=pl.ANY)
VMEM = pl.BlockSpec(memory_space=pltpu.VMEM)


def z_pair(peers, groups):
    planes = groups // 2
    return 2 if planes % 2 == 0 and (E // (peers * planes)) % (2 * P_SIZE) == 0 else 1


def flip(value, bits):
    bit = 1
    while bit <= bits:
        if bits & bit:
            value = value + bit - 2 * bit * (value // bit % 2)
        bit *= 2
    return value


class Place:
    def __init__(self):
        self.peers = lax.axis_size("seq")
        groups = lax.axis_size("batch")
        self.near = z_pair(self.peers, groups)
        self.far = groups // 2 // self.near
        self.s = lax.axis_index("seq")
        b = lax.axis_index("batch")
        self.c = b % 2
        self.zl = b // 2 % self.near
        self.zh = b // 2 // self.near

    def at(self, s=0, zl=0, zh=0, c=0):
        return (flip(self.s, s), (flip(self.zh, zh) * self.near + flip(self.zl, zl)) * 2 + flip(self.c, c))

    def heads_at(self, index, per, width):
        outer = self.far if self.near > 1 else 1
        run = width // outer
        return (((self.s * outer + index // run) * self.near + self.zl) * run + index % run) // per

    def channel_runs(self, width):
        outer = self.far if self.near > 1 else 1
        run = width // outer
        runs = []
        for i in range(outer):
            first = ((self.s * outer + i) * self.near + self.zl) * run
            runs.append((pl.ds(pl.multiple_of(first, 128), run), slice(i * run, (i + 1) * run)))
        return runs

    def column_runs(self, s, zl, width):
        outer = self.far if self.near > 1 else 1
        run = width // (2 * outer)
        runs = []
        for part in range(2):
            for i in range(outer):
                first = part * E + ((s * outer + i) * self.near + zl) * run
                runs.append((pl.ds(pl.multiple_of(first, 128), run), pl.ds((part * outer + i) * run, run)))
        return runs

    def partners(self):
        cube = [self.at(s=o // self.near, zl=o % self.near) for o in range(1, self.peers * self.near)]
        return cube, [self.at(zh=o) for o in range(1, self.far)], [self.at(c=1)]


def greet(devices):
    barrier = pltpu.get_barrier_semaphore()
    for device in devices:
        pl.semaphore_signal(barrier, inc=1, device_id=device, device_id_type=MESH)
    pl.semaphore_wait(barrier, len(devices))


class Mover:
    def __init__(self, send, recv, local):
        self.send, self.recv, self.local = send, recv, local
        self.sent, self.kept = 0, 0
        self.open = []

    def plan(self, src, dst, device):
        copy = pltpu.make_async_remote_copy(
            src_ref=src, dst_ref=dst, send_sem=self.send.at[self.sent], recv_sem=self.recv.at[self.sent],
            device_id=device, device_id_type=MESH,
        )
        self.sent += 1
        self.open.append(copy)
        return copy

    def put(self, src, dst, device):
        copy = self.plan(src, dst, device)
        copy.start()
        return copy

    def plan_keep(self, src, dst):
        self.kept += 1
        return pltpu.make_async_copy(src, dst, self.local.at[self.kept - 1])

    def keep(self, src, dst):
        copy = self.plan_keep(src, dst)
        copy.start()
        return copy

    def close(self):
        for copy in self.open:
            copy.wait_send()


def run_paths(paths):
    paths = list(paths)
    while paths:
        alive = []
        for path in paths:
            try:
                next(path)
                alive.append(path)
            except StopIteration:
                pass
        paths = alive


def turn(paths):
    for path in paths:
        next(path, None)


def bits_of(peers):
    return [1 << i for i in range(peers.bit_length() - 1)]


def combos(bits):
    out = [0]
    for bit in reversed(bits):
        out = [bit | o for o in out] + out
    return out


def cot_order(near):
    bits = bits_of(lax.axis_size("seq"))
    return bits if near else bits[::-1]


def left_over(order):
    return [h for h in combos(order[:-1]) if len(order) > 1 and h & order[-2]]


class Late:
    def __init__(self, src, dst, out_src, out_dst, send, recv):
        me = self.me = Place()
        self.mover = Mover(send, recv, None)
        self.copies, self.far, self.forward = [], [], []
        for o in range(me.near):
            order = cot_order(o)
            for h in left_over(order):
                at = (flip(me.zl, o), flip(me.s, h))
                self.copies.append(self.mover.plan(src.at[at], dst.at[at], me.at(s=order[-1])))
        half = out_src.shape[2] // 2
        for o in range(1, me.far):
            at = (me.zh, me.c, pl.ds(half, half))
            self.far.append(self.mover.plan(out_src.at[at], out_dst.at[at], me.at(zh=o)))
        for o in range(1, me.far):
            at = (flip(me.zh, o), me.c, pl.ds(half, half))
            self.forward.append(self.mover.plan(out_dst.at[at], out_dst.at[at], me.at(c=1)))

    def start(self):
        _, far, sibling = self.me.partners()
        greet([self.me.at(s=bit) for bit in sorted({cot_order(o)[-1] for o in range(self.me.near)})] + far + sibling)
        for copy in self.far + self.copies:
            copy.start()

    def middle(self):
        for far, forward in zip(self.far, self.forward):
            far.wait_recv()
            forward.start()

    def end(self):
        for copy in self.copies + self.forward:
            copy.wait_recv()
        self.mover.close()


def gather_kernel(
    in_ref, out_ref, cot_ref, inputs_ref, gain_ref, step_ref, lengths_ref, width_ref,
    w_ref, o_ref, x_ref, ct_ref, m_ref, inv_ref, rows_ref, steps_ref, meta_ref, send, recv, local,
):
    prepare(inputs_ref, gain_ref, step_ref, lengths_ref, width_ref, rows_ref, inv_ref, steps_ref, meta_ref)
    cot_ref = cot_ref.at[0]
    me = Place()
    s, zl, zh, c = me.s, me.zl, me.zh, me.c
    columns = w_ref.shape[-1] - KEYS - STEP_PAD
    mine, shared = pl.ds(0, columns), pl.ds(columns, KEYS + STEP_PAD)
    cube, far, sibling = me.partners()
    greet(cube + far + sibling)
    mover = Mover(send, recv, local)
    bits = bits_of(me.peers)

    def plane_path(src, dst, order, near, skip=()):
        view = dst.at[flip(zl, near)]
        if near:
            copy = mover.put(src, dst.at[zl, s], me.at(zl=near))
            yield
            copy.wait_recv()
        else:
            own = mover.keep(src, view.at[s])
        held = [0]
        for bit in order:
            copies = []
            for h in held:
                if bit == order[-1] and h in skip:
                    continue
                at = view.at[flip(s, h)]
                copies.append(mover.put(at if near or h else src, at if near else dst.at[zl, flip(s, h)], me.at(s=bit)))
            held = held + [h ^ bit for h in held]
            yield
            for copy in copies:
                copy.wait_recv()
        if not near:
            own.wait()

    def meta_path():
        own = mover.keep(meta_ref, m_ref.at[zl])
        near = [mover.put(meta_ref, m_ref.at[zl], me.at(zl=o)) for o in range(1, me.near)]
        yield
        own.wait()
        for copy in near:
            copy.wait_recv()

    def key_path():
        block = w_ref.at[s, zh, zl, c]
        parts = [
            (in_ref.at[:, pl.ds(2 * E, KEYS)], block.at[:, pl.ds(columns, KEYS)]),
            (steps_ref, block.at[:, pl.ds(columns + KEYS, STEP_PAD)]),
        ]
        own = [mover.keep(*part) for part in parts]
        copies = [mover.put(*part, me.at(zh=o)) for o in range(1, me.far) for part in parts]
        yield
        for copy in own:
            copy.wait()
        for copy in copies:
            copy.wait_recv()
        block = w_ref.at[s, :, zl, c, :, shared]
        copies = [mover.put(block, block, me.at(zl=o)) for o in range(1, me.near)]
        yield
        for copy in copies:
            copy.wait_recv()
        held = [0]
        for bit in bits:
            copies = []
            for h in held:
                block = w_ref.at[flip(s, h), :, :, c, :, shared]
                copies.append(mover.put(block, block, me.at(s=bit)))
            held = held + [h ^ bit for h in held]
            yield
            for copy in copies:
                copy.wait_recv()
        block = w_ref.at[:, :, :, c, :, shared]
        copy = mover.put(block, block, me.at(c=1))
        yield
        copy.wait_recv()

    def spread_path(copies, view):
        last = []
        for o, copy in copies:
            yield
            copy.wait_recv()
            last.append(mover.put(view(flip(zh, o)), view(flip(zh, o)), me.at(c=1)))
        return last

    def out_path():
        own = mover.keep(out_ref, o_ref.at[zh, c])
        part = pl.ds(0, out_ref.shape[0] // 2)
        copies = [(o, mover.put(out_ref.at[part], o_ref.at[zh, c, part], me.at(zh=o))) for o in range(1, me.far)]
        first = mover.put(out_ref, o_ref.at[zh, c], me.at(c=1))
        last = yield from spread_path(copies, lambda h: o_ref.at[h, c, part])
        yield
        own.wait()
        for copy in last + [first]:
            copy.wait_recv()

    def weight_path():
        moves = {}
        for step in range(me.peers):
            for o in range(me.near):
                to_s, to_zl = flip(s, step), flip(zl, o)
                for src, dst in me.column_runs(to_s, to_zl, columns):
                    src = in_ref.at[:, src]
                    dst = w_ref.at[s, zh, zl, c, :, dst]
                    if step or o:
                        copy = mover.put(src, dst, me.at(s=step, zl=o))
                    else:
                        copy = mover.keep(src, dst)
                    moves.setdefault(step, []).append(copy)
        pieces = []
        for step in range(me.peers):
            yield
            for i, copy in enumerate(moves[step]):
                if step == 0 and i < len(moves[0]) // me.near:
                    copy.wait()
                else:
                    copy.wait_recv()
            block = w_ref.at[flip(s, step), zh, :, c, :, mine]
            copies = [(o, mover.put(block, block, me.at(zh=o))) for o in range(1, me.far)]
            pieces.append((step, copies, mover.put(block, block, me.at(c=1))))
        last = []
        for step, copies, first in pieces:
            last.append(first)
            last += yield from spread_path(copies, lambda h, step=step: w_ref.at[flip(s, step), h, :, c, :, mine])
        yield
        for copy in last:
            copy.wait_recv()

    own_x = plane_path(rows_ref, x_ref, bits, 0)
    near_x = [plane_path(rows_ref, x_ref, bits[::-1], o) for o in range(1, me.near)]
    own_c, *near_c = [plane_path(cot_ref, ct_ref, cot_order(o), o, left_over(cot_order(o))) for o in range(me.near)]
    keys, weights, outs, extra = key_path(), weight_path(), out_path(), meta_path()
    near = near_x + near_c
    turn([keys, own_x, own_c, weights] + near + [outs])
    turn([keys, own_x, own_c, keys] + [weights] * me.peers + [keys] + near + [extra])
    turn([own_x, own_c] + near + [keys, outs, weights, keys, weights])
    run_paths([weights, extra, keys, outs, own_x, own_c] + near)
    mover.close()


def remote_params(identity, mib):
    return pltpu.CompilerParams(collective_id=identity, has_side_effects=True, vmem_limit_bytes=mib * 2**20)


def sems(copies, kept):
    return [pltpu.SemaphoreType.DMA((copies,)), pltpu.SemaphoreType.DMA((copies,)), pltpu.SemaphoreType.DMA((kept,))]


def prepare(x_ref, gain_ref, step_ref, lengths_ref, width_ref, normed_ref, inv_ref, steps_ref, meta_ref):
    x = x_ref[0].astype(f32)
    inv = lax.rsqrt(jnp.mean(x * x, axis=1, keepdims=True) + epsilon)
    normed_ref[...] = (x * inv * gain_ref[...]).astype(bf16)
    inv_ref[...] = jnp.broadcast_to(inv, inv_ref.shape)
    steps_ref[...] = jnp.zeros_like(steps_ref)
    steps_ref[:, :H] = step_ref[...]
    lanes = iota(meta_ref.shape, 1)
    meta = jnp.where(lanes == DOCS, width_ref[0], 0)
    for i in range(DOCS):
        meta = jnp.where(lanes == i, lengths_ref[0, i], meta)
    meta_ref[...] = meta


def gather(in_w, out_w, cot, inputs, gain, step_w, lengths, head_width):
    me = Place()
    peers, near, far = me.peers, me.near, me.far
    shape = lambda lead, part: jax.ShapeDtypeStruct(lead + part, bf16)
    rows = inputs.shape[1:]
    columns = 2 * E // (peers * near)
    runs = 2 * (far if near > 1 else 1)
    copies = runs * (peers * near - 1) + (peers + 1) * (2 * far - 1) + 2 * (near * peers - 1)
    copies -= sum(len(left_over(cot_order(o))) for o in range(near))
    copies += 2 * near + peers + 2 * far - 4
    smem = pl.BlockSpec(memory_space=pltpu.SMEM)
    return pl.pallas_call(
        gather_kernel,
        out_shape=[
            shape((peers, far, near, 2), (in_w.shape[0], columns + KEYS + STEP_PAD)),
            shape((far, 2), out_w.shape),
            shape((near, peers), rows),
            shape((near, peers), rows),
            jax.ShapeDtypeStruct((near, 8, LANES), jnp.int32),
            jax.ShapeDtypeStruct((rows[0], LANES), f32),
        ],
        in_specs=[HBM] * 3 + [VMEM] * 3 + [smem] * 2,
        out_specs=[HBM] * 5 + [VMEM],
        scratch_shapes=[
            pltpu.VMEM(rows, bf16), pltpu.VMEM((in_w.shape[0], STEP_PAD), bf16), pltpu.VMEM((8, LANES), jnp.int32)
        ]
        + sems(copies, runs + 6),
        compiler_params=remote_params(0, 58),
        name="gather_all",
    )(in_w, out_w, cot, inputs, gain, step_w, lengths, head_width)


def total_kernel(part_ref, gated_ref, chan_ref, grad_ref, sum_ref, mixed_ref, mine, box, send, recv, local):
    me = Place()
    cube = me.partners()[0]
    greet(cube)
    mover = Mover(send, recv, local)
    chunks = part_ref.shape[0] // 2
    tiles = [slice(lane, lane + LANES) for lane in range(0, gated_ref.shape[1], LANES)]
    mine[...] = part_ref[...]

    def products(i, carry):
        at = pl.ds(pl.multiple_of(i * CHUNK, CHUNK), CHUNK)
        cross = jnp.zeros((CHUNK, LANES), f32)
        for lanes in tiles:
            cross = cross + gated_ref[at, lanes] * (grad_ref[at, lanes] * chan_ref[5:6, lanes])
        row = pl.ds(chunks + i, 1)
        mine[row, :] = jnp.sum(cross.T, axis=0, keepdims=True) * part_ref[row, :]
        return carry

    lax.fori_loop(0, chunks, products, 0)
    copies = [mover.put(mine, box.at[i], device) for i, device in enumerate(cube)]
    total = mine[...]
    for i, copy in enumerate(copies):
        copy.wait_recv()
        total = total + box[i]
    sum_ref[...] = total

    def mix(i, carry):
        at = pl.ds(pl.multiple_of(i * CHUNK, CHUNK), CHUNK)
        inv = lax.rsqrt(jnp.broadcast_to(sum_ref[pl.ds(i, 1), :], (CHUNK, CHUNK)).T + epsilon)
        for lanes in tiles:
            mixed_ref[at, lanes] = (gated_ref[at, lanes] * inv * chan_ref[5:6, lanes]).astype(bf16)
        return carry

    lax.fori_loop(0, chunks, mix, 0)
    mover.close()


def cube_total(part, gated, chan, grad):
    me = Place()
    count = me.peers * me.near - 1
    return pl.pallas_call(
        total_kernel,
        out_shape=[jax.ShapeDtypeStruct(part.shape, f32), jax.ShapeDtypeStruct(gated.shape, bf16)],
        in_specs=[VMEM] * 4,
        out_specs=[VMEM] * 2,
        scratch_shapes=[pltpu.VMEM(part.shape, f32), pltpu.VMEM((count,) + part.shape, f32)] + sems(count, 1),
        compiler_params=remote_params(1, 12),
        name="cube_total",
    )(part, gated, chan, grad)


def add_rows(out, parts):
    shape = out.shape
    tile = min(16, shape[-2])
    lead = [()]
    for size in shape[:-2]:
        lead = [l + (i,) for l in lead for i in range(size)]
    for l in lead:

        def step(i, carry, l=l):
            at = l + (pl.ds(pl.multiple_of(i * tile, tile), tile), slice(None))
            total = parts[0][at].astype(f32)
            for part in parts[1:]:
                total = total + part[at].astype(f32)
            out[at] = total.astype(out.dtype)
            return carry

        lax.fori_loop(0, shape[-2] // tile, step, 0)


def scatter_kernel(
    gn_ref, gw_ref, b_ref, u_ref, p_ref, gain_ref, og_ref, ow_ref, ob_ref, ok_ref, ou_ref,
    n_own, n_box, n_near, b_own, b_box, b_near, w_own, w_box, w_far,
    k_own, k_box, k_near, k_far, k_bits, u_box, send, recv, local,
):
    me = Place()
    s, zl, zh, c = me.s, me.zl, me.zh, me.c
    cube, far, sibling = me.partners()
    greet(cube + far + sibling)
    mover = Mover(send, recv, local)
    bits = bits_of(me.peers)
    columns = w_own.shape[-1]
    mine, shared = pl.ds(0, columns), pl.ds(columns, k_own.shape[-1])

    def rows_path(src, own, box, near_box, out, order, near, arrivals, done=0):
        own, box = own.at[near], box.at[near]
        copies, loads = [], []
        if done:
            half = me.peers // 4
            for j in range(half):
                copies.append(mover.put(src.at[near, j], box.at[j], me.at(s=order[1])))
                loads.append(mover.keep(src.at[near, half + j], own.at[half + j]))
        else:
            at_zl = src.at[flip(zl, near)]
            for j, o in enumerate(combos(order[1:])):
                copies.append(mover.put(at_zl.at[flip(s, order[0] ^ o)], box.at[j], me.at(s=order[0])))
                loads.append(mover.keep(at_zl.at[flip(s, o)], own.at[j]))
        base = 0
        for i in range(done, len(order)):
            rest = order[i + 1 :]
            count = 1 << len(rest)
            offset = (1 << (len(order) - 1)) - count
            coming = []
            for j in range(count):
                yield
                copies[j].wait_recv()
                if i == done:
                    loads[j].wait()
                if rest or near:
                    add_rows(own.at[offset + j], [own.at[offset + j], box.at[base + j]])
                if rest and j < count // 2:
                    coming.append(mover.put(own.at[offset + j], box.at[base + count + j], me.at(s=rest[0])))
            copies = coming
            last = base
            base += count
        end = (1 << (len(order) - 1)) - 1
        if near:
            arrivals.append(mover.put(own.at[end], near_box.at[near - 1], me.at(zl=near)))
            yield
        else:
            yield
            for _ in range(me.near - 1):
                arrivals.pop(0).wait_recv()
            add_rows(out, [own.at[end], box.at[last]] + [near_box.at[o - 1] for o in range(1, me.near)])

    def weight_path():
        order = [(o, k) for o in range(1, me.far) for k in range(me.peers)] + [(0, k) for k in range(me.peers)]
        loads, copies = {}, {}
        for o, k in order:
            copies[o, k] = mover.put(gw_ref.at[flip(s, k), flip(zh, o), :, 1 - c, :, mine], w_box.at[o, k], me.at(c=1))
            loads[o, k] = mover.keep(gw_ref.at[flip(s, k), flip(zh, o), :, c, :, mine], w_own.at[o, k])
        far_copies = {}
        for o, k in order:
            yield
            loads[o, k].wait()
            copies[o, k].wait_recv()
            if o:
                add_rows(w_own.at[o, k], [w_own.at[o, k], w_box.at[o, k]])
                far_copies[o, k] = mover.put(w_own.at[o, k], w_far.at[o - 1, k], me.at(zh=o))
        ends, kept = [], []
        for k in range(me.peers):
            yield
            for o in range(1, me.far):
                far_copies[o, k].wait_recv()
            parts = [w_own.at[0, k], w_box.at[0, k]] + [w_far.at[o - 1, k] for o in range(1, me.far)]
            add_rows(w_own.at[0, k], parts)
            for o in range(me.near):
                for whole, part in me.column_runs(s, zl, columns):
                    src = w_own.at[0, k, flip(zl, o), :, part]
                    if k or o:
                        ends.append(mover.put(src, ow_ref.at[:, whole], me.at(s=k, zl=o)))
                    else:
                        kept.append(mover.keep(src, ow_ref.at[:, whole]))
        yield
        for copy in kept:
            copy.wait()
        for copy in ends:
            copy.wait_recv()

    def key_path():
        blocks = combos(bits)
        copies, loads = [], []
        for j, o in enumerate(blocks):
            copies.append(mover.put(gw_ref.at[flip(s, o), :, :, 1 - c, :, shared], k_box.at[j], me.at(c=1)))
            loads.append(mover.keep(gw_ref.at[flip(s, o), :, :, c, :, shared], k_own.at[j]))
        half = me.peers // 2
        sent = []
        for j in range(me.peers):
            yield
            loads[j].wait()
            copies[j].wait_recv()
            add_rows(k_own.at[j], [k_own.at[j], k_box.at[j]])
            if j < half:
                sent.append(mover.put(k_own.at[j], k_bits.at[j], me.at(s=bits[0])))
        base = 0
        for i, bit in enumerate(bits):
            count = me.peers >> (i + 1)
            offset = me.peers - count
            coming = []
            for j in range(count):
                yield
                sent[j].wait_recv()
                add_rows(k_own.at[offset + j], [k_own.at[offset + j], k_bits.at[base + j]])
                if i + 1 < len(bits) and j < count // 2:
                    coming.append(mover.put(k_own.at[offset + j], k_bits.at[base + count + j], me.at(s=bits[i + 1])))
            base += count
            sent = coming
        end = k_own.at[me.peers - 1]
        copies = [mover.put(end.at[:, flip(zl, o)], k_near.at[o - 1], me.at(zl=o)) for o in range(1, me.near)]
        yield
        for copy in copies:
            copy.wait_recv()
        add_rows(end.at[:, zl], [end.at[:, zl]] + [k_near.at[o - 1] for o in range(1, me.near)])
        copies = [mover.put(end.at[flip(zh, o), zl], k_far.at[o - 1], me.at(zh=o)) for o in range(1, me.far)]
        yield
        for copy in copies:
            copy.wait_recv()
        add_rows(ok_ref, [end.at[zh, zl]] + [k_far.at[o - 1] for o in range(1, me.far)])

    def small_path():
        turns = [me.at(c=1)] + [me.at(zl=o) for o in bits_of(me.near)]
        turns += [me.at(s=o) for o in bits] + [me.at(zh=o) for o in bits_of(me.far)]
        u_box[0] = u_ref[...]
        u_box[0, 6:7, : p_ref.shape[1]] = p_ref[...] / gain_ref[...]
        for i, device in enumerate(turns):
            copy = mover.put(u_box.at[2 * i], u_box.at[2 * i + 1], device)
            yield
            copy.wait_recv()
            u_box[2 * i + 2] = u_box[2 * i] + u_box[2 * i + 1]
        ou_ref[...] = u_box[2 * len(turns)]

    coming_n, coming_b = [], []
    grads = (gn_ref, n_own, n_box, n_near, og_ref)
    branch = (b_ref, b_own, b_box, b_near, ob_ref)
    orders = lambda o: bits if o else bits[::-1]
    near_n = [rows_path(*grads, orders(o), o, coming_n) for o in range(1, me.near)]
    near_b = [rows_path(*branch, orders(o), o, coming_b, 1) for o in range(1, me.near)]
    own_n = rows_path(*grads, orders(0), 0, coming_n)
    own_b = rows_path(*branch, orders(0), 0, coming_b, 1)
    weights, keys, small = weight_path(), key_path(), small_path()
    turn(near_b + near_n + [weights, own_n, keys, own_b, small])
    turn([weights] * (me.far * me.peers) + [keys] * me.peers + [small])
    turn(near_b + near_n + [keys, own_b, small] + near_b + near_n + [keys, small, keys, own_b, own_n])
    run_paths(near_b + near_n + [keys, small, weights, own_b, own_n])
    mover.close()


def scatter(grads, gw, branch, small, products, gain):
    me = Place()
    peers, near, far = me.peers, me.near, me.far
    tokens, width = grads.shape[2:]
    stages = len(bits_of(peers)) + len(bits_of(near)) + len(bits_of(far)) + 1
    vm = lambda *shape: pltpu.VMEM(shape, bf16)
    boxes = lambda part: pltpu.VMEM((2 * stages + 1,) + part.shape, f32)
    keys = KEYS + STEP_PAD
    rows = gw.shape[4]
    block = (near, rows, gw.shape[5] - keys)
    kblock = (near, rows, keys)
    runs = 2 * (far if near > 1 else 1)
    copies = peers * near - 1 + (2 * far - 1) * peers + runs * (peers * near - 1)
    copies += 2 * peers - 1 + near - 1 + far - 1 + stages + peers // 2 * near - 1
    kept = peers * near + far * peers + runs + peers + near * peers // 4
    same = lambda part: jax.ShapeDtypeStruct(part.shape, part.dtype)
    return pl.pallas_call(
        scatter_kernel,
        out_shape=[
            jax.ShapeDtypeStruct((tokens, width), f32),
            jax.ShapeDtypeStruct((rows, 2 * E), bf16),
            jax.ShapeDtypeStruct((tokens, width), f32),
            jax.ShapeDtypeStruct((rows, keys), f32),
            same(small),
        ],
        in_specs=[HBM] * 3 + [VMEM] * 3,
        out_specs=[VMEM, HBM, VMEM, VMEM, VMEM],
        scratch_shapes=[
            vm(near, peers // 2, tokens, width), vm(near, peers - 1, tokens, width), vm(max(near - 1, 1), tokens, width),
            vm(near, peers // 2, tokens, width), vm(near, peers // 2 - 1, tokens, width), vm(max(near - 1, 1), tokens, width),
            vm(far, peers, *block), vm(far, peers, *block), vm(max(far - 1, 1), peers, *block),
            vm(peers, far, *kblock), vm(peers, far, *kblock), vm(max(near - 1, 1), far, *kblock[1:]),
            vm(max(far - 1, 1), *kblock[1:]), vm(peers - 1, far, *kblock), boxes(small),
        ]
        + sems(copies, kept),
        compiler_params=remote_params(2, 40),
        cost_estimate=pl.CostEstimate(flops=0, bytes_accessed=250 * 10**6, transcendentals=0),
        name="scatter_all",
    )(grads, gw, branch, small, products, gain)


class Early:
    def __init__(self, b_ref, go_ref, refs):
        self.b_out, self.o_out, self.b_own, self.b_box, self.o_own, self.o_box, self.o_far, send, recv, local = refs
        me = self.me = Place()
        mover = self.mover = Mover(send, recv, local)
        bits = bits_of(me.peers)
        self.rows, self.outs, self.far = [], [], []
        for o in range(me.near):
            order = bits if o else bits[::-1]
            at_zl = b_ref.at[flip(me.zl, o)]
            for j, left in enumerate(combos(order[1:])):
                put = mover.plan(at_zl.at[flip(me.s, order[0] ^ left)], self.b_box.at[o, j], me.at(s=order[0]))
                self.rows.append((put, mover.plan_keep(at_zl.at[flip(me.s, left)], self.b_own.at[o, j]), (o, j)))
        for o in range(me.far):
            put = mover.plan(go_ref.at[flip(me.zh, o), 1 - me.c], self.o_box.at[o], me.at(c=1))
            self.outs.append((put, mover.plan_keep(go_ref.at[flip(me.zh, o), me.c], self.o_own.at[o])))
        for o in range(1, me.far):
            self.far.append(mover.plan(self.o_own.at[o], self.o_far.at[o - 1], me.at(zh=o)))

    def start(self):
        _, far, sibling = self.me.partners()
        bits = bits_of(self.me.peers)
        greet([self.me.at(s=bit) for bit in sorted({bits[0], bits[-1]})] + far + sibling)
        for put, load in self.outs:
            put.start()
            load.start()
        for put, load, _ in self.rows:
            put.start()
            load.start()

    def middle(self):
        for o, (put, load) in enumerate(self.outs):
            load.wait()
            put.wait_recv()
            if o:
                add_rows(self.o_own.at[o], [self.o_own.at[o], self.o_box.at[o]])
                self.far[o - 1].start()

    def end(self):
        for put, load, at in self.rows:
            load.wait()
            put.wait_recv()
            add_rows(self.b_out.at[at], [self.b_own.at[at], self.b_box.at[at]])
        for put in self.far:
            put.wait_recv()
        add_rows(self.o_out, [self.o_own.at[0], self.o_box.at[0]] + [self.o_far.at[o] for o in range(self.me.far - 1)])
        self.mover.close()


def finish_kernel(
    x_ref, cot_ref, gain_ref, inv_ref, og_ref, ob_ref, ow_ref, ok_ref, u_ref,
    out_ref, gx_ref, gw_ref, gs_ref, gc_ref, gb_ref, gp_ref, gn_ref, g0_ref, g1_ref, g2_ref,
):
    x = x_ref[0].astype(f32)
    out_ref[0] = (x + ob_ref[...]).astype(bf16)
    inv = inv_ref[:, :1]
    scaled = og_ref[...] * gain_ref[...]
    dot = jnp.mean(scaled * x, axis=1, keepdims=True)
    gx_ref[0] = inv * scaled - x * (inv * inv * inv * dot) + cot_ref[0].astype(f32)
    gw_ref[:, : 2 * E] = ow_ref[...].astype(f32)
    gw_ref[:, 2 * E :] = ok_ref[:, :KEYS]
    gs_ref[...] = ok_ref[:, KEYS : KEYS + H]
    gc_ref[...] = u_ref[:CONV, :]
    gb_ref[...] = u_ref[CONV : CONV + 1, :]
    gn_ref[...] = u_ref[5:6, :E]
    gp_ref[...] = u_ref[6:7, : gp_ref.shape[1]]
    for i, ref in enumerate((g0_ref, g1_ref, g2_ref)):
        ref[...] = u_ref[7:8, i * LANES : i * LANES + H]


def finish(inputs, cotangent, gain, inv, sums):
    tokens, width = inputs.shape[1:]
    og, ow, ob, ok, u = sums
    shape = lambda *dims: jax.ShapeDtypeStruct(dims, f32)
    rows = ow.shape[0]
    return pl.pallas_call(
        finish_kernel,
        out_shape=[
            jax.ShapeDtypeStruct(inputs.shape, bf16), shape(*inputs.shape), shape(rows, 2 * E + KEYS), shape(rows, H),
            shape(CONV, E + KEYS), shape(1, E + KEYS), shape(1, width), shape(1, E), shape(1, H), shape(1, H), shape(1, H),
        ],
        in_specs=[VMEM] * 9,
        out_specs=[VMEM] * 11,
        compiler_params=pltpu.CompilerParams(vmem_limit_bytes=32 * 2**20),
        name="finish",
    )(inputs, cotangent, gain, inv, og, ob, ow, ok, u)


def body(
    inputs, cotangent, doc_lengths, head_width, pre_gain, in_weight, step_weight, conv_weight, conv_bias,
    step_bias, decay_log, skip_gain, norm_gain, out_weight,
):
    me = Place()
    peers, near, far = me.peers, me.near, me.far
    tokens, width = inputs.shape[1:]
    span = tokens * peers
    length = span * near
    heads = H // (peers * near)
    inner = heads * P_SIZE
    rows = in_weight.shape[0]
    row = lambda vector: vector[None, :]

    in_w, out_w, normed, cot_all, meta, inv = gather(
        in_weight, out_weight, cotangent, inputs, row(pre_gain), step_weight, doc_lengths, head_width
    )
    in_w = in_w.reshape(width, -1)
    normed = normed.reshape(length, width)
    meta = meta[:, 0, :8]

    params = (conv_weight, row(conv_bias), row(norm_gain), row(step_bias), row(decay_log), row(skip_gain))
    projected = mm(normed, in_w, NN)
    *kept, gated, states, part, chan, head_vec, cot_all, out_w = mixer_forward(
        meta, projected, params, cot_all, out_w, span, heads
    )
    out_w = out_w.reshape(inner, width)
    cot_all = cot_all.reshape(length, width)
    grad_mixed = mm(cot_all, out_w, NT)
    sums, mixed = cube_total(part, gated, chan, grad_mixed)
    branch = mm(mixed, out_w, NN).astype(bf16)
    grad_out = mm(mixed, cot_all, TN).astype(bf16)
    grad_cols, small, branch, grad_out_weight = mixer_backward(
        meta, projected, grad_mixed, chan, conv_weight, head_vec, (*kept, states), sums,
        branch.reshape(near, peers, tokens, width), grad_out.reshape(far, 2, -1, width), span, heads,
    )
    grad_in = mm(normed, grad_cols, TN).astype(bf16)
    grad_normed = mm(grad_cols, in_w, NT)
    products = jnp.sum(grad_normed * normed.astype(f32), axis=0)
    summed = scatter(
        grad_normed.astype(bf16).reshape(near, peers, tokens, width),
        grad_in.reshape(peers, far, near, 2, rows, -1),
        branch,
        small,
        row(products),
        row(pre_gain),
    )
    outs = finish(inputs, cotangent, row(pre_gain), inv, summed)
    output, grad_inputs, grad_in_weight, grad_step_weight, grad_conv_weight = outs[:5]
    grad_conv_bias, grad_pre_gain, grad_norm_gain, grad_step_bias, grad_decay_log, grad_skip = [o[0] for o in outs[5:]]
    return (
        output, grad_inputs, grad_pre_gain, grad_in_weight, grad_step_weight, grad_conv_weight, grad_conv_bias,
        grad_step_bias, grad_decay_log, grad_skip, grad_norm_gain, grad_out_weight,
    )


def solution(mesh):
    both = P(("seq", "batch"), None)
    tok = P("batch", "seq", None)
    in_specs = (
        tok, tok, P("batch", None), P("batch"), P(), both, both, P(), P(), P(), P(), P(), P(), both,
    )
    out_specs = (tok, tok, P(), both, both, P(), P(), P(), P(), P(), P(), both)
    return jax.shard_map(body, mesh=mesh, in_specs=in_specs, out_specs=out_specs, check_vma=False)
```

```python
from functools import partial

import jax
import jax.numpy as jnp
from jax import lax
from jax.experimental import pallas as pl
from jax.experimental.pallas import tpu as pltpu
from jax.sharding import PartitionSpec as P

H = 64
P_SIZE = 64
N = 128
CONV = 4
DOCS = 4
E = 4096
KEYS = 2 * N
STEP_PAD = 128
CHUNK = 128
LANES = 128
epsilon = 1e-05
f32 = jnp.float32
bf16 = jnp.bfloat16


def mm(a, b, dims, precision=None):
    return lax.dot_general(a, b, (dims, ((), ())), precision=precision, preferred_element_type=f32)


NN = ((1,), (0,))
NT = ((1,), (1,))
TN = ((0,), (0,))
exact = lax.Precision.HIGHEST


def pair_cols(low, col, first):
    return jnp.where(low, col[:, first : first + 1], col[:, first + 1 : first + 2])


def iota(shape, axis):
    return lax.broadcasted_iota(jnp.int32, shape, axis)


class Docs:
    def __init__(self, meta_ref, chunk, span):
        per = span // CHUNK
        seq = chunk // per
        self.start = (chunk - seq * per) * CHUNK
        self.ends = []
        total = 0
        for i in range(DOCS - 1):
            total = total + meta_ref[seq, i]
            self.ends.append(total)
        self.count = meta_ref[seq, DOCS]
        self.pos = self.start + iota((CHUNK, 1), 0)
        self.doc = self.index(self.pos)

    def index(self, places):
        found = (places >= self.ends[0]).astype(jnp.int32)
        for end in self.ends[1:]:
            found = found + (places >= end).astype(jnp.int32)
        return found

    def lag(self, by):
        source = self.pos - by
        return ((source >= 0) & (self.index(source) == self.doc)).astype(f32)

    def flow(self):
        return ((self.start > 0) & (self.index(self.start - 1) == self.doc)).astype(f32)

    def row(self):
        return self.index(self.start + iota((1, CHUNK), 1))

    def tail(self):
        return (self.doc == self.index(self.start + CHUNK - 1)).astype(f32)


def shift_down(rows, before, by):
    if by == 0:
        return rows
    moved = pltpu.roll(rows, by, 0)
    top = jnp.where(iota((8, 1), 0) < by, pltpu.roll(before, by, 0), moved[:8])
    return jnp.concatenate([top, moved[8:]], axis=0)


def shift_up(rows, after, by):
    if by == 0:
        return rows
    size = rows.shape[0]
    moved = pltpu.roll(rows, size - by, 0)
    end = jnp.where(iota((8, 1), 0) >= 8 - by, pltpu.roll(after, 8 - by, 0), moved[size - 8 :])
    return jnp.concatenate([moved[: size - 8], end], axis=0)


def silu_slope(v, sig):
    return sig * (1.0 + v * (1.0 - sig))


def own_parameters(chan_ref, head_ref, conv_ref, bias_ref, norm_ref, step_b_ref, decay_ref, skip_ref, heads):
    me = Place()
    inner = heads * P_SIZE
    for whole, part in me.channel_runs(inner):
        chan_ref[:CONV, part] = conv_ref[:, whole]
        chan_ref[CONV : CONV + 1, part] = bias_ref[:, whole]
        chan_ref[5:6, part] = norm_ref[:, whole]
    ids = me.heads_at(iota((1, inner), 1), P_SIZE, inner)
    chosen = (iota((H, inner), 0) == ids).astype(f32)
    chan_ref[6:7, :] = mm(jnp.broadcast_to(skip_ref[...], (8, H)), chosen, NN, exact)[:1]
    chan_ref[7:8, :] = ids.astype(f32)
    lanes = iota((1, LANES), 1)
    ids = jnp.where(lanes < heads, me.heads_at(lanes, 1, heads), -1)
    chosen = (iota((H, LANES), 0) == ids).astype(f32)
    head_ref[...] = jnp.zeros_like(head_ref)
    head_ref[:1, :] = mm(jnp.broadcast_to(step_b_ref[...], (8, H)), chosen, NN, exact)[:1]
    head_ref[1:2, :] = mm(jnp.broadcast_to(jnp.exp(decay_ref[...]), (8, H)), chosen, NN, exact)[:1]
    head_ref[2:3, :] = ids.astype(f32)


def whole_sums(out_ref, chan_sums, key_sums, head_sums, head_ref, chan_ref, heads):
    me = Place()
    inner = heads * P_SIZE
    out_ref[...] = jnp.zeros_like(out_ref)
    for whole, part in me.channel_runs(inner):
        out_ref[:6, whole] = chan_sums[:6, part]
    out_ref[:5, E:] = key_sums[:5, :]
    chosen = (iota((H, LANES), 0) == head_ref[2:3, :].astype(jnp.int32)).astype(f32)
    steps = mm(head_sums[...], chosen, NT, exact)
    chosen = (iota((H, inner), 0) == chan_ref[7:8, :].astype(jnp.int32)).astype(f32)
    skips = mm(chan_sums[...], chosen, NT, exact)
    out_ref[7:8, :H] = steps[:1]
    out_ref[7:8, LANES : LANES + H] = steps[1:2]
    out_ref[7:8, 2 * LANES : 2 * LANES + H] = skips[6:7]


def forward_kernel(
    meta_ref, rows_ref, w_ref, conv_ref, bias_ref, norm_ref, step_b_ref, decay_ref, skip_ref, cot_in, out_in,
    val_out, key_out, vsum_ref, ksum_ref, raw_ref, cum_ref, y_ref, gated_ref, state_ref, sums_ref, chan_ref, head_ref,
    cot_out, out_out, proj_out, state, last_v, last_k, proj_v, send, recv,
    *, span, heads,
):
    i = pl.program_id(0)
    chunks = pl.num_programs(0)
    inner = heads * P_SIZE
    late = Late(cot_in, cot_out, out_in, out_out, send, recv)

    @pl.when(i == 0)
    def _():
        late.start()
        own_parameters(chan_ref, head_ref, conv_ref, bias_ref, norm_ref, step_b_ref, decay_ref, skip_ref, heads)
        state[...] = jnp.zeros_like(state)
        last_v[...] = jnp.zeros_like(last_v)
        last_k[...] = jnp.zeros_like(last_k)

    @pl.when(i % 2 == 0)
    def _():
        for lane in range(0, w_ref.shape[1], 256):
            lanes = slice(lane, min(lane + 256, w_ref.shape[1]))
            proj_v[:, lanes] = mm(rows_ref[...], w_ref[:, lanes], NN)

    proj_ref = proj_v.at[pl.ds(pl.multiple_of(i % 2 * CHUNK, CHUNK), CHUNK)]
    proj_out[...] = proj_ref[...]

    @pl.when(i == chunks - 1)
    def _():
        late.middle()

    docs = Docs(meta_ref, i, span)
    lags = [docs.lag(by) for by in range(1, CONV)]

    def convolve(rows, before, weight, bias):
        total = bias + weight[CONV - 1 :] * rows
        for by in range(1, CONV):
            at = CONV - 1 - by
            total = total + weight[at : at + 1] * (shift_down(rows, before, by) * lags[by - 1])
        return total

    rows_v = proj_ref[:, inner : 2 * inner].astype(bf16).astype(f32)
    vsum = convolve(rows_v, last_v[...], chan_ref[:CONV, :], chan_ref[CONV : CONV + 1, :])
    last_v[...] = rows_v[CHUNK - 8 :]
    vsum_ref[...] = vsum
    val_out[...] = (vsum * jax.nn.sigmoid(vsum)).astype(bf16)
    rows_k = proj_ref[:, 2 * inner : 2 * inner + KEYS].astype(bf16).astype(f32)
    ksum = convolve(rows_k, last_k[...], conv_ref[:, E:], bias_ref[:, E:])
    last_k[...] = rows_k[CHUNK - 8 :]
    ksum_ref[...] = ksum
    keys = (ksum * jax.nn.sigmoid(ksum)).astype(bf16)
    key_out[...] = keys

    rows = iota((CHUNK, CHUNK), 0)
    cols = iota((CHUNK, CHUNK), 1)
    chosen = (rows == head_ref[2:3, :].astype(jnp.int32)).astype(f32)
    raw = mm(proj_ref[:, 2 * inner + KEYS :], chosen, NN, exact) + head_ref[:1, :]
    raw_ref[...] = raw
    dt = jax.nn.softplus(raw)
    cum = mm((rows >= cols).astype(f32), -dt * head_ref[1:2, :], NN, exact)
    cum_ref[...] = cum
    cum_t = cum.T
    dt_t = dt.T

    state_ref[0] = state[...].astype(bf16)
    bias = jnp.where((docs.doc == docs.row()) & (rows >= cols), 0.0, -1e30)
    carry_w = docs.flow() * jnp.exp(cum)
    final_w = docs.tail() * jnp.exp(cum[CHUNK - 1 :, :] - cum) * dt
    gain = carry_w[CHUNK - 1 :, :]
    low = cols < P_SIZE
    low_row = low[:1]
    write = keys[:, :N]
    read = keys[:, N:]
    write_t = write.astype(f32).T.astype(bf16)
    scores = mm(read, write, NT)
    square = jnp.zeros((CHUNK, LANES), f32)
    count = docs.count.astype(f32)
    for pair in range(heads // 2):
        first = 2 * pair
        lanes = slice(pair * 128, pair * 128 + 128)
        xf = val_out[:, lanes].astype(f32)
        weights = []
        for h in (first, first + 1):
            decay = jnp.exp(cum[:, h : h + 1] - cum_t[h : h + 1, :] + bias)
            weights.append((decay * scores * dt_t[h : h + 1, :]).astype(bf16))
        stacked = jnp.concatenate(
            [jnp.where(low, xf, 0.0).astype(bf16), jnp.where(low, 0.0, xf).astype(bf16)], axis=0
        )
        old = state[:, lanes]
        y = mm(jnp.concatenate(weights, axis=1), stacked, NN)
        y = y + pair_cols(low, carry_w, first) * mm(read, old.astype(bf16), NN)
        y = y + chan_ref[6:7, lanes] * xf
        y = jnp.where(chan_ref[7:8, lanes] < count, y, 0.0)
        y_ref[:, lanes] = y
        state[:, lanes] = pair_cols(low_row, gain, first) * old + mm(
            write_t, (pair_cols(low, final_w, first) * xf).astype(bf16), NN
        )
        gate = proj_ref[:, lanes]
        gated = y * (gate * jax.nn.sigmoid(gate))
        gated_ref[:, lanes] = gated
        square = square + gated * gated
    share = 1.0 / (count * P_SIZE)
    sums_ref[pl.ds(i, 1), :] = jnp.sum(square.T, axis=0, keepdims=True) * share
    sums_ref[pl.ds(chunks + i, 1), :] = jnp.full((1, LANES), share, f32)

    @pl.when(i == chunks - 1)
    def _():
        late.end()


def backward_kernel(
    meta_ref, proj_ref, grad_ref, chan_ref, conv_ref, head_ref,
    val_ref, key_ref, vsum_ref, ksum_ref, raw_ref, cum_ref, y_ref, state_ref, sums_ref, branch_ref, go_ref,
    cols_ref, all_sums, b_out, o_out,
    chan_sums, key_sums, head_sums, dstate, dv, next_v, next_k, next_lags, *early_refs,
    span, heads,
):
    chunks = pl.num_programs(0)
    i = chunks - 1 - pl.program_id(0)
    inner = heads * P_SIZE
    early = Early(branch_ref, go_ref, (b_out, o_out) + early_refs)

    @pl.when(pl.program_id(0) == 0)
    def _():
        early.start()
        for ref in (dstate, next_v, next_k, next_lags, chan_sums, key_sums, head_sums):
            ref[...] = jnp.zeros_like(ref)

    docs = Docs(meta_ref, i, span)
    rows = iota((CHUNK, CHUNK), 0)
    cols = iota((CHUNK, CHUNK), 1)
    raw = raw_ref[...]
    dt = jax.nn.softplus(raw)
    cum = cum_ref[...]
    cum_t = cum.T
    count = docs.count.astype(f32)

    def column(row):
        return jnp.broadcast_to(row, (CHUNK, CHUNK)).T

    inv = lax.rsqrt(column(sums_ref[pl.ds(i, 1), :]) + epsilon)
    pull = inv * inv * inv * column(sums_ref[pl.ds(chunks + i, 1), :])

    bias = jnp.where((docs.doc == docs.row()) & (cols >= rows), 0.0, -1e30)
    carry_w = docs.flow() * jnp.exp(cum)
    final_d = docs.tail() * jnp.exp(cum[CHUNK - 1 :, :] - cum)
    final_w = final_d * dt
    gain = carry_w[CHUNK - 1 :, :]
    low = cols < P_SIZE
    low_row = low[:1]
    write = key_ref[:, :N]
    read = key_ref[:, N:]
    read_t = read.astype(f32).T.astype(bf16)
    scores_t = mm(write, read, NT)
    dscores_t = jnp.zeros((CHUNK, CHUNK), f32)
    dwrite = jnp.zeros((CHUNK, N), f32)
    dread = jnp.zeros((CHUNK, N), f32)
    end_row = iota((CHUNK, 1), 0) == CHUNK - 1
    dcum = jnp.zeros((CHUNK, LANES), f32)
    ddt = jnp.zeros((CHUNK, LANES), f32)
    dcum_rows = []
    for pair in range(heads // 2):
        first = 2 * pair
        lanes = slice(pair * 128, pair * 128 + 128)
        gate = proj_ref[:, lanes]
        sig = jax.nn.sigmoid(gate)
        silu = gate * sig
        masked = y_ref[:, lanes]
        gated = masked * silu
        norm_gain = chan_ref[5:6, lanes]
        gm = grad_ref[:, lanes]
        unit = gated * inv
        chan_sums[5:6, lanes] += jnp.sum(gm * unit, axis=0, keepdims=True)
        grad_gated = inv * (gm * norm_gain) - pull * gated
        cols_ref[:, lanes] = (grad_gated * masked * silu_slope(gate, sig)).astype(bf16)
        dy = jnp.where(chan_ref[7:8, lanes] < count, grad_gated * silu, 0.0)
        xf = val_ref[:, lanes].astype(f32)
        dyb = dy.astype(bf16)
        x_stack = jnp.concatenate(
            [jnp.where(low, xf, 0.0).astype(bf16), jnp.where(low, 0.0, xf).astype(bf16)], axis=0
        )
        dy_stack = jnp.concatenate(
            [jnp.where(low, dy, 0.0).astype(bf16), jnp.where(low, 0.0, dy).astype(bf16)], axis=0
        )
        dweights = mm(x_stack, dyb, NT)
        old = state_ref[0, :, lanes]
        grad = dstate[:, lanes]
        gradb = grad.astype(bf16)
        carried = mm(read, old, NN)
        pushed = mm(write, gradb, NN)
        carry_p = pair_cols(low, carry_w, first)
        final_p = pair_cols(low, final_w, first)
        carry_prod = dy * carried
        final_prod = xf * pushed
        gain_prod = jnp.sum(grad * old.astype(f32), axis=0, keepdims=True)
        weights = []
        for which, h in enumerate((first, first + 1)):
            col = dt[:, h : h + 1]
            decay = jnp.exp(cum_t[h : h + 1, :] - cum[:, h : h + 1] + bias)
            weighted = decay * col
            weights.append((weighted * scores_t).astype(bf16))
            dw = dweights[which * CHUNK : (which + 1) * CHUNK]
            dscores_t = dscores_t + dw * weighted
            direct = dw * decay * scores_t
            ddt_in = jnp.sum(direct, axis=1, keepdims=True)
            dcum_rows.append(jnp.sum(direct * col, axis=0, keepdims=True))
            half = low if which == 0 else ~low
            half_row = low_row if which == 0 else ~low_row
            carry_sum = jnp.sum(jnp.where(half, carry_prod, 0.0), axis=1, keepdims=True)
            final_sum = jnp.sum(jnp.where(half, final_prod, 0.0), axis=1, keepdims=True)
            push = final_w[:, h : h + 1] * final_sum
            at_end = jnp.sum(push, axis=0, keepdims=True) + gain[:, h : h + 1] * jnp.sum(
                jnp.where(half_row, gain_prod, 0.0), axis=1, keepdims=True
            )
            here = cols == h
            ddt = jnp.where(here, ddt_in + final_d[:, h : h + 1] * final_sum, ddt)
            dcum = jnp.where(
                here,
                carry_w[:, h : h + 1] * carry_sum - push - col * ddt_in + jnp.where(end_row, at_end, 0.0),
                dcum,
            )
        dx = mm(jnp.concatenate(weights, axis=1), dy_stack, NN)
        dv[:, lanes] = dx + final_p * pushed + chan_ref[6:7, lanes] * dy
        chan_sums[6:7, lanes] += jnp.sum(dy * xf, axis=0, keepdims=True)
        dwrite = dwrite + mm((final_p * xf).astype(bf16), gradb, NT)
        carry_dy = (carry_p * dy).astype(bf16)
        dread = dread + mm(carry_dy, old, NT)
        dstate[:, lanes] = pair_cols(low_row, gain, first) * grad + mm(read_t, carry_dy, NN)
    dsb = dscores_t.astype(bf16)
    dkeys = jnp.concatenate([dwrite + mm(dsb, read, NN), dread + mm(dsb, write, TN)], axis=1)

    extra = jnp.concatenate(dcum_rows + [jnp.zeros((LANES - heads, CHUNK), f32)], axis=0)
    dlog = mm((cols >= rows).astype(f32), dcum + extra.T, NN, exact)
    rate = head_ref[1:2, :]
    grad_step = (ddt - rate * dlog) * jax.nn.sigmoid(raw)
    head_sums[:1, :] += jnp.sum(grad_step, axis=0, keepdims=True)
    head_sums[1:2, :] -= jnp.sum(dt * rate * dlog, axis=0, keepdims=True)
    chosen = (rows == head_ref[2:3, :].astype(jnp.int32)).astype(bf16)
    cols_ref[:, 2 * inner + KEYS :] = mm(grad_step.astype(bf16), chosen, NT).astype(bf16)

    lags = [docs.lag(by) for by in range(1, CONV)]

    def convolve_back(dact, total, rows_in, after, weight, sums):
        dconv = dact * silu_slope(total, jax.nn.sigmoid(total))
        grad_in = weight[CONV - 1 :] * dconv
        sums[CONV : CONV + 1, :] += jnp.sum(dconv, axis=0, keepdims=True)
        sums[CONV - 1 : CONV, :] += jnp.sum(dconv * rows_in, axis=0, keepdims=True)
        for by in range(1, CONV):
            at = CONV - 1 - by
            moved = shift_up(dconv * lags[by - 1], after[...] * next_lags[:, by - 1 : by], by)
            grad_in = grad_in + weight[at : at + 1] * moved
            sums[at : at + 1, :] += jnp.sum(moved * rows_in, axis=0, keepdims=True)
        after[...] = dconv[:8]
        return grad_in.astype(bf16)

    rows_v = proj_ref[:, inner : 2 * inner].astype(bf16).astype(f32)
    cols_ref[:, inner : 2 * inner] = convolve_back(dv[...], vsum_ref[...], rows_v, next_v, chan_ref[:CONV, :], chan_sums)
    rows_k = proj_ref[:, 2 * inner : 2 * inner + KEYS].astype(bf16).astype(f32)
    cols_ref[:, 2 * inner : 2 * inner + KEYS] = convolve_back(
        dkeys, ksum_ref[...], rows_k, next_k, conv_ref[:, E:], key_sums
    )
    for by in range(1, CONV):
        next_lags[:, by - 1 : by] = lags[by - 1][:8]

    @pl.when(pl.program_id(0) == 0)
    def _():
        early.middle()

    @pl.when(pl.program_id(0) == chunks - 1)
    def _():
        whole_sums(all_sums, chan_sums, key_sums, head_sums, head_ref, chan_ref, heads)
        early.end()


def mixer_forward(meta, normed, in_w, params, cot, out_w, span, heads):
    length = normed.shape[0]
    columns = in_w.shape[1]
    inner = heads * P_SIZE
    chunks = length // CHUNK
    copies = sum(len(left_over(cot_order(o))) for o in range(cot.shape[0])) + 2 * (out_w.shape[0] - 1)
    row = lambda width: pl.BlockSpec((CHUNK, width), lambda i: (i, 0))
    all_of = lambda *shape: pl.BlockSpec(shape, lambda i: (0,) * len(shape))
    out = lambda width, dtype: jax.ShapeDtypeStruct((length, width), dtype)
    return pl.pallas_call(
        partial(forward_kernel, span=span, heads=heads),
        grid=(chunks,),
        in_specs=[
            pl.BlockSpec(memory_space=pltpu.SMEM), pl.BlockSpec((2 * CHUNK, normed.shape[1]), lambda i: (i // 2, 0)),
            all_of(*in_w.shape),
        ]
        + [all_of(*part.shape) for part in params]
        + [HBM] * 2,
        out_specs=[
            row(inner), row(KEYS), row(inner), row(KEYS), row(LANES), row(LANES), row(inner), row(inner),
            pl.BlockSpec((1, N, inner), lambda i: (i, 0, 0)), all_of(2 * chunks, LANES),
            all_of(8, inner), all_of(8, LANES), HBM, HBM, row(columns),
        ],
        out_shape=[
            out(inner, bf16), out(KEYS, bf16), out(inner, f32), out(KEYS, f32), out(LANES, f32), out(LANES, f32),
            out(inner, f32), out(inner, f32), jax.ShapeDtypeStruct((chunks, N, inner), bf16),
            jax.ShapeDtypeStruct((2 * chunks, LANES), f32), jax.ShapeDtypeStruct((8, inner), f32),
            jax.ShapeDtypeStruct((8, LANES), f32), jax.ShapeDtypeStruct(cot.shape, bf16),
            jax.ShapeDtypeStruct(out_w.shape, bf16), out(columns, f32),
        ],
        input_output_aliases={3 + len(params): 12, 4 + len(params): 13},
        scratch_shapes=[pltpu.VMEM((N, inner), f32), pltpu.VMEM((8, inner), f32), pltpu.VMEM((8, KEYS), f32)]
        + [pltpu.VMEM((2 * CHUNK, columns), f32)]
        + sems(copies, 1)[:2],
        compiler_params=remote_params(4, 58),
        cost_estimate=pl.CostEstimate(
            flops=length * inner * 1024, bytes_accessed=length * inner * 24, transcendentals=length * heads * CHUNK
        ),
        name="mixer_forward",
    )(meta, normed, in_w, *params, cot, out_w)


def mixer_backward(meta, projected, grad_mixed, chan, conv, head_vec, kept, sums, branch, grad_out, span, heads):
    length = projected.shape[0]
    inner = heads * P_SIZE
    chunks = length // CHUNK
    me = Place()
    near, peers, tokens, width = branch.shape
    far = me.far
    part = grad_out.shape[2:]
    copies = near * peers // 2 + 2 * far - 1
    vm = lambda *shape: pltpu.VMEM(shape, bf16)
    row = lambda width: pl.BlockSpec((CHUNK, width), lambda i: (chunks - 1 - i, 0))
    all_of = lambda *shape: pl.BlockSpec(shape, lambda i: (0,) * len(shape))
    out = lambda width: jax.ShapeDtypeStruct((length, width), bf16)
    return pl.pallas_call(
        partial(backward_kernel, span=span, heads=heads),
        grid=(chunks,),
        in_specs=[
            pl.BlockSpec(memory_space=pltpu.SMEM), row(2 * inner + KEYS + STEP_PAD), row(inner),
            all_of(8, inner), all_of(*conv.shape), all_of(8, LANES),
            row(inner), row(KEYS), row(inner), row(KEYS), row(LANES), row(LANES), row(inner),
            pl.BlockSpec((1, N, inner), lambda i: (chunks - 1 - i, 0, 0)), all_of(2 * chunks, LANES), HBM, HBM,
        ],
        out_specs=[
            row(2 * inner + KEYS + STEP_PAD), all_of(8, conv.shape[1]), VMEM, VMEM,
        ],
        out_shape=[
            out(2 * inner + KEYS + STEP_PAD), jax.ShapeDtypeStruct((8, conv.shape[1]), f32),
            jax.ShapeDtypeStruct((near, peers // 2, tokens, width), bf16), jax.ShapeDtypeStruct(part, f32),
        ],
        scratch_shapes=[
            pltpu.VMEM((8, inner), f32), pltpu.VMEM((8, KEYS), f32), pltpu.VMEM((8, LANES), f32),
            pltpu.VMEM((N, inner), f32), pltpu.VMEM((CHUNK, inner), f32), pltpu.VMEM((8, inner), f32),
            pltpu.VMEM((8, KEYS), f32), pltpu.VMEM((8, LANES), f32),
            vm(near, peers // 2, tokens, width), vm(near, peers // 2, tokens, width),
            vm(far, *part), vm(far, *part), vm(max(far - 1, 1), *part),
        ]
        + sems(copies, near * peers // 2 + far),
        compiler_params=remote_params(3, 32),
        cost_estimate=pl.CostEstimate(
            flops=length * inner * 3072, bytes_accessed=length * inner * 30, transcendentals=length * heads * CHUNK
        ),
        name="mixer_backward",
    )(meta, projected, grad_mixed, chan, conv, head_vec, *kept, sums, branch, grad_out)


MESH = pl.DeviceIdType.MESH
HBM = pl.BlockSpec(memory_space=pl.ANY)
VMEM = pl.BlockSpec(memory_space=pltpu.VMEM)


def z_pair(peers, groups):
    planes = groups // 2
    return 2 if planes % 2 == 0 and (E // (peers * planes)) % (2 * P_SIZE) == 0 else 1


def flip(value, bits):
    bit = 1
    while bit <= bits:
        if bits & bit:
            value = value + bit - 2 * bit * (value // bit % 2)
        bit *= 2
    return value


class Place:
    def __init__(self):
        self.peers = lax.axis_size("seq")
        groups = lax.axis_size("batch")
        self.near = z_pair(self.peers, groups)
        self.far = groups // 2 // self.near
        self.s = lax.axis_index("seq")
        b = lax.axis_index("batch")
        self.c = b % 2
        self.zl = b // 2 % self.near
        self.zh = b // 2 // self.near

    def at(self, s=0, zl=0, zh=0, c=0):
        return (flip(self.s, s), (flip(self.zh, zh) * self.near + flip(self.zl, zl)) * 2 + flip(self.c, c))

    def heads_at(self, index, per, width):
        outer = self.far if self.near > 1 else 1
        run = width // outer
        return (((self.s * outer + index // run) * self.near + self.zl) * run + index % run) // per

    def channel_runs(self, width):
        outer = self.far if self.near > 1 else 1
        run = width // outer
        runs = []
        for i in range(outer):
            first = ((self.s * outer + i) * self.near + self.zl) * run
            runs.append((pl.ds(pl.multiple_of(first, 128), run), slice(i * run, (i + 1) * run)))
        return runs

    def column_runs(self, s, zl, width):
        outer = self.far if self.near > 1 else 1
        run = width // (2 * outer)
        runs = []
        for part in range(2):
            for i in range(outer):
                first = part * E + ((s * outer + i) * self.near + zl) * run
                runs.append((pl.ds(pl.multiple_of(first, 128), run), pl.ds((part * outer + i) * run, run)))
        return runs

    def partners(self):
        cube = [self.at(s=o // self.near, zl=o % self.near) for o in range(1, self.peers * self.near)]
        return cube, [self.at(zh=o) for o in range(1, self.far)], [self.at(c=1)]


def greet(devices):
    barrier = pltpu.get_barrier_semaphore()
    for device in devices:
        pl.semaphore_signal(barrier, inc=1, device_id=device, device_id_type=MESH)
    pl.semaphore_wait(barrier, len(devices))


class Mover:
    def __init__(self, send, recv, local):
        self.send, self.recv, self.local = send, recv, local
        self.sent, self.kept = 0, 0
        self.open = []

    def plan(self, src, dst, device):
        copy = pltpu.make_async_remote_copy(
            src_ref=src, dst_ref=dst, send_sem=self.send.at[self.sent], recv_sem=self.recv.at[self.sent],
            device_id=device, device_id_type=MESH,
        )
        self.sent += 1
        self.open.append(copy)
        return copy

    def put(self, src, dst, device):
        copy = self.plan(src, dst, device)
        copy.start()
        return copy

    def plan_keep(self, src, dst):
        self.kept += 1
        return pltpu.make_async_copy(src, dst, self.local.at[self.kept - 1])

    def keep(self, src, dst):
        copy = self.plan_keep(src, dst)
        copy.start()
        return copy

    def close(self):
        for copy in self.open:
            copy.wait_send()


def run_paths(paths):
    paths = list(paths)
    while paths:
        alive = []
        for path in paths:
            try:
                next(path)
                alive.append(path)
            except StopIteration:
                pass
        paths = alive


def turn(paths):
    for path in paths:
        next(path, None)


def bits_of(peers):
    return [1 << i for i in range(peers.bit_length() - 1)]


def combos(bits):
    out = [0]
    for bit in reversed(bits):
        out = [bit | o for o in out] + out
    return out


def cot_order(near):
    bits = bits_of(lax.axis_size("seq"))
    return bits if near else bits[::-1]


def left_over(order):
    return combos(order[:-1])


class Late:
    def __init__(self, src, dst, out_src, out_dst, send, recv):
        me = self.me = Place()
        self.mover = Mover(send, recv, None)
        self.copies, self.far, self.forward = [], [], []
        for o in range(me.near):
            order = cot_order(o)
            for h in left_over(order):
                at = (flip(me.zl, o), flip(me.s, h))
                self.copies.append(self.mover.plan(src.at[at], dst.at[at], me.at(s=order[-1])))
        for o in range(1, me.far):
            at = (me.zh, me.c)
            self.far.append(self.mover.plan(out_src.at[at], out_dst.at[at], me.at(zh=o)))
        for o in range(1, me.far):
            at = (flip(me.zh, o), me.c)
            self.forward.append(self.mover.plan(out_dst.at[at], out_dst.at[at], me.at(c=1)))

    def start(self):
        _, far, sibling = self.me.partners()
        greet([self.me.at(s=bit) for bit in sorted({cot_order(o)[-1] for o in range(self.me.near)})] + far + sibling)
        for copy in self.far + self.copies:
            copy.start()

    def middle(self):
        for far, forward in zip(self.far, self.forward):
            far.wait_recv()
            forward.start()

    def end(self):
        for copy in self.copies + self.forward:
            copy.wait_recv()
        self.mover.close()


def gather_kernel(
    in_ref, out_ref, cot_ref, inputs_ref, gain_ref, step_ref, lengths_ref, width_ref,
    w_ref, o_ref, x_ref, ct_ref, m_ref, inv_ref, rows_ref, steps_ref, meta_ref, send, recv, local,
):
    prepare(inputs_ref, gain_ref, step_ref, lengths_ref, width_ref, rows_ref, inv_ref, steps_ref, meta_ref)
    cot_ref = cot_ref.at[0]
    me = Place()
    s, zl, zh, c = me.s, me.zl, me.zh, me.c
    columns = w_ref.shape[-1] - KEYS - STEP_PAD
    mine, shared = pl.ds(0, columns), pl.ds(columns, KEYS + STEP_PAD)
    cube, far, sibling = me.partners()
    greet(cube + far + sibling)
    mover = Mover(send, recv, local)
    bits = bits_of(me.peers)

    def plane_path(src, dst, order, near, skip=()):
        view = dst.at[flip(zl, near)]
        if near:
            copy = mover.put(src, dst.at[zl, s], me.at(zl=near))
            yield
            copy.wait_recv()
        else:
            own = mover.keep(src, view.at[s])
        held = [0]
        for bit in order:
            copies = []
            for h in held:
                if bit == order[-1] and h in skip:
                    continue
                at = view.at[flip(s, h)]
                copies.append(mover.put(at if near or h else src, at if near else dst.at[zl, flip(s, h)], me.at(s=bit)))
            held = held + [h ^ bit for h in held]
            yield
            for copy in copies:
                copy.wait_recv()
        if not near:
            own.wait()

    def meta_path():
        own = mover.keep(meta_ref, m_ref.at[zl])
        near = [mover.put(meta_ref, m_ref.at[zl], me.at(zl=o)) for o in range(1, me.near)]
        yield
        own.wait()
        for copy in near:
            copy.wait_recv()

    def key_path():
        block = w_ref.at[s, zh, zl, c]
        parts = [
            (in_ref.at[:, pl.ds(2 * E, KEYS)], block.at[:, pl.ds(columns, KEYS)]),
            (steps_ref, block.at[:, pl.ds(columns + KEYS, STEP_PAD)]),
        ]
        own = [mover.keep(*part) for part in parts]
        copies = [mover.put(*part, me.at(zh=o)) for o in range(1, me.far) for part in parts]
        yield
        for copy in own:
            copy.wait()
        for copy in copies:
            copy.wait_recv()
        block = w_ref.at[s, :, zl, c, :, shared]
        copies = [mover.put(block, block, me.at(zl=o)) for o in range(1, me.near)]
        yield
        for copy in copies:
            copy.wait_recv()
        held = [0]
        for bit in bits:
            copies = []
            for h in held:
                block = w_ref.at[flip(s, h), :, :, c, :, shared]
                copies.append(mover.put(block, block, me.at(s=bit)))
            held = held + [h ^ bit for h in held]
            yield
            for copy in copies:
                copy.wait_recv()
        block = w_ref.at[:, :, :, c, :, shared]
        copy = mover.put(block, block, me.at(c=1))
        yield
        copy.wait_recv()

    def spread_path(copies, view):
        last = []
        for o, copy in copies:
            yield
            copy.wait_recv()
            last.append(mover.put(view(flip(zh, o)), view(flip(zh, o)), me.at(c=1)))
        return last

    def out_path():
        own = mover.keep(out_ref, o_ref.at[zh, c])
        first = mover.put(out_ref, o_ref.at[zh, c], me.at(c=1))
        yield
        own.wait()
        first.wait_recv()

    def weight_path():
        moves = {}
        for step in range(me.peers):
            for o in range(me.near):
                to_s, to_zl = flip(s, step), flip(zl, o)
                for src, dst in me.column_runs(to_s, to_zl, columns):
                    src = in_ref.at[:, src]
                    dst = w_ref.at[s, zh, zl, c, :, dst]
                    if step or o:
                        copy = mover.put(src, dst, me.at(s=step, zl=o))
                    else:
                        copy = mover.keep(src, dst)
                    moves.setdefault(step, []).append(copy)
        pieces = []
        for step in range(me.peers):
            yield
            for i, copy in enumerate(moves[step]):
                if step == 0 and i < len(moves[0]) // me.near:
                    copy.wait()
                else:
                    copy.wait_recv()
            block = w_ref.at[flip(s, step), zh, :, c, :, mine]
            copies = [(o, mover.put(block, block, me.at(zh=o))) for o in range(1, me.far)]
            pieces.append((step, copies, mover.put(block, block, me.at(c=1))))
        last = []
        for step, copies, first in pieces:
            last.append(first)
            last += yield from spread_path(copies, lambda h, step=step: w_ref.at[flip(s, step), h, :, c, :, mine])
        yield
        for copy in last:
            copy.wait_recv()

    own_x = plane_path(rows_ref, x_ref, bits, 0)
    near_x = [plane_path(rows_ref, x_ref, bits[::-1], o) for o in range(1, me.near)]
    own_c, *near_c = [plane_path(cot_ref, ct_ref, cot_order(o), o, left_over(cot_order(o))) for o in range(me.near)]
    keys, weights, outs, extra = key_path(), weight_path(), out_path(), meta_path()
    turn([keys, weights, own_x] + near_x + [own_c, outs, extra])
    turn([keys] + near_x + near_c + [keys] + [weights] * me.peers + [keys] + near_x + [own_x, own_c] + near_c)
    turn([keys, weights, keys, weights, weights, weights] + near_x + [own_x] + near_c)
    run_paths([weights, extra, keys, outs, own_x, own_c] + near_x + near_c)
    mover.close()


def remote_params(identity, mib):
    return pltpu.CompilerParams(collective_id=identity, has_side_effects=True, vmem_limit_bytes=mib * 2**20)


def sems(copies, kept):
    return [pltpu.SemaphoreType.DMA((copies,)), pltpu.SemaphoreType.DMA((copies,)), pltpu.SemaphoreType.DMA((kept,))]


def prepare(x_ref, gain_ref, step_ref, lengths_ref, width_ref, normed_ref, inv_ref, steps_ref, meta_ref):
    x = x_ref[0].astype(f32)
    inv = lax.rsqrt(jnp.mean(x * x, axis=1, keepdims=True) + epsilon)
    normed_ref[...] = (x * inv * gain_ref[...]).astype(bf16)
    inv_ref[...] = jnp.broadcast_to(inv, inv_ref.shape)
    steps_ref[...] = jnp.zeros_like(steps_ref)
    steps_ref[:, :H] = step_ref[...]
    lanes = iota(meta_ref.shape, 1)
    meta = jnp.where(lanes == DOCS, width_ref[0], 0)
    for i in range(DOCS):
        meta = jnp.where(lanes == i, lengths_ref[0, i], meta)
    meta_ref[...] = meta


def gather(in_w, out_w, cot, inputs, gain, step_w, lengths, head_width):
    me = Place()
    peers, near, far = me.peers, me.near, me.far
    shape = lambda lead, part: jax.ShapeDtypeStruct(lead + part, bf16)
    rows = inputs.shape[1:]
    columns = 2 * E // (peers * near)
    runs = 2 * (far if near > 1 else 1)
    copies = runs * (peers * near - 1) + (peers + 1) * (2 * far - 1) + 2 * (near * peers - 1)
    copies -= sum(len(left_over(cot_order(o))) for o in range(near))
    copies += 2 * near + peers + 2 * far - 4
    smem = pl.BlockSpec(memory_space=pltpu.SMEM)
    return pl.pallas_call(
        gather_kernel,
        out_shape=[
            shape((peers, far, near, 2), (in_w.shape[0], columns + KEYS + STEP_PAD)),
            shape((far, 2), out_w.shape),
            shape((near, peers), rows),
            shape((near, peers), rows),
            jax.ShapeDtypeStruct((near, 8, LANES), jnp.int32),
            jax.ShapeDtypeStruct((rows[0], LANES), f32),
        ],
        in_specs=[HBM] * 3 + [VMEM] * 3 + [smem] * 2,
        out_specs=[HBM] * 5 + [VMEM],
        scratch_shapes=[
            pltpu.VMEM(rows, bf16), pltpu.VMEM((in_w.shape[0], STEP_PAD), bf16), pltpu.VMEM((8, LANES), jnp.int32)
        ]
        + sems(copies, runs + 6),
        compiler_params=remote_params(0, 58),
        name="gather_all",
    )(in_w, out_w, cot, inputs, gain, step_w, lengths, head_width)


def total_kernel(part_ref, gated_ref, chan_ref, grad_ref, sum_ref, mixed_ref, mine, box, send, recv, local):
    me = Place()
    cube = me.partners()[0]
    greet(cube)
    mover = Mover(send, recv, local)
    chunks = part_ref.shape[0] // 2
    tiles = [slice(lane, lane + LANES) for lane in range(0, gated_ref.shape[1], LANES)]
    mine[...] = part_ref[...]

    def products(i, carry):
        at = pl.ds(pl.multiple_of(i * CHUNK, CHUNK), CHUNK)
        cross = jnp.zeros((CHUNK, LANES), f32)
        for lanes in tiles:
            cross = cross + gated_ref[at, lanes] * (grad_ref[at, lanes] * chan_ref[5:6, lanes])
        row = pl.ds(chunks + i, 1)
        mine[row, :] = jnp.sum(cross.T, axis=0, keepdims=True) * part_ref[row, :]
        return carry

    lax.fori_loop(0, chunks, products, 0)
    copies = [mover.put(mine, box.at[i], device) for i, device in enumerate(cube)]
    total = mine[...]
    for i, copy in enumerate(copies):
        copy.wait_recv()
        total = total + box[i]
    sum_ref[...] = total

    def mix(i, carry):
        at = pl.ds(pl.multiple_of(i * CHUNK, CHUNK), CHUNK)
        inv = lax.rsqrt(jnp.broadcast_to(sum_ref[pl.ds(i, 1), :], (CHUNK, CHUNK)).T + epsilon)
        for lanes in tiles:
            mixed_ref[at, lanes] = (gated_ref[at, lanes] * inv * chan_ref[5:6, lanes]).astype(bf16)
        return carry

    lax.fori_loop(0, chunks, mix, 0)
    mover.close()


def cube_total(part, gated, chan, grad):
    me = Place()
    count = me.peers * me.near - 1
    return pl.pallas_call(
        total_kernel,
        out_shape=[jax.ShapeDtypeStruct(part.shape, f32), jax.ShapeDtypeStruct(gated.shape, bf16)],
        in_specs=[VMEM] * 4,
        out_specs=[VMEM] * 2,
        scratch_shapes=[pltpu.VMEM(part.shape, f32), pltpu.VMEM((count,) + part.shape, f32)] + sems(count, 1),
        compiler_params=remote_params(1, 12),
        name="cube_total",
    )(part, gated, chan, grad)


def add_rows(out, parts):
    shape = out.shape
    tile = min(16, shape[-2])
    lead = [()]
    for size in shape[:-2]:
        lead = [l + (i,) for l in lead for i in range(size)]
    for l in lead:

        def step(i, carry, l=l):
            at = l + (pl.ds(pl.multiple_of(i * tile, tile), tile), slice(None))
            total = parts[0][at].astype(f32)
            for part in parts[1:]:
                total = total + part[at].astype(f32)
            out[at] = total.astype(out.dtype)
            return carry

        lax.fori_loop(0, shape[-2] // tile, step, 0)


def scatter_kernel(
    gn_ref, gw_ref, b_ref, u_ref, p_ref, gain_ref, og_ref, ow_ref, ob_ref, ok_ref, ou_ref,
    n_own, n_box, n_near, b_own, b_box, b_near, w_own, w_box, w_far,
    k_own, k_box, k_near, k_far, k_bits, u_box, send, recv, local,
):
    me = Place()
    s, zl, zh, c = me.s, me.zl, me.zh, me.c
    cube, far, sibling = me.partners()
    greet(cube + far + sibling)
    mover = Mover(send, recv, local)
    bits = bits_of(me.peers)
    columns = w_own.shape[-1]
    mine, shared = pl.ds(0, columns), pl.ds(columns, k_own.shape[-1])

    def rows_path(src, own, box, near_box, out, order, near, arrivals, done=0):
        own, box = own.at[near], box.at[near]
        copies, loads = [], []
        if done:
            half = me.peers // 4
            for j in range(half):
                copies.append(mover.put(src.at[near, j], box.at[j], me.at(s=order[1])))
                loads.append(mover.keep(src.at[near, half + j], own.at[half + j]))
        else:
            at_zl = src.at[flip(zl, near)]
            for j, o in enumerate(combos(order[1:])):
                copies.append(mover.put(at_zl.at[flip(s, order[0] ^ o)], box.at[j], me.at(s=order[0])))
                loads.append(mover.keep(at_zl.at[flip(s, o)], own.at[j]))
        base = 0
        for i in range(done, len(order)):
            rest = order[i + 1 :]
            count = 1 << len(rest)
            offset = (1 << (len(order) - 1)) - count
            coming = []
            for j in range(count):
                yield
                copies[j].wait_recv()
                if i == done:
                    loads[j].wait()
                if rest or near:
                    add_rows(own.at[offset + j], [own.at[offset + j], box.at[base + j]])
                if rest and j < count // 2:
                    coming.append(mover.put(own.at[offset + j], box.at[base + count + j], me.at(s=rest[0])))
            copies = coming
            last = base
            base += count
        end = (1 << (len(order) - 1)) - 1
        if near:
            arrivals.append(mover.put(own.at[end], near_box.at[near - 1], me.at(zl=near)))
            yield
        else:
            yield
            for _ in range(me.near - 1):
                arrivals.pop(0).wait_recv()
            add_rows(out, [own.at[end], box.at[last]] + [near_box.at[o - 1] for o in range(1, me.near)])

    def weight_path():
        order = [(o, k) for o in range(1, me.far) for k in range(me.peers)] + [(0, k) for k in range(me.peers)]
        loads, copies = {}, {}
        for o, k in order:
            copies[o, k] = mover.put(gw_ref.at[flip(s, k), flip(zh, o), :, 1 - c, :, mine], w_box.at[o, k], me.at(c=1))
            loads[o, k] = mover.keep(gw_ref.at[flip(s, k), flip(zh, o), :, c, :, mine], w_own.at[o, k])
        far_copies = {}
        for o, k in order:
            yield
            loads[o, k].wait()
            copies[o, k].wait_recv()
            if o:
                add_rows(w_own.at[o, k], [w_own.at[o, k], w_box.at[o, k]])
                far_copies[o, k] = mover.put(w_own.at[o, k], w_far.at[o - 1, k], me.at(zh=o))
        ends, kept = [], []
        for k in range(me.peers):
            yield
            for o in range(1, me.far):
                far_copies[o, k].wait_recv()
            parts = [w_own.at[0, k], w_box.at[0, k]] + [w_far.at[o - 1, k] for o in range(1, me.far)]
            add_rows(w_own.at[0, k], parts)
            for o in range(me.near):
                for whole, part in me.column_runs(s, zl, columns):
                    src = w_own.at[0, k, flip(zl, o), :, part]
                    if k or o:
                        ends.append(mover.put(src, ow_ref.at[:, whole], me.at(s=k, zl=o)))
                    else:
                        kept.append(mover.keep(src, ow_ref.at[:, whole]))
        yield
        for copy in kept:
            copy.wait()
        for copy in ends:
            copy.wait_recv()

    def key_path():
        blocks = combos(bits)
        copies, loads = [], []
        for j, o in enumerate(blocks):
            copies.append(mover.put(gw_ref.at[flip(s, o), :, :, 1 - c, :, shared], k_box.at[j], me.at(c=1)))
            loads.append(mover.keep(gw_ref.at[flip(s, o), :, :, c, :, shared], k_own.at[j]))
        half = me.peers // 2
        sent = []
        for j in range(me.peers):
            yield
            loads[j].wait()
            copies[j].wait_recv()
            add_rows(k_own.at[j], [k_own.at[j], k_box.at[j]])
            if j < half:
                sent.append(mover.put(k_own.at[j], k_bits.at[j], me.at(s=bits[0])))
        base = 0
        for i, bit in enumerate(bits):
            count = me.peers >> (i + 1)
            offset = me.peers - count
            coming = []
            for j in range(count):
                yield
                sent[j].wait_recv()
                add_rows(k_own.at[offset + j], [k_own.at[offset + j], k_bits.at[base + j]])
                if i + 1 < len(bits) and j < count // 2:
                    coming.append(mover.put(k_own.at[offset + j], k_bits.at[base + count + j], me.at(s=bits[i + 1])))
            base += count
            sent = coming
        end = k_own.at[me.peers - 1]
        copies = [mover.put(end.at[:, flip(zl, o)], k_near.at[o - 1], me.at(zl=o)) for o in range(1, me.near)]
        yield
        for copy in copies:
            copy.wait_recv()
        add_rows(end.at[:, zl], [end.at[:, zl]] + [k_near.at[o - 1] for o in range(1, me.near)])
        copies = [mover.put(end.at[flip(zh, o), zl], k_far.at[o - 1], me.at(zh=o)) for o in range(1, me.far)]
        yield
        for copy in copies:
            copy.wait_recv()
        add_rows(ok_ref, [end.at[zh, zl]] + [k_far.at[o - 1] for o in range(1, me.far)])

    def small_path():
        turns = [me.at(c=1)] + [me.at(zl=o) for o in bits_of(me.near)]
        turns += [me.at(s=o) for o in bits] + [me.at(zh=o) for o in bits_of(me.far)]
        u_box[0] = u_ref[...]
        u_box[0, 6:7, : p_ref.shape[1]] = p_ref[...] / gain_ref[...]
        for i, device in enumerate(turns):
            copy = mover.put(u_box.at[2 * i], u_box.at[2 * i + 1], device)
            yield
            copy.wait_recv()
            u_box[2 * i + 2] = u_box[2 * i] + u_box[2 * i + 1]
        ou_ref[...] = u_box[2 * len(turns)]

    coming_n, coming_b = [], []
    grads = (gn_ref, n_own, n_box, n_near, og_ref)
    branch = (b_ref, b_own, b_box, b_near, ob_ref)
    orders = lambda o: bits if o else bits[::-1]
    near_n = [rows_path(*grads, orders(o), o, coming_n) for o in range(1, me.near)]
    near_b = [rows_path(*branch, orders(o), o, coming_b, 1) for o in range(1, me.near)]
    own_n = rows_path(*grads, orders(0), 0, coming_n)
    own_b = rows_path(*branch, orders(0), 0, coming_b, 1)
    weights, keys, small = weight_path(), key_path(), small_path()
    turn(near_b + near_n + [weights, own_n, keys, own_b, small])
    turn([weights] * (me.far * me.peers) + [keys] * me.peers + [small])
    turn(near_b + near_n + [keys, own_b, small] + near_b + near_n + [keys, small, keys, own_b, own_n])
    run_paths(near_b + near_n + [keys, small, weights, own_b, own_n])
    mover.close()


def scatter(grads, gw, branch, small, products, gain):
    me = Place()
    peers, near, far = me.peers, me.near, me.far
    tokens, width = grads.shape[2:]
    stages = len(bits_of(peers)) + len(bits_of(near)) + len(bits_of(far)) + 1
    vm = lambda *shape: pltpu.VMEM(shape, bf16)
    boxes = lambda part: pltpu.VMEM((2 * stages + 1,) + part.shape, f32)
    keys = KEYS + STEP_PAD
    rows = gw.shape[4]
    block = (near, rows, gw.shape[5] - keys)
    kblock = (near, rows, keys)
    runs = 2 * (far if near > 1 else 1)
    copies = peers * near - 1 + (2 * far - 1) * peers + runs * (peers * near - 1)
    copies += 2 * peers - 1 + near - 1 + far - 1 + stages + peers // 2 * near - 1
    kept = peers * near + far * peers + runs + peers + near * peers // 4
    same = lambda part: jax.ShapeDtypeStruct(part.shape, part.dtype)
    return pl.pallas_call(
        scatter_kernel,
        out_shape=[
            jax.ShapeDtypeStruct((tokens, width), f32),
            jax.ShapeDtypeStruct((rows, 2 * E), bf16),
            jax.ShapeDtypeStruct((tokens, width), f32),
            jax.ShapeDtypeStruct((rows, keys), f32),
            same(small),
        ],
        in_specs=[HBM] * 3 + [VMEM] * 3,
        out_specs=[VMEM, HBM, VMEM, VMEM, VMEM],
        scratch_shapes=[
            vm(near, peers // 2, tokens, width), vm(near, peers - 1, tokens, width), vm(max(near - 1, 1), tokens, width),
            vm(near, peers // 2, tokens, width), vm(near, peers // 2 - 1, tokens, width), vm(max(near - 1, 1), tokens, width),
            vm(far, peers, *block), vm(far, peers, *block), vm(max(far - 1, 1), peers, *block),
            vm(peers, far, *kblock), vm(peers, far, *kblock), vm(max(near - 1, 1), far, *kblock[1:]),
            vm(max(far - 1, 1), *kblock[1:]), vm(peers - 1, far, *kblock), boxes(small),
        ]
        + sems(copies, kept),
        compiler_params=remote_params(2, 40),
        cost_estimate=pl.CostEstimate(flops=0, bytes_accessed=250 * 10**6, transcendentals=0),
        name="scatter_all",
    )(grads, gw, branch, small, products, gain)


class Early:
    def __init__(self, b_ref, go_ref, refs):
        self.b_out, self.o_out, self.b_own, self.b_box, self.o_own, self.o_box, self.o_far, send, recv, local = refs
        me = self.me = Place()
        mover = self.mover = Mover(send, recv, local)
        bits = bits_of(me.peers)
        self.rows, self.outs, self.far = [], [], []
        for o in range(me.near):
            order = bits if o else bits[::-1]
            at_zl = b_ref.at[flip(me.zl, o)]
            for j, left in enumerate(combos(order[1:])):
                put = mover.plan(at_zl.at[flip(me.s, order[0] ^ left)], self.b_box.at[o, j], me.at(s=order[0]))
                self.rows.append((put, mover.plan_keep(at_zl.at[flip(me.s, left)], self.b_own.at[o, j]), (o, j)))
        for o in range(me.far):
            put = mover.plan(go_ref.at[flip(me.zh, o), 1 - me.c], self.o_box.at[o], me.at(c=1))
            self.outs.append((put, mover.plan_keep(go_ref.at[flip(me.zh, o), me.c], self.o_own.at[o])))
        for o in range(1, me.far):
            self.far.append(mover.plan(self.o_own.at[o], self.o_far.at[o - 1], me.at(zh=o)))

    def start(self):
        _, far, sibling = self.me.partners()
        bits = bits_of(self.me.peers)
        greet([self.me.at(s=bit) for bit in sorted({bits[0], bits[-1]})] + far + sibling)
        for put, load in self.outs:
            put.start()
            load.start()
        for put, load, _ in self.rows:
            put.start()
            load.start()

    def middle(self):
        for o, (put, load) in enumerate(self.outs):
            load.wait()
            put.wait_recv()
            if o:
                add_rows(self.o_own.at[o], [self.o_own.at[o], self.o_box.at[o]])
                self.far[o - 1].start()

    def end(self):
        for put, load, at in self.rows:
            load.wait()
            put.wait_recv()
            add_rows(self.b_out.at[at], [self.b_own.at[at], self.b_box.at[at]])
        for put in self.far:
            put.wait_recv()
        add_rows(self.o_out, [self.o_own.at[0], self.o_box.at[0]] + [self.o_far.at[o] for o in range(self.me.far - 1)])
        self.mover.close()


def finish_kernel(
    x_ref, cot_ref, gain_ref, inv_ref, og_ref, ob_ref, ow_ref, ok_ref, u_ref,
    out_ref, gx_ref, gw_ref, gs_ref, gc_ref, gb_ref, gp_ref, gn_ref, g0_ref, g1_ref, g2_ref,
):
    x = x_ref[0].astype(f32)
    out_ref[0] = (x + ob_ref[...]).astype(bf16)
    inv = inv_ref[:, :1]
    scaled = og_ref[...] * gain_ref[...]
    dot = jnp.mean(scaled * x, axis=1, keepdims=True)
    gx_ref[0] = inv * scaled - x * (inv * inv * inv * dot) + cot_ref[0].astype(f32)
    gw_ref[:, : 2 * E] = ow_ref[...].astype(f32)
    gw_ref[:, 2 * E :] = ok_ref[:, :KEYS]
    gs_ref[...] = ok_ref[:, KEYS : KEYS + H]
    gc_ref[...] = u_ref[:CONV, :]
    gb_ref[...] = u_ref[CONV : CONV + 1, :]
    gn_ref[...] = u_ref[5:6, :E]
    gp_ref[...] = u_ref[6:7, : gp_ref.shape[1]]
    for i, ref in enumerate((g0_ref, g1_ref, g2_ref)):
        ref[...] = u_ref[7:8, i * LANES : i * LANES + H]


def finish(inputs, cotangent, gain, inv, sums):
    tokens, width = inputs.shape[1:]
    og, ow, ob, ok, u = sums
    shape = lambda *dims: jax.ShapeDtypeStruct(dims, f32)
    rows = ow.shape[0]
    return pl.pallas_call(
        finish_kernel,
        out_shape=[
            jax.ShapeDtypeStruct(inputs.shape, bf16), shape(*inputs.shape), shape(rows, 2 * E + KEYS), shape(rows, H),
            shape(CONV, E + KEYS), shape(1, E + KEYS), shape(1, width), shape(1, E), shape(1, H), shape(1, H), shape(1, H),
        ],
        in_specs=[VMEM] * 9,
        out_specs=[VMEM] * 11,
        compiler_params=pltpu.CompilerParams(vmem_limit_bytes=32 * 2**20),
        name="finish",
    )(inputs, cotangent, gain, inv, og, ob, ow, ok, u)


def body(
    inputs, cotangent, doc_lengths, head_width, pre_gain, in_weight, step_weight, conv_weight, conv_bias,
    step_bias, decay_log, skip_gain, norm_gain, out_weight,
):
    me = Place()
    peers, near, far = me.peers, me.near, me.far
    tokens, width = inputs.shape[1:]
    span = tokens * peers
    length = span * near
    heads = H // (peers * near)
    inner = heads * P_SIZE
    rows = in_weight.shape[0]
    row = lambda vector: vector[None, :]

    in_w, out_w, normed, cot_all, meta, inv = gather(
        in_weight, out_weight, cotangent, inputs, row(pre_gain), step_weight, doc_lengths, head_width
    )
    in_w = in_w.reshape(width, -1)
    normed = normed.reshape(length, width)
    meta = meta[:, 0, :8]

    params = (conv_weight, row(conv_bias), row(norm_gain), row(step_bias), row(decay_log), row(skip_gain))
    *kept, gated, states, part, chan, head_vec, cot_all, out_w, projected = mixer_forward(
        meta, normed, in_w, params, cot_all, out_w, span, heads
    )
    out_w = out_w.reshape(inner, width)
    cot_all = cot_all.reshape(length, width)
    grad_mixed = mm(cot_all, out_w, NT)
    sums, mixed = cube_total(part, gated, chan, grad_mixed)
    branch = mm(mixed, out_w, NN).astype(bf16)
    grad_out = mm(mixed, cot_all, TN).astype(bf16)
    grad_cols, small, branch, grad_out_weight = mixer_backward(
        meta, projected, grad_mixed, chan, conv_weight, head_vec, (*kept, states), sums,
        branch.reshape(near, peers, tokens, width), grad_out.reshape(far, 2, -1, width), span, heads,
    )
    grad_in = mm(normed, grad_cols, TN).astype(bf16)
    grad_normed = mm(grad_cols, in_w, NT)
    products = jnp.sum(grad_normed * normed.astype(f32), axis=0)
    summed = scatter(
        grad_normed.astype(bf16).reshape(near, peers, tokens, width),
        grad_in.reshape(peers, far, near, 2, rows, -1),
        branch,
        small,
        row(products),
        row(pre_gain),
    )
    outs = finish(inputs, cotangent, row(pre_gain), inv, summed)
    output, grad_inputs, grad_in_weight, grad_step_weight, grad_conv_weight = outs[:5]
    grad_conv_bias, grad_pre_gain, grad_norm_gain, grad_step_bias, grad_decay_log, grad_skip = [o[0] for o in outs[5:]]
    return (
        output, grad_inputs, grad_pre_gain, grad_in_weight, grad_step_weight, grad_conv_weight, grad_conv_bias,
        grad_step_bias, grad_decay_log, grad_skip, grad_norm_gain, grad_out_weight,
    )


def solution(mesh):
    both = P(("seq", "batch"), None)
    tok = P("batch", "seq", None)
    in_specs = (
        tok, tok, P("batch", None), P("batch"), P(), both, both, P(), P(), P(), P(), P(), P(), both,
    )
    out_specs = (tok, tok, P(), both, both, P(), P(), P(), P(), P(), P(), both)
    return jax.shard_map(body, mesh=mesh, in_specs=in_specs, out_specs=out_specs, check_vma=False)
```

```python
from functools import partial

import jax
import jax.numpy as jnp
from jax import lax
from jax.experimental import pallas as pl
from jax.experimental.pallas import tpu as pltpu
from jax.sharding import PartitionSpec as P

H = 64
P_SIZE = 64
N = 128
CONV = 4
DOCS = 4
E = 4096
KEYS = 2 * N
STEP_PAD = 128
CHUNK = 128
LANES = 128
epsilon = 1e-05
f32 = jnp.float32
bf16 = jnp.bfloat16


def mm(a, b, dims, precision=None):
    return lax.dot_general(a, b, (dims, ((), ())), precision=precision, preferred_element_type=f32)


NN = ((1,), (0,))
NT = ((1,), (1,))
TN = ((0,), (0,))
exact = lax.Precision.HIGHEST


def pair_cols(low, col, first):
    return jnp.where(low, col[:, first : first + 1], col[:, first + 1 : first + 2])


def iota(shape, axis):
    return lax.broadcasted_iota(jnp.int32, shape, axis)


class Docs:
    def __init__(self, meta_ref, chunk, span):
        per = span // CHUNK
        seq = chunk // per
        self.start = (chunk - seq * per) * CHUNK
        self.ends = []
        total = 0
        for i in range(DOCS - 1):
            total = total + meta_ref[seq, 0, i]
            self.ends.append(total)
        self.count = meta_ref[seq, 0, DOCS]
        self.pos = self.start + iota((CHUNK, 1), 0)
        self.doc = self.index(self.pos)

    def index(self, places):
        found = (places >= self.ends[0]).astype(jnp.int32)
        for end in self.ends[1:]:
            found = found + (places >= end).astype(jnp.int32)
        return found

    def lag(self, by):
        source = self.pos - by
        return ((source >= 0) & (self.index(source) == self.doc)).astype(f32)

    def flow(self):
        return ((self.start > 0) & (self.index(self.start - 1) == self.doc)).astype(f32)

    def row(self):
        return self.index(self.start + iota((1, CHUNK), 1))

    def tail(self):
        return (self.doc == self.index(self.start + CHUNK - 1)).astype(f32)


def shift_down(rows, before, by):
    if by == 0:
        return rows
    moved = pltpu.roll(rows, by, 0)
    top = jnp.where(iota((8, 1), 0) < by, pltpu.roll(before, by, 0), moved[:8])
    return jnp.concatenate([top, moved[8:]], axis=0)


def shift_up(rows, after, by):
    if by == 0:
        return rows
    size = rows.shape[0]
    moved = pltpu.roll(rows, size - by, 0)
    end = jnp.where(iota((8, 1), 0) >= 8 - by, pltpu.roll(after, 8 - by, 0), moved[size - 8 :])
    return jnp.concatenate([moved[: size - 8], end], axis=0)


def silu_slope(v, sig):
    return sig * (1.0 + v * (1.0 - sig))


def own_parameters(chan_ref, head_ref, conv_ref, bias_ref, norm_ref, step_b_ref, decay_ref, skip_ref, heads):
    me = Place()
    inner = heads * P_SIZE
    for whole, part in me.channel_runs(inner):
        chan_ref[:CONV, part] = conv_ref[:, whole]
        chan_ref[CONV : CONV + 1, part] = bias_ref[:, whole]
        chan_ref[5:6, part] = norm_ref[:, whole]
    ids = me.heads_at(iota((1, inner), 1), P_SIZE, inner)
    chosen = (iota((H, inner), 0) == ids).astype(f32)
    chan_ref[6:7, :] = mm(jnp.broadcast_to(skip_ref[...], (8, H)), chosen, NN, exact)[:1]
    chan_ref[7:8, :] = ids.astype(f32)
    lanes = iota((1, LANES), 1)
    ids = jnp.where(lanes < heads, me.heads_at(lanes, 1, heads), -1)
    chosen = (iota((H, LANES), 0) == ids).astype(f32)
    head_ref[...] = jnp.zeros_like(head_ref)
    head_ref[:1, :] = mm(jnp.broadcast_to(step_b_ref[...], (8, H)), chosen, NN, exact)[:1]
    head_ref[1:2, :] = mm(jnp.broadcast_to(jnp.exp(decay_ref[...]), (8, H)), chosen, NN, exact)[:1]
    head_ref[2:3, :] = ids.astype(f32)


def whole_sums(out_ref, chan_sums, key_sums, head_sums, head_ref, chan_ref, heads):
    me = Place()
    inner = heads * P_SIZE
    out_ref[...] = jnp.zeros_like(out_ref)
    for whole, part in me.channel_runs(inner):
        out_ref[:6, whole] = chan_sums[:6, part]
    out_ref[:5, E:] = key_sums[:5, :]
    chosen = (iota((H, LANES), 0) == head_ref[2:3, :].astype(jnp.int32)).astype(f32)
    steps = mm(head_sums[...], chosen, NT, exact)
    chosen = (iota((H, inner), 0) == chan_ref[7:8, :].astype(jnp.int32)).astype(f32)
    skips = mm(chan_sums[...], chosen, NT, exact)
    out_ref[7:8, :H] = steps[:1]
    out_ref[7:8, LANES : LANES + H] = steps[1:2]
    out_ref[7:8, 2 * LANES : 2 * LANES + H] = skips[6:7]


def forward_kernel(
    meta_ref, rows_ref, w_ref, conv_ref, bias_ref, norm_ref, step_b_ref, decay_ref, skip_ref, cot_in, out_in,
    val_out, key_out, vsum_ref, ksum_ref, raw_ref, cum_ref, y_ref, gated_ref, state_ref, sums_ref, chan_ref, head_ref,
    cot_out, out_out, proj_out, state, last_v, last_k, proj_v, send, recv,
    *, span, heads,
):
    i = pl.program_id(0)
    chunks = pl.num_programs(0)
    inner = heads * P_SIZE
    late = Late(cot_in, cot_out, out_in, out_out, send, recv)

    @pl.when(i == 0)
    def _():
        late.start()
        own_parameters(chan_ref, head_ref, conv_ref, bias_ref, norm_ref, step_b_ref, decay_ref, skip_ref, heads)
        state[...] = jnp.zeros_like(state)
        last_v[...] = jnp.zeros_like(last_v)
        last_k[...] = jnp.zeros_like(last_k)

    @pl.when(i % 2 == 0)
    def _():
        for lane in range(0, w_ref.shape[1], 512):
            lanes = slice(lane, min(lane + 512, w_ref.shape[1]))
            proj_v[:, lanes] = mm(rows_ref[...], w_ref[:, lanes], NN)

    proj_ref = proj_v.at[pl.ds(pl.multiple_of(i % 2 * CHUNK, CHUNK), CHUNK)]
    proj_out[...] = proj_ref[...]

    @pl.when(i == chunks - 1)
    def _():
        late.middle()

    docs = Docs(meta_ref, i, span)
    lags = [docs.lag(by) for by in range(1, CONV)]

    def convolve(rows, before, weight, bias):
        total = bias + weight[CONV - 1 :] * rows
        for by in range(1, CONV):
            at = CONV - 1 - by
            total = total + weight[at : at + 1] * (shift_down(rows, before, by) * lags[by - 1])
        return total

    rows_v = proj_ref[:, inner : 2 * inner].astype(bf16).astype(f32)
    vsum = convolve(rows_v, last_v[...], chan_ref[:CONV, :], chan_ref[CONV : CONV + 1, :])
    last_v[...] = rows_v[CHUNK - 8 :]
    vsum_ref[...] = vsum
    val_out[...] = (vsum * jax.nn.sigmoid(vsum)).astype(bf16)
    rows_k = proj_ref[:, 2 * inner : 2 * inner + KEYS].astype(bf16).astype(f32)
    ksum = convolve(rows_k, last_k[...], conv_ref[:, E:], bias_ref[:, E:])
    last_k[...] = rows_k[CHUNK - 8 :]
    ksum_ref[...] = ksum
    keys = (ksum * jax.nn.sigmoid(ksum)).astype(bf16)
    key_out[...] = keys

    rows = iota((CHUNK, CHUNK), 0)
    cols = iota((CHUNK, CHUNK), 1)
    chosen = (rows == head_ref[2:3, :].astype(jnp.int32)).astype(f32)
    raw = mm(proj_ref[:, 2 * inner + KEYS :], chosen, NN, exact) + head_ref[:1, :]
    raw_ref[...] = raw
    dt = jax.nn.softplus(raw)
    cum = mm((rows >= cols).astype(f32), -dt * head_ref[1:2, :], NN, exact)
    cum_ref[...] = cum
    cum_t = cum.T
    dt_t = dt.T

    state_ref[0] = state[...].astype(bf16)
    bias = jnp.where((docs.doc == docs.row()) & (rows >= cols), 0.0, -1e30)
    carry_w = docs.flow() * jnp.exp(cum)
    final_w = docs.tail() * jnp.exp(cum[CHUNK - 1 :, :] - cum) * dt
    gain = carry_w[CHUNK - 1 :, :]
    low = cols < P_SIZE
    low_row = low[:1]
    write = keys[:, :N]
    read = keys[:, N:]
    write_t = write.astype(f32).T.astype(bf16)
    scores = mm(read, write, NT)
    square = jnp.zeros((CHUNK, LANES), f32)
    count = docs.count.astype(f32)
    for pair in range(heads // 2):
        first = 2 * pair
        lanes = slice(pair * 128, pair * 128 + 128)
        xf = val_out[:, lanes].astype(f32)
        weights = []
        for h in (first, first + 1):
            decay = jnp.exp(cum[:, h : h + 1] - cum_t[h : h + 1, :] + bias)
            weights.append((decay * scores * dt_t[h : h + 1, :]).astype(bf16))
        stacked = jnp.concatenate(
            [jnp.where(low, xf, 0.0).astype(bf16), jnp.where(low, 0.0, xf).astype(bf16)], axis=0
        )
        old = state[:, lanes]
        y = mm(jnp.concatenate(weights, axis=1), stacked, NN)
        y = y + pair_cols(low, carry_w, first) * mm(read, old.astype(bf16), NN)
        y = y + chan_ref[6:7, lanes] * xf
        y = jnp.where(chan_ref[7:8, lanes] < count, y, 0.0)
        y_ref[:, lanes] = y
        state[:, lanes] = pair_cols(low_row, gain, first) * old + mm(
            write_t, (pair_cols(low, final_w, first) * xf).astype(bf16), NN
        )
        gate = proj_ref[:, lanes]
        gated = y * (gate * jax.nn.sigmoid(gate))
        gated_ref[:, lanes] = gated
        square = square + gated * gated
    share = 1.0 / (count * P_SIZE)
    sums_ref[pl.ds(i, 1), :] = jnp.sum(square.T, axis=0, keepdims=True) * share
    sums_ref[pl.ds(chunks + i, 1), :] = jnp.full((1, LANES), share, f32)

    @pl.when(i == chunks - 1)
    def _():
        late.end()


def head_sums_of(prod, chosen):
    high = prod.astype(bf16)
    low = (prod - high.astype(f32)).astype(bf16)
    return mm(jnp.concatenate([high, low], axis=1), chosen, NN)


def backward_kernel(
    meta_ref, proj_ref, grad_ref, chan_ref, conv_ref, head_ref,
    val_ref, key_ref, vsum_ref, ksum_ref, raw_ref, cum_ref, y_ref, state_ref, sums_ref, branch_ref, go_ref,
    cols_ref, all_sums, b_out, o_out,
    chan_sums, key_sums, head_sums, dstate, dv, next_v, next_k, next_lags, *early_refs,
    span, heads,
):
    chunks = pl.num_programs(0)
    i = chunks - 1 - pl.program_id(0)
    inner = heads * P_SIZE
    early = Early(branch_ref, go_ref, (b_out, o_out) + early_refs)

    @pl.when(pl.program_id(0) == 0)
    def _():
        early.start()
        for ref in (dstate, next_v, next_k, next_lags, chan_sums, key_sums, head_sums):
            ref[...] = jnp.zeros_like(ref)

    docs = Docs(meta_ref, i, span)
    rows = iota((CHUNK, CHUNK), 0)
    cols = iota((CHUNK, CHUNK), 1)
    raw = raw_ref[...]
    dt = jax.nn.softplus(raw)
    cum = cum_ref[...]
    cum_t = cum.T
    count = docs.count.astype(f32)

    def column(row):
        return jnp.broadcast_to(row, (CHUNK, CHUNK)).T

    inv = lax.rsqrt(column(sums_ref[pl.ds(i, 1), :]) + epsilon)
    pull = inv * inv * inv * column(sums_ref[pl.ds(chunks + i, 1), :])

    bias = jnp.where((docs.doc == docs.row()) & (cols >= rows), 0.0, -1e30)
    carry_w = docs.flow() * jnp.exp(cum)
    final_d = docs.tail() * jnp.exp(cum[CHUNK - 1 :, :] - cum)
    final_w = final_d * dt
    gain = carry_w[CHUNK - 1 :, :]
    low = cols < P_SIZE
    low_row = low[:1]
    write = key_ref[:, :N]
    read = key_ref[:, N:]
    read_t = read.astype(f32).T.astype(bf16)
    scores_t = mm(write, read, NT)
    dscores_t = jnp.zeros((CHUNK, CHUNK), f32)
    dwrite = jnp.zeros((CHUNK, N), f32)
    dread = jnp.zeros((CHUNK, N), f32)
    end_row = iota((CHUNK, 1), 0) == CHUNK - 1
    carry_all = jnp.zeros((CHUNK, LANES), f32)
    final_all = jnp.zeros((CHUNK, LANES), f32)
    direct_all = jnp.zeros((CHUNK, LANES), f32)
    gain_rows = []
    dcum_rows = []
    for pair in range(heads // 2):
        first = 2 * pair
        lanes = slice(pair * 128, pair * 128 + 128)
        gate = proj_ref[:, lanes]
        sig = jax.nn.sigmoid(gate)
        silu = gate * sig
        masked = y_ref[:, lanes]
        gated = masked * silu
        norm_gain = chan_ref[5:6, lanes]
        gm = grad_ref[:, lanes]
        unit = gated * inv
        chan_sums[5:6, lanes] += jnp.sum(gm * unit, axis=0, keepdims=True)
        grad_gated = inv * (gm * norm_gain) - pull * gated
        cols_ref[:, lanes] = (grad_gated * masked * silu_slope(gate, sig)).astype(bf16)
        dy = jnp.where(chan_ref[7:8, lanes] < count, grad_gated * silu, 0.0)
        xf = val_ref[:, lanes].astype(f32)
        dyb = dy.astype(bf16)
        x_stack = jnp.concatenate(
            [jnp.where(low, xf, 0.0).astype(bf16), jnp.where(low, 0.0, xf).astype(bf16)], axis=0
        )
        dy_stack = jnp.concatenate(
            [jnp.where(low, dy, 0.0).astype(bf16), jnp.where(low, 0.0, dy).astype(bf16)], axis=0
        )
        dweights = mm(x_stack, dyb, NT)
        old = state_ref[0, :, lanes]
        grad = dstate[:, lanes]
        gradb = grad.astype(bf16)
        carried = mm(read, old, NN)
        pushed = mm(write, gradb, NN)
        carry_p = pair_cols(low, carry_w, first)
        final_p = pair_cols(low, final_w, first)
        chosen = (cols == first + rows // P_SIZE).astype(bf16)
        chosen = jnp.concatenate([chosen, chosen], axis=0)
        carry_all = carry_all + head_sums_of(dy * carried, chosen)
        final_all = final_all + head_sums_of(xf * pushed, chosen)
        gain_rows.append(jnp.sum(grad * old.astype(f32), axis=0, keepdims=True))
        weights = []
        for which, h in enumerate((first, first + 1)):
            col = dt[:, h : h + 1]
            decay = jnp.exp(cum_t[h : h + 1, :] - cum[:, h : h + 1] + bias)
            weighted = decay * col
            weights.append((weighted * scores_t).astype(bf16))
            dw = dweights[which * CHUNK : (which + 1) * CHUNK]
            dscores_t = dscores_t + dw * weighted
            direct = dw * decay * scores_t
            ddt_in = jnp.sum(direct, axis=1, keepdims=True)
            dcum_rows.append(jnp.sum(direct * col, axis=0, keepdims=True))
            direct_all = jnp.where(cols == h, ddt_in, direct_all)
        dx = mm(jnp.concatenate(weights, axis=1), dy_stack, NN)
        dv[:, lanes] = dx + final_p * pushed + chan_ref[6:7, lanes] * dy
        chan_sums[6:7, lanes] += jnp.sum(dy * xf, axis=0, keepdims=True)
        dwrite = dwrite + mm((final_p * xf).astype(bf16), gradb, NT)
        carry_dy = (carry_p * dy).astype(bf16)
        dread = dread + mm(carry_dy, old, NT)
        dstate[:, lanes] = pair_cols(low_row, gain, first) * grad + mm(read_t, carry_dy, NN)
    dsb = dscores_t.astype(bf16)
    dkeys = jnp.concatenate([dwrite + mm(dsb, read, NN), dread + mm(dsb, write, TN)], axis=1)

    chosen = (iota((inner, LANES), 1) == iota((inner, LANES), 0) // P_SIZE).astype(f32)
    gain_all = mm(jnp.broadcast_to(jnp.concatenate(gain_rows, axis=1), (8, inner)), chosen, NN, exact)[:1]
    push = final_w * final_all
    at_end = jnp.sum(push, axis=0, keepdims=True) + gain * gain_all
    ddt = direct_all + final_d * final_all
    dcum = carry_w * carry_all - push - dt * direct_all + jnp.where(end_row, at_end, 0.0)
    extra = jnp.concatenate(dcum_rows + [jnp.zeros((LANES - heads, CHUNK), f32)], axis=0)
    dlog = mm((cols >= rows).astype(f32), dcum + extra.T, NN, exact)
    rate = head_ref[1:2, :]
    grad_step = (ddt - rate * dlog) * jax.nn.sigmoid(raw)
    head_sums[:1, :] += jnp.sum(grad_step, axis=0, keepdims=True)
    head_sums[1:2, :] -= jnp.sum(dt * rate * dlog, axis=0, keepdims=True)
    chosen = (rows == head_ref[2:3, :].astype(jnp.int32)).astype(bf16)
    cols_ref[:, 2 * inner + KEYS :] = mm(grad_step.astype(bf16), chosen, NT).astype(bf16)

    lags = [docs.lag(by) for by in range(1, CONV)]

    def convolve_back(dact, total, rows_in, after, weight, sums):
        dconv = dact * silu_slope(total, jax.nn.sigmoid(total))
        grad_in = weight[CONV - 1 :] * dconv
        sums[CONV : CONV + 1, :] += jnp.sum(dconv, axis=0, keepdims=True)
        sums[CONV - 1 : CONV, :] += jnp.sum(dconv * rows_in, axis=0, keepdims=True)
        for by in range(1, CONV):
            at = CONV - 1 - by
            moved = shift_up(dconv * lags[by - 1], after[...] * next_lags[:, by - 1 : by], by)
            grad_in = grad_in + weight[at : at + 1] * moved
            sums[at : at + 1, :] += jnp.sum(moved * rows_in, axis=0, keepdims=True)
        after[...] = dconv[:8]
        return grad_in.astype(bf16)

    rows_v = proj_ref[:, inner : 2 * inner].astype(bf16).astype(f32)
    cols_ref[:, inner : 2 * inner] = convolve_back(dv[...], vsum_ref[...], rows_v, next_v, chan_ref[:CONV, :], chan_sums)
    rows_k = proj_ref[:, 2 * inner : 2 * inner + KEYS].astype(bf16).astype(f32)
    cols_ref[:, 2 * inner : 2 * inner + KEYS] = convolve_back(
        dkeys, ksum_ref[...], rows_k, next_k, conv_ref[:, E:], key_sums
    )
    for by in range(1, CONV):
        next_lags[:, by - 1 : by] = lags[by - 1][:8]

    @pl.when(pl.program_id(0) == 0)
    def _():
        early.middle()

    @pl.when(pl.program_id(0) == chunks - 1)
    def _():
        whole_sums(all_sums, chan_sums, key_sums, head_sums, head_ref, chan_ref, heads)
        early.end()


def mixer_forward(meta, normed, in_w, params, cot, out_w, span, heads):
    length = normed.shape[0]
    columns = in_w.shape[1]
    inner = heads * P_SIZE
    chunks = length // CHUNK
    copies = sum(len(left_over(cot_order(o))) for o in range(cot.shape[0])) + 2 * (out_w.shape[0] - 1)
    row = lambda width: pl.BlockSpec((CHUNK, width), lambda i: (i, 0))
    all_of = lambda *shape: pl.BlockSpec(shape, lambda i: (0,) * len(shape))
    out = lambda width, dtype: jax.ShapeDtypeStruct((length, width), dtype)
    return pl.pallas_call(
        partial(forward_kernel, span=span, heads=heads),
        grid=(chunks,),
        in_specs=[
            pl.BlockSpec(memory_space=pltpu.SMEM), pl.BlockSpec((2 * CHUNK, normed.shape[1]), lambda i: (i // 2, 0)),
            all_of(*in_w.shape),
        ]
        + [all_of(*part.shape) for part in params]
        + [HBM] * 2,
        out_specs=[
            row(inner), row(KEYS), row(inner), row(KEYS), row(LANES), row(LANES), row(inner), row(inner),
            pl.BlockSpec((1, N, inner), lambda i: (i, 0, 0)), all_of(2 * chunks, LANES),
            all_of(8, inner), all_of(8, LANES), HBM, HBM, row(columns),
        ],
        out_shape=[
            out(inner, bf16), out(KEYS, bf16), out(inner, f32), out(KEYS, f32), out(LANES, f32), out(LANES, f32),
            out(inner, f32), out(inner, f32), jax.ShapeDtypeStruct((chunks, N, inner), bf16),
            jax.ShapeDtypeStruct((2 * chunks, LANES), f32), jax.ShapeDtypeStruct((8, inner), f32),
            jax.ShapeDtypeStruct((8, LANES), f32), jax.ShapeDtypeStruct(cot.shape, bf16),
            jax.ShapeDtypeStruct(out_w.shape, bf16), out(columns, f32),
        ],
        input_output_aliases={3 + len(params): 12, 4 + len(params): 13},
        scratch_shapes=[pltpu.VMEM((N, inner), f32), pltpu.VMEM((8, inner), f32), pltpu.VMEM((8, KEYS), f32)]
        + [pltpu.VMEM((2 * CHUNK, columns), f32)]
        + sems(copies, 1)[:2],
        compiler_params=remote_params(4, 58),
        cost_estimate=pl.CostEstimate(
            flops=length * inner * 1024, bytes_accessed=length * inner * 24, transcendentals=length * heads * CHUNK
        ),
        name="mixer_forward",
    )(meta, normed, in_w, *params, cot, out_w)


def mixer_backward(meta, projected, grad_mixed, chan, conv, head_vec, kept, sums, branch, grad_out, span, heads):
    length = projected.shape[0]
    inner = heads * P_SIZE
    chunks = length // CHUNK
    me = Place()
    near, peers, tokens, width = branch.shape
    far = me.far
    part = grad_out.shape[2:]
    copies = near * peers // 2 + 2 * far - 1
    vm = lambda *shape: pltpu.VMEM(shape, bf16)
    row = lambda width: pl.BlockSpec((CHUNK, width), lambda i: (chunks - 1 - i, 0))
    all_of = lambda *shape: pl.BlockSpec(shape, lambda i: (0,) * len(shape))
    out = lambda width: jax.ShapeDtypeStruct((length, width), bf16)
    return pl.pallas_call(
        partial(backward_kernel, span=span, heads=heads),
        grid=(chunks,),
        in_specs=[
            pl.BlockSpec(memory_space=pltpu.SMEM), row(2 * inner + KEYS + STEP_PAD), row(inner),
            all_of(8, inner), all_of(*conv.shape), all_of(8, LANES),
            row(inner), row(KEYS), row(inner), row(KEYS), row(LANES), row(LANES), row(inner),
            pl.BlockSpec((1, N, inner), lambda i: (chunks - 1 - i, 0, 0)), all_of(2 * chunks, LANES), HBM, HBM,
        ],
        out_specs=[
            row(2 * inner + KEYS + STEP_PAD), all_of(8, conv.shape[1]), VMEM, VMEM,
        ],
        out_shape=[
            out(2 * inner + KEYS + STEP_PAD), jax.ShapeDtypeStruct((8, conv.shape[1]), f32),
            jax.ShapeDtypeStruct((near, peers // 2, tokens, width), bf16), jax.ShapeDtypeStruct(part, f32),
        ],
        scratch_shapes=[
            pltpu.VMEM((8, inner), f32), pltpu.VMEM((8, KEYS), f32), pltpu.VMEM((8, LANES), f32),
            pltpu.VMEM((N, inner), f32), pltpu.VMEM((CHUNK, inner), f32), pltpu.VMEM((8, inner), f32),
            pltpu.VMEM((8, KEYS), f32), pltpu.VMEM((8, LANES), f32),
            vm(near, peers // 2, tokens, width), vm(near, peers // 2, tokens, width),
            vm(far, *part), vm(far, *part), vm(max(far - 1, 1), *part),
        ]
        + sems(copies, near * peers // 2 + far),
        compiler_params=remote_params(3, 32),
        cost_estimate=pl.CostEstimate(
            flops=length * inner * 3072, bytes_accessed=length * inner * 30, transcendentals=length * heads * CHUNK
        ),
        name="mixer_backward",
    )(meta, projected, grad_mixed, chan, conv, head_vec, *kept, sums, branch, grad_out)


MESH = pl.DeviceIdType.MESH
HBM = pl.BlockSpec(memory_space=pl.ANY)
VMEM = pl.BlockSpec(memory_space=pltpu.VMEM)


def z_pair(peers, groups):
    planes = groups // 2
    return 2 if planes % 2 == 0 and (E // (peers * planes)) % (2 * P_SIZE) == 0 else 1


def flip(value, bits):
    bit = 1
    while bit <= bits:
        if bits & bit:
            value = value + bit - 2 * bit * (value // bit % 2)
        bit *= 2
    return value


class Place:
    def __init__(self):
        self.peers = lax.axis_size("seq")
        groups = lax.axis_size("batch")
        self.near = z_pair(self.peers, groups)
        self.far = groups // 2 // self.near
        self.s = lax.axis_index("seq")
        b = lax.axis_index("batch")
        self.c = b % 2
        self.zl = b // 2 % self.near
        self.zh = b // 2 // self.near

    def at(self, s=0, zl=0, zh=0, c=0):
        return (flip(self.s, s), (flip(self.zh, zh) * self.near + flip(self.zl, zl)) * 2 + flip(self.c, c))

    def heads_at(self, index, per, width):
        outer = self.far if self.near > 1 else 1
        run = width // outer
        return (((self.s * outer + index // run) * self.near + self.zl) * run + index % run) // per

    def channel_runs(self, width):
        outer = self.far if self.near > 1 else 1
        run = width // outer
        runs = []
        for i in range(outer):
            first = ((self.s * outer + i) * self.near + self.zl) * run
            runs.append((pl.ds(pl.multiple_of(first, 128), run), slice(i * run, (i + 1) * run)))
        return runs

    def column_runs(self, s, zl, width):
        outer = self.far if self.near > 1 else 1
        run = width // (2 * outer)
        runs = []
        for part in range(2):
            for i in range(outer):
                first = part * E + ((s * outer + i) * self.near + zl) * run
                runs.append((pl.ds(pl.multiple_of(first, 128), run), pl.ds((part * outer + i) * run, run)))
        return runs

    def partners(self):
        cube = [self.at(s=o // self.near, zl=o % self.near) for o in range(1, self.peers * self.near)]
        return cube, [self.at(zh=o) for o in range(1, self.far)], [self.at(c=1)]


def greet(devices):
    barrier = pltpu.get_barrier_semaphore()
    for device in devices:
        pl.semaphore_signal(barrier, inc=1, device_id=device, device_id_type=MESH)
    pl.semaphore_wait(barrier, len(devices))


class Mover:
    def __init__(self, send, recv, local):
        self.send, self.recv, self.local = send, recv, local
        self.sent, self.kept = 0, 0
        self.open = []

    def plan(self, src, dst, device):
        copy = pltpu.make_async_remote_copy(
            src_ref=src, dst_ref=dst, send_sem=self.send.at[self.sent], recv_sem=self.recv.at[self.sent],
            device_id=device, device_id_type=MESH,
        )
        self.sent += 1
        self.open.append(copy)
        return copy

    def put(self, src, dst, device):
        copy = self.plan(src, dst, device)
        copy.start()
        return copy

    def plan_keep(self, src, dst):
        self.kept += 1
        return pltpu.make_async_copy(src, dst, self.local.at[self.kept - 1])

    def keep(self, src, dst):
        copy = self.plan_keep(src, dst)
        copy.start()
        return copy

    def close(self):
        for copy in self.open:
            copy.wait_send()


def run_paths(paths):
    paths = list(paths)
    while paths:
        alive = []
        for path in paths:
            try:
                next(path)
                alive.append(path)
            except StopIteration:
                pass
        paths = alive


def turn(paths):
    for path in paths:
        next(path, None)


def bits_of(peers):
    return [1 << i for i in range(peers.bit_length() - 1)]


def combos(bits):
    out = [0]
    for bit in reversed(bits):
        out = [bit | o for o in out] + out
    return out


def cot_order(near):
    bits = bits_of(lax.axis_size("seq"))
    return bits if near else bits[::-1]


def left_over(order):
    return combos(order[:-1])


class Late:
    def __init__(self, src, dst, out_src, out_dst, send, recv):
        me = self.me = Place()
        self.mover = Mover(send, recv, None)
        self.copies, self.far, self.forward = [], [], []
        for o in range(me.near):
            order = cot_order(o)
            for h in left_over(order):
                at = (flip(me.zl, o), flip(me.s, h))
                self.copies.append(self.mover.plan(src.at[at], dst.at[at], me.at(s=order[-1])))
        for o in range(1, me.far):
            at = (me.zh, me.c)
            self.far.append(self.mover.plan(out_src.at[at], out_dst.at[at], me.at(zh=o)))
        for o in range(1, me.far):
            at = (flip(me.zh, o), me.c)
            self.forward.append(self.mover.plan(out_dst.at[at], out_dst.at[at], me.at(c=1)))

    def start(self):
        _, far, sibling = self.me.partners()
        greet([self.me.at(s=bit) for bit in sorted({cot_order(o)[-1] for o in range(self.me.near)})] + far + sibling)
        for copy in self.far + self.copies:
            copy.start()

    def middle(self):
        for far, forward in zip(self.far, self.forward):
            far.wait_recv()
            forward.start()

    def end(self):
        for copy in self.copies + self.forward:
            copy.wait_recv()
        self.mover.close()


def gather_kernel(
    in_ref, out_ref, cot_ref, inputs_ref, gain_ref, step_ref, lengths_ref, width_ref,
    w_ref, o_ref, x_ref, ct_ref, m_ref, inv_ref, rows_ref, steps_ref, meta_ref, send, recv, local,
):
    prepare(inputs_ref, gain_ref, step_ref, lengths_ref, width_ref, rows_ref, inv_ref, steps_ref, meta_ref)
    cot_ref = cot_ref.at[0]
    me = Place()
    s, zl, zh, c = me.s, me.zl, me.zh, me.c
    columns = w_ref.shape[-1] - KEYS - STEP_PAD
    mine, shared = pl.ds(0, columns), pl.ds(columns, KEYS + STEP_PAD)
    cube, far, sibling = me.partners()
    greet(cube + far + sibling)
    mover = Mover(send, recv, local)
    bits = bits_of(me.peers)

    def plane_path(src, dst, order, near, skip=()):
        view = dst.at[flip(zl, near)]
        if near:
            copy = mover.put(src, dst.at[zl, s], me.at(zl=near))
            yield
            copy.wait_recv()
        else:
            own = mover.keep(src, view.at[s])
        held = [0]
        for bit in order:
            copies = []
            for h in held:
                if bit == order[-1] and h in skip:
                    continue
                at = view.at[flip(s, h)]
                copies.append(mover.put(at if near or h else src, at if near else dst.at[zl, flip(s, h)], me.at(s=bit)))
            held = held + [h ^ bit for h in held]
            yield
            for copy in copies:
                copy.wait_recv()
        if not near:
            own.wait()

    def meta_path():
        own = mover.keep(meta_ref, m_ref.at[zl])
        near = [mover.put(meta_ref, m_ref.at[zl], me.at(zl=o)) for o in range(1, me.near)]
        yield
        own.wait()
        for copy in near:
            copy.wait_recv()

    def key_path():
        block = w_ref.at[s, zh, zl, c]
        parts = [
            (in_ref.at[:, pl.ds(2 * E, KEYS)], block.at[:, pl.ds(columns, KEYS)]),
            (steps_ref, block.at[:, pl.ds(columns + KEYS, STEP_PAD)]),
        ]
        own = [mover.keep(*part) for part in parts]
        copies = [mover.put(*part, me.at(zh=o)) for o in range(1, me.far) for part in parts]
        yield
        for copy in own:
            copy.wait()
        for copy in copies:
            copy.wait_recv()
        block = w_ref.at[s, :, zl, c, :, shared]
        copies = [mover.put(block, block, me.at(zl=o)) for o in range(1, me.near)]
        yield
        for copy in copies:
            copy.wait_recv()
        held = [0]
        for bit in bits:
            copies = []
            for h in held:
                block = w_ref.at[flip(s, h), :, :, c, :, shared]
                copies.append(mover.put(block, block, me.at(s=bit)))
            held = held + [h ^ bit for h in held]
            yield
            for copy in copies:
                copy.wait_recv()
        block = w_ref.at[:, :, :, c, :, shared]
        copy = mover.put(block, block, me.at(c=1))
        yield
        copy.wait_recv()

    def spread_path(copies, view):
        last = []
        for o, copy in copies:
            yield
            copy.wait_recv()
            last.append(mover.put(view(flip(zh, o)), view(flip(zh, o)), me.at(c=1)))
        return last

    def out_path():
        own = mover.keep(out_ref, o_ref.at[zh, c])
        first = mover.put(out_ref, o_ref.at[zh, c], me.at(c=1))
        yield
        own.wait()
        first.wait_recv()

    def weight_path():
        moves = {}
        for step in range(me.peers):
            for o in range(me.near):
                to_s, to_zl = flip(s, step), flip(zl, o)
                for src, dst in me.column_runs(to_s, to_zl, columns):
                    src = in_ref.at[:, src]
                    dst = w_ref.at[s, zh, zl, c, :, dst]
                    if step or o:
                        copy = mover.put(src, dst, me.at(s=step, zl=o))
                    else:
                        copy = mover.keep(src, dst)
                    moves.setdefault(step, []).append(copy)
        pieces = []
        for step in range(me.peers):
            yield
            for i, copy in enumerate(moves[step]):
                if step == 0 and i < len(moves[0]) // me.near:
                    copy.wait()
                else:
                    copy.wait_recv()
            block = w_ref.at[flip(s, step), zh, :, c, :, mine]
            copies = [(o, mover.put(block, block, me.at(zh=o))) for o in range(1, me.far)]
            pieces.append((step, copies, mover.put(block, block, me.at(c=1))))
        last = []
        for step, copies, first in pieces:
            last.append(first)
            last += yield from spread_path(copies, lambda h, step=step: w_ref.at[flip(s, step), h, :, c, :, mine])
        yield
        for copy in last:
            copy.wait_recv()

    own_x = plane_path(rows_ref, x_ref, bits, 0)
    near_x = [plane_path(rows_ref, x_ref, bits[::-1], o) for o in range(1, me.near)]
    own_c, *near_c = [plane_path(cot_ref, ct_ref, cot_order(o), o, left_over(cot_order(o))) for o in range(me.near)]
    keys, weights, outs, extra = key_path(), weight_path(), out_path(), meta_path()
    turn([keys, weights, own_x] + near_x + [own_c, outs, extra])
    turn([keys] + near_x + near_c + [keys] + [weights] * me.peers + [keys] + near_x + [own_x, own_c] + near_c)
    turn([keys, weights, keys, weights, weights, weights] + near_x + [own_x] + near_c)
    run_paths([weights, extra, keys, outs, own_x, own_c] + near_x + near_c)
    mover.close()


def remote_params(identity, mib):
    return pltpu.CompilerParams(collective_id=identity, has_side_effects=True, vmem_limit_bytes=mib * 2**20)


def sems(copies, kept):
    return [pltpu.SemaphoreType.DMA((copies,)), pltpu.SemaphoreType.DMA((copies,)), pltpu.SemaphoreType.DMA((kept,))]


def prepare(x_ref, gain_ref, step_ref, lengths_ref, width_ref, normed_ref, inv_ref, steps_ref, meta_ref):
    x = x_ref[0].astype(f32)
    inv = lax.rsqrt(jnp.mean(x * x, axis=1, keepdims=True) + epsilon)
    normed_ref[...] = (x * inv * gain_ref[...]).astype(bf16)
    inv_ref[...] = jnp.broadcast_to(inv, inv_ref.shape)
    steps_ref[...] = jnp.zeros_like(steps_ref)
    steps_ref[:, :H] = step_ref[...]
    lanes = iota(meta_ref.shape, 1)
    meta = jnp.where(lanes == DOCS, width_ref[0], 0)
    for i in range(DOCS):
        meta = jnp.where(lanes == i, lengths_ref[0, i], meta)
    meta_ref[...] = meta


def gather(in_w, out_w, cot, inputs, gain, step_w, lengths, head_width):
    me = Place()
    peers, near, far = me.peers, me.near, me.far
    shape = lambda lead, part: jax.ShapeDtypeStruct(lead + part, bf16)
    rows = inputs.shape[1:]
    columns = 2 * E // (peers * near)
    runs = 2 * (far if near > 1 else 1)
    copies = runs * (peers * near - 1) + (peers + 1) * (2 * far - 1) + 2 * (near * peers - 1)
    copies -= sum(len(left_over(cot_order(o))) for o in range(near))
    copies += 2 * near + peers + 2 * far - 4
    smem = pl.BlockSpec(memory_space=pltpu.SMEM)
    return pl.pallas_call(
        gather_kernel,
        out_shape=[
            shape((peers, far, near, 2), (in_w.shape[0], columns + KEYS + STEP_PAD)),
            shape((far, 2), out_w.shape),
            shape((near, peers), rows),
            shape((near, peers), rows),
            jax.ShapeDtypeStruct((near, 8, LANES), jnp.int32),
            jax.ShapeDtypeStruct((rows[0], LANES), f32),
        ],
        in_specs=[HBM] * 3 + [VMEM] * 3 + [smem] * 2,
        out_specs=[HBM] * 5 + [VMEM],
        scratch_shapes=[
            pltpu.VMEM(rows, bf16), pltpu.VMEM((in_w.shape[0], STEP_PAD), bf16), pltpu.VMEM((8, LANES), jnp.int32)
        ]
        + sems(copies, runs + 6),
        compiler_params=remote_params(0, 58),
        name="gather_all",
    )(in_w, out_w, cot, inputs, gain, step_w, lengths, head_width)


def total_kernel(part_ref, gated_ref, chan_ref, grad_ref, sum_ref, mixed_ref, mine, box, send, recv, local):
    me = Place()
    cube = me.partners()[0]
    greet(cube)
    mover = Mover(send, recv, local)
    chunks = part_ref.shape[0] // 2
    tiles = [slice(lane, lane + LANES) for lane in range(0, gated_ref.shape[1], LANES)]
    mine[...] = part_ref[...]

    def products(i, carry):
        at = pl.ds(pl.multiple_of(i * CHUNK, CHUNK), CHUNK)
        cross = jnp.zeros((CHUNK, LANES), f32)
        for lanes in tiles:
            cross = cross + gated_ref[at, lanes] * (grad_ref[at, lanes] * chan_ref[5:6, lanes])
        row = pl.ds(chunks + i, 1)
        mine[row, :] = jnp.sum(cross.T, axis=0, keepdims=True) * part_ref[row, :]
        return carry

    lax.fori_loop(0, chunks, products, 0)
    copies = [mover.put(mine, box.at[i], device) for i, device in enumerate(cube)]
    total = mine[...]
    for i, copy in enumerate(copies):
        copy.wait_recv()
        total = total + box[i]
    sum_ref[...] = total

    def mix(i, carry):
        at = pl.ds(pl.multiple_of(i * CHUNK, CHUNK), CHUNK)
        inv = lax.rsqrt(jnp.broadcast_to(sum_ref[pl.ds(i, 1), :], (CHUNK, CHUNK)).T + epsilon)
        for lanes in tiles:
            mixed_ref[at, lanes] = (gated_ref[at, lanes] * inv * chan_ref[5:6, lanes]).astype(bf16)
        return carry

    lax.fori_loop(0, chunks, mix, 0)
    mover.close()


def cube_total(part, gated, chan, grad):
    me = Place()
    count = me.peers * me.near - 1
    return pl.pallas_call(
        total_kernel,
        out_shape=[jax.ShapeDtypeStruct(part.shape, f32), jax.ShapeDtypeStruct(gated.shape, bf16)],
        in_specs=[VMEM] * 4,
        out_specs=[VMEM] * 2,
        scratch_shapes=[pltpu.VMEM(part.shape, f32), pltpu.VMEM((count,) + part.shape, f32)] + sems(count, 1),
        compiler_params=remote_params(1, 12),
        name="cube_total",
    )(part, gated, chan, grad)


def add_rows(out, parts):
    shape = out.shape
    tile = min(16, shape[-2])
    lead = [()]
    for size in shape[:-2]:
        lead = [l + (i,) for l in lead for i in range(size)]
    for l in lead:

        def step(i, carry, l=l):
            at = l + (pl.ds(pl.multiple_of(i * tile, tile), tile), slice(None))
            total = parts[0][at].astype(f32)
            for part in parts[1:]:
                total = total + part[at].astype(f32)
            out[at] = total.astype(out.dtype)
            return carry

        lax.fori_loop(0, shape[-2] // tile, step, 0)


def scatter_kernel(
    gn_ref, gw_ref, b_ref, u_ref, p_ref, gain_ref, og_ref, ow_ref, ob_ref, ok_ref, ou_ref,
    n_own, n_box, n_near, b_own, b_box, b_near, w_own, w_box, w_far,
    k_own, k_box, k_near, k_far, k_bits, u_box, send, recv, local,
):
    me = Place()
    s, zl, zh, c = me.s, me.zl, me.zh, me.c
    cube, far, sibling = me.partners()
    greet(cube + far + sibling)
    mover = Mover(send, recv, local)
    bits = bits_of(me.peers)
    columns = w_own.shape[-1]
    mine, shared = pl.ds(0, columns), pl.ds(columns, k_own.shape[-1])

    def rows_path(src, own, box, near_box, out, order, near, arrivals, done=0):
        own, box = own.at[near], box.at[near]
        copies, loads = [], []
        if done:
            half = me.peers // 4
            for j in range(half):
                copies.append(mover.put(src.at[near, j], box.at[j], me.at(s=order[1])))
                loads.append(mover.keep(src.at[near, half + j], own.at[half + j]))
        else:
            at_zl = src.at[flip(zl, near)]
            for j, o in enumerate(combos(order[1:])):
                copies.append(mover.put(at_zl.at[flip(s, order[0] ^ o)], box.at[j], me.at(s=order[0])))
                loads.append(mover.keep(at_zl.at[flip(s, o)], own.at[j]))
        base = 0
        for i in range(done, len(order)):
            rest = order[i + 1 :]
            count = 1 << len(rest)
            offset = (1 << (len(order) - 1)) - count
            coming = []
            for j in range(count):
                yield
                copies[j].wait_recv()
                if i == done:
                    loads[j].wait()
                if rest or near:
                    add_rows(own.at[offset + j], [own.at[offset + j], box.at[base + j]])
                if rest and j < count // 2:
                    coming.append(mover.put(own.at[offset + j], box.at[base + count + j], me.at(s=rest[0])))
            copies = coming
            last = base
            base += count
        end = (1 << (len(order) - 1)) - 1
        if near:
            arrivals.append(mover.put(own.at[end], near_box.at[near - 1], me.at(zl=near)))
            yield
        else:
            yield
            for _ in range(me.near - 1):
                arrivals.pop(0).wait_recv()
            add_rows(out, [own.at[end], box.at[last]] + [near_box.at[o - 1] for o in range(1, me.near)])

    def weight_path():
        order = [(o, k) for o in range(1, me.far) for k in range(me.peers)] + [(0, k) for k in range(me.peers)]
        loads, copies = {}, {}
        for o, k in order:
            copies[o, k] = mover.put(gw_ref.at[flip(s, k), flip(zh, o), :, 1 - c, :, mine], w_box.at[o, k], me.at(c=1))
            loads[o, k] = mover.keep(gw_ref.at[flip(s, k), flip(zh, o), :, c, :, mine], w_own.at[o, k])
        far_copies = {}
        for o, k in order:
            yield
            loads[o, k].wait()
            copies[o, k].wait_recv()
            if o:
                add_rows(w_own.at[o, k], [w_own.at[o, k], w_box.at[o, k]])
                far_copies[o, k] = mover.put(w_own.at[o, k], w_far.at[o - 1, k], me.at(zh=o))
        ends, kept = [], []
        for k in range(me.peers):
            yield
            for o in range(1, me.far):
                far_copies[o, k].wait_recv()
            parts = [w_own.at[0, k], w_box.at[0, k]] + [w_far.at[o - 1, k] for o in range(1, me.far)]
            add_rows(w_own.at[0, k], parts)
            for o in range(me.near):
                for whole, part in me.column_runs(s, zl, columns):
                    src = w_own.at[0, k, flip(zl, o), :, part]
                    if k or o:
                        ends.append(mover.put(src, ow_ref.at[:, whole], me.at(s=k, zl=o)))
                    else:
                        kept.append(mover.keep(src, ow_ref.at[:, whole]))
        yield
        for copy in kept:
            copy.wait()
        for copy in ends:
            copy.wait_recv()

    def key_path():
        blocks = combos(bits)
        copies, loads = [], []
        for j, o in enumerate(blocks):
            copies.append(mover.put(gw_ref.at[flip(s, o), :, :, 1 - c, :, shared], k_box.at[j], me.at(c=1)))
            loads.append(mover.keep(gw_ref.at[flip(s, o), :, :, c, :, shared], k_own.at[j]))
        half = me.peers // 2
        sent = []
        for j in range(me.peers):
            yield
            loads[j].wait()
            copies[j].wait_recv()
            add_rows(k_own.at[j], [k_own.at[j], k_box.at[j]])
            if j < half:
                sent.append(mover.put(k_own.at[j], k_bits.at[j], me.at(s=bits[0])))
        base = 0
        for i, bit in enumerate(bits):
            count = me.peers >> (i + 1)
            offset = me.peers - count
            coming = []
            for j in range(count):
                yield
                sent[j].wait_recv()
                add_rows(k_own.at[offset + j], [k_own.at[offset + j], k_bits.at[base + j]])
                if i + 1 < len(bits) and j < count // 2:
                    coming.append(mover.put(k_own.at[offset + j], k_bits.at[base + count + j], me.at(s=bits[i + 1])))
            base += count
            sent = coming
        end = k_own.at[me.peers - 1]
        copies = [mover.put(end.at[:, flip(zl, o)], k_near.at[o - 1], me.at(zl=o)) for o in range(1, me.near)]
        yield
        for copy in copies:
            copy.wait_recv()
        add_rows(end.at[:, zl], [end.at[:, zl]] + [k_near.at[o - 1] for o in range(1, me.near)])
        copies = [mover.put(end.at[flip(zh, o), zl], k_far.at[o - 1], me.at(zh=o)) for o in range(1, me.far)]
        yield
        for copy in copies:
            copy.wait_recv()
        add_rows(ok_ref, [end.at[zh, zl]] + [k_far.at[o - 1] for o in range(1, me.far)])

    def small_path():
        turns = [me.at(c=1)] + [me.at(zl=o) for o in bits_of(me.near)]
        turns += [me.at(s=o) for o in bits] + [me.at(zh=o) for o in bits_of(me.far)]
        u_box[0] = u_ref[...]
        u_box[0, 6:7, : p_ref.shape[1]] = p_ref[...] / gain_ref[...]
        for i, device in enumerate(turns):
            copy = mover.put(u_box.at[2 * i], u_box.at[2 * i + 1], device)
            yield
            copy.wait_recv()
            u_box[2 * i + 2] = u_box[2 * i] + u_box[2 * i + 1]
        ou_ref[...] = u_box[2 * len(turns)]

    coming_n, coming_b = [], []
    grads = (gn_ref, n_own, n_box, n_near, og_ref)
    branch = (b_ref, b_own, b_box, b_near, ob_ref)
    orders = lambda o: bits if o else bits[::-1]
    near_n = [rows_path(*grads, orders(o), o, coming_n) for o in range(1, me.near)]
    near_b = [rows_path(*branch, orders(o), o, coming_b, 1) for o in range(1, me.near)]
    own_n = rows_path(*grads, orders(0), 0, coming_n)
    own_b = rows_path(*branch, orders(0), 0, coming_b, 1)
    weights, keys, small = weight_path(), key_path(), small_path()
    turn(near_b + near_n + [weights, own_n, keys, own_b, small])
    turn([weights] * (me.far * me.peers) + [keys] * me.peers + [small])
    turn(near_b + near_n + [keys, own_b, small] + near_b + near_n + [keys, small, keys, own_b, own_n])
    run_paths(near_b + near_n + [keys, small, weights, own_b, own_n])
    mover.close()


def scatter(grads, gw, branch, small, products, gain):
    me = Place()
    peers, near, far = me.peers, me.near, me.far
    tokens, width = grads.shape[2:]
    stages = len(bits_of(peers)) + len(bits_of(near)) + len(bits_of(far)) + 1
    vm = lambda *shape: pltpu.VMEM(shape, bf16)
    boxes = lambda part: pltpu.VMEM((2 * stages + 1,) + part.shape, f32)
    keys = KEYS + STEP_PAD
    rows = gw.shape[4]
    block = (near, rows, gw.shape[5] - keys)
    kblock = (near, rows, keys)
    runs = 2 * (far if near > 1 else 1)
    copies = peers * near - 1 + (2 * far - 1) * peers + runs * (peers * near - 1)
    copies += 2 * peers - 1 + near - 1 + far - 1 + stages + peers // 2 * near - 1
    kept = peers * near + far * peers + runs + peers + near * peers // 4
    same = lambda part: jax.ShapeDtypeStruct(part.shape, part.dtype)
    return pl.pallas_call(
        scatter_kernel,
        out_shape=[
            jax.ShapeDtypeStruct((tokens, width), f32),
            jax.ShapeDtypeStruct((rows, 2 * E), bf16),
            jax.ShapeDtypeStruct((tokens, width), f32),
            jax.ShapeDtypeStruct((rows, keys), f32),
            same(small),
        ],
        in_specs=[HBM] * 3 + [VMEM] * 3,
        out_specs=[VMEM, HBM, VMEM, VMEM, VMEM],
        scratch_shapes=[
            vm(near, peers // 2, tokens, width), vm(near, peers - 1, tokens, width), vm(max(near - 1, 1), tokens, width),
            vm(near, peers // 2, tokens, width), vm(near, peers // 2 - 1, tokens, width), vm(max(near - 1, 1), tokens, width),
            vm(far, peers, *block), vm(far, peers, *block), vm(max(far - 1, 1), peers, *block),
            vm(peers, far, *kblock), vm(peers, far, *kblock), vm(max(near - 1, 1), far, *kblock[1:]),
            vm(max(far - 1, 1), *kblock[1:]), vm(peers - 1, far, *kblock), boxes(small),
        ]
        + sems(copies, kept),
        compiler_params=remote_params(2, 40),
        cost_estimate=pl.CostEstimate(flops=0, bytes_accessed=250 * 10**6, transcendentals=0),
        name="scatter_all",
    )(grads, gw, branch, small, products, gain)


class Early:
    def __init__(self, b_ref, go_ref, refs):
        self.b_out, self.o_out, self.b_own, self.b_box, self.o_own, self.o_box, self.o_far, send, recv, local = refs
        me = self.me = Place()
        mover = self.mover = Mover(send, recv, local)
        bits = bits_of(me.peers)
        self.rows, self.outs, self.far = [], [], []
        for o in range(me.near):
            order = bits if o else bits[::-1]
            at_zl = b_ref.at[flip(me.zl, o)]
            for j, left in enumerate(combos(order[1:])):
                put = mover.plan(at_zl.at[flip(me.s, order[0] ^ left)], self.b_box.at[o, j], me.at(s=order[0]))
                self.rows.append((put, mover.plan_keep(at_zl.at[flip(me.s, left)], self.b_own.at[o, j]), (o, j)))
        for o in range(me.far):
            put = mover.plan(go_ref.at[flip(me.zh, o), 1 - me.c], self.o_box.at[o], me.at(c=1))
            self.outs.append((put, mover.plan_keep(go_ref.at[flip(me.zh, o), me.c], self.o_own.at[o])))
        for o in range(1, me.far):
            self.far.append(mover.plan(self.o_own.at[o], self.o_far.at[o - 1], me.at(zh=o)))

    def start(self):
        _, far, sibling = self.me.partners()
        bits = bits_of(self.me.peers)
        greet([self.me.at(s=bit) for bit in sorted({bits[0], bits[-1]})] + far + sibling)
        for put, load in self.outs:
            put.start()
            load.start()
        for put, load, _ in self.rows:
            put.start()
            load.start()

    def middle(self):
        for o, (put, load) in enumerate(self.outs):
            load.wait()
            put.wait_recv()
            if o:
                add_rows(self.o_own.at[o], [self.o_own.at[o], self.o_box.at[o]])
                self.far[o - 1].start()

    def end(self):
        for put, load, at in self.rows:
            load.wait()
            put.wait_recv()
            add_rows(self.b_out.at[at], [self.b_own.at[at], self.b_box.at[at]])
        for put in self.far:
            put.wait_recv()
        add_rows(self.o_out, [self.o_own.at[0], self.o_box.at[0]] + [self.o_far.at[o] for o in range(self.me.far - 1)])
        self.mover.close()


def finish_kernel(
    x_ref, cot_ref, gain_ref, inv_ref, og_ref, ob_ref, ow_ref, ok_ref, u_ref,
    out_ref, gx_ref, gw_ref, gs_ref, gc_ref, gb_ref, gp_ref, gn_ref, g0_ref, g1_ref, g2_ref,
):
    x = x_ref[0].astype(f32)
    out_ref[0] = (x + ob_ref[...]).astype(bf16)
    inv = inv_ref[:, :1]
    scaled = og_ref[...] * gain_ref[...]
    dot = jnp.mean(scaled * x, axis=1, keepdims=True)
    gx_ref[0] = inv * scaled - x * (inv * inv * inv * dot) + cot_ref[0].astype(f32)
    gw_ref[:, : 2 * E] = ow_ref[...].astype(f32)
    gw_ref[:, 2 * E :] = ok_ref[:, :KEYS]
    gs_ref[...] = ok_ref[:, KEYS : KEYS + H]
    gc_ref[...] = u_ref[:CONV, :]
    gb_ref[...] = u_ref[CONV : CONV + 1, :]
    gn_ref[...] = u_ref[5:6, :E]
    gp_ref[...] = u_ref[6:7, : gp_ref.shape[1]]
    for i, ref in enumerate((g0_ref, g1_ref, g2_ref)):
        ref[...] = u_ref[7:8, i * LANES : i * LANES + H]


def finish(inputs, cotangent, gain, inv, sums):
    tokens, width = inputs.shape[1:]
    og, ow, ob, ok, u = sums
    shape = lambda *dims: jax.ShapeDtypeStruct(dims, f32)
    rows = ow.shape[0]
    return pl.pallas_call(
        finish_kernel,
        out_shape=[
            jax.ShapeDtypeStruct(inputs.shape, bf16), shape(*inputs.shape), shape(rows, 2 * E + KEYS), shape(rows, H),
            shape(CONV, E + KEYS), shape(1, E + KEYS), shape(1, width), shape(1, E), shape(1, H), shape(1, H), shape(1, H),
        ],
        in_specs=[VMEM] * 9,
        out_specs=[VMEM] * 11,
        compiler_params=pltpu.CompilerParams(vmem_limit_bytes=32 * 2**20),
        name="finish",
    )(inputs, cotangent, gain, inv, og, ob, ow, ok, u)


def body(
    inputs, cotangent, doc_lengths, head_width, pre_gain, in_weight, step_weight, conv_weight, conv_bias,
    step_bias, decay_log, skip_gain, norm_gain, out_weight,
):
    me = Place()
    peers, near, far = me.peers, me.near, me.far
    tokens, width = inputs.shape[1:]
    span = tokens * peers
    length = span * near
    heads = H // (peers * near)
    inner = heads * P_SIZE
    rows = in_weight.shape[0]
    row = lambda vector: vector[None, :]

    in_w, out_w, normed, cot_all, meta, inv = gather(
        in_weight, out_weight, cotangent, inputs, row(pre_gain), step_weight, doc_lengths, head_width
    )
    in_w = in_w.reshape(width, -1)
    normed = normed.reshape(length, width)

    params = (conv_weight, row(conv_bias), row(norm_gain), row(step_bias), row(decay_log), row(skip_gain))
    *kept, gated, states, part, chan, head_vec, cot_all, out_w, projected = mixer_forward(
        meta, normed, in_w, params, cot_all, out_w, span, heads
    )
    out_w = out_w.reshape(inner, width)
    cot_all = cot_all.reshape(length, width)
    grad_mixed = mm(cot_all, out_w, NT)
    sums, mixed = cube_total(part, gated, chan, grad_mixed)
    branch = mm(mixed, out_w, NN).astype(bf16)
    grad_out = mm(mixed, cot_all, TN).astype(bf16)
    grad_cols, small, branch, grad_out_weight = mixer_backward(
        meta, projected, grad_mixed, chan, conv_weight, head_vec, (*kept, states), sums,
        branch.reshape(near, peers, tokens, width), grad_out.reshape(far, 2, -1, width), span, heads,
    )
    grad_in = mm(normed, grad_cols, TN).astype(bf16)
    grad_normed = mm(grad_cols, in_w, NT)
    products = jnp.sum(grad_normed * normed.astype(f32), axis=0)
    summed = scatter(
        grad_normed.astype(bf16).reshape(near, peers, tokens, width),
        grad_in.reshape(peers, far, near, 2, rows, -1),
        branch,
        small,
        row(products),
        row(pre_gain),
    )
    outs = finish(inputs, cotangent, row(pre_gain), inv, summed)
    output, grad_inputs, grad_in_weight, grad_step_weight, grad_conv_weight = outs[:5]
    grad_conv_bias, grad_pre_gain, grad_norm_gain, grad_step_bias, grad_decay_log, grad_skip = [o[0] for o in outs[5:]]
    return (
        output, grad_inputs, grad_pre_gain, grad_in_weight, grad_step_weight, grad_conv_weight, grad_conv_bias,
        grad_step_bias, grad_decay_log, grad_skip, grad_norm_gain, grad_out_weight,
    )


def solution(mesh):
    both = P(("seq", "batch"), None)
    tok = P("batch", "seq", None)
    in_specs = (
        tok, tok, P("batch", None), P("batch"), P(), both, both, P(), P(), P(), P(), P(), P(), both,
    )
    out_specs = (tok, tok, P(), both, both, P(), P(), P(), P(), P(), P(), both)
    return jax.shard_map(body, mesh=mesh, in_specs=in_specs, out_specs=out_specs, check_vma=False)
```

```python
from functools import partial

import jax
import jax.numpy as jnp
from jax import lax
from jax.experimental import pallas as pl
from jax.experimental.pallas import tpu as pltpu
from jax.sharding import PartitionSpec as P

H = 64
P_SIZE = 64
N = 128
CONV = 4
DOCS = 4
E = 4096
KEYS = 2 * N
STEP_PAD = 128
CHUNK = 128
LANES = 128
epsilon = 1e-05
f32 = jnp.float32
bf16 = jnp.bfloat16


def mm(a, b, dims, precision=None):
    return lax.dot_general(a, b, (dims, ((), ())), precision=precision, preferred_element_type=f32)


NN = ((1,), (0,))
NT = ((1,), (1,))
TN = ((0,), (0,))
exact = lax.Precision.HIGHEST


def pair_cols(low, col, first):
    return jnp.where(low, col[:, first : first + 1], col[:, first + 1 : first + 2])


def iota(shape, axis):
    return lax.broadcasted_iota(jnp.int32, shape, axis)


class Docs:
    def __init__(self, meta_ref, chunk, span):
        per = span // CHUNK
        seq = chunk // per
        self.start = (chunk - seq * per) * CHUNK
        self.ends = []
        total = 0
        for i in range(DOCS - 1):
            total = total + meta_ref[seq, 0, i]
            self.ends.append(total)
        self.count = meta_ref[seq, 0, DOCS]
        self.pos = self.start + iota((CHUNK, 1), 0)
        self.doc = self.index(self.pos)

    def index(self, places):
        found = (places >= self.ends[0]).astype(jnp.int32)
        for end in self.ends[1:]:
            found = found + (places >= end).astype(jnp.int32)
        return found

    def lag(self, by):
        source = self.pos - by
        return ((source >= 0) & (self.index(source) == self.doc)).astype(f32)

    def flow(self):
        return ((self.start > 0) & (self.index(self.start - 1) == self.doc)).astype(f32)

    def row(self):
        return self.index(self.start + iota((1, CHUNK), 1))

    def tail(self):
        return (self.doc == self.index(self.start + CHUNK - 1)).astype(f32)


def shift_down(rows, before, by):
    if by == 0:
        return rows
    moved = pltpu.roll(rows, by, 0)
    top = jnp.where(iota((8, 1), 0) < by, pltpu.roll(before, by, 0), moved[:8])
    return jnp.concatenate([top, moved[8:]], axis=0)


def shift_up(rows, after, by):
    if by == 0:
        return rows
    size = rows.shape[0]
    moved = pltpu.roll(rows, size - by, 0)
    end = jnp.where(iota((8, 1), 0) >= 8 - by, pltpu.roll(after, 8 - by, 0), moved[size - 8 :])
    return jnp.concatenate([moved[: size - 8], end], axis=0)


def silu_slope(v, sig):
    return sig * (1.0 + v * (1.0 - sig))


def own_parameters(chan_ref, head_ref, conv_ref, bias_ref, norm_ref, step_b_ref, decay_ref, skip_ref, heads):
    me = Place()
    inner = heads * P_SIZE
    for whole, part in me.channel_runs(inner):
        chan_ref[:CONV, part] = conv_ref[:, whole]
        chan_ref[CONV : CONV + 1, part] = bias_ref[:, whole]
        chan_ref[5:6, part] = norm_ref[:, whole]
    ids = me.heads_at(iota((1, inner), 1), P_SIZE, inner)
    chosen = (iota((H, inner), 0) == ids).astype(f32)
    chan_ref[6:7, :] = mm(jnp.broadcast_to(skip_ref[...], (8, H)), chosen, NN, exact)[:1]
    chan_ref[7:8, :] = ids.astype(f32)
    lanes = iota((1, LANES), 1)
    ids = jnp.where(lanes < heads, me.heads_at(lanes, 1, heads), -1)
    chosen = (iota((H, LANES), 0) == ids).astype(f32)
    head_ref[...] = jnp.zeros_like(head_ref)
    head_ref[:1, :] = mm(jnp.broadcast_to(step_b_ref[...], (8, H)), chosen, NN, exact)[:1]
    head_ref[1:2, :] = mm(jnp.broadcast_to(jnp.exp(decay_ref[...]), (8, H)), chosen, NN, exact)[:1]
    head_ref[2:3, :] = ids.astype(f32)


def whole_sums(out_ref, chan_sums, key_sums, head_sums, head_ref, chan_ref, heads):
    me = Place()
    inner = heads * P_SIZE
    out_ref[...] = jnp.zeros_like(out_ref)
    for whole, part in me.channel_runs(inner):
        out_ref[:6, whole] = chan_sums[:6, part]
    out_ref[:5, E:] = key_sums[:5, :]
    chosen = (iota((H, LANES), 0) == head_ref[2:3, :].astype(jnp.int32)).astype(f32)
    steps = mm(head_sums[...], chosen, NT, exact)
    chosen = (iota((H, inner), 0) == chan_ref[7:8, :].astype(jnp.int32)).astype(f32)
    skips = mm(chan_sums[...], chosen, NT, exact)
    out_ref[7:8, :H] = steps[:1]
    out_ref[7:8, LANES : LANES + H] = steps[1:2]
    out_ref[7:8, 2 * LANES : 2 * LANES + H] = skips[6:7]


def forward_kernel(
    meta_ref, rows_ref, w_ref, conv_ref, bias_ref, norm_ref, step_b_ref, decay_ref, skip_ref, cot_in, out_in,
    val_out, key_out, vsum_ref, ksum_ref, raw_ref, cum_ref, y_ref, gated_ref, state_ref, sums_ref, chan_ref, head_ref,
    cot_out, out_out, proj_out, state, last_v, last_k, proj_v, send, recv,
    *, span, heads,
):
    i = pl.program_id(0)
    chunks = pl.num_programs(0)
    inner = heads * P_SIZE
    late = Late(cot_in, cot_out, out_in, out_out, send, recv)

    @pl.when(i == 0)
    def _():
        late.start()
        own_parameters(chan_ref, head_ref, conv_ref, bias_ref, norm_ref, step_b_ref, decay_ref, skip_ref, heads)
        state[...] = jnp.zeros_like(state)
        last_v[...] = jnp.zeros_like(last_v)
        last_k[...] = jnp.zeros_like(last_k)

    @pl.when(i % 2 == 0)
    def _():
        for lane in range(0, w_ref.shape[1], 512):
            lanes = slice(lane, min(lane + 512, w_ref.shape[1]))
            proj_v[:, lanes] = mm(rows_ref[...], w_ref[:, lanes], NN)

    proj_ref = proj_v.at[pl.ds(pl.multiple_of(i % 2 * CHUNK, CHUNK), CHUNK)]
    proj_out[...] = proj_ref[...]

    @pl.when(i == chunks - 1)
    def _():
        late.middle()

    docs = Docs(meta_ref, i, span)
    lags = [docs.lag(by) for by in range(1, CONV)]

    def convolve(rows, before, weight, bias):
        total = bias + weight[CONV - 1 :] * rows
        for by in range(1, CONV):
            at = CONV - 1 - by
            total = total + weight[at : at + 1] * (shift_down(rows, before, by) * lags[by - 1])
        return total

    rows_v = proj_ref[:, inner : 2 * inner].astype(bf16).astype(f32)
    vsum = convolve(rows_v, last_v[...], chan_ref[:CONV, :], chan_ref[CONV : CONV + 1, :])
    last_v[...] = rows_v[CHUNK - 8 :]
    vsum_ref[...] = vsum
    val_out[...] = (vsum * jax.nn.sigmoid(vsum)).astype(bf16)
    rows_k = proj_ref[:, 2 * inner : 2 * inner + KEYS].astype(bf16).astype(f32)
    ksum = convolve(rows_k, last_k[...], conv_ref[:, E:], bias_ref[:, E:])
    last_k[...] = rows_k[CHUNK - 8 :]
    ksum_ref[...] = ksum
    keys = (ksum * jax.nn.sigmoid(ksum)).astype(bf16)
    key_out[...] = keys

    rows = iota((CHUNK, CHUNK), 0)
    cols = iota((CHUNK, CHUNK), 1)
    chosen = (rows == head_ref[2:3, :].astype(jnp.int32)).astype(f32)
    raw = mm(proj_ref[:, 2 * inner + KEYS :], chosen, NN, exact) + head_ref[:1, :]
    raw_ref[...] = raw
    dt = jax.nn.softplus(raw)
    cum = mm((rows >= cols).astype(f32), -dt * head_ref[1:2, :], NN, exact)
    cum_ref[...] = cum
    cum_t = cum.T
    dt_t = dt.T

    state_ref[0] = state[...].astype(bf16)
    bias = jnp.where((docs.doc == docs.row()) & (rows >= cols), 0.0, -1e30)
    carry_w = docs.flow() * jnp.exp(cum)
    final_w = docs.tail() * jnp.exp(cum[CHUNK - 1 :, :] - cum) * dt
    gain = carry_w[CHUNK - 1 :, :]
    low = cols < P_SIZE
    low_row = low[:1]
    write = keys[:, :N]
    read = keys[:, N:]
    write_t = write.astype(f32).T.astype(bf16)
    scores = mm(read, write, NT)
    square = jnp.zeros((CHUNK, LANES), f32)
    count = docs.count.astype(f32)
    for pair in range(heads // 2):
        first = 2 * pair
        lanes = slice(pair * 128, pair * 128 + 128)
        xf = val_out[:, lanes].astype(f32)
        weights = []
        for h in (first, first + 1):
            decay = jnp.exp(cum[:, h : h + 1] - cum_t[h : h + 1, :] + bias)
            weights.append((decay * scores * dt_t[h : h + 1, :]).astype(bf16))
        stacked = jnp.concatenate(
            [jnp.where(low, xf, 0.0).astype(bf16), jnp.where(low, 0.0, xf).astype(bf16)], axis=0
        )
        old = state[:, lanes]
        y = mm(jnp.concatenate(weights, axis=1), stacked, NN)
        y = y + pair_cols(low, carry_w, first) * mm(read, old.astype(bf16), NN)
        y = y + chan_ref[6:7, lanes] * xf
        y = jnp.where(chan_ref[7:8, lanes] < count, y, 0.0)
        y_ref[:, lanes] = y
        state[:, lanes] = pair_cols(low_row, gain, first) * old + mm(
            write_t, (pair_cols(low, final_w, first) * xf).astype(bf16), NN
        )
        gate = proj_ref[:, lanes]
        gated = y * (gate * jax.nn.sigmoid(gate))
        gated_ref[:, lanes] = gated
        square = square + gated * gated
    share = 1.0 / (count * P_SIZE)
    sums_ref[pl.ds(i, 1), :] = jnp.sum(square.T, axis=0, keepdims=True) * share
    sums_ref[pl.ds(chunks + i, 1), :] = jnp.full((1, LANES), share, f32)

    @pl.when(i == chunks - 1)
    def _():
        late.end()


def head_sums_of(prod, chosen):
    high = prod.astype(bf16)
    low = (prod - high.astype(f32)).astype(bf16)
    return mm(jnp.concatenate([high, low], axis=1), chosen, NN)


def backward_kernel(
    meta_ref, proj_ref, grad_ref, chan_ref, conv_ref, head_ref,
    val_ref, key_ref, vsum_ref, ksum_ref, raw_ref, cum_ref, y_ref, state_ref, sums_ref, branch_ref, go_ref,
    cols_ref, all_sums, b_out, o_out,
    chan_sums, key_sums, head_sums, dstate, dv, next_v, next_k, next_lags, *early_refs,
    span, heads,
):
    chunks = pl.num_programs(0)
    i = chunks - 1 - pl.program_id(0)
    inner = heads * P_SIZE
    early = Early(branch_ref, go_ref, (b_out, o_out) + early_refs)

    @pl.when(pl.program_id(0) == 0)
    def _():
        early.start()
        for ref in (dstate, next_v, next_k, next_lags, chan_sums, key_sums, head_sums):
            ref[...] = jnp.zeros_like(ref)

    docs = Docs(meta_ref, i, span)
    rows = iota((CHUNK, CHUNK), 0)
    cols = iota((CHUNK, CHUNK), 1)
    raw = raw_ref[...]
    dt = jax.nn.softplus(raw)
    cum = cum_ref[...]
    cum_t = cum.T
    count = docs.count.astype(f32)

    def column(row):
        return jnp.broadcast_to(row, (CHUNK, CHUNK)).T

    inv = lax.rsqrt(column(sums_ref[pl.ds(i, 1), :]) + epsilon)
    pull = inv * inv * inv * column(sums_ref[pl.ds(chunks + i, 1), :])

    bias = jnp.where((docs.doc == docs.row()) & (cols >= rows), 0.0, -1e30)
    carry_w = docs.flow() * jnp.exp(cum)
    final_d = docs.tail() * jnp.exp(cum[CHUNK - 1 :, :] - cum)
    final_w = final_d * dt
    gain = carry_w[CHUNK - 1 :, :]
    low = cols < P_SIZE
    low_row = low[:1]
    write = key_ref[:, :N]
    read = key_ref[:, N:]
    read_t = read.astype(f32).T.astype(bf16)
    scores_t = mm(write, read, NT)
    dscores_t = jnp.zeros((CHUNK, CHUNK), f32)
    dwrite = jnp.zeros((CHUNK, N), f32)
    dread = jnp.zeros((CHUNK, N), f32)
    end_row = iota((CHUNK, 1), 0) == CHUNK - 1
    carry_all = jnp.zeros((CHUNK, LANES), f32)
    final_all = jnp.zeros((CHUNK, LANES), f32)
    direct_all = jnp.zeros((CHUNK, LANES), f32)
    gain_rows = []
    dcum_rows = []
    for pair in range(heads // 2):
        first = 2 * pair
        lanes = slice(pair * 128, pair * 128 + 128)
        gate = proj_ref[:, lanes]
        sig = jax.nn.sigmoid(gate)
        silu = gate * sig
        masked = y_ref[:, lanes]
        gated = masked * silu
        norm_gain = chan_ref[5:6, lanes]
        gm = grad_ref[:, lanes]
        unit = gated * inv
        chan_sums[5:6, lanes] += jnp.sum(gm * unit, axis=0, keepdims=True)
        grad_gated = inv * (gm * norm_gain) - pull * gated
        cols_ref[:, lanes] = (grad_gated * masked * silu_slope(gate, sig)).astype(bf16)
        dy = jnp.where(chan_ref[7:8, lanes] < count, grad_gated * silu, 0.0)
        xf = val_ref[:, lanes].astype(f32)
        dyb = dy.astype(bf16)
        x_stack = jnp.concatenate(
            [jnp.where(low, xf, 0.0).astype(bf16), jnp.where(low, 0.0, xf).astype(bf16)], axis=0
        )
        dy_stack = jnp.concatenate(
            [jnp.where(low, dy, 0.0).astype(bf16), jnp.where(low, 0.0, dy).astype(bf16)], axis=0
        )
        dweights = mm(x_stack, dyb, NT)
        old = state_ref[0, :, lanes]
        grad = dstate[:, lanes]
        gradb = grad.astype(bf16)
        carried = mm(read, old, NN)
        pushed = mm(write, gradb, NN)
        carry_p = pair_cols(low, carry_w, first)
        final_p = pair_cols(low, final_w, first)
        chosen = (cols == first + rows // P_SIZE).astype(bf16)
        chosen = jnp.concatenate([chosen, chosen], axis=0)
        carry_all = carry_all + head_sums_of(dy * carried, chosen)
        final_all = final_all + head_sums_of(xf * pushed, chosen)
        gain_rows.append(jnp.sum(grad * old.astype(f32), axis=0, keepdims=True))
        weights = []
        for which, h in enumerate((first, first + 1)):
            col = dt[:, h : h + 1]
            decay = jnp.exp(cum_t[h : h + 1, :] - cum[:, h : h + 1] + bias)
            weighted = decay * col
            weights.append((weighted * scores_t).astype(bf16))
            dw = dweights[which * CHUNK : (which + 1) * CHUNK]
            dscores_t = dscores_t + dw * weighted
            direct = dw * decay * scores_t
            ddt_in = jnp.sum(direct, axis=1, keepdims=True)
            dcum_rows.append(jnp.sum(direct * col, axis=0, keepdims=True))
            direct_all = jnp.where(cols == h, ddt_in, direct_all)
        dx = mm(jnp.concatenate(weights, axis=1), dy_stack, NN)
        dv[:, lanes] = dx + final_p * pushed + chan_ref[6:7, lanes] * dy
        chan_sums[6:7, lanes] += jnp.sum(dy * xf, axis=0, keepdims=True)
        dwrite = dwrite + mm((final_p * xf).astype(bf16), gradb, NT)
        carry_dy = (carry_p * dy).astype(bf16)
        dread = dread + mm(carry_dy, old, NT)
        dstate[:, lanes] = pair_cols(low_row, gain, first) * grad + mm(read_t, carry_dy, NN)
    dsb = dscores_t.astype(bf16)
    dkeys = jnp.concatenate([dwrite + mm(dsb, read, NN), dread + mm(dsb, write, TN)], axis=1)

    chosen = (iota((inner, LANES), 1) == iota((inner, LANES), 0) // P_SIZE).astype(f32)
    gain_all = mm(jnp.broadcast_to(jnp.concatenate(gain_rows, axis=1), (8, inner)), chosen, NN, exact)[:1]
    push = final_w * final_all
    at_end = jnp.sum(push, axis=0, keepdims=True) + gain * gain_all
    ddt = direct_all + final_d * final_all
    dcum = carry_w * carry_all - push - dt * direct_all + jnp.where(end_row, at_end, 0.0)
    extra = jnp.concatenate(dcum_rows + [jnp.zeros((LANES - heads, CHUNK), f32)], axis=0)
    dlog = mm((cols >= rows).astype(f32), dcum + extra.T, NN, exact)
    rate = head_ref[1:2, :]
    grad_step = (ddt - rate * dlog) * jax.nn.sigmoid(raw)
    head_sums[:1, :] += jnp.sum(grad_step, axis=0, keepdims=True)
    head_sums[1:2, :] -= jnp.sum(dt * rate * dlog, axis=0, keepdims=True)
    chosen = (rows == head_ref[2:3, :].astype(jnp.int32)).astype(bf16)
    cols_ref[:, 2 * inner + KEYS :] = mm(grad_step.astype(bf16), chosen, NT).astype(bf16)

    lags = [docs.lag(by) for by in range(1, CONV)]

    def convolve_back(dact, total, rows_in, after, weight, sums):
        dconv = dact * silu_slope(total, jax.nn.sigmoid(total))
        grad_in = weight[CONV - 1 :] * dconv
        sums[CONV : CONV + 1, :] += jnp.sum(dconv, axis=0, keepdims=True)
        sums[CONV - 1 : CONV, :] += jnp.sum(dconv * rows_in, axis=0, keepdims=True)
        for by in range(1, CONV):
            at = CONV - 1 - by
            moved = shift_up(dconv * lags[by - 1], after[...] * next_lags[:, by - 1 : by], by)
            grad_in = grad_in + weight[at : at + 1] * moved
            sums[at : at + 1, :] += jnp.sum(moved * rows_in, axis=0, keepdims=True)
        after[...] = dconv[:8]
        return grad_in.astype(bf16)

    rows_v = proj_ref[:, inner : 2 * inner].astype(bf16).astype(f32)
    cols_ref[:, inner : 2 * inner] = convolve_back(dv[...], vsum_ref[...], rows_v, next_v, chan_ref[:CONV, :], chan_sums)
    rows_k = proj_ref[:, 2 * inner : 2 * inner + KEYS].astype(bf16).astype(f32)
    cols_ref[:, 2 * inner : 2 * inner + KEYS] = convolve_back(
        dkeys, ksum_ref[...], rows_k, next_k, conv_ref[:, E:], key_sums
    )
    for by in range(1, CONV):
        next_lags[:, by - 1 : by] = lags[by - 1][:8]

    @pl.when(pl.program_id(0) == 0)
    def _():
        early.middle()

    @pl.when(pl.program_id(0) == chunks - 1)
    def _():
        whole_sums(all_sums, chan_sums, key_sums, head_sums, head_ref, chan_ref, heads)
        early.end()


def mixer_forward(meta, normed, in_w, params, cot, out_w, span, heads):
    length = normed.shape[0]
    columns = in_w.shape[1]
    inner = heads * P_SIZE
    chunks = length // CHUNK
    copies = sum(len(left_over(cot_order(o))) for o in range(cot.shape[0])) + 2 * (out_w.shape[0] - 1)
    row = lambda width: pl.BlockSpec((CHUNK, width), lambda i: (i, 0))
    all_of = lambda *shape: pl.BlockSpec(shape, lambda i: (0,) * len(shape))
    out = lambda width, dtype: jax.ShapeDtypeStruct((length, width), dtype)
    return pl.pallas_call(
        partial(forward_kernel, span=span, heads=heads),
        grid=(chunks,),
        in_specs=[
            pl.BlockSpec(memory_space=pltpu.SMEM), pl.BlockSpec((2 * CHUNK, normed.shape[1]), lambda i: (i // 2, 0)),
            all_of(*in_w.shape),
        ]
        + [all_of(*part.shape) for part in params]
        + [HBM] * 2,
        out_specs=[
            row(inner), row(KEYS), row(inner), row(KEYS), row(LANES), row(LANES), row(inner), row(inner),
            pl.BlockSpec((1, N, inner), lambda i: (i, 0, 0)), all_of(2 * chunks, LANES),
            all_of(8, inner), all_of(8, LANES), HBM, HBM, row(columns),
        ],
        out_shape=[
            out(inner, bf16), out(KEYS, bf16), out(inner, f32), out(KEYS, f32), out(LANES, f32), out(LANES, f32),
            out(inner, f32), out(inner, f32), jax.ShapeDtypeStruct((chunks, N, inner), bf16),
            jax.ShapeDtypeStruct((2 * chunks, LANES), f32), jax.ShapeDtypeStruct((8, inner), f32),
            jax.ShapeDtypeStruct((8, LANES), f32), jax.ShapeDtypeStruct(cot.shape, bf16),
            jax.ShapeDtypeStruct(out_w.shape, bf16), out(columns, f32),
        ],
        input_output_aliases={3 + len(params): 12, 4 + len(params): 13},
        scratch_shapes=[pltpu.VMEM((N, inner), f32), pltpu.VMEM((8, inner), f32), pltpu.VMEM((8, KEYS), f32)]
        + [pltpu.VMEM((2 * CHUNK, columns), f32)]
        + sems(copies, 1)[:2],
        compiler_params=remote_params(4, 58),
        cost_estimate=pl.CostEstimate(
            flops=length * inner * 1024, bytes_accessed=length * inner * 24, transcendentals=length * heads * CHUNK
        ),
        name="mixer_forward",
    )(meta, normed, in_w, *params, cot, out_w)


def mixer_backward(meta, projected, grad_mixed, chan, conv, head_vec, kept, sums, branch, grad_out, span, heads):
    length = projected.shape[0]
    inner = heads * P_SIZE
    chunks = length // CHUNK
    me = Place()
    near, peers, tokens, width = branch.shape
    far = me.far
    part = grad_out.shape[2:]
    copies = near * peers // 2 + 2 * far - 1
    vm = lambda *shape: pltpu.VMEM(shape, bf16)
    row = lambda width: pl.BlockSpec((CHUNK, width), lambda i: (chunks - 1 - i, 0))
    all_of = lambda *shape: pl.BlockSpec(shape, lambda i: (0,) * len(shape))
    out = lambda width: jax.ShapeDtypeStruct((length, width), bf16)
    return pl.pallas_call(
        partial(backward_kernel, span=span, heads=heads),
        grid=(chunks,),
        in_specs=[
            pl.BlockSpec(memory_space=pltpu.SMEM), row(2 * inner + KEYS + STEP_PAD), row(inner),
            all_of(8, inner), all_of(*conv.shape), all_of(8, LANES),
            row(inner), row(KEYS), row(inner), row(KEYS), row(LANES), row(LANES), row(inner),
            pl.BlockSpec((1, N, inner), lambda i: (chunks - 1 - i, 0, 0)), all_of(2 * chunks, LANES), HBM, HBM,
        ],
        out_specs=[
            row(2 * inner + KEYS + STEP_PAD), all_of(8, conv.shape[1]), VMEM, VMEM,
        ],
        out_shape=[
            out(2 * inner + KEYS + STEP_PAD), jax.ShapeDtypeStruct((8, conv.shape[1]), f32),
            jax.ShapeDtypeStruct((near, peers // 2, tokens, width), bf16), jax.ShapeDtypeStruct(part, f32),
        ],
        scratch_shapes=[
            pltpu.VMEM((8, inner), f32), pltpu.VMEM((8, KEYS), f32), pltpu.VMEM((8, LANES), f32),
            pltpu.VMEM((N, inner), f32), pltpu.VMEM((CHUNK, inner), f32), pltpu.VMEM((8, inner), f32),
            pltpu.VMEM((8, KEYS), f32), pltpu.VMEM((8, LANES), f32),
            vm(near, peers // 2, tokens, width), vm(near, peers // 2, tokens, width),
            vm(far, *part), vm(far, *part), vm(max(far - 1, 1), *part),
        ]
        + sems(copies, near * peers // 2 + far),
        compiler_params=remote_params(3, 32),
        cost_estimate=pl.CostEstimate(
            flops=length * inner * 3072, bytes_accessed=length * inner * 30, transcendentals=length * heads * CHUNK
        ),
        name="mixer_backward",
    )(meta, projected, grad_mixed, chan, conv, head_vec, *kept, sums, branch, grad_out)


MESH = pl.DeviceIdType.MESH
HBM = pl.BlockSpec(memory_space=pl.ANY)
VMEM = pl.BlockSpec(memory_space=pltpu.VMEM)


def z_pair(peers, groups):
    planes = groups // 2
    return 2 if planes % 2 == 0 and (E // (peers * planes)) % (2 * P_SIZE) == 0 else 1


def flip(value, bits):
    bit = 1
    while bit <= bits:
        if bits & bit:
            value = value + bit - 2 * bit * (value // bit % 2)
        bit *= 2
    return value


class Place:
    def __init__(self):
        self.peers = lax.axis_size("seq")
        groups = lax.axis_size("batch")
        self.near = z_pair(self.peers, groups)
        self.far = groups // 2 // self.near
        self.s = lax.axis_index("seq")
        b = lax.axis_index("batch")
        self.c = b % 2
        self.zl = b // 2 % self.near
        self.zh = b // 2 // self.near

    def at(self, s=0, zl=0, zh=0, c=0):
        return (flip(self.s, s), (flip(self.zh, zh) * self.near + flip(self.zl, zl)) * 2 + flip(self.c, c))

    def heads_at(self, index, per, width):
        outer = self.far if self.near > 1 else 1
        run = width // outer
        return (((self.s * outer + index // run) * self.near + self.zl) * run + index % run) // per

    def channel_runs(self, width):
        outer = self.far if self.near > 1 else 1
        run = width // outer
        runs = []
        for i in range(outer):
            first = ((self.s * outer + i) * self.near + self.zl) * run
            runs.append((pl.ds(pl.multiple_of(first, 128), run), slice(i * run, (i + 1) * run)))
        return runs

    def column_runs(self, s, zl, width):
        outer = self.far if self.near > 1 else 1
        run = width // (2 * outer)
        runs = []
        for part in range(2):
            for i in range(outer):
                first = part * E + ((s * outer + i) * self.near + zl) * run
                runs.append((pl.ds(pl.multiple_of(first, 128), run), pl.ds((part * outer + i) * run, run)))
        return runs

    def partners(self):
        cube = [self.at(s=o // self.near, zl=o % self.near) for o in range(1, self.peers * self.near)]
        return cube, [self.at(zh=o) for o in range(1, self.far)], [self.at(c=1)]


def greet(devices):
    barrier = pltpu.get_barrier_semaphore()
    for device in devices:
        pl.semaphore_signal(barrier, inc=1, device_id=device, device_id_type=MESH)
    pl.semaphore_wait(barrier, len(devices))


class Mover:
    def __init__(self, send, recv, local):
        self.send, self.recv, self.local = send, recv, local
        self.sent, self.kept = 0, 0
        self.open = []

    def plan(self, src, dst, device):
        copy = pltpu.make_async_remote_copy(
            src_ref=src, dst_ref=dst, send_sem=self.send.at[self.sent], recv_sem=self.recv.at[self.sent],
            device_id=device, device_id_type=MESH,
        )
        self.sent += 1
        self.open.append(copy)
        return copy

    def put(self, src, dst, device):
        copy = self.plan(src, dst, device)
        copy.start()
        return copy

    def plan_keep(self, src, dst):
        self.kept += 1
        return pltpu.make_async_copy(src, dst, self.local.at[self.kept - 1])

    def keep(self, src, dst):
        copy = self.plan_keep(src, dst)
        copy.start()
        return copy

    def close(self):
        for copy in self.open:
            copy.wait_send()


def run_paths(paths):
    paths = list(paths)
    while paths:
        alive = []
        for path in paths:
            try:
                next(path)
                alive.append(path)
            except StopIteration:
                pass
        paths = alive


def turn(paths):
    for path in paths:
        next(path, None)


def bits_of(peers):
    return [1 << i for i in range(peers.bit_length() - 1)]


def combos(bits):
    out = [0]
    for bit in reversed(bits):
        out = [bit | o for o in out] + out
    return out


def cot_order(near):
    bits = bits_of(lax.axis_size("seq"))
    return bits if near else bits[::-1]


def left_over(order):
    return combos(order[:-1])


class Late:
    def __init__(self, src, dst, out_src, out_dst, send, recv):
        me = self.me = Place()
        self.mover = Mover(send, recv, None)
        self.copies, self.far, self.forward = [], [], []
        for o in range(me.near):
            order = cot_order(o)
            for h in left_over(order):
                at = (flip(me.zl, o), flip(me.s, h))
                self.copies.append(self.mover.plan(src.at[at], dst.at[at], me.at(s=order[-1])))
        for o in range(1, me.far):
            at = (me.zh, me.c)
            self.far.append(self.mover.plan(out_src.at[at], out_dst.at[at], me.at(zh=o)))
        for o in range(1, me.far):
            at = (flip(me.zh, o), me.c)
            self.forward.append(self.mover.plan(out_dst.at[at], out_dst.at[at], me.at(c=1)))

    def start(self):
        _, far, sibling = self.me.partners()
        greet([self.me.at(s=bit) for bit in sorted({cot_order(o)[-1] for o in range(self.me.near)})] + far + sibling)
        for copy in self.far + self.copies:
            copy.start()

    def middle(self):
        for far, forward in zip(self.far, self.forward):
            far.wait_recv()
            forward.start()

    def end(self):
        for copy in self.copies + self.forward:
            copy.wait_recv()
        self.mover.close()


def gather_kernel(
    in_ref, out_ref, cot_ref, inputs_ref, gain_ref, step_ref, lengths_ref, width_ref,
    w_ref, o_ref, x_ref, ct_ref, m_ref, inv_ref, rows_ref, steps_ref, meta_ref, send, recv, local,
):
    prepare(inputs_ref, gain_ref, step_ref, lengths_ref, width_ref, rows_ref, inv_ref, steps_ref, meta_ref)
    cot_ref = cot_ref.at[0]
    me = Place()
    s, zl, zh, c = me.s, me.zl, me.zh, me.c
    columns = w_ref.shape[-1] - KEYS - STEP_PAD
    mine, shared = pl.ds(0, columns), pl.ds(columns, KEYS + STEP_PAD)
    cube, far, sibling = me.partners()
    greet(cube + far + sibling)
    mover = Mover(send, recv, local)
    bits = bits_of(me.peers)

    def plane_path(src, dst, order, near, skip=()):
        view = dst.at[flip(zl, near)]
        if near:
            copy = mover.put(src, dst.at[zl, s], me.at(zl=near))
            yield
            copy.wait_recv()
        else:
            own = mover.keep(src, view.at[s])
        held = [0]
        for bit in order:
            copies = []
            for h in held:
                if bit == order[-1] and h in skip:
                    continue
                at = view.at[flip(s, h)]
                copies.append(mover.put(at if near or h else src, at if near else dst.at[zl, flip(s, h)], me.at(s=bit)))
            held = held + [h ^ bit for h in held]
            yield
            for copy in copies:
                copy.wait_recv()
        if not near:
            own.wait()

    def meta_path():
        own = mover.keep(meta_ref, m_ref.at[zl])
        near = [mover.put(meta_ref, m_ref.at[zl], me.at(zl=o)) for o in range(1, me.near)]
        yield
        own.wait()
        for copy in near:
            copy.wait_recv()

    def key_path():
        block = w_ref.at[s, zh, zl, c]
        parts = [
            (in_ref.at[:, pl.ds(2 * E, KEYS)], block.at[:, pl.ds(columns, KEYS)]),
            (steps_ref, block.at[:, pl.ds(columns + KEYS, STEP_PAD)]),
        ]
        own = [mover.keep(*part) for part in parts]
        copies = [mover.put(*part, me.at(zh=o)) for o in range(1, me.far) for part in parts]
        yield
        for copy in own:
            copy.wait()
        for copy in copies:
            copy.wait_recv()
        block = w_ref.at[s, :, zl, c, :, shared]
        copies = [mover.put(block, block, me.at(zl=o)) for o in range(1, me.near)]
        yield
        for copy in copies:
            copy.wait_recv()
        held = [0]
        for bit in bits:
            copies = []
            for h in held:
                block = w_ref.at[flip(s, h), :, :, c, :, shared]
                copies.append(mover.put(block, block, me.at(s=bit)))
            held = held + [h ^ bit for h in held]
            yield
            for copy in copies:
                copy.wait_recv()
        block = w_ref.at[:, :, :, c, :, shared]
        copy = mover.put(block, block, me.at(c=1))
        yield
        copy.wait_recv()

    def spread_path(copies, view):
        last = []
        for o, copy in copies:
            yield
            copy.wait_recv()
            last.append(mover.put(view(flip(zh, o)), view(flip(zh, o)), me.at(c=1)))
        return last

    def out_path():
        own = mover.keep(out_ref, o_ref.at[zh, c])
        first = mover.put(out_ref, o_ref.at[zh, c], me.at(c=1))
        yield
        own.wait()
        first.wait_recv()

    def weight_path():
        moves = {}
        for step in range(me.peers):
            for o in range(me.near):
                to_s, to_zl = flip(s, step), flip(zl, o)
                for src, dst in me.column_runs(to_s, to_zl, columns):
                    src = in_ref.at[:, src]
                    dst = w_ref.at[s, zh, zl, c, :, dst]
                    if step or o:
                        copy = mover.put(src, dst, me.at(s=step, zl=o))
                    else:
                        copy = mover.keep(src, dst)
                    moves.setdefault(step, []).append(copy)
        pieces = []
        for step in range(me.peers):
            yield
            for i, copy in enumerate(moves[step]):
                if step == 0 and i < len(moves[0]) // me.near:
                    copy.wait()
                else:
                    copy.wait_recv()
            block = w_ref.at[flip(s, step), zh, :, c, :, mine]
            copies = [(o, mover.put(block, block, me.at(zh=o))) for o in range(1, me.far)]
            pieces.append((step, copies, mover.put(block, block, me.at(c=1))))
        last = []
        for step, copies, first in pieces:
            last.append(first)
            last += yield from spread_path(copies, lambda h, step=step: w_ref.at[flip(s, step), h, :, c, :, mine])
        yield
        for copy in last:
            copy.wait_recv()

    own_x = plane_path(rows_ref, x_ref, bits, 0)
    near_x = [plane_path(rows_ref, x_ref, bits[::-1], o) for o in range(1, me.near)]
    own_c, *near_c = [plane_path(cot_ref, ct_ref, cot_order(o), o, left_over(cot_order(o))) for o in range(me.near)]
    keys, weights, outs, extra = key_path(), weight_path(), out_path(), meta_path()
    turn([keys, weights, own_x] + near_x + [own_c, outs, extra])
    turn([keys] + near_x + near_c + [keys] + [weights] * me.peers + [keys] + near_x + [own_x, own_c] + near_c)
    turn([keys, weights, keys, weights, weights, weights] + near_x + [own_x] + near_c)
    run_paths([weights, extra, keys, outs, own_x, own_c] + near_x + near_c)
    mover.close()


def remote_params(identity, mib):
    return pltpu.CompilerParams(collective_id=identity, has_side_effects=True, vmem_limit_bytes=mib * 2**20)


def sems(copies, kept):
    return [pltpu.SemaphoreType.DMA((copies,)), pltpu.SemaphoreType.DMA((copies,)), pltpu.SemaphoreType.DMA((kept,))]


def prepare(x_ref, gain_ref, step_ref, lengths_ref, width_ref, normed_ref, inv_ref, steps_ref, meta_ref):
    x = x_ref[0].astype(f32)
    inv = lax.rsqrt(jnp.mean(x * x, axis=1, keepdims=True) + epsilon)
    normed_ref[...] = (x * inv * gain_ref[...]).astype(bf16)
    inv_ref[...] = jnp.broadcast_to(inv, inv_ref.shape)
    steps_ref[...] = jnp.zeros_like(steps_ref)
    steps_ref[:, :H] = step_ref[...]
    lanes = iota(meta_ref.shape, 1)
    meta = jnp.where(lanes == DOCS, width_ref[0], 0)
    for i in range(DOCS):
        meta = jnp.where(lanes == i, lengths_ref[0, i], meta)
    meta_ref[...] = meta


def gather(in_w, out_w, cot, inputs, gain, step_w, lengths, head_width):
    me = Place()
    peers, near, far = me.peers, me.near, me.far
    shape = lambda lead, part: jax.ShapeDtypeStruct(lead + part, bf16)
    rows = inputs.shape[1:]
    columns = 2 * E // (peers * near)
    runs = 2 * (far if near > 1 else 1)
    copies = runs * (peers * near - 1) + (peers + 1) * (2 * far - 1) + 2 * (near * peers - 1)
    copies -= sum(len(left_over(cot_order(o))) for o in range(near))
    copies += 2 * near + peers + 2 * far - 4
    smem = pl.BlockSpec(memory_space=pltpu.SMEM)
    return pl.pallas_call(
        gather_kernel,
        out_shape=[
            shape((peers, far, near, 2), (in_w.shape[0], columns + KEYS + STEP_PAD)),
            shape((far, 2), out_w.shape),
            shape((near, peers), rows),
            shape((near, peers), rows),
            jax.ShapeDtypeStruct((near, 8, LANES), jnp.int32),
            jax.ShapeDtypeStruct((rows[0], LANES), f32),
        ],
        in_specs=[HBM] * 3 + [VMEM] * 3 + [smem] * 2,
        out_specs=[HBM] * 5 + [VMEM],
        scratch_shapes=[
            pltpu.VMEM(rows, bf16), pltpu.VMEM((in_w.shape[0], STEP_PAD), bf16), pltpu.VMEM((8, LANES), jnp.int32)
        ]
        + sems(copies, runs + 6),
        compiler_params=remote_params(0, 58),
        name="gather_all",
    )(in_w, out_w, cot, inputs, gain, step_w, lengths, head_width)


def total_kernel(part_ref, gated_ref, chan_ref, grad_ref, sum_ref, mixed_ref, mine, box, send, recv, local):
    me = Place()
    cube = me.partners()[0]
    greet(cube)
    mover = Mover(send, recv, local)
    chunks = part_ref.shape[0] // 2
    tiles = [slice(lane, lane + LANES) for lane in range(0, gated_ref.shape[1], LANES)]
    mine[...] = part_ref[...]

    def products(i, carry):
        at = pl.ds(pl.multiple_of(i * CHUNK, CHUNK), CHUNK)
        cross = jnp.zeros((CHUNK, LANES), f32)
        for lanes in tiles:
            cross = cross + gated_ref[at, lanes] * (grad_ref[at, lanes] * chan_ref[5:6, lanes])
        row = pl.ds(chunks + i, 1)
        mine[row, :] = jnp.sum(cross.T, axis=0, keepdims=True) * part_ref[row, :]
        return carry

    lax.fori_loop(0, chunks, products, 0)
    copies = [mover.put(mine, box.at[i], device) for i, device in enumerate(cube)]
    total = mine[...]
    for i, copy in enumerate(copies):
        copy.wait_recv()
        total = total + box[i]
    sum_ref[...] = total

    def mix(i, carry):
        at = pl.ds(pl.multiple_of(i * CHUNK, CHUNK), CHUNK)
        inv = lax.rsqrt(jnp.broadcast_to(sum_ref[pl.ds(i, 1), :], (CHUNK, CHUNK)).T + epsilon)
        for lanes in tiles:
            mixed_ref[at, lanes] = (gated_ref[at, lanes] * inv * chan_ref[5:6, lanes]).astype(bf16)
        return carry

    lax.fori_loop(0, chunks, mix, 0)
    mover.close()


def cube_total(part, gated, chan, grad):
    me = Place()
    count = me.peers * me.near - 1
    return pl.pallas_call(
        total_kernel,
        out_shape=[jax.ShapeDtypeStruct(part.shape, f32), jax.ShapeDtypeStruct(gated.shape, bf16)],
        in_specs=[VMEM] * 4,
        out_specs=[VMEM] * 2,
        scratch_shapes=[pltpu.VMEM(part.shape, f32), pltpu.VMEM((count,) + part.shape, f32)] + sems(count, 1),
        compiler_params=remote_params(1, 12),
        name="cube_total",
    )(part, gated, chan, grad)


def add_rows(out, parts):
    shape = out.shape
    tile = min(16, shape[-2])
    lead = [()]
    for size in shape[:-2]:
        lead = [l + (i,) for l in lead for i in range(size)]
    for l in lead:

        def step(i, carry, l=l):
            at = l + (pl.ds(pl.multiple_of(i * tile, tile), tile), slice(None))
            total = parts[0][at].astype(f32)
            for part in parts[1:]:
                total = total + part[at].astype(f32)
            out[at] = total.astype(out.dtype)
            return carry

        lax.fori_loop(0, shape[-2] // tile, step, 0)


def scatter_kernel(
    gn_ref, gw_ref, b_ref, u_ref, p_ref, gain_ref, og_ref, ow_ref, ob_ref, ok_ref, ou_ref,
    n_own, n_box, n_near, b_own, b_box, b_near, w_own, w_box, w_far,
    k_own, k_box, k_near, k_far, k_bits, u_box, send, recv, local,
):
    me = Place()
    s, zl, zh, c = me.s, me.zl, me.zh, me.c
    cube, far, sibling = me.partners()
    greet(cube + far + sibling)
    mover = Mover(send, recv, local)
    bits = bits_of(me.peers)
    columns = w_own.shape[-1]
    mine, shared = pl.ds(0, columns), pl.ds(columns, k_own.shape[-1])

    def rows_path(src, own, box, near_box, out, order, near, arrivals, done=0):
        own, box = own.at[near], box.at[near]
        copies, loads = [], []
        if done:
            half = me.peers // 4
            for j in range(half):
                copies.append(mover.put(src.at[near, j], box.at[j], me.at(s=order[1])))
                loads.append(mover.keep(src.at[near, half + j], own.at[half + j]))
        else:
            at_zl = src.at[flip(zl, near)]
            for j, o in enumerate(combos(order[1:])):
                copies.append(mover.put(at_zl.at[flip(s, order[0] ^ o)], box.at[j], me.at(s=order[0])))
                loads.append(mover.keep(at_zl.at[flip(s, o)], own.at[j]))
        base = 0
        for i in range(done, len(order)):
            rest = order[i + 1 :]
            count = 1 << len(rest)
            offset = (1 << (len(order) - 1)) - count
            coming = []
            for j in range(count):
                yield
                copies[j].wait_recv()
                if i == done:
                    loads[j].wait()
                if rest or near:
                    add_rows(own.at[offset + j], [own.at[offset + j], box.at[base + j]])
                if rest and j < count // 2:
                    coming.append(mover.put(own.at[offset + j], box.at[base + count + j], me.at(s=rest[0])))
            copies = coming
            last = base
            base += count
        end = (1 << (len(order) - 1)) - 1
        if near:
            arrivals.append(mover.put(own.at[end], near_box.at[near - 1], me.at(zl=near)))
            yield
        else:
            yield
            for _ in range(me.near - 1):
                arrivals.pop(0).wait_recv()
            add_rows(out, [own.at[end], box.at[last]] + [near_box.at[o - 1] for o in range(1, me.near)])

    def weight_path():
        order = [(o, k) for o in range(1, me.far) for k in range(me.peers)] + [(0, k) for k in range(me.peers)]
        loads, copies = {}, {}
        for o, k in order:
            copies[o, k] = mover.put(gw_ref.at[flip(s, k), flip(zh, o), :, 1 - c, :, mine], w_box.at[o, k], me.at(c=1))
            loads[o, k] = mover.keep(gw_ref.at[flip(s, k), flip(zh, o), :, c, :, mine], w_own.at[o, k])
        far_copies = {}
        for o, k in order:
            yield
            loads[o, k].wait()
            copies[o, k].wait_recv()
            if o:
                add_rows(w_own.at[o, k], [w_own.at[o, k], w_box.at[o, k]])
                far_copies[o, k] = mover.put(w_own.at[o, k], w_far.at[o - 1, k], me.at(zh=o))
        ends, kept = [], []
        for k in range(me.peers):
            yield
            for o in range(1, me.far):
                far_copies[o, k].wait_recv()
            parts = [w_own.at[0, k], w_box.at[0, k]] + [w_far.at[o - 1, k] for o in range(1, me.far)]
            add_rows(w_own.at[0, k], parts)
            for o in range(me.near):
                for whole, part in me.column_runs(s, zl, columns):
                    src = w_own.at[0, k, flip(zl, o), :, part]
                    if k or o:
                        ends.append(mover.put(src, ow_ref.at[:, whole], me.at(s=k, zl=o)))
                    else:
                        kept.append(mover.keep(src, ow_ref.at[:, whole]))
        yield
        for copy in kept:
            copy.wait()
        for copy in ends:
            copy.wait_recv()

    def key_path():
        blocks = combos(bits)
        copies, loads = [], []
        for j, o in enumerate(blocks):
            copies.append(mover.put(gw_ref.at[flip(s, o), :, :, 1 - c, :, shared], k_box.at[j], me.at(c=1)))
            loads.append(mover.keep(gw_ref.at[flip(s, o), :, :, c, :, shared], k_own.at[j]))
        half = me.peers // 2
        sent = []
        for j in range(me.peers):
            yield
            loads[j].wait()
            copies[j].wait_recv()
            add_rows(k_own.at[j], [k_own.at[j], k_box.at[j]])
            if j < half:
                sent.append(mover.put(k_own.at[j], k_bits.at[j], me.at(s=bits[0])))
        base = 0
        for i, bit in enumerate(bits):
            count = me.peers >> (i + 1)
            offset = me.peers - count
            coming = []
            for j in range(count):
                yield
                sent[j].wait_recv()
                add_rows(k_own.at[offset + j], [k_own.at[offset + j], k_bits.at[base + j]])
                if i + 1 < len(bits) and j < count // 2:
                    coming.append(mover.put(k_own.at[offset + j], k_bits.at[base + count + j], me.at(s=bits[i + 1])))
            base += count
            sent = coming
        end = k_own.at[me.peers - 1]
        copies = [mover.put(end.at[:, flip(zl, o)], k_near.at[o - 1], me.at(zl=o)) for o in range(1, me.near)]
        yield
        for copy in copies:
            copy.wait_recv()
        add_rows(end.at[:, zl], [end.at[:, zl]] + [k_near.at[o - 1] for o in range(1, me.near)])
        copies = [mover.put(end.at[flip(zh, o), zl], k_far.at[o - 1], me.at(zh=o)) for o in range(1, me.far)]
        yield
        for copy in copies:
            copy.wait_recv()
        add_rows(ok_ref, [end.at[zh, zl]] + [k_far.at[o - 1] for o in range(1, me.far)])

    def small_path():
        turns = [me.at(c=1)] + [me.at(zl=o) for o in bits_of(me.near)]
        turns += [me.at(s=o) for o in bits] + [me.at(zh=o) for o in bits_of(me.far)]
        u_box[0] = u_ref[...]
        u_box[0, 6:7, : p_ref.shape[1]] = p_ref[...] / gain_ref[...]
        for i, device in enumerate(turns):
            copy = mover.put(u_box.at[2 * i], u_box.at[2 * i + 1], device)
            yield
            copy.wait_recv()
            u_box[2 * i + 2] = u_box[2 * i] + u_box[2 * i + 1]
        ou_ref[...] = u_box[2 * len(turns)]

    coming_n, coming_b = [], []
    grads = (gn_ref, n_own, n_box, n_near, og_ref)
    branch = (b_ref, b_own, b_box, b_near, ob_ref)
    orders = lambda o: bits if o else bits[::-1]
    near_n = [rows_path(*grads, orders(o), o, coming_n) for o in range(1, me.near)]
    near_b = [rows_path(*branch, orders(o), o, coming_b, 1) for o in range(1, me.near)]
    own_n = rows_path(*grads, orders(0), 0, coming_n)
    own_b = rows_path(*branch, orders(0), 0, coming_b, 1)
    weights, keys, small = weight_path(), key_path(), small_path()
    turn(near_b + near_n + [weights, own_n, keys, own_b, small])
    turn([weights] * (me.far * me.peers) + [keys] * me.peers + [small])
    turn(near_b + near_n + [keys, own_b, small] + near_b + near_n + [keys, small, keys, own_b, own_n])
    run_paths(near_b + near_n + [keys, small, weights, own_b, own_n])
    mover.close()


def scatter(grads, gw, branch, small, products, gain):
    me = Place()
    peers, near, far = me.peers, me.near, me.far
    tokens, width = grads.shape[2:]
    stages = len(bits_of(peers)) + len(bits_of(near)) + len(bits_of(far)) + 1
    vm = lambda *shape: pltpu.VMEM(shape, bf16)
    boxes = lambda part: pltpu.VMEM((2 * stages + 1,) + part.shape, f32)
    keys = KEYS + STEP_PAD
    rows = gw.shape[4]
    block = (near, rows, gw.shape[5] - keys)
    kblock = (near, rows, keys)
    runs = 2 * (far if near > 1 else 1)
    copies = peers * near - 1 + (2 * far - 1) * peers + runs * (peers * near - 1)
    copies += 2 * peers - 1 + near - 1 + far - 1 + stages + peers // 2 * near - 1
    kept = peers * near + far * peers + runs + peers + near * peers // 4
    same = lambda part: jax.ShapeDtypeStruct(part.shape, part.dtype)
    return pl.pallas_call(
        scatter_kernel,
        out_shape=[
            jax.ShapeDtypeStruct((tokens, width), f32),
            jax.ShapeDtypeStruct((rows, 2 * E), bf16),
            jax.ShapeDtypeStruct((tokens, width), f32),
            jax.ShapeDtypeStruct((rows, keys), f32),
            same(small),
        ],
        in_specs=[HBM] * 3 + [VMEM] * 3,
        out_specs=[VMEM, HBM, VMEM, VMEM, VMEM],
        scratch_shapes=[
            vm(near, peers // 2, tokens, width), vm(near, peers - 1, tokens, width), vm(max(near - 1, 1), tokens, width),
            vm(near, peers // 2, tokens, width), vm(near, peers // 2 - 1, tokens, width), vm(max(near - 1, 1), tokens, width),
            vm(far, peers, *block), vm(far, peers, *block), vm(max(far - 1, 1), peers, *block),
            vm(peers, far, *kblock), vm(peers, far, *kblock), vm(max(near - 1, 1), far, *kblock[1:]),
            vm(max(far - 1, 1), *kblock[1:]), vm(peers - 1, far, *kblock), boxes(small),
        ]
        + sems(copies, kept),
        compiler_params=remote_params(2, 40),
        cost_estimate=pl.CostEstimate(flops=0, bytes_accessed=250 * 10**6, transcendentals=0),
        name="scatter_all",
    )(grads, gw, branch, small, products, gain)


class Early:
    def __init__(self, b_ref, go_ref, refs):
        self.b_out, self.o_out, self.b_own, self.b_box, self.o_own, self.o_box, self.o_far, send, recv, local = refs
        me = self.me = Place()
        mover = self.mover = Mover(send, recv, local)
        bits = bits_of(me.peers)
        self.rows, self.outs, self.far = [], [], []
        for o in range(me.near):
            order = bits if o else bits[::-1]
            at_zl = b_ref.at[flip(me.zl, o)]
            for j, left in enumerate(combos(order[1:])):
                put = mover.plan(at_zl.at[flip(me.s, order[0] ^ left)], self.b_box.at[o, j], me.at(s=order[0]))
                self.rows.append((put, mover.plan_keep(at_zl.at[flip(me.s, left)], self.b_own.at[o, j]), (o, j)))
        for o in range(me.far):
            put = mover.plan(go_ref.at[flip(me.zh, o), 1 - me.c], self.o_box.at[o], me.at(c=1))
            self.outs.append((put, mover.plan_keep(go_ref.at[flip(me.zh, o), me.c], self.o_own.at[o])))
        for o in range(1, me.far):
            self.far.append(mover.plan(self.o_own.at[o], self.o_far.at[o - 1], me.at(zh=o)))

    def start(self):
        _, far, sibling = self.me.partners()
        bits = bits_of(self.me.peers)
        greet([self.me.at(s=bit) for bit in sorted({bits[0], bits[-1]})] + far + sibling)
        for put, load in self.outs:
            put.start()
            load.start()
        for put, load, _ in self.rows:
            put.start()
            load.start()

    def middle(self):
        for o, (put, load) in enumerate(self.outs):
            load.wait()
            put.wait_recv()
            if o:
                add_rows(self.o_own.at[o], [self.o_own.at[o], self.o_box.at[o]])
                self.far[o - 1].start()

    def end(self):
        for put, load, at in self.rows:
            load.wait()
            put.wait_recv()
            add_rows(self.b_out.at[at], [self.b_own.at[at], self.b_box.at[at]])
        for put in self.far:
            put.wait_recv()
        add_rows(self.o_out, [self.o_own.at[0], self.o_box.at[0]] + [self.o_far.at[o] for o in range(self.me.far - 1)])
        self.mover.close()


def finish_kernel(
    x_ref, cot_ref, gain_ref, inv_ref, go_ref, og_ref, ob_ref, ow_ref, ok_ref, u_ref,
    out_ref, gx_ref, gw_ref, gs_ref, oo_ref, gc_ref, gb_ref, gp_ref, gn_ref, g0_ref, g1_ref, g2_ref,
):
    x = x_ref[0].astype(f32)
    out_ref[0] = (x + ob_ref[...]).astype(bf16)
    inv = inv_ref[:, :1]
    scaled = og_ref[...] * gain_ref[...]
    dot = jnp.mean(scaled * x, axis=1, keepdims=True)
    gx_ref[0] = inv * scaled - x * (inv * inv * inv * dot) + cot_ref[0].astype(f32)
    gw_ref[:, : 2 * E] = ow_ref[...].astype(f32)
    gw_ref[:, 2 * E :] = ok_ref[:, :KEYS]
    gs_ref[...] = ok_ref[:, KEYS : KEYS + H]
    oo_ref[...] = go_ref[...]
    gc_ref[...] = u_ref[:CONV, :]
    gb_ref[...] = u_ref[CONV : CONV + 1, :]
    gn_ref[...] = u_ref[5:6, :E]
    gp_ref[...] = u_ref[6:7, : gp_ref.shape[1]]
    for i, ref in enumerate((g0_ref, g1_ref, g2_ref)):
        ref[...] = u_ref[7:8, i * LANES : i * LANES + H]


def finish(inputs, cotangent, gain, inv, grad_out, sums):
    tokens, width = inputs.shape[1:]
    og, ow, ob, ok, u = sums
    shape = lambda *dims: jax.ShapeDtypeStruct(dims, f32)
    rows = ow.shape[0]
    return pl.pallas_call(
        finish_kernel,
        out_shape=[
            jax.ShapeDtypeStruct(inputs.shape, bf16), shape(*inputs.shape), shape(rows, 2 * E + KEYS), shape(rows, H),
            shape(*grad_out.shape), shape(CONV, E + KEYS), shape(1, E + KEYS), shape(1, width), shape(1, E), shape(1, H), shape(1, H), shape(1, H),
        ],
        in_specs=[VMEM] * 10,
        out_specs=[VMEM] * 12,
        compiler_params=pltpu.CompilerParams(vmem_limit_bytes=32 * 2**20),
        name="finish",
    )(inputs, cotangent, gain, inv, grad_out, og, ob, ow, ok, u)


def body(
    inputs, cotangent, doc_lengths, head_width, pre_gain, in_weight, step_weight, conv_weight, conv_bias,
    step_bias, decay_log, skip_gain, norm_gain, out_weight,
):
    me = Place()
    peers, near, far = me.peers, me.near, me.far
    tokens, width = inputs.shape[1:]
    span = tokens * peers
    length = span * near
    heads = H // (peers * near)
    inner = heads * P_SIZE
    rows = in_weight.shape[0]
    row = lambda vector: vector[None, :]

    in_w, out_w, normed, cot_all, meta, inv = gather(
        in_weight, out_weight, cotangent, inputs, row(pre_gain), step_weight, doc_lengths, head_width
    )
    in_w = in_w.reshape(width, -1)
    normed = normed.reshape(length, width)

    params = (conv_weight, row(conv_bias), row(norm_gain), row(step_bias), row(decay_log), row(skip_gain))
    *kept, gated, states, part, chan, head_vec, cot_all, out_w, projected = mixer_forward(
        meta, normed, in_w, params, cot_all, out_w, span, heads
    )
    out_w = out_w.reshape(inner, width)
    cot_all = cot_all.reshape(length, width)
    grad_mixed = mm(cot_all, out_w, NT)
    sums, mixed = cube_total(part, gated, chan, grad_mixed)
    branch = mm(mixed, out_w, NN).astype(bf16)
    grad_out = mm(mixed, cot_all, TN).astype(bf16)
    grad_cols, small, branch, grad_out_weight = mixer_backward(
        meta, projected, grad_mixed, chan, conv_weight, head_vec, (*kept, states), sums,
        branch.reshape(near, peers, tokens, width), grad_out.reshape(far, 2, -1, width), span, heads,
    )
    grad_in = mm(normed, grad_cols, TN).astype(bf16)
    grad_normed = mm(grad_cols, in_w, NT)
    products = jnp.sum(grad_normed * normed.astype(f32), axis=0)
    summed = scatter(
        grad_normed.astype(bf16).reshape(near, peers, tokens, width),
        grad_in.reshape(peers, far, near, 2, rows, -1),
        branch,
        small,
        row(products),
        row(pre_gain),
    )
    outs = finish(inputs, cotangent, row(pre_gain), inv, grad_out_weight, summed)
    output, grad_inputs, grad_in_weight, grad_step_weight, grad_out_weight, grad_conv_weight = outs[:6]
    grad_conv_bias, grad_pre_gain, grad_norm_gain, grad_step_bias, grad_decay_log, grad_skip = [o[0] for o in outs[6:]]
    return (
        output, grad_inputs, grad_pre_gain, grad_in_weight, grad_step_weight, grad_conv_weight, grad_conv_bias,
        grad_step_bias, grad_decay_log, grad_skip, grad_norm_gain, grad_out_weight,
    )


def solution(mesh):
    both = P(("seq", "batch"), None)
    tok = P("batch", "seq", None)
    in_specs = (
        tok, tok, P("batch", None), P("batch"), P(), both, both, P(), P(), P(), P(), P(), P(), both,
    )
    out_specs = (tok, tok, P(), both, both, P(), P(), P(), P(), P(), P(), both)
    return jax.shard_map(body, mesh=mesh, in_specs=in_specs, out_specs=out_specs, check_vma=False)
```
